32 devices in a mesh: ctx: 8 (over z, x), fsdp: 4 (over y, core).
Axes of the slice: x: 2, y: 2, z: 4, core: 2. Of those that a mesh axis runs over, the one named last changes fastest.
Arguments:
- tokens: bfloat16 [4, 1024, 1536], P('fsdp', 'ctx'), may hold values from -6 to 6
- query_key_value_weight: bfloat16 [1536, 2560], P('fsdp'), may hold values from -0.15625 to 0.15625
- output_weight: bfloat16 [1536, 1536], P('fsdp'), may hold values from -0.75 to 0.75
- routing_weight: bfloat16 [1536, 8], P('fsdp'), may hold values from -0.109375 to 0.109375
- gain_attn: bfloat16 [1536], P('fsdp'), may hold values from 0.5 to 1.5
- gain_moe: bfloat16 [1536], P('fsdp'), may hold values from 0.5 to 1.5
- w_experts: bfloat16 [8, 1536, 3072], P('fsdp'), may hold values from -0.15625 to 0.15625
- doc_starts: int32 [4, 8], P('fsdp'), may hold values from 0 to 1023, as said below
- routes: int32 [4, 1024, 2], P('fsdp', 'ctx'), may hold values from 0 to 7, all different within a row; in each aligned block of 128 rows (0 to 127, 128 to 255, ..., all dimensions but the last counted through in order) at most 64 rows name the same one
- cotangent: bfloat16 [4, 1024, 1536], P('fsdp', 'ctx'), may hold values from -6 to 6
Outputs:
- output: bfloat16 [4, 1024, 1536], P('fsdp', 'ctx')
- d_tokens: bfloat16 [4, 1024, 1536], P('fsdp', 'ctx')
- d_w_qkv: float32 [1536, 2560], P('fsdp')
- d_w_out: float32 [1536, 1536], P('fsdp')
- d_w_router: float32 [1536, 8], P('fsdp')
- d_gain_attn: float32 [1536], P('fsdp')
- d_gain_moe: float32 [1536], P('fsdp')
- d_w_experts: float32 [8, 1536, 3072], P('fsdp')
The draws below stay inside these ranges and needn't reach their ends.
Inputs may be any that keep to these rules, and one draw needn't show every extreme that they name: `doc_starts`: in each stream the starts begin with 0 and rise strictly; one document begins within the first 128 positions and ends within the last 128. `routes`: A token's two experts differ. Among the 128 tokens of one device each expert is named at most 64 times, a bound that some block reaches.
All inputs are finite; a program needn't handle non-finite values.
Results may differ from the reference program's by a relative error of at most 0.025.
Values may be sent and summed in bfloat16 or wider, within the bound.
No kernel may reach another device: no remote copies, remote signals or barrier semaphores. Data moves between devices by JAX's collectives and lax.ppermute only.
A program may use at most 640 MiB of HBM per device.

```python
import math
import jax
import jax.numpy as jnp
import numpy as np
from jax import lax

D = 1536
HQ = 24
HK = 8
HD = 64
FF = 1024
EXPERTS = 8
TOP = 2
NDOC = 8
TOK_DEV = 128
STREAMS = 4
STREAM = 1024
CAP = 64
QKV = 2560


def draw_doc_starts(key, part):
    key = jax.random.fold_in(key, 7)

    def one_stream(stream_key):
        head_key, tail_key = jax.random.split(stream_key)
        head_starts = 1 + jax.random.permutation(head_key, TOK_DEV - 1)[:3]
        tail_starts = STREAM - TOK_DEV + 1 + jax.random.permutation(tail_key, TOK_DEV - 1)[:NDOC - 4]
        return jnp.concatenate([jnp.zeros((1,), jnp.int32), jnp.sort(head_starts).astype(jnp.int32), jnp.sort(tail_starts).astype(jnp.int32)])
    return jax.vmap(one_stream)(jax.random.split(key, STREAMS))


def shard_levels(own_key, shape, cuts, smallest, high):
    level = 1.0
    for axis_at, parts in cuts:
        heights = jax.random.uniform(jax.random.fold_in(jax.random.fold_in(own_key, 6), axis_at), (parts,), jnp.float32, smallest / len(cuts), high / len(cuts))
        level = level * jnp.repeat(jnp.exp(heights), shape[axis_at] // parts).reshape((-1,) + (1,) * (len(shape) - 1 - axis_at))
    return level


def shared_out(key, own, number, rows, count, top, reach, lean):
    order = jax.random.permutation(key, count)
    heavy_load, common = load_shares(count, rows * top, reach, lean, True), load_shares(count, rows * top, reach, lean, False)
    places = jnp.arange(count)

    def named(tallies, turn):
        used = int((tallies > 0).sum())
        fixed = max(1, used // 4)
        moved = fixed + (places - fixed + turn * (used - fixed)) % max(1, count - fixed)
        return jnp.zeros((count,), jnp.int32).at[order[jnp.where(places < fixed, places, moved)]].set(jnp.asarray(tallies, jnp.int32))

    tallies = jnp.where(number % 4 == 0, named(heavy_load, number // 4), named(common, number - number // 4 - 1))
    mixed = jax.random.permutation(jax.random.fold_in(own, 3), count)
    source_of, taker = mixed[0:count // 2 * 2:2], mixed[1:count // 2 * 2:2]
    margin = jnp.minimum(tallies[source_of] - 1, reach - tallies[taker]) // 2
    margin = jnp.where((source_of == order[0]) | (taker == order[0]) | (tallies[taker] == 0), 0, jnp.maximum(margin, 0))
    moved = jax.random.randint(jax.random.fold_in(own, 4), (count // 2,), 0, 1 << 20) % (margin + 1)
    tallies = tallies.at[source_of].add(-moved).at[taker].add(moved)
    labels = jnp.searchsorted(jnp.cumsum(tallies), jnp.arange(rows * top), side="right").astype(jnp.int32)
    grid = labels.reshape(top, rows).T
    grid = grid[jax.random.permutation(jax.random.fold_in(own, 1), rows)]
    turn = jax.random.randint(jax.random.fold_in(own, 2), (rows, 1), 0, top)
    return jnp.take_along_axis(grid, (jnp.arange(top)[None, :] + turn) % top, axis=1)


def load_shares(count, total, limit, skew, full):
    weights = [(1 << 20) // math.isqrt(standing ** skew) + 1 for standing in range(1, count + 1)]
    largest = limit if full else min(limit, max(-(-total // count), total * weights[0] // sum(weights)))
    least = 1 if total - largest >= count - 1 else 0
    holding, rest = [largest] + [least] * (count - 1), total - largest - least * (count - 1)
    while rest > 0:
        movable = [i for i in range(1, count) if holding[i] < largest] or [i for i in range(1, count) if holding[i] < limit]
        mass, remaining = sum([weights[i] for i in movable]), rest
        for i in movable:
            more = min(limit - holding[i], max(1, remaining * weights[i] // mass), rest)
            holding[i] = holding[i] + more
            rest = rest - more
    return np.array(holding)


def scatter_about(rng, shape, width, most, cuts=(), kind=jnp.bfloat16):
    values = jax.random.normal(rng, shape, jnp.float32) * width
    if len(cuts) > 0:
        values = shard_levels(rng, shape, cuts, -0.22, 0.18) * values
    return jnp.clip(values, min=-most, max=most).astype(kind)


def setup_inputs(seed: int = 0) -> dict:
    splits = jax.random.split(jax.random.key(seed), 11)
    tokens = scatter_about(splits[0], (STREAMS, STREAM, D), 1.0, 6.0, ((0, 4), (1, 8)))
    query_key_value_weight = scatter_about(splits[1], (D, QKV), D ** -0.5, 0.15625, ((0, 4),))
    output_weight = scatter_about(splits[2], (HQ * HD, D), HD ** -0.5, 0.75, ((0, 4),))
    routing_weight = scatter_about(splits[3], (D, EXPERTS), (2 * D) ** -0.5, 0.109375, ((0, 4),))
    gain_attn = jnp.clip(1.0 + 0.1 * jax.random.normal(splits[4], (D,), jnp.float32), 0.5, 1.5).astype(jnp.bfloat16)
    gain_moe = jnp.clip(1.0 + 0.1 * jax.random.normal(splits[5], (D,), jnp.float32), 0.5, 1.5).astype(jnp.bfloat16)
    w_experts = scatter_about(splits[6], (EXPERTS, D, 3 * FF), D ** -0.5, 0.15625, ((0, 4),))
    doc_starts = draw_doc_starts(jax.random.fold_in(splits[10], 71), 0)
    routes_keys = jax.random.split(jax.random.fold_in(splits[8], 1), STREAMS * STREAM // TOK_DEV)
    routes_turns = jax.random.permutation(jax.random.fold_in(splits[8], 3), STREAMS * STREAM // TOK_DEV)
    routes = jax.vmap(lambda own, number: shared_out(jax.random.fold_in(splits[8], 2), own, number, TOK_DEV, EXPERTS, TOP, CAP, 1))(routes_keys, routes_turns).reshape((STREAMS, STREAM, TOP))
    cotangent = scatter_about(splits[9], (STREAMS, STREAM, D), 1.0, 6.0, ((0, 4), (1, 8)))
    return dict(tokens=tokens, query_key_value_weight=query_key_value_weight, output_weight=output_weight, routing_weight=routing_weight, gain_attn=gain_attn, gain_moe=gain_moe, w_experts=w_experts, doc_starts=doc_starts, routes=routes, cotangent=cotangent)


EXACT_MATMUL = lax.Precision.HIGHEST
NORM_EPS = 1e-05
MASK_NEG = -1e+30

@jax.custom_vjp
def low(v):
    return lax.optimization_barrier(v.astype(jnp.bfloat16)).astype(jnp.float32)

@jax.custom_vjp
def low_back(v):
    return v

def low_keep(v):
    return (low(v), None)

def low_pass(kept, grad):
    return (grad,)

def back_keep(v):
    return (v, None)

def back_low(kept, grad):
    return (low(grad),)
low.defvjp(low_keep, low_pass)
low_back.defvjp(back_keep, back_low)

def rms_norm(values, gain_vec):
    return values * lax.rsqrt(lax.optimization_barrier(jnp.mean(values * values, axis=-1, keepdims=True)) + NORM_EPS) * gain_vec

def doc_index(doc_bounds, positions):
    hits = (positions[:, None] >= doc_bounds[None, :]).astype(jnp.int32)
    return lax.optimization_barrier(jnp.sum(hits, axis=1)).astype(jnp.int32)

def route_slots(choices):
    flat_ids = choices.reshape(-1).astype(jnp.int32)
    one_hot = (flat_ids[:, None] == jnp.arange(EXPERTS, dtype=jnp.int32)[None, :]).astype(jnp.int32)
    running = jnp.cumsum(one_hot, axis=0).astype(jnp.int32)
    ranking = lax.optimization_barrier(jnp.sum((running - 1) * one_hot, axis=1)).astype(jnp.int32)
    return (flat_ids * CAP + ranking).astype(jnp.int32)

def slot_owner(route_slot):
    route_total = route_slot.shape[0]
    slot_source = jnp.zeros((EXPERTS * CAP,), jnp.int32).at[route_slot].set(jnp.arange(route_total, dtype=jnp.int32))
    slot_filled = jnp.zeros((EXPERTS * CAP,), jnp.int32).at[route_slot].set(jnp.ones((route_total,), jnp.int32))
    return (slot_source, slot_filled)

def attention(queries, kv_pairs, doc_starts):
    length = queries.shape[1]
    q_block = math.gcd(length, 512)
    block_count = length // q_block
    head_group = HQ // HK
    kv_width = HK * HD
    zero_index = jnp.zeros((), jnp.int32)

    def one_block(index):
        stream = (index // block_count).astype(jnp.int32)
        first_row = (index % block_count * q_block).astype(jnp.int32)
        q_rows = lax.dynamic_slice(queries, (stream, first_row, zero_index), (1, q_block, HQ * HD))[0]
        q_rows = q_rows.reshape(q_block, HK, head_group, HD)
        stream_pairs = lax.dynamic_index_in_dim(kv_pairs, stream, 0, keepdims=False)
        key_rows = stream_pairs[:, :kv_width].reshape(length, HK, HD)
        value_rows = stream_pairs[:, kv_width:].reshape(length, HK, HD)
        doc_bounds = lax.dynamic_index_in_dim(doc_starts, stream, 0, keepdims=False)
        query_pos = first_row + jnp.arange(q_block, dtype=jnp.int32)
        key_pos = jnp.arange(length, dtype=jnp.int32)
        allowed = (key_pos[None, :] <= query_pos[:, None]) & (doc_index(doc_bounds, key_pos)[None, :] == doc_index(doc_bounds, query_pos)[:, None])
        scores = low_back(jnp.einsum('tkgd,skd->kgts', q_rows, key_rows, precision=EXACT_MATMUL) * HD ** (-0.5))
        scores = jnp.where(allowed, scores, MASK_NEG)
        highest = lax.optimization_barrier(jnp.max(scores, axis=-1, keepdims=True))
        weights = jnp.exp(scores - highest)
        weights = weights / lax.optimization_barrier(jnp.sum(weights, axis=-1, keepdims=True))
        result = jnp.einsum('kgts,skd->tkgd', low(weights), value_rows, precision=EXACT_MATMUL)
        return result.reshape(q_block, HQ * HD)
    blocks = lax.map(jax.checkpoint(one_block), jnp.arange(queries.shape[0] * block_count, dtype=jnp.int32))
    return blocks.reshape(queries.shape[0], length, HQ * HD)

def experts(rows, choices, kernel):
    device_total = rows.shape[0]
    route_slot = jax.vmap(route_slots)(choices)
    slot_source, slot_filled = jax.vmap(slot_owner)(route_slot)

    def one_expert(expert):
        offset = (expert * CAP).astype(jnp.int32)
        source_tok = lax.dynamic_slice_in_dim(slot_source, offset, CAP, 1) // TOP
        live_slot = lax.dynamic_slice_in_dim(slot_filled, offset, CAP, 1)
        taken = jax.vmap(lambda table, picks: table[picks])(rows, source_tok)
        taken = low_back(jnp.where(live_slot[:, :, None] > 0, taken, 0.0))
        weight = lax.dynamic_index_in_dim(kernel, expert, 0, keepdims=False)
        both = low_back(jnp.einsum('ncd,df->ncf', taken, weight[:, :2 * FF], precision=EXACT_MATMUL))
        hidden = low(jax.nn.silu(both[..., :FF]) * both[..., FF:])
        return low(low_back(jnp.einsum('ncf,df->ncd', hidden, weight[:, 2 * FF:], precision=EXACT_MATMUL)))
    results = lax.map(jax.checkpoint(one_expert), jnp.arange(EXPERTS, dtype=jnp.int32))
    expert_of = route_slot // CAP
    ranking = route_slot % CAP
    device_ids = jnp.arange(device_total, dtype=jnp.int32)[:, None]
    flat_index = (expert_of * device_total + device_ids) * CAP + ranking
    flat_out = results.reshape(-1, D)[flat_index.reshape(-1)]
    return flat_out.reshape(device_total, TOK_DEV, TOP, D)

def layer(input_rows, query_key_value_weight, output_weight, routing_weight, gain_attn, gain_moe, w_experts, doc_starts, routes):
    streams = input_rows.shape[0]
    length = input_rows.shape[1]
    normalized_rows = low(rms_norm(input_rows, gain_attn))
    projected = low(low_back(jnp.einsum('zvp,pi->zvi', normalized_rows, query_key_value_weight, precision=EXACT_MATMUL)))
    attention_result = attention(projected[..., :HQ * HD], projected[..., HQ * HD:], doc_starts)
    attention_result = low(low_back(attention_result))
    midway_state = input_rows + low_back(jnp.einsum('zat,tb->zab', attention_result, output_weight, precision=EXACT_MATMUL))
    second_branch = low(rms_norm(midway_state, gain_moe))
    router_scores = low_back(jnp.einsum('zvp,pi->zvi', second_branch, routing_weight, precision=EXACT_MATMUL))
    picked = jnp.take_along_axis(router_scores, routes, axis=-1)
    gates = jax.nn.softmax(picked, axis=-1)
    device_total = streams * (length // TOK_DEV)
    routed = experts(second_branch.reshape(device_total, TOK_DEV, D), routes.reshape(device_total, TOK_DEV, TOP), w_experts)
    branch = lax.optimization_barrier(jnp.sum(gates.reshape(device_total, TOK_DEV, TOP, 1) * routed, axis=2))
    return midway_state + branch.reshape(streams, length, D)

def reference(tokens, query_key_value_weight, output_weight, routing_weight, gain_attn, gain_moe, w_experts, doc_starts, routes, cotangent):
    floats = tuple((value.astype(jnp.float32) for value in (tokens, query_key_value_weight, output_weight, routing_weight, gain_attn, gain_moe, w_experts)))

    def forward(input_rows, qkv_w, out_w, router_w, attn_g, moe_g, expert_w):
        return layer(input_rows, qkv_w, out_w, router_w, attn_g, moe_g, expert_w, doc_starts, routes)
    result, pullback = jax.vjp(forward, *floats)
    grads = pullback(cotangent.astype(jnp.float32))
    return (result.astype(jnp.bfloat16), grads[0].astype(jnp.bfloat16), grads[1], grads[2], grads[3], grads[4], grads[5], grads[6])
```

```python
import jax
import jax.numpy as jnp
from jax import lax
from jax.sharding import PartitionSpec as P

HQ = 24
HK = 8
HD = 64
GROUP = HQ // HK
FF = 1024
EXPERTS = 8
CAP = 64
Q_COLS = HQ * HD
K_COLS = HK * HD
HEAD_COLS = GROUP * HD + 2 * HD
SMALL = 16

NORM_EPS = 1e-05
MASK_NEG = -1e30
BF = jnp.bfloat16
F32 = jnp.float32


def dot(a, b):
    return jnp.dot(a, b, preferred_element_type=F32)


def dot_t(a, b):
    return lax.dot_general(a, b, (((1,), (1,)), ((), ())), preferred_element_type=F32)


def t_dot(a, b):
    return lax.dot_general(a, b, (((0,), (0,)), ((), ())), preferred_element_type=F32)


def rms_factor(values):
    return lax.rsqrt(jnp.mean(values * values, axis=-1, keepdims=True) + NORM_EPS)


def rms_input_grad(values, factor, gain_vec, incoming):
    inner = incoming * gain_vec
    cubed = factor * factor * factor
    return factor * inner - values * cubed * jnp.mean(inner * values, axis=-1, keepdims=True)


def doc_index(doc_bounds, positions):
    hits = (positions[:, None] >= doc_bounds[None, :]).astype(jnp.int32)
    return jnp.sum(hits, axis=1)


def to_all(value, axis):
    return lax.all_to_all(value, axis, 0, 0, tiled=True)


def gathered(value, axis):
    return lax.all_gather(value, axis, axis=0, tiled=True)


def reduced(value, axis):
    return lax.psum_scatter(value, axis, scatter_dimension=0, tiled=True)


def route_tables(routes, first, count):
    ids = jnp.arange(EXPERTS, dtype=jnp.int32)
    picked = jnp.any(routes[..., None] == ids, axis=-2)
    mine = jnp.any(routes[..., None] == (first + jnp.arange(count, dtype=jnp.int32)), axis=-2)
    taken = mine.astype(jnp.int32)
    rank = jnp.cumsum(taken, axis=-2) - taken
    return picked, mine, rank


def slot_matrix(mine, rank):
    slots = jnp.arange(CAP, dtype=jnp.int32)[:, None]
    mine_t = jnp.swapaxes(mine, -1, -2)[:, :, None, :]
    rank_t = jnp.swapaxes(rank, -1, -2)[:, :, None, :]
    return (mine_t & (rank_t == slots)).astype(BF)


def gate_table(second, router, picked):
    logits = jnp.einsum("btd,de->bte", second, router, preferred_element_type=F32)
    logits = jnp.where(picked, logits, MASK_NEG)
    return jax.nn.softmax(logits, axis=-1)


def attention_forward(q, k, v, allowed):
    length = q.shape[0]
    scores = jnp.einsum(
        "tgd,sd->gts", q.reshape(length, GROUP, HD), k, preferred_element_type=F32
    ) * HD ** (-0.5)
    highest = jnp.max(jnp.where(allowed, scores, MASK_NEG), axis=-1, keepdims=True)
    weights = jnp.where(allowed, jnp.exp(scores - highest), 0.0)
    total = jnp.sum(weights, axis=-1, keepdims=True)
    total = jnp.where(total == 0.0, 1.0, total)
    log_norm = highest + jnp.log(total)
    probs = (weights / total).astype(BF)
    attended = jnp.einsum("gts,sd->tgd", probs, v, preferred_element_type=F32)
    return attended.reshape(length, GROUP * HD), log_norm


def attention_backward(q, k, v, allowed, log_norm, attended, grads):
    length = q.shape[0]
    scale = HD ** (-0.5)
    q3 = q.reshape(length, GROUP, HD)
    g3 = grads.reshape(length, GROUP, HD)
    delta = jnp.sum(g3.astype(F32) * attended.reshape(length, GROUP, HD), axis=-1).T
    scores = jnp.einsum("tgd,sd->gts", q3, k, preferred_element_type=F32) * scale
    probs = jnp.where(allowed, jnp.exp(scores - log_norm), 0.0)
    d_probs = jnp.einsum("tgd,sd->gts", g3, v, preferred_element_type=F32)
    d_scores = (probs * (d_probs - delta[..., None])).astype(BF)
    d_q = jnp.einsum("gts,sd->tgd", d_scores, k, preferred_element_type=F32) * scale
    d_k = jnp.einsum("gts,tgd->sd", d_scores, q3, preferred_element_type=F32) * scale
    d_v = jnp.einsum("gts,tgd->sd", probs.astype(BF), g3, preferred_element_type=F32)
    return jnp.concatenate([d_q.reshape(length, GROUP * HD), d_k, d_v], axis=1).astype(BF)


def expert_pass(rows, d_out, w_experts):
    both = jnp.einsum("erd,edf->erf", rows, w_experts[:, :, : 2 * FF], preferred_element_type=F32)
    gate, up = both[..., :FF], both[..., FF:]
    sigma = jax.nn.sigmoid(gate)
    hidden = (gate * sigma * up).astype(BF)
    out = jnp.einsum(
        "erf,edf->erd", hidden, w_experts[:, :, 2 * FF :], preferred_element_type=F32
    ).astype(BF)
    d_hidden = jnp.einsum(
        "erd,edf->erf", d_out, w_experts[:, :, 2 * FF :], preferred_element_type=F32
    )
    d_both = jnp.concatenate(
        [d_hidden * up * sigma * (1.0 + gate * (1.0 - sigma)), d_hidden * gate * sigma], axis=-1
    ).astype(BF)
    d_rows = jnp.einsum(
        "erf,edf->erd", d_both, w_experts[:, :, : 2 * FF], preferred_element_type=F32
    ).astype(BF)
    return out, d_rows


def expert_weight_grad(rows, d_out, w_experts):
    both = jnp.einsum("erd,edf->erf", rows, w_experts[:, :, : 2 * FF], preferred_element_type=F32)
    gate, up = both[..., :FF], both[..., FF:]
    sigma = jax.nn.sigmoid(gate)
    hidden = (gate * sigma * up).astype(BF)
    d_hidden = jnp.einsum(
        "erd,edf->erf", d_out, w_experts[:, :, 2 * FF :], preferred_element_type=F32
    )
    d_both = jnp.concatenate(
        [d_hidden * up * sigma * (1.0 + gate * (1.0 - sigma)), d_hidden * gate * sigma], axis=-1
    ).astype(BF)
    inward = jnp.einsum("erd,erf->edf", rows, d_both, preferred_element_type=F32)
    down = jnp.einsum("erd,erf->edf", d_out, hidden, preferred_element_type=F32)
    return jnp.concatenate([inward, down], axis=-1)


def per_device(
    tokens,
    query_key_value_weight,
    output_weight,
    routing_weight,
    gain_attn,
    gain_moe,
    w_experts,
    doc_starts,
    routes,
    cotangent,
):
    spans = lax.axis_size("ctx")
    shards = lax.axis_size("fsdp")
    here = lax.axis_index("ctx")
    shard = lax.axis_index("fsdp")
    tok_count, width = tokens.shape[1:]
    local_experts = w_experts.shape[0]
    copies = spans // HK
    head = here // copies
    length = spans * tok_count
    blocks = spans * shards
    everyone = ("ctx", "fsdp")

    shard_rows = query_key_value_weight.shape[0]
    head_w = jnp.concatenate(
        [
            lax.dynamic_slice_in_dim(query_key_value_weight, head * GROUP * HD, GROUP * HD, 1),
            lax.dynamic_slice_in_dim(query_key_value_weight, Q_COLS + head * HD, HD, 1),
            lax.dynamic_slice_in_dim(query_key_value_weight, Q_COLS + K_COLS + head * HD, HD, 1),
            routing_weight,
            gain_attn[:, None],
            gain_moe[:, None],
        ],
        axis=1,
    )
    head_w = gathered(head_w, "fsdp")
    router_w = head_w[:, HEAD_COLS : HEAD_COLS + EXPERTS]
    attn_g = head_w[:, HEAD_COLS + EXPERTS].astype(F32)
    moe_g = head_w[:, HEAD_COLS + EXPERTS + 1].astype(F32)
    head_w = head_w[:, :HEAD_COLS]
    out_w = gathered(output_weight, "fsdp")
    qkv_w = gathered(query_key_value_weight, "fsdp")

    route_cols = jnp.pad(routes[0].astype(BF), ((0, 0), (0, 126)))
    grads_all = gathered(jnp.concatenate([cotangent[0], route_cols], axis=1), everyone)
    routes_all = grads_all[:, width : width + 2].astype(jnp.int32).reshape(blocks, tok_count, 2)
    grads_all = grads_all[:, :width].reshape(blocks, tok_count, width)

    stream = gathered(tokens[0], "ctx")
    stream_f = stream.astype(F32)
    normed = (stream_f * rms_factor(stream_f) * attn_g).astype(BF)
    mixed = dot(normed, head_w).astype(BF)
    q = mixed[:, : GROUP * HD]
    k = mixed[:, GROUP * HD : GROUP * HD + HD]
    v = mixed[:, GROUP * HD + HD :]
    pos = jnp.arange(length, dtype=jnp.int32)
    docs = doc_index(doc_starts[0], pos)
    active = (pos // tok_count) % copies == here % copies
    allowed = (pos[None, :] <= pos[:, None]) & (docs[None, :] == docs[:, None]) & active[:, None]
    attended, log_norm = attention_forward(q, k, v, allowed)
    attended_low = attended.astype(BF)
    attended_all = gathered(attended_low, "ctx").reshape(HK, copies, length, GROUP * HD)
    if copies > 1:
        attended_all = jnp.sum(attended_all, axis=1)
    attended_all = attended_all.reshape(HK, length, GROUP * HD)

    own = to_all(attended_low, "ctx").reshape(HK, copies, tok_count, GROUP * HD)
    own = jnp.sum(own, axis=1) if copies > 1 else own[:, 0]
    own = own.transpose(1, 0, 2).reshape(tok_count, Q_COLS)
    x = tokens[0].astype(F32)
    middle = x + dot(own, out_w)
    second_factor = rms_factor(middle)
    second = (middle * second_factor * moe_g).astype(BF)

    second_near = gathered(second, "fsdp").reshape(shards, tok_count, width)
    first_expert = shard * local_experts
    picked, mine, rank = route_tables(routes_all, first_expert, local_experts)

    def near(table):
        return lax.dynamic_slice_in_dim(table, here * shards, shards, 0)

    hot = slot_matrix(mine, rank)
    hot_near = near(hot)
    grads_near = near(grads_all)
    gates_near = lax.dynamic_slice_in_dim(
        gate_table(second_near, router_w, near(picked)), first_expert, local_experts, 2
    )

    def gather_rows(table, onehot):
        rows = jnp.einsum("best,btd->ebsd", onehot, table, preferred_element_type=F32)
        return rows.reshape(local_experts, -1, width)

    def slot_gates(gates, onehot):
        found = jnp.sum(onehot.astype(F32) * jnp.swapaxes(gates, 1, 2)[:, :, None, :], axis=-1)
        return found.swapaxes(0, 1).reshape(local_experts, -1, 1)

    near_rows = gather_rows(second_near, hot_near).astype(BF)
    near_gates = slot_gates(gates_near, hot_near)
    near_grads = gather_rows(grads_near, hot_near)
    near_d_out = (near_gates * near_grads).astype(BF)
    expert_out, d_rows = expert_pass(near_rows, near_d_out, w_experts)
    d_gates = jnp.sum(near_grads * expert_out.astype(F32), axis=-1)
    gated = (near_gates * expert_out.astype(F32)).astype(BF)

    def scatter_rows(rows):
        rows = rows.reshape(local_experts, shards, CAP, width)
        return jnp.einsum("best,ebsd->btd", hot_near, rows, preferred_element_type=F32).astype(BF)

    d_gates = d_gates.reshape(local_experts, shards, CAP).swapaxes(0, 1)
    d_gates = jnp.sum(hot_near.astype(F32) * d_gates[..., None], axis=2).swapaxes(1, 2)
    d_gates = jnp.pad(d_gates, ((0, 0), (0, 0), (0, EXPERTS - local_experts)))
    d_gates = jnp.roll(d_gates, first_expert, axis=2)
    coarse = d_gates.astype(BF)
    fine = (d_gates - coarse.astype(F32)).astype(BF)
    fill = jnp.zeros((shards, tok_count, 128 - 2 * EXPERTS), BF)
    back = jnp.concatenate([scatter_rows(d_rows), coarse, fine, fill], axis=2)
    back = to_all(back.reshape(shards * tok_count, -1), "fsdp").reshape(shards, tok_count, -1)
    back = jnp.sum(back.astype(F32), axis=0)
    branch = reduced(scatter_rows(gated).reshape(shards * tok_count, width), "fsdp")
    output = (middle + branch.astype(F32)).astype(BF)

    grad = cotangent[0].astype(F32)
    d_gates = back[:, width : width + EXPERTS] + back[:, width + EXPERTS : width + 2 * EXPERTS]
    own_picked = jnp.any(routes[0][:, :, None] == jnp.arange(EXPERTS, dtype=jnp.int32), axis=1)
    gates = gate_table(second[None], router_w, own_picked[None])[0]
    d_picked = gates * (d_gates - jnp.sum(gates * d_gates, axis=-1, keepdims=True))
    d_logits = jnp.where(own_picked, d_picked, 0.0).astype(BF)
    d_router = t_dot(second, d_logits)
    d_second = dot_t(d_logits, router_w) + back[:, :width]
    d_gain_moe = jnp.sum(d_second * middle * second_factor, axis=0)
    d_middle = grad + rms_input_grad(middle, second_factor, moe_g, d_second)
    d_proj = d_middle.astype(BF)
    d_attended = dot_t(d_proj, out_w).astype(BF)

    chunk = width // spans
    d_attended = d_attended.reshape(tok_count, HK, 1, GROUP * HD)
    d_attended = jnp.broadcast_to(d_attended, (tok_count, HK, copies, GROUP * HD))
    d_attended = d_attended.reshape(tok_count, spans, GROUP * HD)
    sent = jnp.concatenate([d_attended, d_proj.reshape(tok_count, spans, chunk)], axis=2)
    sent = to_all(sent.swapaxes(0, 1).reshape(length, -1), "ctx")
    d_mixed = attention_backward(
        q, k, v, allowed, log_norm, attended, sent[:, : GROUP * HD]
    )
    d_head_w = t_dot(normed, d_mixed)
    d_out_w = jnp.einsum(
        "hte,td->hed", attended_all, sent[:, GROUP * HD :], preferred_element_type=F32
    ).reshape(Q_COLS, chunk)
    small = jnp.concatenate(
        [d_router, d_gain_moe[:, None], jnp.zeros((width, SMALL - EXPERTS - 1), F32)], axis=1
    )
    weight_grads = jnp.concatenate([d_head_w, d_out_w, small], axis=1).astype(BF)
    weight_grads = reduced(weight_grads, "fsdp")
    weight_grads = gathered(weight_grads, "ctx").reshape(spans, shard_rows, -1).astype(F32)
    by_head = weight_grads[:, :, :HEAD_COLS].reshape(HK, copies, shard_rows, HEAD_COLS)
    by_head = jnp.sum(by_head, axis=1).swapaxes(0, 1)

    def columns(part):
        return part.reshape(shard_rows, -1)

    d_qkv_w = jnp.concatenate(
        [
            columns(by_head[:, :, : GROUP * HD]),
            columns(by_head[:, :, GROUP * HD : GROUP * HD + HD]),
            columns(by_head[:, :, GROUP * HD + HD :]),
        ],
        axis=1,
    )
    d_out_w = columns(weight_grads[:, :, HEAD_COLS : HEAD_COLS + chunk].swapaxes(0, 1))
    small = jnp.sum(weight_grads[:, :, HEAD_COLS + chunk :], axis=0)
    d_router_w = small[:, :EXPERTS]
    d_gain_moe = small[:, EXPERTS]
    d_gain_attn = jnp.sum(
        d_qkv_w * query_key_value_weight.astype(F32), axis=1
    ) / gain_attn.astype(F32)

    d_home = to_all(d_mixed, "ctx").reshape(HK, copies, tok_count, HEAD_COLS)
    d_home = jnp.sum(d_home.astype(F32), axis=1).astype(BF) if copies > 1 else d_home[:, 0]
    d_home = d_home.swapaxes(0, 1)
    d_home = jnp.concatenate(
        [
            d_home[:, :, : GROUP * HD].reshape(tok_count, -1),
            d_home[:, :, GROUP * HD : GROUP * HD + HD].reshape(tok_count, -1),
            d_home[:, :, GROUP * HD + HD :].reshape(tok_count, -1),
        ],
        axis=1,
    )
    d_normed = dot_t(d_home, qkv_w)
    d_tokens = (d_middle + rms_input_grad(x, rms_factor(x), attn_g, d_normed)).astype(BF)

    second_all = gathered(second, everyone).reshape(blocks, tok_count, width)
    gates_all = lax.dynamic_slice_in_dim(
        gate_table(second_all, router_w, picked), first_expert, local_experts, 2
    )
    all_rows = gather_rows(second_all, hot).astype(BF)
    all_d_out = (slot_gates(gates_all, hot) * gather_rows(grads_all, hot)).astype(BF)
    d_w_experts = expert_weight_grad(all_rows, all_d_out, w_experts)
    return (
        output[None],
        d_tokens[None],
        d_qkv_w,
        d_out_w,
        d_router_w,
        d_gain_attn,
        d_gain_moe,
        d_w_experts,
    )


def solution(mesh):
    placed = (
        P("fsdp", "ctx", None),
        P("fsdp", None),
        P("fsdp", None),
        P("fsdp", None),
        P("fsdp"),
        P("fsdp"),
        P("fsdp", None, None),
        P("fsdp", None),
        P("fsdp", "ctx", None),
        P("fsdp", "ctx", None),
    )
    return jax.shard_map(
        per_device,
        mesh=mesh,
        in_specs=placed,
        out_specs=(
            P("fsdp", "ctx", None),
            P("fsdp", "ctx", None),
            P("fsdp", None),
            P("fsdp", None),
            P("fsdp", None),
            P("fsdp"),
            P("fsdp"),
            P("fsdp", None, None),
        ),
        check_vma=False,
    )
```

```python
import functools

import jax
import jax.numpy as jnp
from jax import lax
from jax.experimental import pallas as pl
from jax.experimental.pallas import tpu as pltpu
from jax.sharding import PartitionSpec as P

HQ = 24
HK = 8
HD = 64
GROUP = HQ // HK
FF = 1024
EXPERTS = 8
CAP = 64
Q_COLS = HQ * HD
K_COLS = HK * HD
HEAD_COLS = GROUP * HD + 2 * HD
SMALL = 16
LANES = 128
TILE = 256
CHUNK = 512
WINDOW = 2 * CAP + 16
SEGMENT = 32

NORM_EPS = 1e-05
MASK_NEG = -1e30
BF = jnp.bfloat16
F32 = jnp.float32


def dot(a, b):
    return jnp.dot(a, b, preferred_element_type=F32)


def dot_t(a, b):
    return lax.dot_general(a, b, (((1,), (1,)), ((), ())), preferred_element_type=F32)


def t_dot(a, b):
    return lax.dot_general(a, b, (((0,), (0,)), ((), ())), preferred_element_type=F32)


def iota(shape, axis):
    return lax.broadcasted_iota(jnp.int32, shape, axis)


def rms_factor(values):
    return lax.rsqrt(jnp.mean(values * values, axis=-1, keepdims=True) + NORM_EPS)


def rms_input_grad(values, factor, gain_vec, incoming):
    inner = incoming * gain_vec
    cubed = factor * factor * factor
    return factor * inner - values * cubed * jnp.mean(inner * values, axis=-1, keepdims=True)


def doc_index(doc_bounds, positions):
    hits = (positions[:, None] >= doc_bounds[None, :]).astype(jnp.int32)
    return jnp.sum(hits, axis=1)


def to_all(value, axis):
    return lax.all_to_all(value, axis, 0, 0, tiled=True)


def gathered(value, axis):
    return lax.all_gather(value, axis, axis=0, tiled=True)


def exchanged(value, axis, distance):
    count = lax.axis_size(axis)
    return lax.ppermute(value, axis, [(i, i ^ distance) for i in range(count)])


def near_blocks(own):
    blocks = {0: own}
    distance = lax.axis_size("fsdp") // 2
    while distance:
        blocks.update({r ^ distance: exchanged(b, "fsdp", distance) for r, b in blocks.items()})
        distance //= 2
    return [blocks[r] for r in range(len(blocks))]


def near_sum(blocks):
    distance = 1
    while distance < lax.axis_size("fsdp"):
        blocks = {
            r: blocks[r].astype(F32)
            + exchanged(blocks[r ^ distance].astype(BF), "fsdp", distance).astype(F32)
            for r in range(0, lax.axis_size("fsdp"), 2 * distance)
        }
        distance *= 2
    return blocks[0]


def in_order(blocks, own):
    stacked = jnp.stack(blocks)
    return jnp.take(stacked, jnp.arange(len(blocks), dtype=jnp.int32) ^ own, axis=0)


def span_blocks(own):
    spans = lax.axis_size("ctx")
    half = own.shape[0] // 2
    first, last = own[:half], own[half:]
    pair = jnp.stack([first, exchanged(first, "ctx", 1)])
    firsts = [pair] + [exchanged(pair, "ctx", d) for d in range(2, spans, 2)]
    lasts = jnp.stack([last] + [exchanged(last, "ctx", d) for d in range(2, spans, 2)])
    other = exchanged(lasts, "ctx", 1)
    return [
        jnp.concatenate([firsts[r // 2][r % 2], (other if r % 2 else lasts)[r // 2]])
        for r in range(spans)
    ]


def picked_gates(second, router_t, chosen):
    logits = dot_t(router_t, second)
    ids = iota(logits.shape, 0)
    picked = (ids == chosen[0:1, :]) | (ids == chosen[1:2, :])
    logits = jnp.where(picked, logits, MASK_NEG)
    parts = jnp.where(picked, jnp.exp(logits - jnp.max(logits, axis=0, keepdims=True)), 0.0)
    return picked, parts / jnp.sum(parts, axis=0, keepdims=True)


def swiglu_grads(gate, up, d_hidden):
    sigma = 1.0 / (1.0 + jnp.exp(-gate))
    passed = gate * sigma
    d_gate = d_hidden * up * sigma * (1.0 + gate * (1.0 - sigma))
    return (passed * up).astype(BF), d_gate.astype(BF), (d_hidden * passed).astype(BF)


def near_kernel(shards, shard_ref, *refs):
    second, grads = refs[:shards], refs[shards : 2 * shards]
    chosen, router_t, w_gate, w_up, w_down = refs[2 * shards : 2 * shards + 5]
    branch_out = refs[2 * shards + 5 : 3 * shards + 5]
    back_out = refs[3 * shards + 5 : 4 * shards + 5]
    hot, rows, cots, d_outs, slot_gate, out_acc, row_acc, branch_acc, back_acc = refs[
        4 * shards + 5 :
    ]
    expert, tile = pl.program_id(0), pl.program_id(1)
    tokens = second[0].shape[0]
    width = second[0].shape[1]
    wanted = shard_ref[0] * pl.num_programs(0) + expert

    @pl.when(tile == 0)
    def _():
        before = (iota((tokens, tokens), 0) < iota((tokens, tokens), 1)).astype(BF)
        for f in range(shards):
            picked, gates = picked_gates(second[f][...], router_t[...], chosen[f])
            ranks = dot(picked.astype(BF), before)
            found = (iota(ranks.shape, 0) == wanted) & picked
            rank = jnp.sum(jnp.where(found, ranks + 1.0, 0.0), axis=0, keepdims=True)
            gate = jnp.sum(jnp.where(found, gates, 0.0), axis=0, keepdims=True)
            match = iota((CAP, tokens), 0).astype(F32) + 1.0 == rank
            one_hot = match.astype(BF)
            place = pl.ds(f * CAP, CAP)
            hot[f] = one_hot
            found_gate = jnp.sum(jnp.where(match, gate, 0.0), axis=1, keepdims=True)
            slot_gate[place, :] = jnp.broadcast_to(found_gate, (CAP, LANES))
            rows[place, :] = dot(one_hot, second[f][...]).astype(BF)
            cot = dot(one_hot, grads[f][:, :width])
            cots[place, :] = cot.astype(BF)
            d_outs[place, :] = (found_gate * cot).astype(BF)
        out_acc[...] = jnp.zeros_like(out_acc)
        row_acc[...] = jnp.zeros_like(row_acc)

    hidden, d_gate, d_up = swiglu_grads(
        dot(rows[...], w_gate[0]), dot(rows[...], w_up[0]), dot(d_outs[...], w_down[0])
    )
    out_acc[...] += dot_t(hidden, w_down[0])
    row_acc[...] += dot_t(d_gate, w_gate[0]) + dot_t(d_up, w_up[0])

    @pl.when(tile == pl.num_programs(1) - 1)
    def _():
        last = expert == pl.num_programs(0) - 1
        for f in range(shards):
            place = pl.ds(f * CAP, CAP)
            out = out_acc[place, :].astype(BF).astype(F32)
            d_gates = jnp.sum(cots[place, :].astype(F32) * out, axis=1, keepdims=True)
            gated = (slot_gate[place, 0:1] * out).astype(BF)
            lane = iota((CAP, LANES), 1)
            coarse = d_gates.astype(BF).astype(F32)
            extra = jnp.where(lane == wanted, coarse, 0.0)
            extra = extra + jnp.where(lane == EXPERTS + wanted, d_gates - coarse, 0.0)

            def add(acc, part, columns):
                @pl.when(expert == 0)
                def _():
                    acc[f, :, columns] = part

                @pl.when(expert > 0)
                def _():
                    acc[f, :, columns] += part

            add(branch_acc, t_dot(hot[f], gated), slice(0, width))
            add(back_acc, t_dot(hot[f], row_acc[place, :].astype(BF)), slice(0, width))
            add(back_acc, t_dot(hot[f], extra.astype(BF)), slice(width, width + LANES))

            @pl.when(last)
            def _():
                branch_out[f][...] = branch_acc[f].astype(BF)
                back_out[f][...] = back_acc[f].astype(BF)


def near_experts(second, grads, chosen, router_t, w_experts, shard):
    shards = len(second)
    tokens, width = second[0].shape
    experts = w_experts.shape[0]
    slots = shards * CAP
    tiles = FF // TILE

    def whole(shape):
        return pl.BlockSpec(shape, lambda e, j, s: (0,) * len(shape))

    def weight(part):
        return pl.BlockSpec((1, width, TILE), lambda e, j, s: (e, 0, part * tiles + j))

    outs = pl.pallas_call(
        functools.partial(near_kernel, shards),
        grid_spec=pltpu.PrefetchScalarGridSpec(
            num_scalar_prefetch=1,
            grid=(experts, tiles),
            in_specs=[whole((tokens, width))] * shards
            + [whole((tokens, width + LANES))] * shards
            + [whole(chosen.shape), whole(router_t.shape), weight(0), weight(1), weight(2)],
            out_specs=[whole((tokens, width))] * shards
            + [whole((tokens, width + LANES))] * shards,
            scratch_shapes=[
                pltpu.VMEM((shards, CAP, tokens), BF),
                pltpu.VMEM((slots, width), BF),
                pltpu.VMEM((slots, width), BF),
                pltpu.VMEM((slots, width), BF),
                pltpu.VMEM((slots, LANES), F32),
                pltpu.VMEM((slots, width), F32),
                pltpu.VMEM((slots, width), F32),
                pltpu.VMEM((shards, tokens, width), F32),
                pltpu.VMEM((shards, tokens, width + LANES), F32),
            ],
        ),
        out_shape=[jax.ShapeDtypeStruct((tokens, width), BF)] * shards
        + [jax.ShapeDtypeStruct((tokens, width + LANES), BF)] * shards,
        compiler_params=pltpu.CompilerParams(vmem_limit_bytes=56 * 1024 * 1024),
        cost_estimate=pl.CostEstimate(
            flops=12 * experts * slots * width * FF,
            bytes_accessed=w_experts.size * 2,
            transcendentals=experts * slots * FF,
        ),
        name="near_experts",
    )(shard.reshape(1), *second, *grads, chosen, router_t, w_experts, w_experts, w_experts)
    return outs[:shards], outs[shards:]


def far_kernel(
    meta,
    chosen,
    places,
    router_t,
    second_ref,
    grads_ref,
    w_gate,
    w_up,
    w_down,
    out_ref,
    rows,
    d_outs,
    act,
    fetched,
    tile_out,
    fetch_sem,
    store_sem,
):
    expert, tile = pl.program_id(0), pl.program_id(1)
    tiles = pl.num_programs(1)
    step = expert * tiles + tile
    slot = lax.rem(step, 2)
    groups = chosen.shape[0]
    size = chosen.shape[2]
    width = w_gate.shape[1]
    wanted = meta[pl.num_programs(0), 0] + expert
    count = meta[expert, groups]
    chunks = jnp.maximum((count + CHUNK - 1) // CHUNK, 1)

    def stores(which, e, j):
        return [
            pltpu.make_async_copy(
                tile_out.at[which, i],
                out_ref.at[e, :, pl.ds(pl.multiple_of(i * FF + j * TILE, TILE), TILE)],
                store_sem.at[which, i],
            )
            for i in range(3)
        ]

    def fetches(which, g):
        at = pl.ds(pl.multiple_of(g * size, size), size)
        return [
            pltpu.make_async_copy(
                ref.at[at, pl.ds(0, width)], fetched.at[which, i], fetch_sem.at[which, i]
            )
            for i, ref in enumerate((second_ref, grads_ref))
        ]

    @pl.when(tile == 0)
    def _():
        for copy in fetches(0, 0):
            copy.start()
        tail = pl.ds(pl.multiple_of((chunks - 1) * CHUNK, CHUNK), CHUNK)
        rows[tail, :] = jnp.zeros((CHUNK, width), BF)
        d_outs[tail, :] = jnp.zeros((CHUNK, width), BF)

        @pl.loop(0, groups)
        def _(g):
            which = lax.rem(g, 2)
            for copy in fetches(which, g):
                copy.wait()

            @pl.when(g + 1 < groups)
            def _():
                for copy in fetches(1 - which, g + 1):
                    copy.start()

            second, grads = fetched[which, 0], fetched[which, 1]
            picked, gates = picked_gates(second, router_t[...], chosen[g])
            found = (iota(gates.shape, 0) == wanted) & picked
            gate = jnp.sum(jnp.where(found, gates, 0.0), axis=0, keepdims=True)
            start = meta[expert, g]
            base = start // 16 * 16
            match = iota((WINDOW, size), 0) == places[expert, pl.ds(g, 1), :] - base
            one_hot = match.astype(BF)
            found_gate = jnp.sum(jnp.where(match, gate, 0.0), axis=1, keepdims=True)
            at = pl.ds(pl.multiple_of(base, 16), 16)
            rest = pl.ds(pl.multiple_of(base + 16, 16), WINDOW - 16)
            held = iota((16, width), 0) < start - base
            for ref, new in (
                (rows, dot(one_hot, second).astype(BF)),
                (d_outs, (found_gate * dot(one_hot, grads)).astype(BF)),
            ):
                ref[at, :] = jnp.where(held, ref[at, :], new[:16])
                ref[rest, :] = new[16:]

    @pl.loop(0, chunks)
    def _(i):
        at = pl.ds(pl.multiple_of(i * CHUNK, CHUNK), CHUNK)
        hidden, d_gate, d_up = swiglu_grads(
            dot(rows[at, :], w_gate[0]), dot(rows[at, :], w_up[0]), dot(d_outs[at, :], w_down[0])
        )
        act[0, at, :] = d_gate
        act[1, at, :] = d_up
        act[2, at, :] = hidden

    @pl.when(step >= 2)
    def _():
        for copy in stores(slot, (step - 2) // tiles, lax.rem(step - 2, tiles)):
            copy.wait()

    for k in range(1, act.shape[1] // CHUNK + 1):

        @pl.when(chunks == k)
        def _():
            upto = k * CHUNK
            tile_out[slot, 0] = t_dot(rows[:upto, :], act[0, :upto, :])
            tile_out[slot, 1] = t_dot(rows[:upto, :], act[1, :upto, :])
            tile_out[slot, 2] = t_dot(d_outs[:upto, :], act[2, :upto, :])

    for copy in stores(slot, expert, tile):
        copy.start()

    @pl.when(step == pl.num_programs(0) * tiles - 1)
    def _():
        for copy in stores(1 - slot, (step - 1) // tiles, lax.rem(step - 1, tiles)):
            copy.wait()
        for copy in stores(slot, expert, tile):
            copy.wait()


def far_weight_grads(meta, chosen, places, router_t, second, grads, w_experts):
    experts, width = w_experts.shape[:2]
    groups, _, size = chosen.shape
    tiles = FF // TILE
    most = groups * size // 2

    def whole(shape):
        return pl.BlockSpec(shape, lambda e, j, s: (0,) * len(shape))

    def weight(part):
        return pl.BlockSpec((1, width, TILE), lambda e, j, s: (e, 0, part * tiles + j))

    return pl.pallas_call(
        far_kernel,
        grid_spec=pltpu.PrefetchScalarGridSpec(
            num_scalar_prefetch=1,
            grid=(experts, tiles),
            in_specs=[
                whole(chosen.shape),
                whole(places.shape),
                whole(router_t.shape),
                pl.BlockSpec(memory_space=pl.ANY),
                pl.BlockSpec(memory_space=pl.ANY),
                weight(0),
                weight(1),
                weight(2),
            ],
            out_specs=pl.BlockSpec(memory_space=pl.ANY),
            scratch_shapes=[
                pltpu.VMEM((most + WINDOW, width), BF),
                pltpu.VMEM((most + WINDOW, width), BF),
                pltpu.VMEM((3, most, TILE), BF),
                pltpu.VMEM((2, 2, size, width), BF),
                pltpu.VMEM((2, 3, width, TILE), F32),
                pltpu.SemaphoreType.DMA((2, 2)),
                pltpu.SemaphoreType.DMA((2, 3)),
            ],
        ),
        out_shape=jax.ShapeDtypeStruct((experts, width, 3 * FF), F32),
        compiler_params=pltpu.CompilerParams(vmem_limit_bytes=56 * 1024 * 1024),
        cost_estimate=pl.CostEstimate(
            flops=12 * experts * most * width * FF,
            bytes_accessed=w_experts.size * 6 + 4 * experts * groups * size * width,
            transcendentals=experts * most * FF,
        ),
        name="far_weight_grads",
    )(meta, chosen, places, router_t, second, grads, w_experts, w_experts, w_experts)


def attention_forward(q, k, v, allowed):
    length = q.shape[0]
    scores = jnp.einsum(
        "tgd,sd->gts", q.reshape(length, GROUP, HD), k, preferred_element_type=F32
    ) * HD ** (-0.5)
    highest = jnp.max(jnp.where(allowed, scores, MASK_NEG), axis=-1, keepdims=True)
    weights = jnp.where(allowed, jnp.exp(scores - highest), 0.0)
    total = jnp.sum(weights, axis=-1, keepdims=True)
    total = jnp.where(total == 0.0, 1.0, total)
    log_norm = highest + jnp.log(total)
    probs = (weights / total).astype(BF)
    attended = jnp.einsum("gts,sd->tgd", probs, v, preferred_element_type=F32)
    return attended.reshape(length, GROUP * HD), log_norm


def attention_backward(q, k, v, allowed, log_norm, attended, grads):
    length = q.shape[0]
    scale = HD ** (-0.5)
    q3 = q.reshape(length, GROUP, HD)
    g3 = grads.reshape(length, GROUP, HD)
    delta = jnp.sum(g3.astype(F32) * attended.reshape(length, GROUP, HD), axis=-1).T
    scores = jnp.einsum("tgd,sd->gts", q3, k, preferred_element_type=F32) * scale
    probs = jnp.where(allowed, jnp.exp(scores - log_norm), 0.0)
    d_probs = jnp.einsum("tgd,sd->gts", g3, v, preferred_element_type=F32)
    d_scores = (probs * (d_probs - delta[..., None])).astype(BF)
    d_q = jnp.einsum("gts,sd->tgd", d_scores, k, preferred_element_type=F32) * scale
    d_k = jnp.einsum("gts,tgd->sd", d_scores, q3, preferred_element_type=F32) * scale
    d_v = jnp.einsum("gts,tgd->sd", probs.astype(BF), g3, preferred_element_type=F32)
    return jnp.concatenate([d_q.reshape(length, GROUP * HD), d_k, d_v], axis=1).astype(BF)


def per_device(
    tokens,
    query_key_value_weight,
    output_weight,
    routing_weight,
    gain_attn,
    gain_moe,
    w_experts,
    doc_starts,
    routes,
    cotangent,
):
    spans = lax.axis_size("ctx")
    shards = lax.axis_size("fsdp")
    here = lax.axis_index("ctx")
    shard = lax.axis_index("fsdp")
    tok_count, width = tokens.shape[1:]
    local_experts = w_experts.shape[0]
    copies = spans // HK
    head = here // copies
    length = spans * tok_count
    blocks = spans * shards
    everyone = ("ctx", "fsdp")
    first_expert = shard * local_experts

    route_cols = jnp.pad(routes[0].astype(BF), ((0, 0), (0, LANES - 2)))
    sent = jnp.concatenate([cotangent[0], route_cols], axis=1)
    grads_all = gathered(sent, everyone)

    shard_rows = query_key_value_weight.shape[0]
    head_w = jnp.concatenate(
        [
            lax.dynamic_slice_in_dim(query_key_value_weight, head * GROUP * HD, GROUP * HD, 1),
            lax.dynamic_slice_in_dim(query_key_value_weight, Q_COLS + head * HD, HD, 1),
            lax.dynamic_slice_in_dim(query_key_value_weight, Q_COLS + K_COLS + head * HD, HD, 1),
            routing_weight,
            gain_attn[:, None],
            gain_moe[:, None],
        ],
        axis=1,
    )
    head_w = in_order(near_blocks(head_w), shard).reshape(width, -1)
    router_w = head_w[:, HEAD_COLS : HEAD_COLS + EXPERTS]
    router_t = jnp.pad(router_w.T, ((0, 16 - EXPERTS), (0, 0)))
    attn_g = head_w[:, HEAD_COLS + EXPERTS].astype(F32)
    moe_g = head_w[:, HEAD_COLS + EXPERTS + 1].astype(F32)
    head_w = head_w[:, :HEAD_COLS]

    stream = in_order(span_blocks(tokens[0]), here).reshape(length, width)
    out_w = near_blocks(output_weight)
    qkv_w = near_blocks(query_key_value_weight)
    stream_f = stream.astype(F32)
    normed = (stream_f * rms_factor(stream_f) * attn_g).astype(BF)
    mixed = dot(normed, head_w).astype(BF)
    q = mixed[:, : GROUP * HD]
    k = mixed[:, GROUP * HD : GROUP * HD + HD]
    v = mixed[:, GROUP * HD + HD :]
    pos = jnp.arange(length, dtype=jnp.int32)
    docs = doc_index(doc_starts[0], pos)
    active = (pos // tok_count) % copies == here % copies
    allowed = (pos[None, :] <= pos[:, None]) & (docs[None, :] == docs[:, None]) & active[:, None]
    attended, log_norm = attention_forward(q, k, v, allowed)
    attended_low = attended.astype(BF)

    own = to_all(attended_low, "ctx").reshape(HK, copies, tok_count, GROUP * HD)
    own = jnp.sum(own, axis=1) if copies > 1 else own[:, 0]
    by_shard = jnp.arange(shards, dtype=jnp.int32) ^ shard
    own = own.reshape(shards, HK // shards, tok_count, GROUP * HD).swapaxes(1, 2)
    own = jnp.take(own, by_shard, axis=0).reshape(shards, tok_count, -1)
    x = tokens[0].astype(F32)
    middle = x
    for r in range(shards):
        middle = middle + dot(own[r], out_w[r])
    second_factor = rms_factor(middle)
    second = (middle * second_factor * moe_g).astype(BF)
    second_near = near_blocks(second)
    second_all = gathered(second, everyone)

    grads_all, second_near = lax.optimization_barrier((grads_all, second_near))
    chosen = grads_all[:, width : width + 2].astype(jnp.int32).reshape(blocks, tok_count, 2)
    chosen = chosen.swapaxes(1, 2)
    chosen_near = jnp.take(chosen, here * shards + by_shard, axis=0)
    grads_near = [
        lax.dynamic_slice_in_dim(grads_all, (here * shards + (shard ^ r)) * tok_count, tok_count, 0)
        for r in range(shards)
    ]
    branch, back = near_experts(
        second_near, grads_near, chosen_near, router_t, w_experts, shard
    )
    back = near_sum(back)
    output = (middle + near_sum(branch)).astype(BF)

    grad = cotangent[0].astype(F32)
    d_gates = back[:, width : width + EXPERTS] + back[:, width + EXPERTS : width + 2 * EXPERTS]
    own_picked = jnp.any(routes[0][:, :, None] == jnp.arange(EXPERTS, dtype=jnp.int32), axis=1)
    gates = jax.nn.softmax(jnp.where(own_picked, dot(second, router_w), MASK_NEG), axis=-1)
    d_picked = gates * (d_gates - jnp.sum(gates * d_gates, axis=-1, keepdims=True))
    d_logits = jnp.where(own_picked, d_picked, 0.0).astype(BF)
    d_router = t_dot(second, d_logits)
    d_second = dot_t(d_logits, router_w) + back[:, :width]
    d_gain_moe = jnp.sum(d_second * middle * second_factor, axis=0)
    d_middle = grad + rms_input_grad(middle, second_factor, moe_g, d_second)
    d_proj = d_middle.astype(BF)
    d_attended = in_order([dot_t(d_proj, out_w[r]).astype(BF) for r in range(shards)], shard)

    chunk = width // spans
    d_attended = d_attended.reshape(shards, tok_count, HK // shards, 1, GROUP * HD)
    d_attended = d_attended.transpose(0, 2, 3, 1, 4)
    d_attended = jnp.broadcast_to(
        d_attended, (shards, HK // shards, copies, tok_count, GROUP * HD)
    ).reshape(spans, tok_count, GROUP * HD)
    sent = jnp.concatenate(
        [d_attended, d_proj.reshape(tok_count, spans, chunk).swapaxes(0, 1)], axis=2
    )
    sent = to_all(sent.reshape(length, -1), "ctx")
    d_mixed = attention_backward(
        q, k, v, allowed, log_norm, attended, sent[:, : GROUP * HD]
    )
    attended_all = gathered(attended_low, "ctx").reshape(HK, copies, length, GROUP * HD)
    attended_all = jnp.sum(attended_all, axis=1) if copies > 1 else attended_all[:, 0]
    d_out_w = jnp.einsum(
        "hte,td->hed", attended_all, sent[:, GROUP * HD :], preferred_element_type=F32
    ).reshape(Q_COLS, chunk)
    small = jnp.concatenate(
        [d_router, d_gain_moe[:, None], jnp.zeros((width, SMALL - EXPERTS - 1), F32)], axis=1
    )
    d_head_w = t_dot(normed, d_mixed)

    def whole_columns(part):
        part = part.astype(BF)
        terms = [
            lax.dynamic_slice_in_dim(part, (shard ^ r) * shard_rows, shard_rows, 0)
            for r in range(shards)
        ]
        part = gathered(near_sum(terms).astype(BF), "ctx")
        return part.reshape(spans, shard_rows, -1).astype(F32)

    late = whole_columns(jnp.concatenate([d_head_w, d_out_w, small], axis=1))
    by_head = late[:, :, :HEAD_COLS].reshape(HK, copies, shard_rows, HEAD_COLS)
    by_head = jnp.sum(by_head, axis=1).swapaxes(0, 1)

    def columns(part):
        return part.reshape(shard_rows, -1)

    d_qkv_w = jnp.concatenate(
        [
            columns(by_head[:, :, : GROUP * HD]),
            columns(by_head[:, :, GROUP * HD : GROUP * HD + HD]),
            columns(by_head[:, :, GROUP * HD + HD :]),
        ],
        axis=1,
    )
    d_out_w = columns(late[:, :, HEAD_COLS : HEAD_COLS + chunk].swapaxes(0, 1))
    small = jnp.sum(late[:, :, HEAD_COLS + chunk :], axis=0)
    d_router_w = small[:, :EXPERTS]
    d_gain_moe = small[:, EXPERTS]
    d_gain_attn = jnp.sum(
        d_qkv_w * query_key_value_weight.astype(F32), axis=1
    ) / gain_attn.astype(F32)

    d_home = to_all(d_mixed, "ctx").reshape(HK, copies, tok_count, HEAD_COLS)
    d_home = jnp.sum(d_home.astype(F32), axis=1).astype(BF) if copies > 1 else d_home[:, 0]
    d_home = d_home.swapaxes(0, 1)
    d_home = jnp.concatenate(
        [
            d_home[:, :, : GROUP * HD].reshape(tok_count, -1),
            d_home[:, :, GROUP * HD : GROUP * HD + HD].reshape(tok_count, -1),
            d_home[:, :, GROUP * HD + HD :].reshape(tok_count, -1),
        ],
        axis=1,
    )
    d_normed = in_order([dot_t(d_home, qkv_w[r]) for r in range(shards)], shard)
    d_normed = d_normed.swapaxes(0, 1).reshape(tok_count, width)
    d_tokens = (d_middle + rms_input_grad(x, rms_factor(x), attn_g, d_normed)).astype(BF)

    segment = min(blocks, SEGMENT)
    parts = blocks // segment
    local_ids = (first_expert + jnp.arange(local_experts, dtype=jnp.int32))[:, None, None]
    mine = (chosen[None, :, 0] == local_ids) | (chosen[None, :, 1] == local_ids)
    before = jnp.arange(tok_count)[:, None] < jnp.arange(tok_count)[None, :]
    rank = jnp.einsum(
        "ebt,tu->ebu", mine.astype(BF), before.astype(BF), preferred_element_type=F32
    ).astype(jnp.int32)
    held = jnp.sum(mine.astype(jnp.int32), axis=2).reshape(local_experts, parts, segment)
    start = jnp.cumsum(held, axis=2) - held
    rank = rank.reshape(local_experts, parts, segment, tok_count)
    mine = mine.reshape(local_experts, parts, segment, tok_count)
    places = jnp.where(mine, rank + start[..., None], -WINDOW * segment)
    places = places.reshape(local_experts, parts, segment // 2, 2 * tok_count)
    meta = jnp.concatenate(
        [start[:, :, ::2], jnp.sum(held, axis=2, keepdims=True)], axis=2
    ).swapaxes(0, 1)
    meta = jnp.pad(meta, ((0, 0), (0, 1), (0, 0)))
    meta = meta.at[:, local_experts, 0].set(first_expert)
    pairs = chosen.reshape(parts, segment // 2, 2, 2, tok_count).swapaxes(2, 3)
    pairs = pairs.reshape(parts, segment // 2, 2, 2 * tok_count)
    rows = segment * tok_count
    d_w_experts = [
        far_weight_grads(
            meta[i],
            pairs[i],
            places[:, i],
            router_t,
            second_all[i * rows : (i + 1) * rows],
            grads_all[i * rows : (i + 1) * rows],
            w_experts,
        )
        for i in range(parts)
    ]
    d_w_experts = sum(d_w_experts[1:], d_w_experts[0])
    return (
        output[None],
        d_tokens[None],
        d_qkv_w,
        d_out_w,
        d_router_w,
        d_gain_attn,
        d_gain_moe,
        d_w_experts,
    )


def solution(mesh):
    placed = (
        P("fsdp", "ctx", None),
        P("fsdp", None),
        P("fsdp", None),
        P("fsdp", None),
        P("fsdp"),
        P("fsdp"),
        P("fsdp", None, None),
        P("fsdp", None),
        P("fsdp", "ctx", None),
        P("fsdp", "ctx", None),
    )
    return jax.shard_map(
        per_device,
        mesh=mesh,
        in_specs=placed,
        out_specs=(
            P("fsdp", "ctx", None),
            P("fsdp", "ctx", None),
            P("fsdp", None),
            P("fsdp", None),
            P("fsdp", None),
            P("fsdp"),
            P("fsdp"),
            P("fsdp", None, None),
        ),
        check_vma=False,
    )
```

```python
import functools

import jax
import jax.numpy as jnp
from jax import lax
from jax.experimental import pallas as pl
from jax.experimental.pallas import tpu as pltpu
from jax.sharding import PartitionSpec as P

HQ = 24
HK = 8
HD = 64
GROUP = HQ // HK
FF = 1024
EXPERTS = 8
CAP = 64
Q_COLS = HQ * HD
K_COLS = HK * HD
HEAD_COLS = GROUP * HD + 2 * HD
SMALL = 16
LANES = 128
TILE = 256
CHUNK = 256
FAR_PARTS = 2
SEGMENT = 32
DEPTHS = (1, 2, 3, 4, 6, 8)

NORM_EPS = 1e-05
MASK_NEG = -1e30
BF = jnp.bfloat16
F32 = jnp.float32


def dot(a, b):
    return jnp.dot(a, b, preferred_element_type=F32)


def dot_t(a, b):
    return lax.dot_general(a, b, (((1,), (1,)), ((), ())), preferred_element_type=F32)


def t_dot(a, b):
    return lax.dot_general(a, b, (((0,), (0,)), ((), ())), preferred_element_type=F32)


def iota(shape, axis):
    return lax.broadcasted_iota(jnp.int32, shape, axis)


def rms_factor(values):
    return lax.rsqrt(jnp.mean(values * values, axis=-1, keepdims=True) + NORM_EPS)


def rms_input_grad(values, factor, gain_vec, incoming):
    inner = incoming * gain_vec
    cubed = factor * factor * factor
    return factor * inner - values * cubed * jnp.mean(inner * values, axis=-1, keepdims=True)


def doc_index(doc_bounds, positions):
    hits = (positions[:, None] >= doc_bounds[None, :]).astype(jnp.int32)
    return jnp.sum(hits, axis=1)


def to_all(value, axis):
    return lax.all_to_all(value, axis, 0, 0, tiled=True)


def gathered(value, axis):
    return lax.all_gather(value, axis, axis=0, tiled=True)


def exchanged(value, axis, distance):
    count = lax.axis_size(axis)
    return lax.ppermute(value, axis, [(i, i ^ distance) for i in range(count)])


def near_blocks(own):
    blocks = {0: own}
    distance = lax.axis_size("fsdp") // 2
    while distance:
        blocks.update({r ^ distance: exchanged(b, "fsdp", distance) for r, b in blocks.items()})
        distance //= 2
    return [blocks[r] for r in range(len(blocks))]


def near_sum(blocks):
    distance = 1
    while distance < lax.axis_size("fsdp"):
        blocks = {
            r: blocks[r].astype(F32)
            + exchanged(blocks[r ^ distance].astype(BF), "fsdp", distance).astype(F32)
            for r in range(0, lax.axis_size("fsdp"), 2 * distance)
        }
        distance *= 2
    return blocks[0]


def in_order(blocks, own):
    stacked = jnp.stack(blocks)
    return jnp.take(stacked, jnp.arange(len(blocks), dtype=jnp.int32) ^ own, axis=0)


def span_blocks(own):
    spans = lax.axis_size("ctx")
    half = own.shape[0] // 2
    first, last = own[:half], own[half:]
    pair = jnp.stack([first, exchanged(first, "ctx", 1)])
    firsts = [pair] + [exchanged(pair, "ctx", d) for d in range(2, spans, 2)]
    lasts = jnp.stack([last] + [exchanged(last, "ctx", d) for d in range(2, spans, 2)])
    other = exchanged(lasts, "ctx", 1)
    return [
        jnp.concatenate([firsts[r // 2][r % 2], (other if r % 2 else lasts)[r // 2]])
        for r in range(spans)
    ]


def picked_gates(second, router_t, chosen):
    logits = dot_t(router_t, second)
    ids = iota(logits.shape, 0)
    picked = (ids == chosen[0:1, :]) | (ids == chosen[1:2, :])
    logits = jnp.where(picked, logits, MASK_NEG)
    parts = jnp.where(picked, jnp.exp(logits - jnp.max(logits, axis=0, keepdims=True)), 0.0)
    return picked, parts / jnp.sum(parts, axis=0, keepdims=True)


def swiglu_grads(gate, up, d_hidden):
    sigma = 1.0 / (1.0 + jnp.exp(-gate))
    passed = gate * sigma
    d_gate = d_hidden * up * sigma * (1.0 + gate * (1.0 - sigma))
    return (passed * up).astype(BF), d_gate.astype(BF), (d_hidden * passed).astype(BF)


def near_kernel(shards, shard_ref, *refs):
    second, grads = refs[:shards], refs[shards : 2 * shards]
    chosen, router_t, w_gate, w_up, w_down = refs[2 * shards : 2 * shards + 5]
    branch_out = refs[2 * shards + 5 : 3 * shards + 5]
    back_out = refs[3 * shards + 5 : 4 * shards + 5]
    hot, rows, cots, d_outs, slot_gate, out_acc, row_acc, branch_acc, back_acc = refs[
        4 * shards + 5 :
    ]
    expert, tile = pl.program_id(0), pl.program_id(1)
    tokens = second[0].shape[0]
    width = second[0].shape[1]
    wanted = shard_ref[0] * pl.num_programs(0) + expert

    @pl.when(tile == 0)
    def _():
        before = (iota((tokens, tokens), 0) < iota((tokens, tokens), 1)).astype(BF)
        for f in range(shards):
            picked, gates = picked_gates(second[f][...], router_t[...], chosen[f])
            ranks = dot(picked.astype(BF), before)
            found = (iota(ranks.shape, 0) == wanted) & picked
            rank = jnp.sum(jnp.where(found, ranks + 1.0, 0.0), axis=0, keepdims=True)
            gate = jnp.sum(jnp.where(found, gates, 0.0), axis=0, keepdims=True)
            match = iota((CAP, tokens), 0).astype(F32) + 1.0 == rank
            one_hot = match.astype(BF)
            place = pl.ds(f * CAP, CAP)
            hot[f] = one_hot
            found_gate = jnp.sum(jnp.where(match, gate, 0.0), axis=1, keepdims=True)
            slot_gate[place, :] = jnp.broadcast_to(found_gate, (CAP, LANES))
            rows[place, :] = dot(one_hot, second[f][...]).astype(BF)
            cot = dot(one_hot, grads[f][:, :width])
            cots[place, :] = cot.astype(BF)
            d_outs[place, :] = (found_gate * cot).astype(BF)
        out_acc[...] = jnp.zeros_like(out_acc)
        row_acc[...] = jnp.zeros_like(row_acc)

    hidden, d_gate, d_up = swiglu_grads(
        dot(rows[...], w_gate[0]), dot(rows[...], w_up[0]), dot(d_outs[...], w_down[0])
    )
    out_acc[...] += dot_t(hidden, w_down[0])
    row_acc[...] += dot_t(d_gate, w_gate[0]) + dot_t(d_up, w_up[0])

    @pl.when(tile == pl.num_programs(1) - 1)
    def _():
        last = expert == pl.num_programs(0) - 1
        for f in range(shards):
            place = pl.ds(f * CAP, CAP)
            out = out_acc[place, :].astype(BF).astype(F32)
            d_gates = jnp.sum(cots[place, :].astype(F32) * out, axis=1, keepdims=True)
            gated = (slot_gate[place, 0:1] * out).astype(BF)
            lane = iota((CAP, LANES), 1)
            coarse = d_gates.astype(BF).astype(F32)
            extra = jnp.where(lane == wanted, coarse, 0.0)
            extra = extra + jnp.where(lane == EXPERTS + wanted, d_gates - coarse, 0.0)

            def add(acc, part, columns):
                @pl.when(expert == 0)
                def _():
                    acc[f, :, columns] = part

                @pl.when(expert > 0)
                def _():
                    acc[f, :, columns] += part

            add(branch_acc, t_dot(hot[f], gated), slice(0, width))
            add(back_acc, t_dot(hot[f], row_acc[place, :].astype(BF)), slice(0, width))
            add(back_acc, t_dot(hot[f], extra.astype(BF)), slice(width, width + LANES))

            @pl.when(last)
            def _():
                branch_out[f][...] = branch_acc[f].astype(BF)
                back_out[f][...] = back_acc[f].astype(BF)


def near_experts(second, grads, chosen, router_t, w_experts, shard):
    shards = len(second)
    tokens, width = second[0].shape
    experts = w_experts.shape[0]
    slots = shards * CAP
    tiles = FF // TILE

    def whole(shape):
        return pl.BlockSpec(shape, lambda e, j, s: (0,) * len(shape))

    def weight(part):
        return pl.BlockSpec((1, width, TILE), lambda e, j, s: (e, 0, part * tiles + j))

    outs = pl.pallas_call(
        functools.partial(near_kernel, shards),
        grid_spec=pltpu.PrefetchScalarGridSpec(
            num_scalar_prefetch=1,
            grid=(experts, tiles),
            in_specs=[whole((tokens, width))] * shards
            + [whole((tokens, width + LANES))] * shards
            + [whole(chosen.shape), whole(router_t.shape), weight(0), weight(1), weight(2)],
            out_specs=[whole((tokens, width))] * shards
            + [whole((tokens, width + LANES))] * shards,
            scratch_shapes=[
                pltpu.VMEM((shards, CAP, tokens), BF),
                pltpu.VMEM((slots, width), BF),
                pltpu.VMEM((slots, width), BF),
                pltpu.VMEM((slots, width), BF),
                pltpu.VMEM((slots, LANES), F32),
                pltpu.VMEM((slots, width), F32),
                pltpu.VMEM((slots, width), F32),
                pltpu.VMEM((shards, tokens, width), F32),
                pltpu.VMEM((shards, tokens, width + LANES), F32),
            ],
        ),
        out_shape=[jax.ShapeDtypeStruct((tokens, width), BF)] * shards
        + [jax.ShapeDtypeStruct((tokens, width + LANES), BF)] * shards,
        compiler_params=pltpu.CompilerParams(vmem_limit_bytes=56 * 1024 * 1024),
        cost_estimate=pl.CostEstimate(
            flops=12 * experts * slots * width * FF,
            bytes_accessed=w_experts.size * 2,
            transcendentals=experts * slots * FF,
        ),
        name="near_experts",
    )(shard.reshape(1), *second, *grads, chosen, router_t, w_experts, w_experts, w_experts)
    return outs[:shards], outs[shards:]


def far_kernel(
    part,
    meta,
    chosen,
    places,
    router_t,
    second_ref,
    grads_ref,
    w_gate,
    w_up,
    w_down,
    *rest,
):
    held_ref = rest[0] if len(rest) == 9 else None
    out_ref, rows, d_outs, act, fetched, tile_out, fetch_sem, store_sem = rest[-8:]
    expert, tile = pl.program_id(0), pl.program_id(1)
    tiles = pl.num_programs(1)
    step = expert * tiles + tile
    slot = lax.rem(step, 2)
    groups = chosen.shape[0]
    size = chosen.shape[2]
    each = grads_ref.shape[2]
    width = w_gate.shape[1]
    window = size + 16
    wanted = meta[pl.num_programs(0), 0] + expert
    count = meta[expert, groups]
    chunks = jnp.maximum((count + CHUNK - 1) // CHUNK, 1)

    def stores(which, e, j, back=False):
        pairs = [
            (
                tile_out.at[which, i],
                (held_ref if back else out_ref).at[
                    e, :, pl.ds(pl.multiple_of(i * FF + j * TILE, TILE), TILE)
                ],
            )
            for i in range(3)
        ]
        return [
            pltpu.make_async_copy(b, a, store_sem.at[which, i])
            if back
            else pltpu.make_async_copy(a, b, store_sem.at[which, i])
            for i, (a, b) in enumerate(pairs)
        ]

    def fetches(which, g):
        step_blocks = size // each
        at = pl.ds(g * step_blocks, step_blocks)
        return [
            pltpu.make_async_copy(
                second_ref.at[at], fetched.at[which, 0], fetch_sem.at[which, 0]
            ),
            pltpu.make_async_copy(
                grads_ref.at[at, part, :, pl.ds(0, width)],
                fetched.at[which, 1],
                fetch_sem.at[which, 1],
            ),
        ]

    @pl.when(tile == 0)
    def _():
        for copy in fetches(0, 0):
            copy.start()
        tail = pl.ds(pl.multiple_of((chunks - 1) * CHUNK, CHUNK), CHUNK)
        rows[tail, :] = jnp.zeros((CHUNK, width), BF)
        d_outs[tail, :] = jnp.zeros((CHUNK, width), BF)

        @pl.loop(0, groups)
        def _(g):
            which = lax.rem(g, 2)
            for copy in fetches(which, g):
                copy.wait()

            @pl.when(g + 1 < groups)
            def _():
                for copy in fetches(1 - which, g + 1):
                    copy.start()

            second = fetched[which, 0].reshape(size, width)
            grads = fetched[which, 1].reshape(size, width)
            picked, gates = picked_gates(second, router_t[...], chosen[g])
            found = (iota(gates.shape, 0) == wanted) & picked
            gate = jnp.sum(jnp.where(found, gates, 0.0), axis=0, keepdims=True)
            start = meta[expert, g]
            base = start // 16 * 16
            match = iota((window, size), 0) == places[expert, pl.ds(g, 1), :] - base
            one_hot = match.astype(BF)
            found_gate = jnp.sum(jnp.where(match, gate, 0.0), axis=1, keepdims=True)
            at = pl.ds(pl.multiple_of(base, 16), 16)
            after = pl.ds(pl.multiple_of(base + 16, 16), window - 16)
            held = iota((16, width), 0) < start - base
            for ref, new in (
                (rows, dot(one_hot, second).astype(BF)),
                (d_outs, (found_gate * dot(one_hot, grads)).astype(BF)),
            ):
                ref[at, :] = jnp.where(held, ref[at, :], new[:16])
                ref[after, :] = new[16:]

    @pl.when(step >= 2)
    def _():
        for copy in stores(slot, (step - 2) // tiles, lax.rem(step - 2, tiles)):
            copy.wait()

    if held_ref is not None:
        for copy in stores(slot, expert, tile, back=True):
            copy.start()

    @pl.loop(0, chunks)
    def _(i):
        at = pl.ds(pl.multiple_of(i * CHUNK, CHUNK), CHUNK)
        hidden, d_gate, d_up = swiglu_grads(
            dot(rows[at, :], w_gate[0]), dot(rows[at, :], w_up[0]), dot(d_outs[at, :], w_down[0])
        )
        act[0, at, :] = d_gate
        act[1, at, :] = d_up
        act[2, at, :] = hidden

    if held_ref is not None:
        for copy in stores(slot, expert, tile, back=True):
            copy.wait()

    most = act.shape[1] // CHUNK
    depths = [k for k in DEPTHS if k < most] + [most]
    for low, k in zip([0] + depths[:-1], depths):

        @pl.when((chunks > low) & (chunks <= k))
        def _():
            if k - low > 1:
                for extra in range(low + 1, k):

                    @pl.when(chunks == extra)
                    def _():
                        spare = slice(extra * CHUNK, k * CHUNK)
                        empty = jnp.zeros(((k - extra) * CHUNK, width), BF)
                        rows[spare, :] = empty
                        d_outs[spare, :] = empty
                        for i in range(3):
                            act[i, spare, :] = empty[:, :TILE]

            upto = k * CHUNK
            for i, left in enumerate((rows, rows, d_outs)):
                product = t_dot(left[:upto, :], act[i, :upto, :])
                if held_ref is None:
                    tile_out[slot, i] = product
                else:
                    tile_out[slot, i] += product

    for copy in stores(slot, expert, tile):
        copy.start()

    @pl.when(step == pl.num_programs(0) * tiles - 1)
    def _():
        for copy in stores(1 - slot, (step - 1) // tiles, lax.rem(step - 1, tiles)):
            copy.wait()
        for copy in stores(slot, expert, tile):
            copy.wait()


def far_weight_grads(part, meta, chosen, places, router_t, second, grads, w_experts, held):
    experts, width = w_experts.shape[:2]
    groups, _, size = chosen.shape
    each = grads.shape[2]
    tiles = FF // TILE
    most = groups * size

    def whole(shape):
        return pl.BlockSpec(shape, lambda e, j, s: (0,) * len(shape))

    def weight(part):
        return pl.BlockSpec((1, width, TILE), lambda e, j, s: (e, 0, part * tiles + j))

    anywhere = pl.BlockSpec(memory_space=pl.ANY)
    before = () if held is None else (held,)
    return pl.pallas_call(
        functools.partial(far_kernel, part),
        grid_spec=pltpu.PrefetchScalarGridSpec(
            num_scalar_prefetch=1,
            grid=(experts, tiles),
            in_specs=[
                whole(chosen.shape),
                whole(places.shape),
                whole(router_t.shape),
                anywhere,
                anywhere,
                weight(0),
                weight(1),
                weight(2),
            ]
            + [anywhere] * len(before),
            out_specs=anywhere,
            scratch_shapes=[
                pltpu.VMEM((most + size + 16, width), BF),
                pltpu.VMEM((most + size + 16, width), BF),
                pltpu.VMEM((3, most, TILE), BF),
                pltpu.VMEM((2, 2, size // each, each, width), BF),
                pltpu.VMEM((2, 3, width, TILE), F32),
                pltpu.SemaphoreType.DMA((2, 2)),
                pltpu.SemaphoreType.DMA((2, 3)),
            ],
        ),
        out_shape=jax.ShapeDtypeStruct((experts, width, 3 * FF), F32),
        input_output_aliases={9: 0} if before else {},
        compiler_params=pltpu.CompilerParams(vmem_limit_bytes=56 * 1024 * 1024),
        cost_estimate=pl.CostEstimate(
            flops=4 * experts * most * width * FF,
            bytes_accessed=w_experts.size * 6 + 4 * groups * size * width,
            transcendentals=experts * most * FF,
        ),
        name="far_weight_grads",
    )(meta, chosen, places, router_t, second, grads, w_experts, w_experts, w_experts, *before)


def attention_forward(q, k, v, allowed):
    length = q.shape[0]
    scores = jnp.einsum(
        "tgd,sd->gts", q.reshape(length, GROUP, HD), k, preferred_element_type=F32
    ) * HD ** (-0.5)
    highest = jnp.max(jnp.where(allowed, scores, MASK_NEG), axis=-1, keepdims=True)
    weights = jnp.where(allowed, jnp.exp(scores - highest), 0.0)
    total = jnp.sum(weights, axis=-1, keepdims=True)
    total = jnp.where(total == 0.0, 1.0, total)
    log_norm = highest + jnp.log(total)
    probs = (weights / total).astype(BF)
    attended = jnp.einsum("gts,sd->tgd", probs, v, preferred_element_type=F32)
    return attended.reshape(length, GROUP * HD), log_norm


def attention_backward(q, k, v, allowed, log_norm, attended, grads):
    length = q.shape[0]
    scale = HD ** (-0.5)
    q3 = q.reshape(length, GROUP, HD)
    g3 = grads.reshape(length, GROUP, HD)
    delta = jnp.sum(g3.astype(F32) * attended.reshape(length, GROUP, HD), axis=-1).T
    scores = jnp.einsum("tgd,sd->gts", q3, k, preferred_element_type=F32) * scale
    probs = jnp.where(allowed, jnp.exp(scores - log_norm), 0.0)
    d_probs = jnp.einsum("tgd,sd->gts", g3, v, preferred_element_type=F32)
    d_scores = (probs * (d_probs - delta[..., None])).astype(BF)
    d_q = jnp.einsum("gts,sd->tgd", d_scores, k, preferred_element_type=F32) * scale
    d_k = jnp.einsum("gts,tgd->sd", d_scores, q3, preferred_element_type=F32) * scale
    d_v = jnp.einsum("gts,tgd->sd", probs.astype(BF), g3, preferred_element_type=F32)
    return jnp.concatenate([d_q.reshape(length, GROUP * HD), d_k, d_v], axis=1).astype(BF)


def per_device(
    tokens,
    query_key_value_weight,
    output_weight,
    routing_weight,
    gain_attn,
    gain_moe,
    w_experts,
    doc_starts,
    routes,
    cotangent,
):
    spans = lax.axis_size("ctx")
    shards = lax.axis_size("fsdp")
    here = lax.axis_index("ctx")
    shard = lax.axis_index("fsdp")
    tok_count, width = tokens.shape[1:]
    local_experts = w_experts.shape[0]
    copies = spans // HK
    head = here // copies
    length = spans * tok_count
    blocks = spans * shards
    everyone = ("ctx", "fsdp")
    first_expert = shard * local_experts

    route_cols = jnp.pad(routes[0].astype(BF), ((0, 0), (0, LANES - 2)))
    sent = jnp.concatenate([cotangent[0], route_cols], axis=1)
    grads_all = gathered(sent, everyone)

    shard_rows = query_key_value_weight.shape[0]
    head_w = jnp.concatenate(
        [
            lax.dynamic_slice_in_dim(query_key_value_weight, head * GROUP * HD, GROUP * HD, 1),
            lax.dynamic_slice_in_dim(query_key_value_weight, Q_COLS + head * HD, HD, 1),
            lax.dynamic_slice_in_dim(query_key_value_weight, Q_COLS + K_COLS + head * HD, HD, 1),
            routing_weight,
            gain_attn[:, None],
            gain_moe[:, None],
        ],
        axis=1,
    )
    head_w = in_order(near_blocks(head_w), shard).reshape(width, -1)
    router_w = head_w[:, HEAD_COLS : HEAD_COLS + EXPERTS]
    router_t = jnp.pad(router_w.T, ((0, 16 - EXPERTS), (0, 0)))
    attn_g = head_w[:, HEAD_COLS + EXPERTS].astype(F32)
    moe_g = head_w[:, HEAD_COLS + EXPERTS + 1].astype(F32)
    head_w = head_w[:, :HEAD_COLS]

    stream = in_order(span_blocks(tokens[0]), here).reshape(length, width)
    output_weight, stream = lax.optimization_barrier((output_weight, stream))
    out_w = near_blocks(output_weight)
    stream_f = stream.astype(F32)
    normed = (stream_f * rms_factor(stream_f) * attn_g).astype(BF)
    mixed = dot(normed, head_w).astype(BF)
    q = mixed[:, : GROUP * HD]
    k = mixed[:, GROUP * HD : GROUP * HD + HD]
    v = mixed[:, GROUP * HD + HD :]
    pos = jnp.arange(length, dtype=jnp.int32)
    docs = doc_index(doc_starts[0], pos)
    active = (pos // tok_count) % copies == here % copies
    allowed = (pos[None, :] <= pos[:, None]) & (docs[None, :] == docs[:, None]) & active[:, None]
    attended, log_norm = attention_forward(q, k, v, allowed)
    attended_low = attended.astype(BF)

    own = to_all(attended_low, "ctx").reshape(HK, copies, tok_count, GROUP * HD)
    own = jnp.sum(own, axis=1) if copies > 1 else own[:, 0]
    by_shard = jnp.arange(shards, dtype=jnp.int32) ^ shard
    own = own.reshape(shards, HK // shards, tok_count, GROUP * HD).swapaxes(1, 2)
    own = jnp.take(own, by_shard, axis=0).reshape(shards, tok_count, -1)
    x = tokens[0].astype(F32)
    middle = x
    for r in range(shards):
        middle = middle + dot(own[r], out_w[r])
    second_factor = rms_factor(middle)
    second = (middle * second_factor * moe_g).astype(BF)
    second_near = near_blocks(second)
    each = tok_count // FAR_PARTS
    second_all = [gathered(second[i * each : (i + 1) * each], everyone) for i in range(FAR_PARTS)]
    attended_low, later_qkv, second_near = lax.optimization_barrier(
        (attended_low, query_key_value_weight, second_near)
    )
    qkv_w = near_blocks(later_qkv)
    attended_all = span_blocks(attended_low)

    grads_all, second_near = lax.optimization_barrier((grads_all, second_near))
    chosen = grads_all[:, width : width + 2].astype(jnp.int32).reshape(blocks, tok_count, 2)
    chosen = chosen.swapaxes(1, 2)
    chosen_near = jnp.take(chosen, here * shards + by_shard, axis=0)
    grads_near = [
        lax.dynamic_slice_in_dim(grads_all, (here * shards + (shard ^ r)) * tok_count, tok_count, 0)
        for r in range(shards)
    ]
    branch, back = near_experts(
        second_near, grads_near, chosen_near, router_t, w_experts, shard
    )
    back = near_sum(back)
    output = (middle + near_sum(branch)).astype(BF)

    grad = cotangent[0].astype(F32)
    d_gates = back[:, width : width + EXPERTS] + back[:, width + EXPERTS : width + 2 * EXPERTS]
    own_picked = jnp.any(routes[0][:, :, None] == jnp.arange(EXPERTS, dtype=jnp.int32), axis=1)
    gates = jax.nn.softmax(jnp.where(own_picked, dot(second, router_w), MASK_NEG), axis=-1)
    d_picked = gates * (d_gates - jnp.sum(gates * d_gates, axis=-1, keepdims=True))
    d_logits = jnp.where(own_picked, d_picked, 0.0).astype(BF)
    d_router = t_dot(second, d_logits)
    d_second = dot_t(d_logits, router_w) + back[:, :width]
    d_gain_moe = jnp.sum(d_second * middle * second_factor, axis=0)
    d_middle = grad + rms_input_grad(middle, second_factor, moe_g, d_second)
    d_proj = d_middle.astype(BF)
    d_attended = in_order([dot_t(d_proj, out_w[r]).astype(BF) for r in range(shards)], shard)

    chunk = width // spans
    d_attended = d_attended.reshape(shards, tok_count, HK // shards, 1, GROUP * HD)
    d_attended = d_attended.transpose(0, 2, 3, 1, 4)
    d_attended = jnp.broadcast_to(
        d_attended, (shards, HK // shards, copies, tok_count, GROUP * HD)
    ).reshape(spans, tok_count, GROUP * HD)
    sent = jnp.concatenate(
        [d_attended, d_proj.reshape(tok_count, spans, chunk).swapaxes(0, 1)], axis=2
    )
    sent = to_all(sent.reshape(length, -1), "ctx")
    d_mixed = attention_backward(
        q, k, v, allowed, log_norm, attended, sent[:, : GROUP * HD]
    )
    d_out_w = in_order([t_dot(block, sent[:, GROUP * HD :]) for block in attended_all], here)
    d_out_w = jnp.sum(d_out_w.reshape(HK, copies, GROUP * HD, chunk), axis=1)
    d_out_w = d_out_w.reshape(Q_COLS, chunk)
    small = jnp.concatenate(
        [d_router, d_gain_moe[:, None], jnp.zeros((width, SMALL - EXPERTS - 1), F32)], axis=1
    )
    d_head_w = t_dot(normed, d_mixed)

    def whole_columns(part):
        part = part.astype(BF)
        terms = [
            lax.dynamic_slice_in_dim(part, (shard ^ r) * shard_rows, shard_rows, 0)
            for r in range(shards)
        ]
        part = gathered(near_sum(terms).astype(BF), "ctx")
        return part.reshape(spans, shard_rows, -1).astype(F32)

    late = whole_columns(jnp.concatenate([d_head_w, d_out_w, small], axis=1))
    by_head = late[:, :, :HEAD_COLS].reshape(HK, copies, shard_rows, HEAD_COLS)
    by_head = jnp.sum(by_head, axis=1).swapaxes(0, 1)

    def columns(part):
        return part.reshape(shard_rows, -1)

    d_qkv_w = jnp.concatenate(
        [
            columns(by_head[:, :, : GROUP * HD]),
            columns(by_head[:, :, GROUP * HD : GROUP * HD + HD]),
            columns(by_head[:, :, GROUP * HD + HD :]),
        ],
        axis=1,
    )
    d_out_w = columns(late[:, :, HEAD_COLS : HEAD_COLS + chunk].swapaxes(0, 1))
    small = jnp.sum(late[:, :, HEAD_COLS + chunk :], axis=0)
    d_router_w = small[:, :EXPERTS]
    d_gain_moe = small[:, EXPERTS]
    d_gain_attn = jnp.sum(
        d_qkv_w * query_key_value_weight.astype(F32), axis=1
    ) / gain_attn.astype(F32)

    d_home = to_all(d_mixed, "ctx").reshape(HK, copies, tok_count, HEAD_COLS)
    d_home = jnp.sum(d_home.astype(F32), axis=1).astype(BF) if copies > 1 else d_home[:, 0]
    d_home = d_home.swapaxes(0, 1)
    d_home = jnp.concatenate(
        [
            d_home[:, :, : GROUP * HD].reshape(tok_count, -1),
            d_home[:, :, GROUP * HD : GROUP * HD + HD].reshape(tok_count, -1),
            d_home[:, :, GROUP * HD + HD :].reshape(tok_count, -1),
        ],
        axis=1,
    )
    d_normed = in_order([dot_t(d_home, qkv_w[r]) for r in range(shards)], shard)
    d_normed = d_normed.swapaxes(0, 1).reshape(tok_count, width)
    d_tokens = (d_middle + rms_input_grad(x, rms_factor(x), attn_g, d_normed)).astype(BF)

    segment = min(blocks, SEGMENT)
    joined = 2 * LANES // each
    groups = segment // joined
    local_ids = (first_expert + jnp.arange(local_experts, dtype=jnp.int32))[:, None, None]
    before = jnp.arange(each)[:, None] < jnp.arange(each)[None, :]
    d_w_experts = None
    for i in range(FAR_PARTS):
        for j in range(blocks // segment):
            inside = slice(j * segment, (j + 1) * segment)
            part = chosen[inside, :, i * each : (i + 1) * each]
            mine = (part[None, :, 0] == local_ids) | (part[None, :, 1] == local_ids)
            rank = jnp.einsum(
                "ebt,tu->ebu", mine.astype(BF), before.astype(BF), preferred_element_type=F32
            ).astype(jnp.int32)
            held = jnp.sum(mine.astype(jnp.int32), axis=2)
            start = jnp.cumsum(held, axis=1) - held
            places = jnp.where(mine, rank + start[..., None], -segment * each - 32)
            places = places.reshape(local_experts, groups, joined * each)
            meta = jnp.concatenate(
                [start[:, ::joined], jnp.sum(held, axis=1, keepdims=True)], axis=1
            )
            meta = jnp.pad(meta, ((0, 1), (0, 0))).at[local_experts, 0].set(first_expert)
            part = part.reshape(groups, joined, 2, each).swapaxes(1, 2)
            d_w_experts = far_weight_grads(
                i,
                meta,
                part.reshape(groups, 2, joined * each),
                places,
                router_t,
                second_all[i].reshape(blocks, each, width)[inside],
                grads_all.reshape(blocks, FAR_PARTS, each, width + LANES)[inside],
                w_experts,
                d_w_experts,
            )
    return (
        output[None],
        d_tokens[None],
        d_qkv_w,
        d_out_w,
        d_router_w,
        d_gain_attn,
        d_gain_moe,
        d_w_experts,
    )


def solution(mesh):
    placed = (
        P("fsdp", "ctx", None),
        P("fsdp", None),
        P("fsdp", None),
        P("fsdp", None),
        P("fsdp"),
        P("fsdp"),
        P("fsdp", None, None),
        P("fsdp", None),
        P("fsdp", "ctx", None),
        P("fsdp", "ctx", None),
    )
    return jax.shard_map(
        per_device,
        mesh=mesh,
        in_specs=placed,
        out_specs=(
            P("fsdp", "ctx", None),
            P("fsdp", "ctx", None),
            P("fsdp", None),
            P("fsdp", None),
            P("fsdp", None),
            P("fsdp"),
            P("fsdp"),
            P("fsdp", None, None),
        ),
        check_vma=False,
    )
```

```python
import functools

import jax
import jax.numpy as jnp
from jax import lax
from jax.experimental import pallas as pl
from jax.experimental.pallas import tpu as pltpu
from jax.sharding import PartitionSpec as P

HQ = 24
HK = 8
HD = 64
GROUP = HQ // HK
FF = 1024
EXPERTS = 8
CAP = 64
Q_COLS = HQ * HD
K_COLS = HK * HD
HEAD_COLS = GROUP * HD + 2 * HD
SMALL = 16
LANES = 128
TILE = 256
CHUNK = 256
SEGMENT = 32
JOINED = 2
DEPTHS = (1, 2, 3, 4, 6, 8)

NORM_EPS = 1e-05
MASK_NEG = -1e30
BF = jnp.bfloat16
F32 = jnp.float32


def dot(a, b):
    return jnp.dot(a, b, preferred_element_type=F32)


def dot_t(a, b):
    return lax.dot_general(a, b, (((1,), (1,)), ((), ())), preferred_element_type=F32)


def t_dot(a, b):
    return lax.dot_general(a, b, (((0,), (0,)), ((), ())), preferred_element_type=F32)


def iota(shape, axis):
    return lax.broadcasted_iota(jnp.int32, shape, axis)


def rms_factor(values):
    return lax.rsqrt(jnp.mean(values * values, axis=-1, keepdims=True) + NORM_EPS)


def rms_input_grad(values, factor, gain_vec, incoming):
    inner = incoming * gain_vec
    cubed = factor * factor * factor
    return factor * inner - values * cubed * jnp.mean(inner * values, axis=-1, keepdims=True)


def doc_index(doc_bounds, positions):
    hits = (positions[:, None] >= doc_bounds[None, :]).astype(jnp.int32)
    return jnp.sum(hits, axis=1)


def to_all(value, axis):
    return lax.all_to_all(value, axis, 0, 0, tiled=True)


def gathered(value, axis):
    return lax.all_gather(value, axis, axis=0, tiled=True)


def exchanged(value, axis, distance):
    count = lax.axis_size(axis)
    return lax.ppermute(value, axis, [(i, i ^ distance) for i in range(count)])


def near_blocks(own):
    blocks = {0: own}
    distance = lax.axis_size("fsdp") // 2
    while distance:
        blocks.update({r ^ distance: exchanged(b, "fsdp", distance) for r, b in blocks.items()})
        distance //= 2
    return [blocks[r] for r in range(len(blocks))]


def near_sum(blocks):
    distance = 1
    while distance < lax.axis_size("fsdp"):
        blocks = {
            r: blocks[r].astype(F32)
            + exchanged(blocks[r ^ distance].astype(BF), "fsdp", distance).astype(F32)
            for r in range(0, lax.axis_size("fsdp"), 2 * distance)
        }
        distance *= 2
    return blocks[0]


def in_order(blocks, own):
    stacked = jnp.stack(blocks)
    return jnp.take(stacked, jnp.arange(len(blocks), dtype=jnp.int32) ^ own, axis=0)


def line_blocks(own):
    spans = lax.axis_size("ctx")
    return jnp.stack([own] + [exchanged(own, "ctx", d) for d in range(2, spans, 2)])


def span_blocks(own):
    half = own.shape[0] // 2
    same = [line_blocks(part) for part in (own[:half], own[half:])]
    other = [exchanged(part, "ctx", 1) for part in same]
    return [
        jnp.concatenate([part[r // 2] for part in (other if r % 2 else same)])
        for r in range(lax.axis_size("ctx"))
    ]


def all_blocks(line):
    spans, shards = lax.axis_size("ctx"), lax.axis_size("fsdp")
    sets = [
        [(2 * pair + side) * shards + f for side in range(2) for f in range(shards)]
        for pair in range(spans // 2)
    ]
    merged = lax.all_gather(line, ("ctx", "fsdp"), axis=0, tiled=True, axis_index_groups=sets)
    return merged.reshape(-1, line.shape[-1])


def picked_gates(second, router_t, chosen):
    logits = dot_t(router_t, second)
    ids = iota(logits.shape, 0)
    picked = (ids == chosen[0:1, :]) | (ids == chosen[1:2, :])
    logits = jnp.where(picked, logits, MASK_NEG)
    parts = jnp.where(picked, jnp.exp(logits - jnp.max(logits, axis=0, keepdims=True)), 0.0)
    return picked, parts / jnp.sum(parts, axis=0, keepdims=True)


def swiglu_grads(gate, up, d_hidden):
    sigma = 1.0 / (1.0 + jnp.exp(-gate))
    passed = gate * sigma
    d_gate = d_hidden * up * sigma * (1.0 + gate * (1.0 - sigma))
    return (passed * up).astype(BF), d_gate.astype(BF), (d_hidden * passed).astype(BF)


def near_kernel(shards, shard_ref, *refs):
    second, grads = refs[:shards], refs[shards : 2 * shards]
    chosen, router_t, w_gate, w_up, w_down = refs[2 * shards : 2 * shards + 5]
    branch_out = refs[2 * shards + 5 : 3 * shards + 5]
    back_out = refs[3 * shards + 5 : 4 * shards + 5]
    hot, rows, cots, d_outs, slot_gate, out_acc, row_acc, branch_acc, back_acc = refs[
        4 * shards + 5 :
    ]
    expert, tile = pl.program_id(0), pl.program_id(1)
    tokens = second[0].shape[0]
    width = second[0].shape[1]
    wanted = shard_ref[0] * pl.num_programs(0) + expert

    @pl.when(tile == 0)
    def _():
        before = (iota((tokens, tokens), 0) < iota((tokens, tokens), 1)).astype(BF)
        for f in range(shards):
            picked, gates = picked_gates(second[f][...], router_t[...], chosen[f])
            ranks = dot(picked.astype(BF), before)
            found = (iota(ranks.shape, 0) == wanted) & picked
            rank = jnp.sum(jnp.where(found, ranks + 1.0, 0.0), axis=0, keepdims=True)
            gate = jnp.sum(jnp.where(found, gates, 0.0), axis=0, keepdims=True)
            match = iota((CAP, tokens), 0).astype(F32) + 1.0 == rank
            one_hot = match.astype(BF)
            place = pl.ds(f * CAP, CAP)
            hot[f] = one_hot
            found_gate = jnp.sum(jnp.where(match, gate, 0.0), axis=1, keepdims=True)
            slot_gate[place, :] = jnp.broadcast_to(found_gate, (CAP, LANES))
            rows[place, :] = dot(one_hot, second[f][...]).astype(BF)
            cot = dot(one_hot, grads[f][:, :width])
            cots[place, :] = cot.astype(BF)
            d_outs[place, :] = (found_gate * cot).astype(BF)
        out_acc[...] = jnp.zeros_like(out_acc)
        row_acc[...] = jnp.zeros_like(row_acc)

    hidden, d_gate, d_up = swiglu_grads(
        dot(rows[...], w_gate[0]), dot(rows[...], w_up[0]), dot(d_outs[...], w_down[0])
    )
    out_acc[...] += dot_t(hidden, w_down[0])
    row_acc[...] += dot_t(d_gate, w_gate[0]) + dot_t(d_up, w_up[0])

    @pl.when(tile == pl.num_programs(1) - 1)
    def _():
        last = expert == pl.num_programs(0) - 1
        for f in range(shards):
            place = pl.ds(f * CAP, CAP)
            out = out_acc[place, :].astype(BF).astype(F32)
            d_gates = jnp.sum(cots[place, :].astype(F32) * out, axis=1, keepdims=True)
            gated = (slot_gate[place, 0:1] * out).astype(BF)
            lane = iota((CAP, LANES), 1)
            coarse = d_gates.astype(BF).astype(F32)
            extra = jnp.where(lane == wanted, coarse, 0.0)
            extra = extra + jnp.where(lane == EXPERTS + wanted, d_gates - coarse, 0.0)

            def add(acc, part, columns):
                @pl.when(expert == 0)
                def _():
                    acc[f, :, columns] = part

                @pl.when(expert > 0)
                def _():
                    acc[f, :, columns] += part

            add(branch_acc, t_dot(hot[f], gated), slice(0, width))
            add(back_acc, t_dot(hot[f], row_acc[place, :].astype(BF)), slice(0, width))
            add(back_acc, t_dot(hot[f], extra.astype(BF)), slice(width, width + LANES))

            @pl.when(last)
            def _():
                branch_out[f][...] = branch_acc[f].astype(BF)
                back_out[f][...] = back_acc[f].astype(BF)


def near_experts(second, grads, chosen, router_t, w_experts, shard):
    shards = len(second)
    tokens, width = second[0].shape
    experts = w_experts.shape[0]
    slots = shards * CAP
    tiles = FF // TILE

    def whole(shape):
        return pl.BlockSpec(shape, lambda e, j, s: (0,) * len(shape))

    def weight(part):
        return pl.BlockSpec((1, width, TILE), lambda e, j, s: (e, 0, part * tiles + j))

    outs = pl.pallas_call(
        functools.partial(near_kernel, shards),
        grid_spec=pltpu.PrefetchScalarGridSpec(
            num_scalar_prefetch=1,
            grid=(experts, tiles),
            in_specs=[whole((tokens, width))] * shards
            + [whole((tokens, width + LANES))] * shards
            + [whole(chosen.shape), whole(router_t.shape), weight(0), weight(1), weight(2)],
            out_specs=[whole((tokens, width))] * shards
            + [whole((tokens, width + LANES))] * shards,
            scratch_shapes=[
                pltpu.VMEM((shards, CAP, tokens), BF),
                pltpu.VMEM((slots, width), BF),
                pltpu.VMEM((slots, width), BF),
                pltpu.VMEM((slots, width), BF),
                pltpu.VMEM((slots, LANES), F32),
                pltpu.VMEM((slots, width), F32),
                pltpu.VMEM((slots, width), F32),
                pltpu.VMEM((shards, tokens, width), F32),
                pltpu.VMEM((shards, tokens, width + LANES), F32),
            ],
        ),
        out_shape=[jax.ShapeDtypeStruct((tokens, width), BF)] * shards
        + [jax.ShapeDtypeStruct((tokens, width + LANES), BF)] * shards,
        compiler_params=pltpu.CompilerParams(vmem_limit_bytes=56 * 1024 * 1024),
        cost_estimate=pl.CostEstimate(
            flops=12 * experts * slots * width * FF,
            bytes_accessed=w_experts.size * 2,
            transcendentals=experts * slots * FF,
        ),
        name="near_experts",
    )(shard.reshape(1), *second, *grads, chosen, router_t, w_experts, w_experts, w_experts)
    return outs[:shards], outs[shards:]


def far_kernel(
    meta,
    chosen,
    places,
    router_t,
    second_ref,
    grads_ref,
    w_gate,
    w_up,
    w_down,
    out_ref,
    rows,
    d_outs,
    act,
    fetched,
    tile_out,
    fetch_sem,
    store_sem,
):
    experts = rows.shape[0]
    expert, tile = pl.program_id(0), pl.program_id(1)
    tiles = pl.num_programs(1)
    step = expert * tiles + tile
    slot = lax.rem(step, 2)
    groups = chosen.shape[0]
    size = chosen.shape[2]
    width = w_gate.shape[1]
    window = JOINED * CAP + 16

    def count_chunks(e):
        return jnp.maximum((meta[e, groups] + CHUNK - 1) // CHUNK, 1)

    chunks = count_chunks(expert)

    def stores(which, e, j):
        return [
            pltpu.make_async_copy(
                tile_out.at[which, i],
                out_ref.at[e, :, pl.ds(pl.multiple_of(i * FF + j * TILE, TILE), TILE)],
                store_sem.at[which, i],
            )
            for i in range(3)
        ]

    def fetches(which, g):
        at = pl.ds(pl.multiple_of(g * size, size), size)
        return [
            pltpu.make_async_copy(
                ref.at[at, pl.ds(0, width)], fetched.at[which, i], fetch_sem.at[which, i]
            )
            for i, ref in enumerate((second_ref, grads_ref))
        ]

    @pl.when(step == 0)
    def _():
        for copy in fetches(0, 0):
            copy.start()
        for e in range(experts):
            tail = pl.ds(pl.multiple_of((count_chunks(e) - 1) * CHUNK, CHUNK), CHUNK)
            rows[e, tail, :] = jnp.zeros((CHUNK, width), BF)
            d_outs[e, tail, :] = jnp.zeros((CHUNK, width), BF)

        @pl.loop(0, groups)
        def _(g):
            which = lax.rem(g, 2)
            for copy in fetches(which, g):
                copy.wait()

            @pl.when(g + 1 < groups)
            def _():
                for copy in fetches(1 - which, g + 1):
                    copy.start()

            second, grads = fetched[which, 0], fetched[which, 1]
            picked, gates = picked_gates(second, router_t[...], chosen[g])
            starts = [meta[e, g] for e in range(experts)]
            bases = [start // 16 * 16 for start in starts]
            matches, found_gates = [], []
            for e in range(experts):
                found = (iota(gates.shape, 0) == meta[experts, 0] + e) & picked
                gate = jnp.sum(jnp.where(found, gates, 0.0), axis=0, keepdims=True)
                match = iota((window, size), 0) == places[e, pl.ds(g, 1), :] - bases[e]
                matches.append(match.astype(BF))
                found_gates.append(
                    jnp.sum(jnp.where(match, gate, 0.0), axis=1, keepdims=True)
                )
            one_hot = jnp.concatenate(matches, axis=0)
            new_rows = dot(one_hot, second).astype(BF)
            new_grads = (jnp.concatenate(found_gates, axis=0) * dot(one_hot, grads)).astype(BF)
            for e in range(experts):
                at = pl.ds(pl.multiple_of(bases[e], 16), 16)
                rest = pl.ds(pl.multiple_of(bases[e] + 16, 16), window - 16)
                held = iota((16, width), 0) < starts[e] - bases[e]
                for ref, new in ((rows, new_rows), (d_outs, new_grads)):
                    new = new[e * window : (e + 1) * window]
                    ref[e, at, :] = jnp.where(held, ref[e, at, :], new[:16])
                    ref[e, rest, :] = new[16:]

    @pl.loop(0, chunks)
    def _(i):
        at = pl.ds(pl.multiple_of(i * CHUNK, CHUNK), CHUNK)
        row, d_out = rows[expert, at, :], d_outs[expert, at, :]
        hidden, d_gate, d_up = swiglu_grads(
            dot(row, w_gate[0]), dot(row, w_up[0]), dot(d_out, w_down[0])
        )
        act[0, at, :] = d_gate
        act[1, at, :] = d_up
        act[2, at, :] = hidden

    @pl.when(step >= 2)
    def _():
        for copy in stores(slot, (step - 2) // tiles, lax.rem(step - 2, tiles)):
            copy.wait()

    most = act.shape[1] // CHUNK
    depths = [k for k in DEPTHS if k < most] + [most]
    for low, k in zip([0] + depths[:-1], depths):

        @pl.when((chunks > low) & (chunks <= k))
        def _():
            for extra in range(low + 1, k):

                @pl.when(chunks == extra)
                def _():
                    spare = slice(extra * CHUNK, k * CHUNK)
                    empty = jnp.zeros(((k - extra) * CHUNK, width), BF)
                    rows[expert, spare, :] = empty
                    d_outs[expert, spare, :] = empty
                    for i in range(3):
                        act[i, spare, :] = empty[:, :TILE]

            upto = k * CHUNK
            for i, left in enumerate((rows, rows, d_outs)):
                tile_out[slot, i] = t_dot(left[expert, :upto, :], act[i, :upto, :])

    for copy in stores(slot, expert, tile):
        copy.start()

    @pl.when(step == pl.num_programs(0) * tiles - 1)
    def _():
        for copy in stores(1 - slot, (step - 1) // tiles, lax.rem(step - 1, tiles)):
            copy.wait()
        for copy in stores(slot, expert, tile):
            copy.wait()


def far_weight_grads(meta, chosen, places, router_t, second, grads, w_experts):
    experts, width = w_experts.shape[:2]
    groups, _, size = chosen.shape
    tiles = FF // TILE
    most = groups * JOINED * CAP
    held = most + JOINED * CAP + 16

    def whole(shape):
        return pl.BlockSpec(shape, lambda e, j, s: (0,) * len(shape))

    def weight(part):
        return pl.BlockSpec((1, width, TILE), lambda e, j, s: (e, 0, part * tiles + j))

    anywhere = pl.BlockSpec(memory_space=pl.ANY)
    return pl.pallas_call(
        far_kernel,
        grid_spec=pltpu.PrefetchScalarGridSpec(
            num_scalar_prefetch=1,
            grid=(experts, tiles),
            in_specs=[
                whole(chosen.shape),
                whole(places.shape),
                whole(router_t.shape),
                anywhere,
                anywhere,
                weight(0),
                weight(1),
                weight(2),
            ],
            out_specs=anywhere,
            scratch_shapes=[
                pltpu.VMEM((experts, held, width), BF),
                pltpu.VMEM((experts, held, width), BF),
                pltpu.VMEM((3, most, TILE), BF),
                pltpu.VMEM((2, 2, size, width), BF),
                pltpu.VMEM((2, 3, width, TILE), F32),
                pltpu.SemaphoreType.DMA((2, 2)),
                pltpu.SemaphoreType.DMA((2, 3)),
            ],
        ),
        out_shape=jax.ShapeDtypeStruct((experts, width, 3 * FF), F32),
        compiler_params=pltpu.CompilerParams(vmem_limit_bytes=58 * 1024 * 1024),
        cost_estimate=pl.CostEstimate(
            flops=8 * experts * most * width * FF,
            bytes_accessed=w_experts.size * 6 + 4 * groups * size * width,
            transcendentals=experts * most * FF,
        ),
        name="far_weight_grads",
    )(meta, chosen, places, router_t, second, grads, w_experts, w_experts, w_experts)


def attention_forward(q, k, v, allowed):
    length = q.shape[0]
    scores = jnp.einsum(
        "tgd,sd->gts", q.reshape(length, GROUP, HD), k, preferred_element_type=F32
    ) * HD ** (-0.5)
    highest = jnp.max(jnp.where(allowed, scores, MASK_NEG), axis=-1, keepdims=True)
    weights = jnp.where(allowed, jnp.exp(scores - highest), 0.0)
    total = jnp.sum(weights, axis=-1, keepdims=True)
    total = jnp.where(total == 0.0, 1.0, total)
    log_norm = highest + jnp.log(total)
    probs = (weights / total).astype(BF)
    attended = jnp.einsum("gts,sd->tgd", probs, v, preferred_element_type=F32)
    return attended.reshape(length, GROUP * HD), log_norm


def attention_backward(q, k, v, allowed, log_norm, attended, grads):
    length = q.shape[0]
    scale = HD ** (-0.5)
    q3 = q.reshape(length, GROUP, HD)
    g3 = grads.reshape(length, GROUP, HD)
    delta = jnp.sum(g3.astype(F32) * attended.reshape(length, GROUP, HD), axis=-1).T
    scores = jnp.einsum("tgd,sd->gts", q3, k, preferred_element_type=F32) * scale
    probs = jnp.where(allowed, jnp.exp(scores - log_norm), 0.0)
    d_probs = jnp.einsum("tgd,sd->gts", g3, v, preferred_element_type=F32)
    d_scores = (probs * (d_probs - delta[..., None])).astype(BF)
    d_q = jnp.einsum("gts,sd->tgd", d_scores, k, preferred_element_type=F32) * scale
    d_k = jnp.einsum("gts,tgd->sd", d_scores, q3, preferred_element_type=F32) * scale
    d_v = jnp.einsum("gts,tgd->sd", probs.astype(BF), g3, preferred_element_type=F32)
    return jnp.concatenate([d_q.reshape(length, GROUP * HD), d_k, d_v], axis=1).astype(BF)


def per_device(
    tokens,
    query_key_value_weight,
    output_weight,
    routing_weight,
    gain_attn,
    gain_moe,
    w_experts,
    doc_starts,
    routes,
    cotangent,
):
    spans = lax.axis_size("ctx")
    shards = lax.axis_size("fsdp")
    here = lax.axis_index("ctx")
    shard = lax.axis_index("fsdp")
    tok_count, width = tokens.shape[1:]
    local_experts = w_experts.shape[0]
    copies = spans // HK
    head = here // copies
    length = spans * tok_count
    blocks = spans * shards
    first_expert = shard * local_experts

    route_cols = jnp.pad(routes[0].astype(BF), ((0, 0), (0, LANES - 2)))
    sent = jnp.concatenate([cotangent[0], route_cols], axis=1)

    shard_rows = query_key_value_weight.shape[0]
    head_w = jnp.concatenate(
        [
            lax.dynamic_slice_in_dim(query_key_value_weight, head * GROUP * HD, GROUP * HD, 1),
            lax.dynamic_slice_in_dim(query_key_value_weight, Q_COLS + head * HD, HD, 1),
            lax.dynamic_slice_in_dim(query_key_value_weight, Q_COLS + K_COLS + head * HD, HD, 1),
            routing_weight,
            gain_attn[:, None],
            gain_moe[:, None],
        ],
        axis=1,
    )
    head_w = in_order(near_blocks(head_w), shard).reshape(width, -1)
    router_w = head_w[:, HEAD_COLS : HEAD_COLS + EXPERTS]
    router_t = jnp.pad(router_w.T, ((0, 16 - EXPERTS), (0, 0)))
    attn_g = head_w[:, HEAD_COLS + EXPERTS].astype(F32)
    moe_g = head_w[:, HEAD_COLS + EXPERTS + 1].astype(F32)
    head_w = head_w[:, :HEAD_COLS]

    stream = in_order(span_blocks(tokens[0]), here).reshape(length, width)
    sent, output_weight, stream = lax.optimization_barrier((sent, output_weight, stream))
    out_w = near_blocks(output_weight)
    grads_near = near_blocks(sent)
    grads_all = all_blocks(line_blocks(sent))
    stream_f = stream.astype(F32)
    normed = (stream_f * rms_factor(stream_f) * attn_g).astype(BF)
    mixed = dot(normed, head_w).astype(BF)
    q = mixed[:, : GROUP * HD]
    k = mixed[:, GROUP * HD : GROUP * HD + HD]
    v = mixed[:, GROUP * HD + HD :]
    pos = jnp.arange(length, dtype=jnp.int32)
    docs = doc_index(doc_starts[0], pos)
    active = (pos // tok_count) % copies == here % copies
    allowed = (pos[None, :] <= pos[:, None]) & (docs[None, :] == docs[:, None]) & active[:, None]
    attended, log_norm = attention_forward(q, k, v, allowed)
    attended_low = attended.astype(BF)

    own = to_all(attended_low, "ctx").reshape(HK, copies, tok_count, GROUP * HD)
    own = jnp.sum(own, axis=1) if copies > 1 else own[:, 0]
    by_shard = jnp.arange(shards, dtype=jnp.int32) ^ shard
    own = own.reshape(shards, HK // shards, tok_count, GROUP * HD).swapaxes(1, 2)
    own = jnp.take(own, by_shard, axis=0).reshape(shards, tok_count, -1)
    x = tokens[0].astype(F32)
    middle = x
    for r in range(shards):
        middle = middle + dot(own[r], out_w[r])
    second_factor = rms_factor(middle)
    second = (middle * second_factor * moe_g).astype(BF)
    second_near = near_blocks(second)
    second_line = line_blocks(second)
    second_all = all_blocks(second_line)
    attended_low, later_qkv, second_near, second_line = lax.optimization_barrier(
        (attended_low, query_key_value_weight, second_near, second_line)
    )
    qkv_w = near_blocks(later_qkv)
    attended_all = span_blocks(attended_low)

    def routes_of(payload):
        return payload[:, width : width + 2].astype(jnp.int32).reshape(-1, tok_count, 2).swapaxes(1, 2)

    chosen_near = jnp.concatenate([routes_of(block) for block in grads_near])
    branch, back = near_experts(
        second_near, grads_near, chosen_near, router_t, w_experts, shard
    )
    back = near_sum(back)
    output = (middle + near_sum(branch)).astype(BF)

    grad = cotangent[0].astype(F32)
    d_gates = back[:, width : width + EXPERTS] + back[:, width + EXPERTS : width + 2 * EXPERTS]
    own_picked = jnp.any(routes[0][:, :, None] == jnp.arange(EXPERTS, dtype=jnp.int32), axis=1)
    gates = jax.nn.softmax(jnp.where(own_picked, dot(second, router_w), MASK_NEG), axis=-1)
    d_picked = gates * (d_gates - jnp.sum(gates * d_gates, axis=-1, keepdims=True))
    d_logits = jnp.where(own_picked, d_picked, 0.0).astype(BF)
    d_router = t_dot(second, d_logits)
    d_second = dot_t(d_logits, router_w) + back[:, :width]
    d_gain_moe = jnp.sum(d_second * middle * second_factor, axis=0)
    d_middle = grad + rms_input_grad(middle, second_factor, moe_g, d_second)
    d_proj = d_middle.astype(BF)
    d_attended = in_order([dot_t(d_proj, out_w[r]).astype(BF) for r in range(shards)], shard)

    chunk = width // spans
    d_attended = d_attended.reshape(shards, tok_count, HK // shards, 1, GROUP * HD)
    d_attended = d_attended.transpose(0, 2, 3, 1, 4)
    d_attended = jnp.broadcast_to(
        d_attended, (shards, HK // shards, copies, tok_count, GROUP * HD)
    ).reshape(spans, tok_count, GROUP * HD)
    sent = jnp.concatenate(
        [d_attended, d_proj.reshape(tok_count, spans, chunk).swapaxes(0, 1)], axis=2
    )
    sent = to_all(sent.reshape(length, -1), "ctx")
    d_mixed = attention_backward(
        q, k, v, allowed, log_norm, attended, sent[:, : GROUP * HD]
    )
    d_out_w = in_order([t_dot(block, sent[:, GROUP * HD :]) for block in attended_all], here)
    d_out_w = jnp.sum(d_out_w.reshape(HK, copies, GROUP * HD, chunk), axis=1)
    d_out_w = d_out_w.reshape(Q_COLS, chunk)
    small = jnp.concatenate(
        [d_router, d_gain_moe[:, None], jnp.zeros((width, SMALL - EXPERTS - 1), F32)], axis=1
    )
    d_head_w = t_dot(normed, d_mixed)

    def whole_columns(part):
        part = part.astype(BF)
        terms = [
            lax.dynamic_slice_in_dim(part, (shard ^ r) * shard_rows, shard_rows, 0)
            for r in range(shards)
        ]
        part = gathered(near_sum(terms).astype(BF), "ctx")
        return part.reshape(spans, shard_rows, -1).astype(F32)

    late = whole_columns(jnp.concatenate([d_head_w, d_out_w, small], axis=1))
    by_head = late[:, :, :HEAD_COLS].reshape(HK, copies, shard_rows, HEAD_COLS)
    by_head = jnp.sum(by_head, axis=1).swapaxes(0, 1)

    def columns(part):
        return part.reshape(shard_rows, -1)

    d_qkv_w = jnp.concatenate(
        [
            columns(by_head[:, :, : GROUP * HD]),
            columns(by_head[:, :, GROUP * HD : GROUP * HD + HD]),
            columns(by_head[:, :, GROUP * HD + HD :]),
        ],
        axis=1,
    )
    d_out_w = columns(late[:, :, HEAD_COLS : HEAD_COLS + chunk].swapaxes(0, 1))
    small = jnp.sum(late[:, :, HEAD_COLS + chunk :], axis=0)
    d_router_w = small[:, :EXPERTS]
    d_gain_moe = small[:, EXPERTS]
    d_gain_attn = jnp.sum(
        d_qkv_w * query_key_value_weight.astype(F32), axis=1
    ) / gain_attn.astype(F32)

    d_home = to_all(d_mixed, "ctx").reshape(HK, copies, tok_count, HEAD_COLS)
    d_home = jnp.sum(d_home.astype(F32), axis=1).astype(BF) if copies > 1 else d_home[:, 0]
    d_home = d_home.swapaxes(0, 1)
    d_home = jnp.concatenate(
        [
            d_home[:, :, : GROUP * HD].reshape(tok_count, -1),
            d_home[:, :, GROUP * HD : GROUP * HD + HD].reshape(tok_count, -1),
            d_home[:, :, GROUP * HD + HD :].reshape(tok_count, -1),
        ],
        axis=1,
    )
    d_normed = in_order([dot_t(d_home, qkv_w[r]) for r in range(shards)], shard)
    d_normed = d_normed.swapaxes(0, 1).reshape(tok_count, width)
    d_tokens = (d_middle + rms_input_grad(x, rms_factor(x), attn_g, d_normed)).astype(BF)

    chosen = routes_of(grads_all)
    segment = min(blocks, SEGMENT)
    groups = segment // JOINED
    local_ids = (first_expert + jnp.arange(local_experts, dtype=jnp.int32))[:, None, None]
    before = jnp.arange(tok_count)[:, None] < jnp.arange(tok_count)[None, :]
    parts = []
    for j in range(blocks // segment):
        inside = slice(j * segment, (j + 1) * segment)
        part = chosen[inside]
        mine = (part[None, :, 0] == local_ids) | (part[None, :, 1] == local_ids)
        rank = jnp.einsum(
            "ebt,tu->ebu", mine.astype(BF), before.astype(BF), preferred_element_type=F32
        ).astype(jnp.int32)
        held = jnp.sum(mine.astype(jnp.int32), axis=2)
        start = jnp.cumsum(held, axis=1) - held
        places = jnp.where(mine, rank + start[..., None], -(2**20))
        meta = jnp.concatenate([start[:, ::JOINED], jnp.sum(held, axis=1, keepdims=True)], axis=1)
        meta = jnp.pad(meta, ((0, 1), (0, 0))).at[local_experts, 0].set(first_expert)
        part = part.reshape(groups, JOINED, 2, tok_count).swapaxes(1, 2)
        tokens_in = slice(j * segment * tok_count, (j + 1) * segment * tok_count)
        parts.append(
            far_weight_grads(
                meta,
                part.reshape(groups, 2, JOINED * tok_count),
                places.reshape(local_experts, groups, JOINED * tok_count),
                router_t,
                second_all[tokens_in],
                grads_all[tokens_in],
                w_experts,
            )
        )
    d_w_experts = sum(parts[1:], parts[0])
    return (
        output[None],
        d_tokens[None],
        d_qkv_w,
        d_out_w,
        d_router_w,
        d_gain_attn,
        d_gain_moe,
        d_w_experts,
    )


def solution(mesh):
    placed = (
        P("fsdp", "ctx", None),
        P("fsdp", None),
        P("fsdp", None),
        P("fsdp", None),
        P("fsdp"),
        P("fsdp"),
        P("fsdp", None, None),
        P("fsdp", None),
        P("fsdp", "ctx", None),
        P("fsdp", "ctx", None),
    )
    return jax.shard_map(
        per_device,
        mesh=mesh,
        in_specs=placed,
        out_specs=(
            P("fsdp", "ctx", None),
            P("fsdp", "ctx", None),
            P("fsdp", None),
            P("fsdp", None),
            P("fsdp", None),
            P("fsdp"),
            P("fsdp"),
            P("fsdp", None, None),
        ),
        check_vma=False,
    )
```

```python
import functools

import jax
import jax.numpy as jnp
from jax import lax
from jax.experimental import pallas as pl
from jax.experimental.pallas import tpu as pltpu
from jax.sharding import PartitionSpec as P

HQ = 24
HK = 8
HD = 64
GROUP = HQ // HK
FF = 1024
EXPERTS = 8
CAP = 64
Q_COLS = HQ * HD
K_COLS = HK * HD
HEAD = GROUP * HD
HEAD_COLS = HEAD + 2 * HD
SCALE = HD**-0.5
EXTRA = 16
LANES = 128
TILE = 256
CHUNK = 256
SEGMENT = 32
JOINED = 2
QUERIES = 256
DEPTHS = (1, 2, 3, 4, 6, 8)
VMEM = 58 * 1024 * 1024

NORM_EPS = 1e-05
MASK_NEG = -1e30
BF = jnp.bfloat16
F32 = jnp.float32


def dot(a, b):
    return jnp.dot(a, b, preferred_element_type=F32)


def dot_t(a, b):
    return lax.dot_general(a, b, (((1,), (1,)), ((), ())), preferred_element_type=F32)


def t_dot(a, b):
    return lax.dot_general(a, b, (((0,), (0,)), ((), ())), preferred_element_type=F32)


def iota(shape, axis):
    return lax.broadcasted_iota(jnp.int32, shape, axis)


def rms_factor(values):
    return lax.rsqrt(jnp.mean(values * values, axis=-1, keepdims=True) + NORM_EPS)


def rms_input_grad(values, factor, gain_vec, incoming):
    inner = incoming * gain_vec
    cubed = factor * factor * factor
    return factor * inner - values * cubed * jnp.mean(inner * values, axis=-1, keepdims=True)


def to_all(value, axis):
    return lax.all_to_all(value, axis, 0, 0, tiled=True)


def exchanged(value, axis, distance):
    count = lax.axis_size(axis)
    return lax.ppermute(value, axis, [(i, i ^ distance) for i in range(count)])


def near_blocks(own):
    blocks = {0: own}
    distance = lax.axis_size("fsdp") // 2
    while distance:
        blocks.update({r ^ distance: exchanged(b, "fsdp", distance) for r, b in blocks.items()})
        distance //= 2
    return [blocks[r] for r in range(len(blocks))]


def near_terms(blocks):
    shards = lax.axis_size("fsdp")
    terms = {r: [block] for r, block in enumerate(blocks)}
    distance = 1

    def total(parts):
        if len(parts) == 1:
            return parts[0]
        return sum((part.astype(F32) for part in parts[1:]), parts[0].astype(F32)).astype(BF)

    while distance < shards:
        terms = {
            r: terms[r] + [exchanged(total(terms[r ^ distance]), "fsdp", distance)]
            for r in range(0, shards, 2 * distance)
        }
        distance *= 2
    return terms[0]


def line_blocks(own):
    spans = lax.axis_size("ctx")
    return jnp.stack([own] + [exchanged(own, "ctx", d) for d in range(2, spans, 2)])


def span_pieces(own):
    half = own.shape[0] // 2
    same = [line_blocks(part) for part in (own[:half], own[half:])]
    return same + [exchanged(part, "ctx", 1) for part in same]


def all_blocks(line):
    spans, shards = lax.axis_size("ctx"), lax.axis_size("fsdp")
    sets = [
        [(2 * pair + side) * shards + f for side in range(2) for f in range(shards)]
        for pair in range(spans // 2)
    ]
    return lax.all_gather(line, ("ctx", "fsdp"), axis=0, tiled=True, axis_index_groups=sets)


def after(values, *others):
    return lax.optimization_barrier((values, others))[0]


def whole(array):
    shape = array.shape
    return pl.BlockSpec(shape, lambda *_: (0,) * len(shape))


def anywhere():
    return pl.BlockSpec(memory_space=pl.ANY)


def place_pieces(here, pieces, target, sems):
    copies = []
    for i, piece in enumerate(pieces):
        odd, last = divmod(i, 2)
        rows = piece.shape[1]
        for j in range(piece.shape[0]):
            copies.append(
                pltpu.make_async_copy(
                    piece.at[j],
                    target.at[here ^ (2 * j + odd), pl.ds(last * rows, rows)],
                    sems.at[i, j],
                )
            )
    for copy in copies:
        copy.start()
    return copies


def doc_of(starts, positions):
    found = jnp.zeros(positions.shape, jnp.int32)
    for i in range(starts.shape[0]):
        found = found + (positions >= starts[i]).astype(jnp.int32)
    return found


def visible(starts, here, copies, tokens, first, rows, keys):
    query = first + iota((rows, 1), 0)
    key = iota((1, keys), 1)
    allowed = (key <= query) & (doc_of(starts, key) == doc_of(starts, query))
    if copies > 1:
        allowed = allowed & (lax.rem(query // tokens, copies) == lax.rem(here, copies))
    return allowed


def stream_kernel(
    copies,
    place,
    starts,
    *refs,
):
    shards = len(refs) - 15
    pieces, weights, side = refs[:4], refs[4 : 4 + shards], refs[4 + shards]
    normed, mixed, attended_low, attended, log_norm, rows, weight, piece_sems, weight_sems = refs[
        5 + shards : 14 + shards
    ]
    here, shard = place[0], place[1]
    spans, tokens, width = rows.shape
    length = spans * tokens
    copying = place_pieces(here, pieces, rows, piece_sems)
    loading = [
        pltpu.make_async_copy(ref, weight.at[shard ^ r], weight_sems.at[r])
        for r, ref in enumerate(weights)
    ]
    for copy in loading:
        copy.start()
    for copy in loading + copying:
        copy.wait()
    head_weight = weight[...].reshape(width, HEAD_COLS)
    gain = side[EXPERTS : EXPERTS + 1, :].astype(F32)

    @pl.loop(0, spans)
    def _(span):
        x = rows[span].astype(F32)
        low = (x * rms_factor(x) * gain).astype(BF)
        at = pl.ds(pl.multiple_of(span * tokens, tokens), tokens)
        normed[at, :] = low
        mixed[at, :] = dot(low, head_weight).astype(BF)

    for first in range(0, length, QUERIES):
        keys = first + QUERIES
        at = slice(first, keys)
        allowed = visible(starts, here, copies, tokens, first, QUERIES, keys)
        for g in range(GROUP):
            columns = slice(g * HD, (g + 1) * HD)
            scores = dot_t(mixed[at, columns], mixed[:keys, HEAD : HEAD + HD]) * SCALE
            scores = jnp.where(allowed, scores, MASK_NEG)
            highest = jnp.max(scores, axis=1, keepdims=True)
            parts = jnp.where(allowed, jnp.exp(scores - highest), 0.0)
            total = jnp.sum(parts, axis=1, keepdims=True)
            total = jnp.where(total == 0.0, 1.0, total)
            log_norm[at, g : g + 1] = highest + jnp.log(total)
            result = dot((parts / total).astype(BF), mixed[:keys, HEAD + HD :])
            attended[at, columns] = result
            attended_low[at, columns] = result.astype(BF)


def stream_attention(place, starts, pieces, head_weights, side, copies):
    spans, tokens = 2 * pieces[0].shape[0], 2 * pieces[0].shape[1]
    width = pieces[0].shape[2]
    length = spans * tokens
    shards = len(head_weights)
    return pl.pallas_call(
        functools.partial(stream_kernel, copies),
        grid_spec=pltpu.PrefetchScalarGridSpec(
            num_scalar_prefetch=2,
            grid=(1,),
            in_specs=[anywhere()] * (4 + shards) + [whole(side)],
            out_specs=[
                pl.BlockSpec((length, columns), lambda *_: (0, 0))
                for columns in (width, HEAD_COLS, HEAD, HEAD, LANES)
            ],
            scratch_shapes=[
                pltpu.VMEM((spans, tokens, width), BF),
                pltpu.VMEM((shards, width // shards, HEAD_COLS), BF),
                pltpu.SemaphoreType.DMA((4, spans // 2)),
                pltpu.SemaphoreType.DMA((shards,)),
                pltpu.SMEM((1,), jnp.int32),
            ],
        ),
        out_shape=[
            jax.ShapeDtypeStruct((length, columns), kind)
            for columns, kind in (
                (width, BF),
                (HEAD_COLS, BF),
                (HEAD, BF),
                (HEAD, F32),
                (LANES, F32),
            )
        ],
        compiler_params=pltpu.CompilerParams(vmem_limit_bytes=VMEM),
        cost_estimate=pl.CostEstimate(
            flops=2 * length * width * HEAD_COLS + 4 * length * length * HEAD,
            bytes_accessed=8 * length * width,
            transcendentals=GROUP * length * length,
        ),
        name="stream_attention",
    )(place, starts, *pieces, *head_weights, side)


def home_kernel(copies, place, own, tokens, side, *refs):
    weights, (middle, second) = refs[:-2], refs[-2:]
    shards = len(weights)
    heads = HK // shards
    total = tokens[...].astype(F32)
    for r, weight in enumerate(weights):
        first = (place[1] ^ r) * heads
        for h in range(heads):
            part = own[(first + h) * copies]
            for i in range(1, copies):
                part = part + own[(first + h) * copies + i]
            total = total + dot(part, weight[h * HEAD : (h + 1) * HEAD, :])
    middle[...] = total
    gain = side[EXPERTS + 1 : EXPERTS + 2, :].astype(F32)
    second[...] = (total * rms_factor(total) * gain).astype(BF)


def home_forward(place, own, tokens, side, weights, copies):
    args = (own, tokens, side, *weights)
    return pl.pallas_call(
        functools.partial(home_kernel, copies),
        grid_spec=pltpu.PrefetchScalarGridSpec(
            num_scalar_prefetch=1,
            grid=(1,),
            in_specs=[whole(a) for a in args],
            out_specs=[whole(tokens)] * 2,
        ),
        out_shape=[
            jax.ShapeDtypeStruct(tokens.shape, F32),
            jax.ShapeDtypeStruct(tokens.shape, BF),
        ],
        compiler_params=pltpu.CompilerParams(vmem_limit_bytes=VMEM),
        cost_estimate=pl.CostEstimate(
            flops=2 * tokens.size * tokens.shape[1],
            bytes_accessed=8 * tokens.size + 2 * tokens.shape[1] ** 2,
            transcendentals=tokens.shape[0],
        ),
        name="home_forward",
    )(place, *args)


def turn_kernel(copies, term_count, place, *refs):
    terms, refs = refs[:term_count], refs[term_count:]
    middle_ref, second_ref, grad, routes, side, *weights = refs[:-3]
    d_middle_out, sent, small = refs[-3:]
    shards = len(weights)
    heads = HK // shards
    width = middle_ref.shape[1]
    back = terms[0][...].astype(F32)
    for term in terms[1:]:
        back = back + term[...].astype(F32)
    middle, second = middle_ref[...], second_ref[...]
    d_gates = back[:, width : width + EXTRA]
    ids = iota(d_gates.shape, 1)
    d_gates = d_gates + back[:, width + EXPERTS : width + EXPERTS + EXTRA]
    picked = (ids == routes[:, 0:1]) | (ids == routes[:, 1:2])
    logits = jnp.where(picked, dot_t(second, side[...]), MASK_NEG)
    gates = jnp.where(picked, jnp.exp(logits - jnp.max(logits, axis=1, keepdims=True)), 0.0)
    gates = gates / jnp.sum(gates, axis=1, keepdims=True)
    d_gates = jnp.where(picked, d_gates, 0.0)
    d_picked = gates * (d_gates - jnp.sum(gates * d_gates, axis=1, keepdims=True))
    d_logits = d_picked.astype(BF)
    d_second = dot(d_logits, side[...]) + back[:, :width]
    factor = rms_factor(middle)
    small[...] = t_dot(d_logits, second)
    small[EXPERTS : EXPERTS + 1, :] = jnp.sum(d_second * middle * factor, axis=0, keepdims=True)
    gain = side[EXPERTS + 1 : EXPERTS + 2, :].astype(F32)
    d_middle = grad[...].astype(F32) + rms_input_grad(middle, factor, gain, d_second)
    d_middle_out[...] = d_middle
    d_proj = d_middle.astype(BF)
    for r, weight in enumerate(weights):
        d_heads = dot_t(d_proj, weight[...]).astype(BF)
        for h in range(heads):
            for i in range(copies):
                spot = ((place[1] ^ r) * heads + h) * copies + i
                sent[spot, :, :HEAD] = d_heads[:, h * HEAD : (h + 1) * HEAD]
    chunk = sent.shape[2] - HEAD
    for span in range(sent.shape[0]):
        sent[span, :, HEAD:] = d_proj[:, span * chunk : (span + 1) * chunk]


def home_turn(place, terms, middle, second, grad, routes, side, weights, spans):
    args = (*terms, middle, second, grad, routes, side, *weights)
    tokens, width = middle.shape
    shapes = [
        jax.ShapeDtypeStruct((tokens, width), F32),
        jax.ShapeDtypeStruct((spans, tokens, HEAD + width // spans), BF),
        jax.ShapeDtypeStruct((EXTRA, width), F32),
    ]
    return pl.pallas_call(
        functools.partial(turn_kernel, spans // HK, len(terms)),
        grid_spec=pltpu.PrefetchScalarGridSpec(
            num_scalar_prefetch=1,
            grid=(1,),
            in_specs=[whole(a) for a in args],
            out_specs=[whole(shape) for shape in shapes],
        ),
        out_shape=shapes,
        compiler_params=pltpu.CompilerParams(vmem_limit_bytes=VMEM),
        cost_estimate=pl.CostEstimate(
            flops=2 * tokens * width * width,
            bytes_accessed=24 * tokens * width + 2 * width * width,
            transcendentals=tokens,
        ),
        name="home_turn",
    )(place, *args)


def stream_grad_kernel(
    copies, place, starts, pieces0, pieces1, pieces2, pieces3, sent, mixed, attended, log_norm,
    normed, small, d_mixed, out, everyones, d_kv, sems
):
    here, shard = place[0], place[1]
    length, width = normed.shape
    spans = everyones.shape[0]
    tokens = length // spans
    shards = out.shape[0]
    shard_rows = width // shards
    heads = HK // shards
    copying = place_pieces(here, (pieces0, pieces1, pieces2, pieces3), everyones, sems)
    d_kv[...] = jnp.zeros_like(d_kv)
    for first in range(0, length, QUERIES):
        keys = first + QUERIES
        at = slice(first, keys)
        allowed = visible(starts, here, copies, tokens, first, QUERIES, keys)
        k, v = mixed[:keys, HEAD : HEAD + HD], mixed[:keys, HEAD + HD :]
        for g in range(GROUP):
            columns = slice(g * HD, (g + 1) * HD)
            q, grad = mixed[at, columns], sent[at, columns]
            delta = jnp.sum(grad.astype(F32) * attended[at, columns], axis=1, keepdims=True)
            scores = dot_t(q, k) * SCALE
            probs = jnp.where(allowed, jnp.exp(scores - log_norm[at, g : g + 1]), 0.0)
            d_scores = (probs * (dot_t(grad, v) - delta)).astype(BF)
            d_mixed[at, columns] = (dot(d_scores, k) * SCALE).astype(BF)
            d_kv[0, :keys, :] += t_dot(d_scores, q)
            d_kv[1, :keys, :] += t_dot(probs.astype(BF), grad)
    d_mixed[:, HEAD : HEAD + HD] = (d_kv[0] * SCALE).astype(BF)
    d_mixed[:, HEAD + HD :] = d_kv[1].astype(BF)
    for copy in copying:
        copy.wait()
    d_proj = sent[:, HEAD:]
    low = small[...].astype(BF)
    for f in range(shards):
        spot = shard ^ f
        columns = slice(f * shard_rows, (f + 1) * shard_rows)
        out[spot, :shard_rows, :HEAD_COLS] = t_dot(normed[:, columns], d_mixed[...]).astype(BF)
        for h in range(heads):
            first = (f * heads + h) * copies
            part = everyones[first]
            for i in range(1, copies):
                part = part + everyones[first + i]
            out[spot, h * HEAD : (h + 1) * HEAD, HEAD_COLS:] = t_dot(part, d_proj).astype(BF)
        out[spot, shard_rows:, :] = jnp.zeros((EXTRA, out.shape[2]), BF)
        out[spot, shard_rows:, :shard_rows] = low[:, columns]


def stream_backward(place, starts, pieces, sent, mixed, attended, log_norm, normed, small, shards):
    args = (sent, mixed, attended, log_norm, normed, small)
    length, width = normed.shape
    spans = 2 * pieces[0].shape[0]
    shapes = [
        jax.ShapeDtypeStruct(mixed.shape, BF),
        jax.ShapeDtypeStruct(
            (shards, width // shards + EXTRA, HEAD_COLS + width // spans), BF
        ),
    ]
    return pl.pallas_call(
        functools.partial(stream_grad_kernel, spans // HK),
        grid_spec=pltpu.PrefetchScalarGridSpec(
            num_scalar_prefetch=2,
            grid=(1,),
            in_specs=[anywhere()] * 4 + [whole(a) for a in args],
            out_specs=[whole(shape) for shape in shapes],
            scratch_shapes=[
                pltpu.VMEM((spans, length, HEAD), BF),
                pltpu.VMEM((2, length, HD), F32),
                pltpu.SemaphoreType.DMA((4, spans // 2)),
            ],
        ),
        out_shape=shapes,
        compiler_params=pltpu.CompilerParams(vmem_limit_bytes=VMEM),
        cost_estimate=pl.CostEstimate(
            flops=2 * length * width * (HEAD_COLS + width // spans) + 10 * length * length * HEAD,
            bytes_accessed=8 * length * width,
            transcendentals=GROUP * length * length,
        ),
        name="stream_backward",
    )(place, starts, *pieces, *args)


def home_grad_kernel(copies, place, d_home, tokens, side, d_middle, *refs):
    weight_refs, (d_tokens, weight, mixed, d_normed, sems) = refs[:-5], refs[-5:]
    shards = len(weight_refs)
    loading = [
        pltpu.make_async_copy(ref, weight.at[place[1] ^ r], sems.at[r])
        for r, ref in enumerate(weight_refs)
    ]
    for copy in loading:
        copy.start()
    for head in range(HK):
        part = d_home[head * copies]
        if copies > 1:
            part = part.astype(F32)
            for i in range(1, copies):
                part = part + d_home[head * copies + i].astype(F32)
            part = part.astype(BF)
        mixed[:, head * HEAD : (head + 1) * HEAD] = part[:, :HEAD]
        key = Q_COLS + head * HD
        mixed[:, key : key + HD] = part[:, HEAD : HEAD + HD]
        value = key + K_COLS
        mixed[:, value : value + HD] = part[:, HEAD + HD :]
    for copy in loading:
        copy.wait()
    rows = weight.shape[1]
    for f in range(shards):
        d_normed[:, f * rows : (f + 1) * rows] = dot_t(mixed[...], weight[f])
    x = tokens[...].astype(F32)
    gain = side[EXPERTS : EXPERTS + 1, :].astype(F32)
    d_x = rms_input_grad(x, rms_factor(x), gain, d_normed[...])
    d_tokens[...] = (d_middle[...] + d_x).astype(BF)


def home_backward(place, d_home, tokens, side, d_middle, weights, copies):
    args = (d_home, tokens, side, d_middle)
    count, width = tokens.shape
    shards = len(weights)
    columns = Q_COLS + 2 * K_COLS
    return pl.pallas_call(
        functools.partial(home_grad_kernel, copies),
        grid_spec=pltpu.PrefetchScalarGridSpec(
            num_scalar_prefetch=1,
            grid=(1,),
            in_specs=[whole(a) for a in args] + [anywhere()] * shards,
            out_specs=whole(tokens),
            scratch_shapes=[
                pltpu.VMEM((shards, width // shards, columns), BF),
                pltpu.VMEM((count, columns), BF),
                pltpu.VMEM((count, width), F32),
                pltpu.SemaphoreType.DMA((shards,)),
            ],
        ),
        out_shape=jax.ShapeDtypeStruct(tokens.shape, BF),
        compiler_params=pltpu.CompilerParams(vmem_limit_bytes=VMEM),
        cost_estimate=pl.CostEstimate(
            flops=2 * count * width * columns,
            bytes_accessed=2 * width * columns + 12 * count * width,
            transcendentals=count,
        ),
        name="home_backward",
    )(place, *args, *weights)


def collect_kernel(copies, late, own_weight, d_qkv, d_out, small, d_gain):
    rows = own_weight.shape[0]
    chunk = late.shape[2] - HEAD_COLS
    for head in range(HK):
        part = late[head * copies, :rows, :HEAD_COLS].astype(F32)
        for i in range(1, copies):
            part = part + late[head * copies + i, :rows, :HEAD_COLS].astype(F32)
        d_qkv[:, head * HEAD : (head + 1) * HEAD] = part[:, :HEAD]
        key = Q_COLS + head * HD
        d_qkv[:, key : key + HD] = part[:, HEAD : HEAD + HD]
        value = key + K_COLS
        d_qkv[:, value : value + HD] = part[:, HEAD + HD :]
    total = jnp.zeros((EXTRA, rows), F32)
    for span in range(late.shape[0]):
        d_out[:, span * chunk : (span + 1) * chunk] = late[span, :rows, HEAD_COLS:].astype(F32)
        total = total + late[span, rows:, :rows].astype(F32)
    small[...] = total
    d_gain[...] = jnp.sum(d_qkv[...] * own_weight[...].astype(F32), axis=1, keepdims=True)


def collected(late, own_weight, width, copies):
    rows, columns = own_weight.shape
    shapes = [
        jax.ShapeDtypeStruct((rows, columns), F32),
        jax.ShapeDtypeStruct((rows, width), F32),
        jax.ShapeDtypeStruct((EXTRA, rows), F32),
        jax.ShapeDtypeStruct((rows, 1), F32),
    ]
    return pl.pallas_call(
        functools.partial(collect_kernel, copies),
        grid=(1,),
        in_specs=[whole(late), whole(own_weight)],
        out_specs=[whole(shape) for shape in shapes],
        out_shape=shapes,
        compiler_params=pltpu.CompilerParams(vmem_limit_bytes=VMEM),
        name="collected",
    )(late, own_weight)


def picked_gates(second, router_t, chosen):
    logits = dot_t(router_t, second)
    ids = iota(logits.shape, 0)
    picked = (ids == chosen[0:1, :]) | (ids == chosen[1:2, :])
    logits = jnp.where(picked, logits, MASK_NEG)
    parts = jnp.where(picked, jnp.exp(logits - jnp.max(logits, axis=0, keepdims=True)), 0.0)
    return picked, parts / jnp.sum(parts, axis=0, keepdims=True)


def swiglu_grads(gate, up, d_hidden):
    sigma = 1.0 / (1.0 + jnp.exp(-gate))
    passed = gate * sigma
    d_gate = d_hidden * up * sigma * (1.0 + gate * (1.0 - sigma))
    return (passed * up).astype(BF), d_gate.astype(BF), (d_hidden * passed).astype(BF)


def near_kernel(shards, place, *refs):
    second, grads = refs[:shards], refs[shards : 2 * shards]
    router_t, w_gate, w_up, w_down = refs[2 * shards : 2 * shards + 4]
    branch_out = refs[2 * shards + 4 : 3 * shards + 4]
    back_out = refs[3 * shards + 4 : 4 * shards + 4]
    hot, rows, cots, d_outs, slot_gate, out_acc, row_acc, branch_acc, back_acc = refs[
        4 * shards + 4 :
    ]
    expert, tile = pl.program_id(0), pl.program_id(1)
    tokens = second[0].shape[0]
    width = second[0].shape[1]
    wanted = place[1] * pl.num_programs(0) + expert

    @pl.when(tile == 0)
    def _():
        before = (iota((tokens, tokens), 0) < iota((tokens, tokens), 1)).astype(BF)
        for f in range(shards):
            chosen = grads[f][tokens : tokens + EXTRA, :tokens].astype(F32).astype(jnp.int32)
            picked, gates = picked_gates(second[f][...], router_t[...], chosen)
            ranks = dot(picked.astype(BF), before)
            found = (iota(ranks.shape, 0) == wanted) & picked
            rank = jnp.sum(jnp.where(found, ranks + 1.0, 0.0), axis=0, keepdims=True)
            gate = jnp.sum(jnp.where(found, gates, 0.0), axis=0, keepdims=True)
            match = iota((CAP, tokens), 0).astype(F32) + 1.0 == rank
            one_hot = match.astype(BF)
            place = pl.ds(f * CAP, CAP)
            hot[f] = one_hot
            found_gate = jnp.sum(jnp.where(match, gate, 0.0), axis=1, keepdims=True)
            slot_gate[place, :] = jnp.broadcast_to(found_gate, (CAP, LANES))
            rows[place, :] = dot(one_hot, second[f][...]).astype(BF)
            cot = dot(one_hot, grads[f][:tokens, :])
            cots[place, :] = cot.astype(BF)
            d_outs[place, :] = (found_gate * cot).astype(BF)
        out_acc[...] = jnp.zeros_like(out_acc)
        row_acc[...] = jnp.zeros_like(row_acc)

    hidden, d_gate, d_up = swiglu_grads(
        dot(rows[...], w_gate[0]), dot(rows[...], w_up[0]), dot(d_outs[...], w_down[0])
    )
    out_acc[...] += dot_t(hidden, w_down[0])
    row_acc[...] += dot_t(d_gate, w_gate[0]) + dot_t(d_up, w_up[0])

    @pl.when(tile == pl.num_programs(1) - 1)
    def _():
        last = expert == pl.num_programs(0) - 1
        for f in range(shards):
            place = pl.ds(f * CAP, CAP)
            out = out_acc[place, :].astype(BF).astype(F32)
            d_gates = jnp.sum(cots[place, :].astype(F32) * out, axis=1, keepdims=True)
            gated = (slot_gate[place, 0:1] * out).astype(BF)
            lane = iota((CAP, LANES), 1)
            coarse = d_gates.astype(BF).astype(F32)
            extra = jnp.where(lane == wanted, coarse, 0.0)
            extra = extra + jnp.where(lane == EXPERTS + wanted, d_gates - coarse, 0.0)

            def add(acc, part, columns):
                @pl.when(expert == 0)
                def _():
                    acc[f, :, columns] = part

                @pl.when(expert > 0)
                def _():
                    acc[f, :, columns] += part

            add(branch_acc, t_dot(hot[f], gated), slice(0, width))
            add(back_acc, t_dot(hot[f], row_acc[place, :].astype(BF)), slice(0, width))
            add(back_acc, t_dot(hot[f], extra.astype(BF)), slice(width, width + LANES))

            @pl.when(last)
            def _():
                branch_out[f][...] = branch_acc[f].astype(BF)
                back_out[f][...] = back_acc[f].astype(BF)


def near_experts(place, second, grads, router_t, w_experts):
    shards = len(second)
    tokens, width = second[0].shape
    experts = w_experts.shape[0]
    slots = shards * CAP
    tiles = FF // TILE
    shapes = [jax.ShapeDtypeStruct((tokens, width), BF)] * shards
    shapes += [jax.ShapeDtypeStruct((tokens, width + LANES), BF)] * shards

    def weight(part):
        return pl.BlockSpec((1, width, TILE), lambda e, j, s: (e, 0, part * tiles + j))

    outs = pl.pallas_call(
        functools.partial(near_kernel, shards),
        grid_spec=pltpu.PrefetchScalarGridSpec(
            num_scalar_prefetch=1,
            grid=(experts, tiles),
            in_specs=[whole(a) for a in (*second, *grads, router_t)]
            + [weight(0), weight(1), weight(2)],
            out_specs=[whole(shape) for shape in shapes],
            scratch_shapes=[
                pltpu.VMEM((shards, CAP, tokens), BF),
                pltpu.VMEM((slots, width), BF),
                pltpu.VMEM((slots, width), BF),
                pltpu.VMEM((slots, width), BF),
                pltpu.VMEM((slots, LANES), F32),
                pltpu.VMEM((slots, width), F32),
                pltpu.VMEM((slots, width), F32),
                pltpu.VMEM((shards, tokens, width), F32),
                pltpu.VMEM((shards, tokens, width + LANES), F32),
            ],
        ),
        out_shape=shapes,
        compiler_params=pltpu.CompilerParams(vmem_limit_bytes=VMEM),
        cost_estimate=pl.CostEstimate(
            flops=12 * experts * slots * width * FF,
            bytes_accessed=w_experts.size * 2,
            transcendentals=experts * slots * FF,
        ),
        name="near_experts",
    )(place, *second, *grads, router_t, w_experts, w_experts, w_experts)
    return outs[:shards], outs[shards:]


def far_kernel(
    place,
    router_t,
    second_ref,
    grads_ref,
    w_gate,
    w_up,
    w_down,
    out_ref,
    rows,
    d_outs,
    act,
    fetched_rows,
    fetched_grads,
    tile_out,
    counts,
    fetch_sem,
    store_sem,
):
    experts = rows.shape[0]
    expert, tile = pl.program_id(0), pl.program_id(1)
    tiles = pl.num_programs(1)
    step = expert * tiles + tile
    slot = lax.rem(step, 2)
    groups = second_ref.shape[0] // JOINED
    tokens, width = second_ref.shape[1:]
    size = JOINED * tokens
    window = JOINED * CAP + 16

    def stores(which, e, j):
        return [
            pltpu.make_async_copy(
                tile_out.at[which, i],
                out_ref.at[e, :, pl.ds(pl.multiple_of(i * FF + j * TILE, TILE), TILE)],
                store_sem.at[which, i],
            )
            for i in range(3)
        ]

    def fetches(which, g):
        at = pl.ds(g * JOINED, JOINED)
        return [
            pltpu.make_async_copy(ref.at[at], buffer.at[which], fetch_sem.at[which, i])
            for i, (ref, buffer) in enumerate(
                ((second_ref, fetched_rows), (grads_ref, fetched_grads))
            )
        ]

    @pl.when(step == 0)
    def _():
        for copy in fetches(0, 0):
            copy.start()
        before = (iota((size, size), 0) < iota((size, size), 1)).astype(BF)

        def gather(g, starts):
            which = lax.rem(g, 2)
            for copy in fetches(which, g):
                copy.wait()

            @pl.when(g + 1 < groups)
            def _():
                for copy in fetches(1 - which, g + 1):
                    copy.start()

            second = fetched_rows[which].reshape(size, width)
            grads = fetched_grads[which, :, :tokens].reshape(size, width)
            chosen = jnp.concatenate(
                [fetched_grads[which, b, tokens : tokens + EXTRA, :LANES] for b in range(JOINED)],
                axis=1,
            )
            chosen = chosen.astype(F32).astype(jnp.int32)
            picked, gates = picked_gates(second, router_t[...], chosen)
            ranks = dot(picked.astype(BF), before)
            ids = iota(ranks.shape, 0)
            bases = [start // 16 * 16 for start in starts]
            matches, found_gates, ends = [], [], []
            for e in range(experts):
                found = (ids == place[1] * experts + e) & picked
                gate = jnp.sum(jnp.where(found, gates, 0.0), axis=0, keepdims=True)
                rank = jnp.sum(jnp.where(found, ranks + 1.0, 0.0), axis=0, keepdims=True)
                shift = (starts[e] - bases[e]).astype(F32)
                spot = jnp.where(rank > 0.0, rank + (shift - 1.0), -1.0)
                match = iota((window, size), 0).astype(F32) == spot
                matches.append(match.astype(BF))
                found_gates.append(
                    jnp.sum(jnp.where(match, gate, 0.0), axis=1, keepdims=True)
                )
                ends.append(starts[e] + jnp.sum((rank > 0.0).astype(jnp.int32)))
            one_hot = jnp.concatenate(matches, axis=0)
            new_rows = dot(one_hot, second).astype(BF)
            new_grads = (jnp.concatenate(found_gates, axis=0) * dot(one_hot, grads)).astype(BF)
            for e in range(experts):
                at = pl.ds(pl.multiple_of(bases[e], 16), 16)
                rest = pl.ds(pl.multiple_of(bases[e] + 16, 16), window - 16)
                held = iota((16, width), 0) < starts[e] - bases[e]
                for ref, new in ((rows, new_rows), (d_outs, new_grads)):
                    new = new[e * window : (e + 1) * window]
                    ref[e, at, :] = jnp.where(held, ref[e, at, :], new[:16])
                    ref[e, rest, :] = new[16:]
            return tuple(ends)

        ends = lax.fori_loop(0, groups, gather, (jnp.int32(0),) * experts)
        for e in range(experts):
            counts[e] = ends[e]
            spare = pl.ds(pl.multiple_of((ends[e] + 15) // 16 * 16, 16), CHUNK)
            rows[e, spare, :] = jnp.zeros((CHUNK, width), BF)
            d_outs[e, spare, :] = jnp.zeros((CHUNK, width), BF)

    chunks = jnp.maximum((counts[expert] + CHUNK - 1) // CHUNK, 1)

    @pl.loop(0, chunks)
    def _(i):
        at = pl.ds(pl.multiple_of(i * CHUNK, CHUNK), CHUNK)
        row, d_out = rows[expert, at, :], d_outs[expert, at, :]
        hidden, d_gate, d_up = swiglu_grads(
            dot(row, w_gate[0]), dot(row, w_up[0]), dot(d_out, w_down[0])
        )
        act[0, at, :] = d_gate
        act[1, at, :] = d_up
        act[2, at, :] = hidden

    @pl.when(step >= 2)
    def _():
        for copy in stores(slot, (step - 2) // tiles, lax.rem(step - 2, tiles)):
            copy.wait()

    most = act.shape[1] // CHUNK
    depths = [k for k in DEPTHS if k < most] + [most]
    for low, k in zip([0] + depths[:-1], depths):

        @pl.when((chunks > low) & (chunks <= k))
        def _():
            for extra in range(low + 1, k):

                @pl.when(chunks == extra)
                def _():
                    spare = slice(extra * CHUNK, k * CHUNK)
                    empty = jnp.zeros(((k - extra) * CHUNK, width), BF)
                    rows[expert, spare, :] = empty
                    d_outs[expert, spare, :] = empty
                    for i in range(3):
                        act[i, spare, :] = empty[:, :TILE]

            upto = k * CHUNK
            for i, left in enumerate((rows, rows, d_outs)):
                tile_out[slot, i] = t_dot(left[expert, :upto, :], act[i, :upto, :])

    for copy in stores(slot, expert, tile):
        copy.start()

    @pl.when(step == pl.num_programs(0) * tiles - 1)
    def _():
        for copy in stores(1 - slot, (step - 1) // tiles, lax.rem(step - 1, tiles)):
            copy.wait()
        for copy in stores(slot, expert, tile):
            copy.wait()


def far_weight_grads(place, router_t, second, grads, w_experts):
    experts, width = w_experts.shape[:2]
    blocks, tokens = second.shape[:2]
    tiles = FF // TILE
    most = blocks * CAP
    held = most + CHUNK + 16

    def weight(part):
        return pl.BlockSpec((1, width, TILE), lambda e, j, s: (e, 0, part * tiles + j))

    return pl.pallas_call(
        far_kernel,
        grid_spec=pltpu.PrefetchScalarGridSpec(
            num_scalar_prefetch=1,
            grid=(experts, tiles),
            in_specs=[
                whole(router_t),
                anywhere(),
                anywhere(),
                weight(0),
                weight(1),
                weight(2),
            ],
            out_specs=anywhere(),
            scratch_shapes=[
                pltpu.VMEM((experts, held, width), BF),
                pltpu.VMEM((experts, held, width), BF),
                pltpu.VMEM((3, most, TILE), BF),
                pltpu.VMEM((2, JOINED, tokens, width), BF),
                pltpu.VMEM((2, JOINED, tokens + EXTRA, width), BF),
                pltpu.VMEM((2, 3, width, TILE), F32),
                pltpu.SMEM((experts,), jnp.int32),
                pltpu.SemaphoreType.DMA((2, 2)),
                pltpu.SemaphoreType.DMA((2, 3)),
            ],
        ),
        out_shape=jax.ShapeDtypeStruct((experts, width, 3 * FF), F32),
        compiler_params=pltpu.CompilerParams(vmem_limit_bytes=VMEM),
        cost_estimate=pl.CostEstimate(
            flops=8 * experts * most * width * FF,
            bytes_accessed=w_experts.size * 6 + 4 * blocks * tokens * width,
            transcendentals=experts * most * FF,
        ),
        name="far_weight_grads",
    )(place, router_t, second, grads, w_experts, w_experts, w_experts)


def per_device(
    tokens,
    query_key_value_weight,
    output_weight,
    routing_weight,
    gain_attn,
    gain_moe,
    w_experts,
    doc_starts,
    routes,
    cotangent,
):
    spans = lax.axis_size("ctx")
    shards = lax.axis_size("fsdp")
    here = lax.axis_index("ctx")
    shard = lax.axis_index("fsdp")
    place = jnp.stack([here, shard]).astype(jnp.int32)
    x, grad = tokens[0], cotangent[0]
    tok_count, width = x.shape
    shard_rows = query_key_value_weight.shape[0]
    copies = spans // HK
    head = here // copies
    length = spans * tok_count
    blocks = spans * shards

    side = jnp.concatenate(
        [
            routing_weight.T,
            gain_attn[None],
            gain_moe[None],
            jnp.zeros((EXTRA - EXPERTS - 2, shard_rows), BF),
        ]
    )
    head_w = jnp.concatenate(
        [
            lax.dynamic_slice_in_dim(query_key_value_weight, head * HEAD, HEAD, 1),
            lax.dynamic_slice_in_dim(query_key_value_weight, Q_COLS + head * HD, HD, 1),
            lax.dynamic_slice_in_dim(query_key_value_weight, Q_COLS + K_COLS + head * HD, HD, 1),
        ],
        axis=1,
    )
    side = jnp.stack(near_blocks(side))
    side = jnp.take(side, jnp.arange(shards, dtype=jnp.int32) ^ shard, axis=0)
    side = side.swapaxes(0, 1).reshape(EXTRA, width)
    head_w = near_blocks(head_w)
    pieces = span_pieces(x)

    payload = jnp.concatenate(
        [grad, jnp.pad(routes[0].T.astype(BF), ((0, EXTRA - 2), (0, width - tok_count)))]
    )
    payload, output_weight = after((payload, output_weight), pieces)
    out_w = near_blocks(output_weight)
    grads_near = near_blocks(payload)
    grads_line = line_blocks(payload)
    grads_all = all_blocks(grads_line)

    normed, mixed, attended_low, attended, log_norm = stream_attention(
        place, doc_starts[0], pieces, head_w, side, copies
    )

    attended_low, grads_line = after((attended_low, grads_line), grads_near)
    own = to_all(attended_low, "ctx").reshape(spans, tok_count, HEAD)
    middle, second = home_forward(place, own, x, side, out_w, copies)
    second_near = near_blocks(second)
    second_line = line_blocks(second)
    second_all = all_blocks(second_line)

    branch, back = near_experts(place, second_near, grads_near, side, w_experts)
    back = after(back, second_line)
    later_qkv, attended_low = after((query_key_value_weight, attended_low), back)
    qkv_w = near_blocks(later_qkv)
    attended_pieces = span_pieces(attended_low)
    terms = after(near_terms(back), grads_all)
    branch_terms = near_terms(branch)
    output = sum((term.astype(F32) for term in branch_terms), middle).astype(BF)

    d_middle, sent, small = home_turn(
        place, terms, middle, second, grad, routes[0], side, out_w, spans
    )

    sent = to_all(sent.reshape(length, -1), "ctx")
    d_mixed, grads_out = stream_backward(
        place, doc_starts[0], attended_pieces, sent, mixed, attended, log_norm, normed, small, shards
    )
    late = near_terms([grads_out[r] for r in range(shards)])
    late = sum((term.astype(F32) for term in late[1:]), late[0].astype(F32)).astype(BF)
    late = lax.all_gather(after(late, second_all), "ctx", axis=0)

    d_home = to_all(d_mixed, "ctx").reshape(spans, tok_count, HEAD_COLS)
    d_tokens = home_backward(place, d_home, x, side, d_middle, qkv_w, copies)

    second_all = second_all.reshape(blocks, tok_count, width)
    grads_all = grads_all.reshape(blocks, tok_count + EXTRA, width)
    segment = min(blocks, SEGMENT)
    parts = [
        far_weight_grads(
            place, side, second_all[i : i + segment], grads_all[i : i + segment], w_experts
        )
        for i in range(0, blocks, segment)
    ]
    d_w_experts = sum(parts[1:], parts[0])

    d_qkv_w, d_out_w, small, d_gain_attn = collected(
        late, query_key_value_weight, width, copies
    )
    return (
        output[None],
        d_tokens[None],
        d_qkv_w,
        d_out_w,
        small[:EXPERTS].T,
        d_gain_attn[:, 0] / gain_attn.astype(F32),
        small[EXPERTS],
        d_w_experts,
    )


def solution(mesh):
    placed = (
        P("fsdp", "ctx", None),
        P("fsdp", None),
        P("fsdp", None),
        P("fsdp", None),
        P("fsdp"),
        P("fsdp"),
        P("fsdp", None, None),
        P("fsdp", None),
        P("fsdp", "ctx", None),
        P("fsdp", "ctx", None),
    )
    return jax.shard_map(
        per_device,
        mesh=mesh,
        in_specs=placed,
        out_specs=(
            P("fsdp", "ctx", None),
            P("fsdp", "ctx", None),
            P("fsdp", None),
            P("fsdp", None),
            P("fsdp", None),
            P("fsdp"),
            P("fsdp"),
            P("fsdp", None, None),
        ),
        check_vma=False,
    )
```

```python
import functools

import jax
import jax.numpy as jnp
from jax import lax
from jax.experimental import pallas as pl
from jax.experimental.pallas import tpu as pltpu
from jax.sharding import PartitionSpec as P

HQ = 24
HK = 8
HD = 64
GROUP = HQ // HK
FF = 1024
EXPERTS = 8
CAP = 64
Q_COLS = HQ * HD
K_COLS = HK * HD
HEAD = GROUP * HD
HEAD_COLS = HEAD + 2 * HD
SCALE = HD**-0.5
EXTRA = 16
LANES = 128
TILE = 256
CHUNK = 256
SEGMENT = 32
JOINED = 2
QUERIES = 256
DEPTHS = (1, 2, 3, 4, 6, 8)
VMEM = 58 * 1024 * 1024

NORM_EPS = 1e-05
MASK_NEG = -1e30
BF = jnp.bfloat16
F32 = jnp.float32


def dot(a, b):
    return jnp.dot(a, b, preferred_element_type=F32)


def dot_t(a, b):
    return lax.dot_general(a, b, (((1,), (1,)), ((), ())), preferred_element_type=F32)


def t_dot(a, b):
    return lax.dot_general(a, b, (((0,), (0,)), ((), ())), preferred_element_type=F32)


def iota(shape, axis):
    return lax.broadcasted_iota(jnp.int32, shape, axis)


def rms_factor(values):
    return lax.rsqrt(jnp.mean(values * values, axis=-1, keepdims=True) + NORM_EPS)


def rms_input_grad(values, factor, gain_vec, incoming):
    inner = incoming * gain_vec
    cubed = factor * factor * factor
    return factor * inner - values * cubed * jnp.mean(inner * values, axis=-1, keepdims=True)


def to_all(value, axis):
    return lax.all_to_all(value, axis, 0, 0, tiled=True)


def gathered(value, axis):
    return lax.all_gather(value, axis, axis=0, tiled=True)


def exchanged(value, axis, distance):
    count = lax.axis_size(axis)
    return lax.ppermute(value, axis, [(i, i ^ distance) for i in range(count)])


def near_blocks(own):
    blocks = {0: own}
    distance = lax.axis_size("fsdp") // 2
    while distance:
        blocks.update({r ^ distance: exchanged(b, "fsdp", distance) for r, b in blocks.items()})
        distance //= 2
    return [blocks[r] for r in range(len(blocks))]


def near_terms(blocks):
    shards = lax.axis_size("fsdp")
    terms = {r: [block] for r, block in enumerate(blocks)}
    distance = 1

    def total(parts):
        if len(parts) == 1:
            return parts[0]
        return sum((part.astype(F32) for part in parts[1:]), parts[0].astype(F32)).astype(BF)

    while distance < shards:
        terms = {
            r: terms[r] + [exchanged(total(terms[r ^ distance]), "fsdp", distance)]
            for r in range(0, shards, 2 * distance)
        }
        distance *= 2
    return terms[0]


def line_blocks(own):
    spans = lax.axis_size("ctx")
    return jnp.stack([own] + [exchanged(own, "ctx", d) for d in range(2, spans, 2)])


def span_pieces(own, *others):
    half = own.shape[0] // 2
    same = [line_blocks(part) for part in (own[:half], own[half:])]
    same = after(same, *others)
    return same + [exchanged(part, "ctx", 1) for part in same]


def all_blocks(line):
    spans, shards = lax.axis_size("ctx"), lax.axis_size("fsdp")
    sets = [
        [(2 * pair + side) * shards + f for side in range(2) for f in range(shards)]
        for pair in range(spans // 2)
    ]
    return lax.all_gather(line, ("ctx", "fsdp"), axis=0, tiled=True, axis_index_groups=sets)


def after(values, *others):
    return lax.optimization_barrier((values, others))[0]


def time_of(microseconds):
    return pl.CostEstimate(flops=0, bytes_accessed=microseconds * 3_600_000, transcendentals=0)


def whole(array):
    shape = array.shape
    return pl.BlockSpec(shape, lambda *_: (0,) * len(shape))


def anywhere():
    return pl.BlockSpec(memory_space=pl.ANY)


def place_pieces(here, pieces, target, sems):
    copies = []
    for i, piece in enumerate(pieces):
        odd, last = divmod(i, 2)
        rows = piece.shape[1]
        for j in range(piece.shape[0]):
            copies.append(
                pltpu.make_async_copy(
                    piece.at[j],
                    target.at[here ^ (2 * j + odd), pl.ds(last * rows, rows)],
                    sems.at[i, j],
                )
            )
    for copy in copies:
        copy.start()
    return copies


def doc_of(starts, positions):
    found = jnp.zeros(positions.shape, jnp.int32)
    for i in range(starts.shape[0]):
        found = found + (positions >= starts[i]).astype(jnp.int32)
    return found


def visible(starts, here, copies, tokens, first, rows, keys):
    query = first + iota((rows, 1), 0)
    key = iota((1, keys), 1)
    allowed = (key <= query) & (doc_of(starts, key) == doc_of(starts, query))
    if copies > 1:
        allowed = allowed & (lax.rem(query // tokens, copies) == lax.rem(here, copies))
    return allowed


def stream_kernel(
    copies,
    place,
    starts,
    *refs,
):
    shards = len(refs) - 15
    pieces, weights, side = refs[:4], refs[4 : 4 + shards], refs[4 + shards]
    normed, mixed, attended_low, attended, log_norm, rows, weight, piece_sems, weight_sems = refs[
        5 + shards : 14 + shards
    ]
    here, shard = place[0], place[1]
    spans, tokens, width = rows.shape
    length = spans * tokens
    copying = place_pieces(here, pieces, rows, piece_sems)
    loading = [
        pltpu.make_async_copy(ref, weight.at[shard ^ r], weight_sems.at[r])
        for r, ref in enumerate(weights)
    ]
    for copy in loading:
        copy.start()
    for copy in loading + copying:
        copy.wait()
    head_weight = weight[...].reshape(width, HEAD_COLS)
    gain = side[EXPERTS : EXPERTS + 1, :].astype(F32)

    @pl.loop(0, spans)
    def _(span):
        x = rows[span].astype(F32)
        low = (x * rms_factor(x) * gain).astype(BF)
        at = pl.ds(pl.multiple_of(span * tokens, tokens), tokens)
        normed[at, :] = low
        mixed[at, :] = dot(low, head_weight).astype(BF)

    for first in range(0, length, QUERIES):
        keys = first + QUERIES
        at = slice(first, keys)
        allowed = visible(starts, here, copies, tokens, first, QUERIES, keys)
        for g in range(GROUP):
            columns = slice(g * HD, (g + 1) * HD)
            scores = dot_t(mixed[at, columns], mixed[:keys, HEAD : HEAD + HD]) * SCALE
            scores = jnp.where(allowed, scores, MASK_NEG)
            highest = jnp.max(scores, axis=1, keepdims=True)
            parts = jnp.where(allowed, jnp.exp(scores - highest), 0.0)
            total = jnp.sum(parts, axis=1, keepdims=True)
            total = jnp.where(total == 0.0, 1.0, total)
            log_norm[at, g : g + 1] = highest + jnp.log(total)
            result = dot((parts / total).astype(BF), mixed[:keys, HEAD + HD :])
            attended[at, columns] = result
            attended_low[at, columns] = result.astype(BF)


def stream_attention(place, starts, pieces, head_weights, side, copies):
    spans, tokens = 2 * pieces[0].shape[0], 2 * pieces[0].shape[1]
    width = pieces[0].shape[2]
    length = spans * tokens
    shards = len(head_weights)
    return pl.pallas_call(
        functools.partial(stream_kernel, copies),
        grid_spec=pltpu.PrefetchScalarGridSpec(
            num_scalar_prefetch=2,
            grid=(1,),
            in_specs=[anywhere()] * (4 + shards) + [whole(side)],
            out_specs=[
                pl.BlockSpec((length, columns), lambda *_: (0, 0))
                for columns in (width, HEAD_COLS, HEAD, HEAD, LANES)
            ],
            scratch_shapes=[
                pltpu.VMEM((spans, tokens, width), BF),
                pltpu.VMEM((shards, width // shards, HEAD_COLS), BF),
                pltpu.SemaphoreType.DMA((4, spans // 2)),
                pltpu.SemaphoreType.DMA((shards,)),
                pltpu.SMEM((1,), jnp.int32),
            ],
        ),
        out_shape=[
            jax.ShapeDtypeStruct((length, columns), kind)
            for columns, kind in (
                (width, BF),
                (HEAD_COLS, BF),
                (HEAD, BF),
                (HEAD, F32),
                (LANES, F32),
            )
        ],
        compiler_params=pltpu.CompilerParams(vmem_limit_bytes=VMEM),
        cost_estimate=time_of(16),
        name="stream_attention",
    )(place, starts, *pieces, *head_weights, side)


def home_kernel(copies, own, tokens, side, weight, middle, second):
    total = tokens[...].astype(F32)
    for head in range(HK):
        part = own[head * copies]
        for i in range(1, copies):
            part = part + own[head * copies + i]
        total = total + dot(part, weight[head * HEAD : (head + 1) * HEAD, :])
    middle[...] = total
    gain = side[EXPERTS + 1 : EXPERTS + 2, :].astype(F32)
    second[...] = (total * rms_factor(total) * gain).astype(BF)


def home_forward(own, tokens, side, weight, copies):
    args = (own, tokens, side, weight)
    return pl.pallas_call(
        functools.partial(home_kernel, copies),
        grid=(1,),
        in_specs=[whole(a) for a in args],
        out_specs=[whole(tokens)] * 2,
        out_shape=[
            jax.ShapeDtypeStruct(tokens.shape, F32),
            jax.ShapeDtypeStruct(tokens.shape, BF),
        ],
        compiler_params=pltpu.CompilerParams(vmem_limit_bytes=VMEM),
        cost_estimate=time_of(5),
        name="home_forward",
    )(*args)


def turn_kernel(copies, term_count, *refs):
    terms, refs = refs[:term_count], refs[term_count:]
    middle_ref, second_ref, grad, routes, side, weight, d_middle_out, sent, small = refs
    width = middle_ref.shape[1]
    back = terms[0][...].astype(F32)
    for term in terms[1:]:
        back = back + term[...].astype(F32)
    middle, second = middle_ref[...], second_ref[...]
    d_gates = back[:, width : width + EXTRA]
    ids = iota(d_gates.shape, 1)
    d_gates = d_gates + back[:, width + EXPERTS : width + EXPERTS + EXTRA]
    picked = (ids == routes[:, 0:1]) | (ids == routes[:, 1:2])
    logits = jnp.where(picked, dot_t(second, side[...]), MASK_NEG)
    gates = jnp.where(picked, jnp.exp(logits - jnp.max(logits, axis=1, keepdims=True)), 0.0)
    gates = gates / jnp.sum(gates, axis=1, keepdims=True)
    d_gates = jnp.where(picked, d_gates, 0.0)
    d_picked = gates * (d_gates - jnp.sum(gates * d_gates, axis=1, keepdims=True))
    d_logits = d_picked.astype(BF)
    d_second = dot(d_logits, side[...]) + back[:, :width]
    factor = rms_factor(middle)
    small[...] = t_dot(d_logits, second)
    small[EXPERTS : EXPERTS + 1, :] = jnp.sum(d_second * middle * factor, axis=0, keepdims=True)
    gain = side[EXPERTS + 1 : EXPERTS + 2, :].astype(F32)
    d_middle = grad[...].astype(F32) + rms_input_grad(middle, factor, gain, d_second)
    d_middle_out[...] = d_middle
    d_proj = d_middle.astype(BF)
    for head in range(HK):
        d_head = dot_t(d_proj, weight[head * HEAD : (head + 1) * HEAD, :]).astype(BF)
        for i in range(copies):
            sent[head * copies + i, :, :HEAD] = d_head
    chunk = sent.shape[2] - HEAD
    for span in range(sent.shape[0]):
        sent[span, :, HEAD:] = d_proj[:, span * chunk : (span + 1) * chunk]


def home_turn(terms, middle, second, grad, routes, side, weight, spans):
    args = (*terms, middle, second, grad, routes, side, weight)
    tokens, width = middle.shape
    shapes = [
        jax.ShapeDtypeStruct((tokens, width), F32),
        jax.ShapeDtypeStruct((spans, tokens, HEAD + width // spans), BF),
        jax.ShapeDtypeStruct((EXTRA, width), F32),
    ]
    return pl.pallas_call(
        functools.partial(turn_kernel, spans // HK, len(terms)),
        grid=(1,),
        in_specs=[whole(a) for a in args],
        out_specs=[whole(shape) for shape in shapes],
        out_shape=shapes,
        compiler_params=pltpu.CompilerParams(vmem_limit_bytes=VMEM),
        cost_estimate=time_of(7),
        name="home_turn",
    )(*args)


def stream_grad_kernel(
    copies, place, starts, pieces0, pieces1, pieces2, pieces3, sent, mixed, attended, log_norm,
    normed, small, d_mixed, out, everyones, d_kv, sems
):
    here, shard = place[0], place[1]
    length, width = normed.shape
    spans = everyones.shape[0]
    tokens = length // spans
    shards = out.shape[0]
    shard_rows = width // shards
    heads = HK // shards
    copying = place_pieces(here, (pieces0, pieces1, pieces2, pieces3), everyones, sems)
    d_kv[...] = jnp.zeros_like(d_kv)
    for first in range(0, length, QUERIES):
        keys = first + QUERIES
        at = slice(first, keys)
        allowed = visible(starts, here, copies, tokens, first, QUERIES, keys)
        k, v = mixed[:keys, HEAD : HEAD + HD], mixed[:keys, HEAD + HD :]
        for g in range(GROUP):
            columns = slice(g * HD, (g + 1) * HD)
            q, grad = mixed[at, columns], sent[at, columns]
            delta = jnp.sum(grad.astype(F32) * attended[at, columns], axis=1, keepdims=True)
            scores = dot_t(q, k) * SCALE
            probs = jnp.where(allowed, jnp.exp(scores - log_norm[at, g : g + 1]), 0.0)
            d_scores = (probs * (dot_t(grad, v) - delta)).astype(BF)
            d_mixed[at, columns] = (dot(d_scores, k) * SCALE).astype(BF)
            d_kv[0, :keys, :] += t_dot(d_scores, q)
            d_kv[1, :keys, :] += t_dot(probs.astype(BF), grad)
    d_mixed[:, HEAD : HEAD + HD] = (d_kv[0] * SCALE).astype(BF)
    d_mixed[:, HEAD + HD :] = d_kv[1].astype(BF)
    for copy in copying:
        copy.wait()
    d_proj = sent[:, HEAD:]
    low = small[...].astype(BF)
    for f in range(shards):
        spot = shard ^ f
        columns = slice(f * shard_rows, (f + 1) * shard_rows)
        out[spot, :shard_rows, :HEAD_COLS] = t_dot(normed[:, columns], d_mixed[...]).astype(BF)
        for h in range(heads):
            first = (f * heads + h) * copies
            part = everyones[first]
            for i in range(1, copies):
                part = part + everyones[first + i]
            out[spot, h * HEAD : (h + 1) * HEAD, HEAD_COLS:] = t_dot(part, d_proj).astype(BF)
        out[spot, shard_rows:, :] = jnp.zeros((EXTRA, out.shape[2]), BF)
        out[spot, shard_rows:, :shard_rows] = low[:, columns]


def stream_backward(place, starts, pieces, sent, mixed, attended, log_norm, normed, small, shards):
    args = (sent, mixed, attended, log_norm, normed, small)
    length, width = normed.shape
    spans = 2 * pieces[0].shape[0]
    shapes = [
        jax.ShapeDtypeStruct(mixed.shape, BF),
        jax.ShapeDtypeStruct(
            (shards, width // shards + EXTRA, HEAD_COLS + width // spans), BF
        ),
    ]
    return pl.pallas_call(
        functools.partial(stream_grad_kernel, spans // HK),
        grid_spec=pltpu.PrefetchScalarGridSpec(
            num_scalar_prefetch=2,
            grid=(1,),
            in_specs=[anywhere()] * 4 + [whole(a) for a in args],
            out_specs=[whole(shape) for shape in shapes],
            scratch_shapes=[
                pltpu.VMEM((spans, length, HEAD), BF),
                pltpu.VMEM((2, length, HD), F32),
                pltpu.SemaphoreType.DMA((4, spans // 2)),
            ],
        ),
        out_shape=shapes,
        compiler_params=pltpu.CompilerParams(vmem_limit_bytes=VMEM),
        cost_estimate=time_of(17),
        name="stream_backward",
    )(place, starts, *pieces, *args)


def home_grad_kernel(copies, d_home, tokens, side, d_middle, weight, d_tokens, mixed):
    for head in range(HK):
        part = d_home[head * copies]
        if copies > 1:
            part = part.astype(F32)
            for i in range(1, copies):
                part = part + d_home[head * copies + i].astype(F32)
            part = part.astype(BF)
        mixed[:, head * HEAD : (head + 1) * HEAD] = part[:, :HEAD]
        key = Q_COLS + head * HD
        mixed[:, key : key + HD] = part[:, HEAD : HEAD + HD]
        value = key + K_COLS
        mixed[:, value : value + HD] = part[:, HEAD + HD :]
    d_normed = dot_t(mixed[...], weight[...])
    x = tokens[...].astype(F32)
    gain = side[EXPERTS : EXPERTS + 1, :].astype(F32)
    d_x = rms_input_grad(x, rms_factor(x), gain, d_normed)
    d_tokens[...] = (d_middle[...] + d_x).astype(BF)


def home_backward(d_home, tokens, side, d_middle, weight, copies):
    args = (d_home, tokens, side, d_middle, weight)
    return pl.pallas_call(
        functools.partial(home_grad_kernel, copies),
        grid=(1,),
        in_specs=[whole(a) for a in args],
        out_specs=whole(tokens),
        scratch_shapes=[pltpu.VMEM((tokens.shape[0], Q_COLS + 2 * K_COLS), BF)],
        out_shape=jax.ShapeDtypeStruct(tokens.shape, BF),
        compiler_params=pltpu.CompilerParams(vmem_limit_bytes=VMEM),
        cost_estimate=time_of(8),
        name="home_backward",
    )(*args)


def collect_kernel(copies, late, own_weight, d_qkv, d_out, small, d_gain):
    rows = own_weight.shape[0]
    chunk = late.shape[2] - HEAD_COLS
    for head in range(HK):
        part = late[head * copies, :rows, :HEAD_COLS].astype(F32)
        for i in range(1, copies):
            part = part + late[head * copies + i, :rows, :HEAD_COLS].astype(F32)
        d_qkv[:, head * HEAD : (head + 1) * HEAD] = part[:, :HEAD]
        key = Q_COLS + head * HD
        d_qkv[:, key : key + HD] = part[:, HEAD : HEAD + HD]
        value = key + K_COLS
        d_qkv[:, value : value + HD] = part[:, HEAD + HD :]
    total = jnp.zeros((EXTRA, rows), F32)
    for span in range(late.shape[0]):
        d_out[:, span * chunk : (span + 1) * chunk] = late[span, :rows, HEAD_COLS:].astype(F32)
        total = total + late[span, rows:, :rows].astype(F32)
    small[...] = total
    d_gain[...] = jnp.sum(d_qkv[...] * own_weight[...].astype(F32), axis=1, keepdims=True)


def collected(late, own_weight, width, copies):
    rows, columns = own_weight.shape
    shapes = [
        jax.ShapeDtypeStruct((rows, columns), F32),
        jax.ShapeDtypeStruct((rows, width), F32),
        jax.ShapeDtypeStruct((EXTRA, rows), F32),
        jax.ShapeDtypeStruct((rows, 1), F32),
    ]
    return pl.pallas_call(
        functools.partial(collect_kernel, copies),
        grid=(1,),
        in_specs=[whole(late), whole(own_weight)],
        out_specs=[whole(shape) for shape in shapes],
        out_shape=shapes,
        compiler_params=pltpu.CompilerParams(vmem_limit_bytes=VMEM),
        cost_estimate=time_of(7),
        name="collected",
    )(late, own_weight)


def picked_gates(second, router_t, chosen):
    logits = dot_t(router_t, second)
    ids = iota(logits.shape, 0)
    picked = (ids == chosen[0:1, :]) | (ids == chosen[1:2, :])
    logits = jnp.where(picked, logits, MASK_NEG)
    parts = jnp.where(picked, jnp.exp(logits - jnp.max(logits, axis=0, keepdims=True)), 0.0)
    return picked, parts / jnp.sum(parts, axis=0, keepdims=True)


def swiglu_grads(gate, up, d_hidden):
    sigma = 1.0 / (1.0 + jnp.exp(-gate))
    passed = gate * sigma
    d_gate = d_hidden * up * sigma * (1.0 + gate * (1.0 - sigma))
    return (passed * up).astype(BF), d_gate.astype(BF), (d_hidden * passed).astype(BF)


def near_kernel(shards, place, *refs):
    second, grads = refs[:shards], refs[shards : 2 * shards]
    router_t, w_gate, w_up, w_down = refs[2 * shards : 2 * shards + 4]
    branch_out = refs[2 * shards + 4 : 3 * shards + 4]
    back_out = refs[3 * shards + 4 : 4 * shards + 4]
    hot, rows, cots, d_outs, slot_gate, out_acc, row_acc, branch_acc, back_acc = refs[
        4 * shards + 4 :
    ]
    expert, tile = pl.program_id(0), pl.program_id(1)
    tokens = second[0].shape[0]
    width = second[0].shape[1]
    wanted = place[1] * pl.num_programs(0) + expert

    @pl.when(tile == 0)
    def _():
        before = (iota((tokens, tokens), 0) < iota((tokens, tokens), 1)).astype(BF)
        for f in range(shards):
            chosen = grads[f][tokens : tokens + EXTRA, :tokens].astype(F32).astype(jnp.int32)
            picked, gates = picked_gates(second[f][...], router_t[...], chosen)
            ranks = dot(picked.astype(BF), before)
            found = (iota(ranks.shape, 0) == wanted) & picked
            rank = jnp.sum(jnp.where(found, ranks + 1.0, 0.0), axis=0, keepdims=True)
            gate = jnp.sum(jnp.where(found, gates, 0.0), axis=0, keepdims=True)
            match = iota((CAP, tokens), 0).astype(F32) + 1.0 == rank
            one_hot = match.astype(BF)
            place = pl.ds(f * CAP, CAP)
            hot[f] = one_hot
            found_gate = jnp.sum(jnp.where(match, gate, 0.0), axis=1, keepdims=True)
            slot_gate[place, :] = jnp.broadcast_to(found_gate, (CAP, LANES))
            rows[place, :] = dot(one_hot, second[f][...]).astype(BF)
            cot = dot(one_hot, grads[f][:tokens, :])
            cots[place, :] = cot.astype(BF)
            d_outs[place, :] = (found_gate * cot).astype(BF)
        out_acc[...] = jnp.zeros_like(out_acc)
        row_acc[...] = jnp.zeros_like(row_acc)

    hidden, d_gate, d_up = swiglu_grads(
        dot(rows[...], w_gate[0]), dot(rows[...], w_up[0]), dot(d_outs[...], w_down[0])
    )
    out_acc[...] += dot_t(hidden, w_down[0])
    row_acc[...] += dot_t(d_gate, w_gate[0]) + dot_t(d_up, w_up[0])

    @pl.when(tile == pl.num_programs(1) - 1)
    def _():
        last = expert == pl.num_programs(0) - 1
        for f in range(shards):
            place = pl.ds(f * CAP, CAP)
            out = out_acc[place, :].astype(BF).astype(F32)
            d_gates = jnp.sum(cots[place, :].astype(F32) * out, axis=1, keepdims=True)
            gated = (slot_gate[place, 0:1] * out).astype(BF)
            lane = iota((CAP, LANES), 1)
            coarse = d_gates.astype(BF).astype(F32)
            extra = jnp.where(lane == wanted, coarse, 0.0)
            extra = extra + jnp.where(lane == EXPERTS + wanted, d_gates - coarse, 0.0)

            def add(acc, part, columns):
                @pl.when(expert == 0)
                def _():
                    acc[f, :, columns] = part

                @pl.when(expert > 0)
                def _():
                    acc[f, :, columns] += part

            add(branch_acc, t_dot(hot[f], gated), slice(0, width))
            add(back_acc, t_dot(hot[f], row_acc[place, :].astype(BF)), slice(0, width))
            add(back_acc, t_dot(hot[f], extra.astype(BF)), slice(width, width + LANES))

            @pl.when(last)
            def _():
                branch_out[f][...] = branch_acc[f].astype(BF)
                back_out[f][...] = back_acc[f].astype(BF)


def near_experts(place, second, grads, router_t, w_experts):
    shards = len(second)
    tokens, width = second[0].shape
    experts = w_experts.shape[0]
    slots = shards * CAP
    tiles = FF // TILE
    shapes = [jax.ShapeDtypeStruct((tokens, width), BF)] * shards
    shapes += [jax.ShapeDtypeStruct((tokens, width + LANES), BF)] * shards

    def weight(part):
        return pl.BlockSpec((1, width, TILE), lambda e, j, s: (e, 0, part * tiles + j))

    outs = pl.pallas_call(
        functools.partial(near_kernel, shards),
        grid_spec=pltpu.PrefetchScalarGridSpec(
            num_scalar_prefetch=1,
            grid=(experts, tiles),
            in_specs=[whole(a) for a in (*second, *grads, router_t)]
            + [weight(0), weight(1), weight(2)],
            out_specs=[whole(shape) for shape in shapes],
            scratch_shapes=[
                pltpu.VMEM((shards, CAP, tokens), BF),
                pltpu.VMEM((slots, width), BF),
                pltpu.VMEM((slots, width), BF),
                pltpu.VMEM((slots, width), BF),
                pltpu.VMEM((slots, LANES), F32),
                pltpu.VMEM((slots, width), F32),
                pltpu.VMEM((slots, width), F32),
                pltpu.VMEM((shards, tokens, width), F32),
                pltpu.VMEM((shards, tokens, width + LANES), F32),
            ],
        ),
        out_shape=shapes,
        compiler_params=pltpu.CompilerParams(vmem_limit_bytes=VMEM),
        cost_estimate=time_of(26),
        name="near_experts",
    )(place, *second, *grads, router_t, w_experts, w_experts, w_experts)
    return outs[:shards], outs[shards:]


def far_kernel(
    place,
    router_t,
    second_ref,
    grads_ref,
    w_gate,
    w_up,
    w_down,
    out_ref,
    rows,
    d_outs,
    act,
    fetched_rows,
    fetched_grads,
    tile_out,
    counts,
    fetch_sem,
    store_sem,
):
    experts = rows.shape[0]
    expert, tile = pl.program_id(0), pl.program_id(1)
    tiles = pl.num_programs(1)
    step = expert * tiles + tile
    slot = lax.rem(step, 2)
    groups = second_ref.shape[0] // JOINED
    tokens, width = second_ref.shape[1:]
    size = JOINED * tokens
    window = JOINED * CAP + 16

    def stores(which, e, j):
        return [
            pltpu.make_async_copy(
                tile_out.at[which, i],
                out_ref.at[e, :, pl.ds(pl.multiple_of(i * FF + j * TILE, TILE), TILE)],
                store_sem.at[which, i],
            )
            for i in range(3)
        ]

    def fetches(which, g):
        at = pl.ds(g * JOINED, JOINED)
        return [
            pltpu.make_async_copy(ref.at[at], buffer.at[which], fetch_sem.at[which, i])
            for i, (ref, buffer) in enumerate(
                ((second_ref, fetched_rows), (grads_ref, fetched_grads))
            )
        ]

    @pl.when(step == 0)
    def _():
        for copy in fetches(0, 0):
            copy.start()
        before = (iota((size, size), 0) < iota((size, size), 1)).astype(BF)

        def gather(g, starts):
            which = lax.rem(g, 2)
            for copy in fetches(which, g):
                copy.wait()

            @pl.when(g + 1 < groups)
            def _():
                for copy in fetches(1 - which, g + 1):
                    copy.start()

            second = fetched_rows[which].reshape(size, width)
            grads = fetched_grads[which, :, :tokens].reshape(size, width)
            chosen = jnp.concatenate(
                [fetched_grads[which, b, tokens : tokens + EXTRA, :LANES] for b in range(JOINED)],
                axis=1,
            )
            chosen = chosen.astype(F32).astype(jnp.int32)
            picked, gates = picked_gates(second, router_t[...], chosen)
            ranks = dot(picked.astype(BF), before)
            ids = iota(ranks.shape, 0)
            bases = [start // 16 * 16 for start in starts]
            matches, found_gates, ends = [], [], []
            for e in range(experts):
                found = (ids == place[1] * experts + e) & picked
                gate = jnp.sum(jnp.where(found, gates, 0.0), axis=0, keepdims=True)
                rank = jnp.sum(jnp.where(found, ranks + 1.0, 0.0), axis=0, keepdims=True)
                shift = (starts[e] - bases[e]).astype(F32)
                spot = jnp.where(rank > 0.0, rank + (shift - 1.0), -1.0)
                match = iota((window, size), 0).astype(F32) == spot
                matches.append(match.astype(BF))
                found_gates.append(
                    jnp.sum(jnp.where(match, gate, 0.0), axis=1, keepdims=True)
                )
                ends.append(starts[e] + jnp.sum((rank > 0.0).astype(jnp.int32)))
            one_hot = jnp.concatenate(matches, axis=0)
            new_rows = dot(one_hot, second).astype(BF)
            new_grads = (jnp.concatenate(found_gates, axis=0) * dot(one_hot, grads)).astype(BF)
            for e in range(experts):
                at = pl.ds(pl.multiple_of(bases[e], 16), 16)
                rest = pl.ds(pl.multiple_of(bases[e] + 16, 16), window - 16)
                held = iota((16, width), 0) < starts[e] - bases[e]
                for ref, new in ((rows, new_rows), (d_outs, new_grads)):
                    new = new[e * window : (e + 1) * window]
                    ref[e, at, :] = jnp.where(held, ref[e, at, :], new[:16])
                    ref[e, rest, :] = new[16:]
            return tuple(ends)

        ends = lax.fori_loop(0, groups, gather, (jnp.int32(0),) * experts)
        for e in range(experts):
            counts[e] = ends[e]
            spare = pl.ds(pl.multiple_of((ends[e] + 15) // 16 * 16, 16), CHUNK)
            rows[e, spare, :] = jnp.zeros((CHUNK, width), BF)
            d_outs[e, spare, :] = jnp.zeros((CHUNK, width), BF)

    chunks = jnp.maximum((counts[expert] + CHUNK - 1) // CHUNK, 1)

    @pl.loop(0, chunks)
    def _(i):
        at = pl.ds(pl.multiple_of(i * CHUNK, CHUNK), CHUNK)
        row, d_out = rows[expert, at, :], d_outs[expert, at, :]
        hidden, d_gate, d_up = swiglu_grads(
            dot(row, w_gate[0]), dot(row, w_up[0]), dot(d_out, w_down[0])
        )
        act[0, at, :] = d_gate
        act[1, at, :] = d_up
        act[2, at, :] = hidden

    @pl.when(step >= 2)
    def _():
        for copy in stores(slot, (step - 2) // tiles, lax.rem(step - 2, tiles)):
            copy.wait()

    most = act.shape[1] // CHUNK
    depths = [k for k in DEPTHS if k < most] + [most]
    for low, k in zip([0] + depths[:-1], depths):

        @pl.when((chunks > low) & (chunks <= k))
        def _():
            for extra in range(low + 1, k):

                @pl.when(chunks == extra)
                def _():
                    spare = slice(extra * CHUNK, k * CHUNK)
                    empty = jnp.zeros(((k - extra) * CHUNK, width), BF)
                    rows[expert, spare, :] = empty
                    d_outs[expert, spare, :] = empty
                    for i in range(3):
                        act[i, spare, :] = empty[:, :TILE]

            upto = k * CHUNK
            for i, left in enumerate((rows, rows, d_outs)):
                tile_out[slot, i] = t_dot(left[expert, :upto, :], act[i, :upto, :])

    for copy in stores(slot, expert, tile):
        copy.start()

    @pl.when(step == pl.num_programs(0) * tiles - 1)
    def _():
        for copy in stores(1 - slot, (step - 1) // tiles, lax.rem(step - 1, tiles)):
            copy.wait()
        for copy in stores(slot, expert, tile):
            copy.wait()


def far_weight_grads(place, router_t, second, grads, w_experts):
    experts, width = w_experts.shape[:2]
    blocks, tokens = second.shape[:2]
    tiles = FF // TILE
    most = blocks * CAP
    held = most + CHUNK + 16

    def weight(part):
        return pl.BlockSpec((1, width, TILE), lambda e, j, s: (e, 0, part * tiles + j))

    return pl.pallas_call(
        far_kernel,
        grid_spec=pltpu.PrefetchScalarGridSpec(
            num_scalar_prefetch=1,
            grid=(experts, tiles),
            in_specs=[
                whole(router_t),
                anywhere(),
                anywhere(),
                weight(0),
                weight(1),
                weight(2),
            ],
            out_specs=anywhere(),
            scratch_shapes=[
                pltpu.VMEM((experts, held, width), BF),
                pltpu.VMEM((experts, held, width), BF),
                pltpu.VMEM((3, most, TILE), BF),
                pltpu.VMEM((2, JOINED, tokens, width), BF),
                pltpu.VMEM((2, JOINED, tokens + EXTRA, width), BF),
                pltpu.VMEM((2, 3, width, TILE), F32),
                pltpu.SMEM((experts,), jnp.int32),
                pltpu.SemaphoreType.DMA((2, 2)),
                pltpu.SemaphoreType.DMA((2, 3)),
            ],
        ),
        out_shape=jax.ShapeDtypeStruct((experts, width, 3 * FF), F32),
        compiler_params=pltpu.CompilerParams(vmem_limit_bytes=VMEM),
        cost_estimate=time_of(80),
        name="far_weight_grads",
    )(place, router_t, second, grads, w_experts, w_experts, w_experts)


def per_device(
    tokens,
    query_key_value_weight,
    output_weight,
    routing_weight,
    gain_attn,
    gain_moe,
    w_experts,
    doc_starts,
    routes,
    cotangent,
):
    spans = lax.axis_size("ctx")
    shards = lax.axis_size("fsdp")
    here = lax.axis_index("ctx")
    shard = lax.axis_index("fsdp")
    place = jnp.stack([here, shard]).astype(jnp.int32)
    x, grad = tokens[0], cotangent[0]
    tok_count, width = x.shape
    shard_rows = query_key_value_weight.shape[0]
    copies = spans // HK
    head = here // copies
    length = spans * tok_count
    blocks = spans * shards

    side = jnp.concatenate(
        [
            routing_weight.T,
            gain_attn[None],
            gain_moe[None],
            jnp.zeros((EXTRA - EXPERTS - 2, shard_rows), BF),
        ]
    )
    head_w = jnp.concatenate(
        [
            lax.dynamic_slice_in_dim(query_key_value_weight, head * HEAD, HEAD, 1),
            lax.dynamic_slice_in_dim(query_key_value_weight, Q_COLS + head * HD, HD, 1),
            lax.dynamic_slice_in_dim(query_key_value_weight, Q_COLS + K_COLS + head * HD, HD, 1),
        ],
        axis=1,
    )
    side = jnp.stack(near_blocks(side))
    side = jnp.take(side, jnp.arange(shards, dtype=jnp.int32) ^ shard, axis=0)
    side = side.swapaxes(0, 1).reshape(EXTRA, width)
    head_w = near_blocks(head_w)
    out_w = gathered(output_weight, "fsdp")
    qkv_w = gathered(after(query_key_value_weight, out_w), "fsdp")
    pieces = span_pieces(x, side, head_w)

    payload = jnp.concatenate(
        [grad, jnp.pad(routes[0].T.astype(BF), ((0, EXTRA - 2), (0, width - tok_count)))]
    )
    payload = after(payload, pieces)
    grads_near = near_blocks(payload)
    grads_line = line_blocks(payload)
    grads_all = all_blocks(grads_line)

    normed, mixed, attended_low, attended, log_norm = stream_attention(
        place, doc_starts[0], pieces, head_w, side, copies
    )

    attended_low = after(attended_low, grads_line, grads_near)
    own = to_all(attended_low, "ctx").reshape(spans, tok_count, HEAD)
    middle, second = home_forward(own, x, side, out_w, copies)
    second_near = near_blocks(second)
    second_line = line_blocks(second)
    second_all = all_blocks(second_line)

    branch, back = near_experts(place, second_near, grads_near, side, w_experts)
    attended_pieces = span_pieces(after(attended_low, second_line), back)
    back = after(back, attended_pieces[:2])
    terms = after(near_terms(back), grads_all)
    branch_terms = near_terms(branch)
    output = sum((term.astype(F32) for term in branch_terms), middle).astype(BF)

    d_middle, sent, small = home_turn(
        terms, middle, second, grad, routes[0], side, out_w, spans
    )

    sent = to_all(sent.reshape(length, -1), "ctx")
    d_mixed, grads_out = stream_backward(
        place, doc_starts[0], attended_pieces, sent, mixed, attended, log_norm, normed, small, shards
    )
    late = near_terms([grads_out[r] for r in range(shards)])
    late = sum((term.astype(F32) for term in late[1:]), late[0].astype(F32)).astype(BF)
    late = lax.all_gather(after(late, second_all), "ctx", axis=0)

    d_home = to_all(d_mixed, "ctx").reshape(spans, tok_count, HEAD_COLS)
    d_tokens = home_backward(d_home, x, side, d_middle, qkv_w, copies)

    second_all = second_all.reshape(blocks, tok_count, width)
    grads_all = grads_all.reshape(blocks, tok_count + EXTRA, width)
    segment = min(blocks, SEGMENT)
    parts = [
        far_weight_grads(
            place, side, second_all[i : i + segment], grads_all[i : i + segment], w_experts
        )
        for i in range(0, blocks, segment)
    ]
    d_w_experts = sum(parts[1:], parts[0])

    d_qkv_w, d_out_w, small, d_gain_attn = collected(
        late, query_key_value_weight, width, copies
    )
    return (
        output[None],
        d_tokens[None],
        d_qkv_w,
        d_out_w,
        small[:EXPERTS].T,
        d_gain_attn[:, 0] / gain_attn.astype(F32),
        small[EXPERTS],
        d_w_experts,
    )


def solution(mesh):
    placed = (
        P("fsdp", "ctx", None),
        P("fsdp", None),
        P("fsdp", None),
        P("fsdp", None),
        P("fsdp"),
        P("fsdp"),
        P("fsdp", None, None),
        P("fsdp", None),
        P("fsdp", "ctx", None),
        P("fsdp", "ctx", None),
    )
    return jax.shard_map(
        per_device,
        mesh=mesh,
        in_specs=placed,
        out_specs=(
            P("fsdp", "ctx", None),
            P("fsdp", "ctx", None),
            P("fsdp", None),
            P("fsdp", None),
            P("fsdp", None),
            P("fsdp"),
            P("fsdp"),
            P("fsdp", None, None),
        ),
        check_vma=False,
    )
```

```python
import functools

import jax
import jax.numpy as jnp
from jax import lax
from jax.experimental import pallas as pl
from jax.experimental.pallas import tpu as pltpu
from jax.sharding import PartitionSpec as P

HQ = 24
HK = 8
HD = 64
GROUP = HQ // HK
FF = 1024
EXPERTS = 8
CAP = 64
Q_COLS = HQ * HD
K_COLS = HK * HD
HEAD = GROUP * HD
HEAD_COLS = HEAD + 2 * HD
SCALE = HD**-0.5
EXTRA = 16
LANES = 128
TILE = 256
CHUNK = 256
SEGMENT = 32
JOINED = 2
QUERIES = 256
DEPTHS = (1, 2, 3, 4, 6, 8)
VMEM = 58 * 1024 * 1024

NORM_EPS = 1e-05
MASK_NEG = -1e30
BF = jnp.bfloat16
F32 = jnp.float32


def dot(a, b):
    return jnp.dot(a, b, preferred_element_type=F32)


def dot_t(a, b):
    return lax.dot_general(a, b, (((1,), (1,)), ((), ())), preferred_element_type=F32)


def t_dot(a, b):
    return lax.dot_general(a, b, (((0,), (0,)), ((), ())), preferred_element_type=F32)


def iota(shape, axis):
    return lax.broadcasted_iota(jnp.int32, shape, axis)


def rms_factor(values):
    return lax.rsqrt(jnp.mean(values * values, axis=-1, keepdims=True) + NORM_EPS)


def rms_input_grad(values, factor, gain_vec, incoming):
    inner = incoming * gain_vec
    cubed = factor * factor * factor
    return factor * inner - values * cubed * jnp.mean(inner * values, axis=-1, keepdims=True)


def to_all(value, axis):
    return lax.all_to_all(value, axis, 0, 0, tiled=True)


def gathered(value, axis):
    return lax.all_gather(value, axis, axis=0, tiled=True)


def exchanged(value, axis, distance):
    count = lax.axis_size(axis)
    return lax.ppermute(value, axis, [(i, i ^ distance) for i in range(count)])


def near_blocks(own):
    blocks = {0: own}
    distance = lax.axis_size("fsdp") // 2
    while distance:
        blocks.update({r ^ distance: exchanged(b, "fsdp", distance) for r, b in blocks.items()})
        distance //= 2
    return [blocks[r] for r in range(len(blocks))]


def near_terms(blocks):
    shards = lax.axis_size("fsdp")
    terms = {r: [block] for r, block in enumerate(blocks)}
    distance = 1

    def total(parts):
        if len(parts) == 1:
            return parts[0]
        return sum((part.astype(F32) for part in parts[1:]), parts[0].astype(F32)).astype(BF)

    while distance < shards:
        terms = {
            r: terms[r] + [exchanged(total(terms[r ^ distance]), "fsdp", distance)]
            for r in range(0, shards, 2 * distance)
        }
        distance *= 2
    return terms[0]


def line_blocks(own):
    spans = lax.axis_size("ctx")
    return jnp.stack([own] + [exchanged(own, "ctx", d) for d in range(2, spans, 2)])


def span_pieces(own, *others):
    half = own.shape[0] // 2
    same = [line_blocks(part) for part in (own[:half], own[half:])]
    same = after(same, *others)
    return same + [exchanged(part, "ctx", 1) for part in same]


def all_blocks(line):
    spans, shards = lax.axis_size("ctx"), lax.axis_size("fsdp")
    sets = [
        [(2 * pair + side) * shards + f for side in range(2) for f in range(shards)]
        for pair in range(spans // 2)
    ]
    return lax.all_gather(line, ("ctx", "fsdp"), axis=0, tiled=True, axis_index_groups=sets)


def after(values, *others):
    return lax.optimization_barrier((values, others))[0]


def time_of(microseconds):
    return pl.CostEstimate(flops=0, bytes_accessed=microseconds * 3_600_000, transcendentals=0)


def whole(array):
    shape = array.shape
    return pl.BlockSpec(shape, lambda *_: (0,) * len(shape))


def anywhere():
    return pl.BlockSpec(memory_space=pl.ANY)


def place_pieces(here, pieces, target, sems):
    copies = []
    for i, piece in enumerate(pieces):
        odd, last = divmod(i, 2)
        rows = piece.shape[1]
        for j in range(piece.shape[0]):
            copies.append(
                pltpu.make_async_copy(
                    piece.at[j],
                    target.at[here ^ (2 * j + odd), pl.ds(last * rows, rows)],
                    sems.at[i, j],
                )
            )
    for copy in copies:
        copy.start()
    return copies


def doc_of(starts, positions):
    found = jnp.zeros(positions.shape, jnp.int32)
    for i in range(starts.shape[0]):
        found = found + (positions >= starts[i]).astype(jnp.int32)
    return found


def visible(starts, here, copies, tokens, first, rows, keys):
    query = first + iota((rows, 1), 0)
    key = iota((1, keys), 1)
    allowed = (key <= query) & (doc_of(starts, key) == doc_of(starts, query))
    if copies > 1:
        allowed = allowed & (lax.rem(query // tokens, copies) == lax.rem(here, copies))
    return allowed


def stream_kernel(
    copies,
    place,
    starts,
    *refs,
):
    shards = len(refs) - 15
    pieces, weights, side = refs[:4], refs[4 : 4 + shards], refs[4 + shards]
    normed, mixed, attended_low, attended, log_norm, rows, weight, piece_sems, weight_sems = refs[
        5 + shards : 14 + shards
    ]
    here, shard = place[0], place[1]
    spans, tokens, width = rows.shape
    length = spans * tokens
    copying = place_pieces(here, pieces, rows, piece_sems)
    loading = [
        pltpu.make_async_copy(ref, weight.at[shard ^ r], weight_sems.at[r])
        for r, ref in enumerate(weights)
    ]
    for copy in loading:
        copy.start()
    for copy in loading + copying:
        copy.wait()
    head_weight = weight[...].reshape(width, HEAD_COLS)
    gain = side[EXPERTS : EXPERTS + 1, :].astype(F32)

    @pl.loop(0, spans)
    def _(span):
        x = rows[span].astype(F32)
        low = (x * rms_factor(x) * gain).astype(BF)
        at = pl.ds(pl.multiple_of(span * tokens, tokens), tokens)
        normed[at, :] = low
        mixed[at, :] = dot(low, head_weight).astype(BF)

    for first in range(0, length, QUERIES):
        keys = first + QUERIES
        at = slice(first, keys)
        allowed = visible(starts, here, copies, tokens, first, QUERIES, keys)
        for g in range(GROUP):
            columns = slice(g * HD, (g + 1) * HD)
            scores = dot_t(mixed[at, columns], mixed[:keys, HEAD : HEAD + HD]) * SCALE
            scores = jnp.where(allowed, scores, MASK_NEG)
            highest = jnp.max(scores, axis=1, keepdims=True)
            parts = jnp.where(allowed, jnp.exp(scores - highest), 0.0)
            total = jnp.sum(parts, axis=1, keepdims=True)
            total = jnp.where(total == 0.0, 1.0, total)
            log_norm[at, g : g + 1] = highest + jnp.log(total)
            result = dot((parts / total).astype(BF), mixed[:keys, HEAD + HD :])
            attended[at, columns] = result
            attended_low[at, columns] = result.astype(BF)


def stream_attention(place, starts, pieces, head_weights, side, copies):
    spans, tokens = 2 * pieces[0].shape[0], 2 * pieces[0].shape[1]
    width = pieces[0].shape[2]
    length = spans * tokens
    shards = len(head_weights)
    return pl.pallas_call(
        functools.partial(stream_kernel, copies),
        grid_spec=pltpu.PrefetchScalarGridSpec(
            num_scalar_prefetch=2,
            grid=(1,),
            in_specs=[anywhere()] * (4 + shards) + [whole(side)],
            out_specs=[
                pl.BlockSpec((length, columns), lambda *_: (0, 0))
                for columns in (width, HEAD_COLS, HEAD, HEAD, LANES)
            ],
            scratch_shapes=[
                pltpu.VMEM((spans, tokens, width), BF),
                pltpu.VMEM((shards, width // shards, HEAD_COLS), BF),
                pltpu.SemaphoreType.DMA((4, spans // 2)),
                pltpu.SemaphoreType.DMA((shards,)),
                pltpu.SMEM((1,), jnp.int32),
            ],
        ),
        out_shape=[
            jax.ShapeDtypeStruct((length, columns), kind)
            for columns, kind in (
                (width, BF),
                (HEAD_COLS, BF),
                (HEAD, BF),
                (HEAD, F32),
                (LANES, F32),
            )
        ],
        compiler_params=pltpu.CompilerParams(vmem_limit_bytes=VMEM),
        cost_estimate=time_of(16),
        name="stream_attention",
    )(place, starts, *pieces, *head_weights, side)


def home_kernel(copies, own, tokens, side, weight, middle, second):
    total = tokens[...].astype(F32)
    for head in range(HK):
        part = own[head * copies]
        for i in range(1, copies):
            part = part + own[head * copies + i]
        total = total + dot(part, weight[head * HEAD : (head + 1) * HEAD, :])
    middle[...] = total
    gain = side[EXPERTS + 1 : EXPERTS + 2, :].astype(F32)
    second[...] = (total * rms_factor(total) * gain).astype(BF)


def home_forward(own, tokens, side, weight, copies):
    args = (own, tokens, side, weight)
    return pl.pallas_call(
        functools.partial(home_kernel, copies),
        grid=(1,),
        in_specs=[whole(a) for a in args],
        out_specs=[whole(tokens)] * 2,
        out_shape=[
            jax.ShapeDtypeStruct(tokens.shape, F32),
            jax.ShapeDtypeStruct(tokens.shape, BF),
        ],
        compiler_params=pltpu.CompilerParams(vmem_limit_bytes=VMEM),
        cost_estimate=time_of(5),
        name="home_forward",
    )(*args)


def turn_kernel(copies, term_count, *refs):
    terms, refs = refs[:term_count], refs[term_count:]
    middle_ref, second_ref, grad, routes, side, weight, d_middle_out, sent, small = refs
    width = middle_ref.shape[1]
    back = terms[0][...].astype(F32)
    for term in terms[1:]:
        back = back + term[...].astype(F32)
    middle, second = middle_ref[...], second_ref[...]
    d_gates = back[:, width : width + EXTRA]
    ids = iota(d_gates.shape, 1)
    d_gates = d_gates + back[:, width + EXPERTS : width + EXPERTS + EXTRA]
    picked = (ids == routes[:, 0:1]) | (ids == routes[:, 1:2])
    logits = jnp.where(picked, dot_t(second, side[...]), MASK_NEG)
    gates = jnp.where(picked, jnp.exp(logits - jnp.max(logits, axis=1, keepdims=True)), 0.0)
    gates = gates / jnp.sum(gates, axis=1, keepdims=True)
    d_gates = jnp.where(picked, d_gates, 0.0)
    d_picked = gates * (d_gates - jnp.sum(gates * d_gates, axis=1, keepdims=True))
    d_logits = d_picked.astype(BF)
    d_second = dot(d_logits, side[...]) + back[:, :width]
    factor = rms_factor(middle)
    small[...] = t_dot(d_logits, second)
    small[EXPERTS : EXPERTS + 1, :] = jnp.sum(d_second * middle * factor, axis=0, keepdims=True)
    gain = side[EXPERTS + 1 : EXPERTS + 2, :].astype(F32)
    d_middle = grad[...].astype(F32) + rms_input_grad(middle, factor, gain, d_second)
    d_middle_out[...] = d_middle
    d_proj = d_middle.astype(BF)
    for head in range(HK):
        d_head = dot_t(d_proj, weight[head * HEAD : (head + 1) * HEAD, :]).astype(BF)
        for i in range(copies):
            sent[head * copies + i, :, :HEAD] = d_head
    chunk = sent.shape[2] - HEAD
    for span in range(sent.shape[0]):
        sent[span, :, HEAD:] = d_proj[:, span * chunk : (span + 1) * chunk]


def home_turn(terms, middle, second, grad, routes, side, weight, spans):
    args = (*terms, middle, second, grad, routes, side, weight)
    tokens, width = middle.shape
    shapes = [
        jax.ShapeDtypeStruct((tokens, width), F32),
        jax.ShapeDtypeStruct((spans, tokens, HEAD + width // spans), BF),
        jax.ShapeDtypeStruct((EXTRA, width), F32),
    ]
    return pl.pallas_call(
        functools.partial(turn_kernel, spans // HK, len(terms)),
        grid=(1,),
        in_specs=[whole(a) for a in args],
        out_specs=[whole(shape) for shape in shapes],
        out_shape=shapes,
        compiler_params=pltpu.CompilerParams(vmem_limit_bytes=VMEM),
        cost_estimate=time_of(7),
        name="home_turn",
    )(*args)


def stream_grad_kernel(
    copies, place, starts, pieces0, pieces1, pieces2, pieces3, sent, mixed, attended, log_norm,
    normed, small, d_mixed, out, everyones, d_kv, sems
):
    here, shard = place[0], place[1]
    length, width = normed.shape
    spans = everyones.shape[0]
    tokens = length // spans
    shards = out.shape[0]
    shard_rows = width // shards
    heads = HK // shards
    copying = place_pieces(here, (pieces0, pieces1, pieces2, pieces3), everyones, sems)
    d_kv[...] = jnp.zeros_like(d_kv)
    for first in range(0, length, QUERIES):
        keys = first + QUERIES
        at = slice(first, keys)
        allowed = visible(starts, here, copies, tokens, first, QUERIES, keys)
        k, v = mixed[:keys, HEAD : HEAD + HD], mixed[:keys, HEAD + HD :]
        for g in range(GROUP):
            columns = slice(g * HD, (g + 1) * HD)
            q, grad = mixed[at, columns], sent[at, columns]
            delta = jnp.sum(grad.astype(F32) * attended[at, columns], axis=1, keepdims=True)
            scores = dot_t(q, k) * SCALE
            probs = jnp.where(allowed, jnp.exp(scores - log_norm[at, g : g + 1]), 0.0)
            d_scores = (probs * (dot_t(grad, v) - delta)).astype(BF)
            d_mixed[at, columns] = (dot(d_scores, k) * SCALE).astype(BF)
            d_kv[0, :keys, :] += t_dot(d_scores, q)
            d_kv[1, :keys, :] += t_dot(probs.astype(BF), grad)
    d_mixed[:, HEAD : HEAD + HD] = (d_kv[0] * SCALE).astype(BF)
    d_mixed[:, HEAD + HD :] = d_kv[1].astype(BF)
    for copy in copying:
        copy.wait()
    d_proj = sent[:, HEAD:]
    low = small[...].astype(BF)
    for f in range(shards):
        spot = shard ^ f
        columns = slice(f * shard_rows, (f + 1) * shard_rows)
        out[spot, :shard_rows, :HEAD_COLS] = t_dot(normed[:, columns], d_mixed[...]).astype(BF)
        for h in range(heads):
            first = (f * heads + h) * copies
            part = everyones[first]
            for i in range(1, copies):
                part = part + everyones[first + i]
            out[spot, h * HEAD : (h + 1) * HEAD, HEAD_COLS:] = t_dot(part, d_proj).astype(BF)
        out[spot, shard_rows:, :] = jnp.zeros((EXTRA, out.shape[2]), BF)
        out[spot, shard_rows:, :shard_rows] = low[:, columns]


def stream_backward(place, starts, pieces, sent, mixed, attended, log_norm, normed, small, shards):
    args = (sent, mixed, attended, log_norm, normed, small)
    length, width = normed.shape
    spans = 2 * pieces[0].shape[0]
    shapes = [
        jax.ShapeDtypeStruct(mixed.shape, BF),
        jax.ShapeDtypeStruct(
            (shards, width // shards + EXTRA, HEAD_COLS + width // spans), BF
        ),
    ]
    return pl.pallas_call(
        functools.partial(stream_grad_kernel, spans // HK),
        grid_spec=pltpu.PrefetchScalarGridSpec(
            num_scalar_prefetch=2,
            grid=(1,),
            in_specs=[anywhere()] * 4 + [whole(a) for a in args],
            out_specs=[whole(shape) for shape in shapes],
            scratch_shapes=[
                pltpu.VMEM((spans, length, HEAD), BF),
                pltpu.VMEM((2, length, HD), F32),
                pltpu.SemaphoreType.DMA((4, spans // 2)),
            ],
        ),
        out_shape=shapes,
        compiler_params=pltpu.CompilerParams(vmem_limit_bytes=VMEM),
        cost_estimate=time_of(17),
        name="stream_backward",
    )(place, starts, *pieces, *args)


def home_grad_kernel(copies, d_home, tokens, side, d_middle, weight, d_tokens, mixed):
    for head in range(HK):
        part = d_home[head * copies]
        if copies > 1:
            part = part.astype(F32)
            for i in range(1, copies):
                part = part + d_home[head * copies + i].astype(F32)
            part = part.astype(BF)
        mixed[:, head * HEAD : (head + 1) * HEAD] = part[:, :HEAD]
        key = Q_COLS + head * HD
        mixed[:, key : key + HD] = part[:, HEAD : HEAD + HD]
        value = key + K_COLS
        mixed[:, value : value + HD] = part[:, HEAD + HD :]
    d_normed = dot_t(mixed[...], weight[...])
    x = tokens[...].astype(F32)
    gain = side[EXPERTS : EXPERTS + 1, :].astype(F32)
    d_x = rms_input_grad(x, rms_factor(x), gain, d_normed)
    d_tokens[...] = (d_middle[...] + d_x).astype(BF)


def home_backward(d_home, tokens, side, d_middle, weight, copies):
    args = (d_home, tokens, side, d_middle, weight)
    return pl.pallas_call(
        functools.partial(home_grad_kernel, copies),
        grid=(1,),
        in_specs=[whole(a) for a in args],
        out_specs=whole(tokens),
        scratch_shapes=[pltpu.VMEM((tokens.shape[0], Q_COLS + 2 * K_COLS), BF)],
        out_shape=jax.ShapeDtypeStruct(tokens.shape, BF),
        compiler_params=pltpu.CompilerParams(vmem_limit_bytes=VMEM),
        cost_estimate=time_of(8),
        name="home_backward",
    )(*args)


def collect_kernel(copies, late, own_weight, d_qkv, d_out, small, d_gain):
    rows = own_weight.shape[0]
    chunk = late.shape[2] - HEAD_COLS
    for head in range(HK):
        part = late[head * copies, :rows, :HEAD_COLS].astype(F32)
        for i in range(1, copies):
            part = part + late[head * copies + i, :rows, :HEAD_COLS].astype(F32)
        d_qkv[:, head * HEAD : (head + 1) * HEAD] = part[:, :HEAD]
        key = Q_COLS + head * HD
        d_qkv[:, key : key + HD] = part[:, HEAD : HEAD + HD]
        value = key + K_COLS
        d_qkv[:, value : value + HD] = part[:, HEAD + HD :]
    total = jnp.zeros((EXTRA, rows), F32)
    for span in range(late.shape[0]):
        d_out[:, span * chunk : (span + 1) * chunk] = late[span, :rows, HEAD_COLS:].astype(F32)
        total = total + late[span, rows:, :rows].astype(F32)
    small[...] = total
    d_gain[...] = jnp.sum(d_qkv[...] * own_weight[...].astype(F32), axis=1, keepdims=True)


def collected(late, own_weight, width, copies):
    rows, columns = own_weight.shape
    shapes = [
        jax.ShapeDtypeStruct((rows, columns), F32),
        jax.ShapeDtypeStruct((rows, width), F32),
        jax.ShapeDtypeStruct((EXTRA, rows), F32),
        jax.ShapeDtypeStruct((rows, 1), F32),
    ]
    return pl.pallas_call(
        functools.partial(collect_kernel, copies),
        grid=(1,),
        in_specs=[whole(late), whole(own_weight)],
        out_specs=[whole(shape) for shape in shapes],
        out_shape=shapes,
        compiler_params=pltpu.CompilerParams(vmem_limit_bytes=VMEM),
        cost_estimate=time_of(7),
        name="collected",
    )(late, own_weight)


def picked_gates(second, router_t, chosen):
    logits = dot_t(router_t, second)
    ids = iota(logits.shape, 0)
    picked = (ids == chosen[0:1, :]) | (ids == chosen[1:2, :])
    logits = jnp.where(picked, logits, MASK_NEG)
    parts = jnp.where(picked, jnp.exp(logits - jnp.max(logits, axis=0, keepdims=True)), 0.0)
    return picked, parts / jnp.sum(parts, axis=0, keepdims=True)


def swiglu_grads(gate, up, d_hidden):
    sigma = 1.0 / (1.0 + jnp.exp(-gate))
    passed = gate * sigma
    d_gate = d_hidden * up * sigma * (1.0 + gate * (1.0 - sigma))
    return (passed * up).astype(BF), d_gate.astype(BF), (d_hidden * passed).astype(BF)


def near_kernel(shards, place, *refs):
    second, grads = refs[:shards], refs[shards : 2 * shards]
    router_t, w_gate, w_up, w_down = refs[2 * shards : 2 * shards + 4]
    branch_out = refs[2 * shards + 4 : 3 * shards + 4]
    back_out = refs[3 * shards + 4 : 4 * shards + 4]
    hot, rows, cots, d_outs, slot_gate, out_acc, row_acc, branch_acc, back_acc = refs[
        4 * shards + 4 :
    ]
    expert, tile = pl.program_id(0), pl.program_id(1)
    tokens = second[0].shape[0]
    width = second[0].shape[1]
    wanted = place[1] * pl.num_programs(0) + expert

    @pl.when(tile == 0)
    def _():
        before = (iota((tokens, tokens), 0) < iota((tokens, tokens), 1)).astype(BF)
        for f in range(shards):
            chosen = grads[f][tokens : tokens + EXTRA, :tokens].astype(F32).astype(jnp.int32)
            picked, gates = picked_gates(second[f][...], router_t[...], chosen)
            ranks = dot(picked.astype(BF), before)
            found = (iota(ranks.shape, 0) == wanted) & picked
            rank = jnp.sum(jnp.where(found, ranks + 1.0, 0.0), axis=0, keepdims=True)
            gate = jnp.sum(jnp.where(found, gates, 0.0), axis=0, keepdims=True)
            match = iota((CAP, tokens), 0).astype(F32) + 1.0 == rank
            one_hot = match.astype(BF)
            place = pl.ds(f * CAP, CAP)
            hot[f] = one_hot
            found_gate = jnp.sum(jnp.where(match, gate, 0.0), axis=1, keepdims=True)
            slot_gate[place, :] = jnp.broadcast_to(found_gate, (CAP, LANES))
            rows[place, :] = dot(one_hot, second[f][...]).astype(BF)
            cot = dot(one_hot, grads[f][:tokens, :])
            cots[place, :] = cot.astype(BF)
            d_outs[place, :] = (found_gate * cot).astype(BF)
        out_acc[...] = jnp.zeros_like(out_acc)
        row_acc[...] = jnp.zeros_like(row_acc)

    hidden, d_gate, d_up = swiglu_grads(
        dot(rows[...], w_gate[0]), dot(rows[...], w_up[0]), dot(d_outs[...], w_down[0])
    )
    out_acc[...] += dot_t(hidden, w_down[0])
    row_acc[...] += dot_t(d_gate, w_gate[0]) + dot_t(d_up, w_up[0])

    @pl.when(tile == pl.num_programs(1) - 1)
    def _():
        last = expert == pl.num_programs(0) - 1
        for f in range(shards):
            place = pl.ds(f * CAP, CAP)
            out = out_acc[place, :].astype(BF).astype(F32)
            d_gates = jnp.sum(cots[place, :].astype(F32) * out, axis=1, keepdims=True)
            gated = (slot_gate[place, 0:1] * out).astype(BF)
            lane = iota((CAP, LANES), 1)
            coarse = d_gates.astype(BF).astype(F32)
            extra = jnp.where(lane == wanted, coarse, 0.0)
            extra = extra + jnp.where(lane == EXPERTS + wanted, d_gates - coarse, 0.0)

            def add(acc, part, columns):
                @pl.when(expert == 0)
                def _():
                    acc[f, :, columns] = part

                @pl.when(expert > 0)
                def _():
                    acc[f, :, columns] += part

            add(branch_acc, t_dot(hot[f], gated), slice(0, width))
            add(back_acc, t_dot(hot[f], row_acc[place, :].astype(BF)), slice(0, width))
            add(back_acc, t_dot(hot[f], extra.astype(BF)), slice(width, width + LANES))

            @pl.when(last)
            def _():
                branch_out[f][...] = branch_acc[f].astype(BF)
                back_out[f][...] = back_acc[f].astype(BF)


def near_experts(place, second, grads, router_t, w_experts):
    shards = len(second)
    tokens, width = second[0].shape
    experts = w_experts.shape[0]
    slots = shards * CAP
    tiles = FF // TILE
    shapes = [jax.ShapeDtypeStruct((tokens, width), BF)] * shards
    shapes += [jax.ShapeDtypeStruct((tokens, width + LANES), BF)] * shards

    def weight(part):
        return pl.BlockSpec((1, width, TILE), lambda e, j, s: (e, 0, part * tiles + j))

    outs = pl.pallas_call(
        functools.partial(near_kernel, shards),
        grid_spec=pltpu.PrefetchScalarGridSpec(
            num_scalar_prefetch=1,
            grid=(experts, tiles),
            in_specs=[whole(a) for a in (*second, *grads, router_t)]
            + [weight(0), weight(1), weight(2)],
            out_specs=[whole(shape) for shape in shapes],
            scratch_shapes=[
                pltpu.VMEM((shards, CAP, tokens), BF),
                pltpu.VMEM((slots, width), BF),
                pltpu.VMEM((slots, width), BF),
                pltpu.VMEM((slots, width), BF),
                pltpu.VMEM((slots, LANES), F32),
                pltpu.VMEM((slots, width), F32),
                pltpu.VMEM((slots, width), F32),
                pltpu.VMEM((shards, tokens, width), F32),
                pltpu.VMEM((shards, tokens, width + LANES), F32),
            ],
        ),
        out_shape=shapes,
        compiler_params=pltpu.CompilerParams(vmem_limit_bytes=VMEM),
        cost_estimate=time_of(26),
        name="near_experts",
    )(place, *second, *grads, router_t, w_experts, w_experts, w_experts)
    return outs[:shards], outs[shards:]


def far_kernel(
    place,
    router_t,
    second_ref,
    grads_ref,
    w_gate,
    w_up,
    w_down,
    out_ref,
    rows,
    d_outs,
    act,
    fetched_rows,
    fetched_grads,
    tile_out,
    counts,
    fetch_sem,
    store_sem,
):
    experts = rows.shape[0]
    expert, tile = pl.program_id(0), pl.program_id(1)
    tiles = pl.num_programs(1)
    step = expert * tiles + tile
    slot = lax.rem(step, 2)
    groups = second_ref.shape[0] // JOINED
    tokens, width = second_ref.shape[1:]
    size = JOINED * tokens
    window = JOINED * CAP + 16

    def stores(which, e, j):
        return [
            pltpu.make_async_copy(
                tile_out.at[which, i],
                out_ref.at[e, :, pl.ds(pl.multiple_of(i * FF + j * TILE, TILE), TILE)],
                store_sem.at[which, i],
            )
            for i in range(3)
        ]

    def fetches(which, g):
        at = pl.ds(g * JOINED, JOINED)
        return [
            pltpu.make_async_copy(ref.at[at], buffer.at[which], fetch_sem.at[which, i])
            for i, (ref, buffer) in enumerate(
                ((second_ref, fetched_rows), (grads_ref, fetched_grads))
            )
        ]

    @pl.when(step == 0)
    def _():
        for copy in fetches(0, 0):
            copy.start()
        before = (iota((size, size), 0) < iota((size, size), 1)).astype(BF)

        def gather(g, starts):
            which = lax.rem(g, 2)
            for copy in fetches(which, g):
                copy.wait()

            @pl.when(g + 1 < groups)
            def _():
                for copy in fetches(1 - which, g + 1):
                    copy.start()

            second = fetched_rows[which].reshape(size, width)
            grads = fetched_grads[which, :, :tokens].reshape(size, width)
            chosen = jnp.concatenate(
                [fetched_grads[which, b, tokens : tokens + EXTRA, :LANES] for b in range(JOINED)],
                axis=1,
            )
            chosen = chosen.astype(F32).astype(jnp.int32)
            picked, gates = picked_gates(second, router_t[...], chosen)
            ranks = dot(picked.astype(BF), before)
            ids = iota(ranks.shape, 0)
            bases = [start // 16 * 16 for start in starts]
            matches, found_gates, ends = [], [], []
            for e in range(experts):
                found = (ids == place[1] * experts + e) & picked
                gate = jnp.sum(jnp.where(found, gates, 0.0), axis=0, keepdims=True)
                rank = jnp.sum(jnp.where(found, ranks + 1.0, 0.0), axis=0, keepdims=True)
                shift = (starts[e] - bases[e]).astype(F32)
                spot = jnp.where(rank > 0.0, rank + (shift - 1.0), -1.0)
                match = iota((window, size), 0).astype(F32) == spot
                matches.append(match.astype(BF))
                found_gates.append(
                    jnp.sum(jnp.where(match, gate, 0.0), axis=1, keepdims=True)
                )
                ends.append(starts[e] + jnp.sum((rank > 0.0).astype(jnp.int32)))
            one_hot = jnp.concatenate(matches, axis=0)
            new_rows = dot(one_hot, second).astype(BF)
            new_grads = (jnp.concatenate(found_gates, axis=0) * dot(one_hot, grads)).astype(BF)
            for e in range(experts):
                at = pl.ds(pl.multiple_of(bases[e], 16), 16)
                rest = pl.ds(pl.multiple_of(bases[e] + 16, 16), window - 16)
                held = iota((16, width), 0) < starts[e] - bases[e]
                for ref, new in ((rows, new_rows), (d_outs, new_grads)):
                    new = new[e * window : (e + 1) * window]
                    ref[e, at, :] = jnp.where(held, ref[e, at, :], new[:16])
                    ref[e, rest, :] = new[16:]
            return tuple(ends)

        ends = lax.fori_loop(0, groups, gather, (jnp.int32(0),) * experts)
        for e in range(experts):
            counts[e] = ends[e]
            spare = pl.ds(pl.multiple_of((ends[e] + 15) // 16 * 16, 16), CHUNK)
            rows[e, spare, :] = jnp.zeros((CHUNK, width), BF)
            d_outs[e, spare, :] = jnp.zeros((CHUNK, width), BF)

    chunks = jnp.maximum((counts[expert] + CHUNK - 1) // CHUNK, 1)

    @pl.loop(0, chunks)
    def _(i):
        at = pl.ds(pl.multiple_of(i * CHUNK, CHUNK), CHUNK)
        row, d_out = rows[expert, at, :], d_outs[expert, at, :]
        hidden, d_gate, d_up = swiglu_grads(
            dot(row, w_gate[0]), dot(row, w_up[0]), dot(d_out, w_down[0])
        )
        act[0, at, :] = d_gate
        act[1, at, :] = d_up
        act[2, at, :] = hidden

    @pl.when(step >= 2)
    def _():
        for copy in stores(slot, (step - 2) // tiles, lax.rem(step - 2, tiles)):
            copy.wait()

    most = act.shape[1] // CHUNK
    depths = [k for k in DEPTHS if k < most] + [most]
    for low, k in zip([0] + depths[:-1], depths):

        @pl.when((chunks > low) & (chunks <= k))
        def _():
            for extra in range(low + 1, k):

                @pl.when(chunks == extra)
                def _():
                    spare = slice(extra * CHUNK, k * CHUNK)
                    empty = jnp.zeros(((k - extra) * CHUNK, width), BF)
                    rows[expert, spare, :] = empty
                    d_outs[expert, spare, :] = empty
                    for i in range(3):
                        act[i, spare, :] = empty[:, :TILE]

            upto = k * CHUNK
            for i, left in enumerate((rows, rows, d_outs)):
                tile_out[slot, i] = t_dot(left[expert, :upto, :], act[i, :upto, :])

    for copy in stores(slot, expert, tile):
        copy.start()

    @pl.when(step == pl.num_programs(0) * tiles - 1)
    def _():
        for copy in stores(1 - slot, (step - 1) // tiles, lax.rem(step - 1, tiles)):
            copy.wait()
        for copy in stores(slot, expert, tile):
            copy.wait()


def far_weight_grads(place, router_t, second, grads, w_experts):
    experts, width = w_experts.shape[:2]
    blocks, tokens = second.shape[:2]
    tiles = FF // TILE
    most = blocks * CAP
    held = most + CHUNK + 16

    def weight(part):
        return pl.BlockSpec((1, width, TILE), lambda e, j, s: (e, 0, part * tiles + j))

    return pl.pallas_call(
        far_kernel,
        grid_spec=pltpu.PrefetchScalarGridSpec(
            num_scalar_prefetch=1,
            grid=(experts, tiles),
            in_specs=[
                whole(router_t),
                anywhere(),
                anywhere(),
                weight(0),
                weight(1),
                weight(2),
            ],
            out_specs=anywhere(),
            scratch_shapes=[
                pltpu.VMEM((experts, held, width), BF),
                pltpu.VMEM((experts, held, width), BF),
                pltpu.VMEM((3, most, TILE), BF),
                pltpu.VMEM((2, JOINED, tokens, width), BF),
                pltpu.VMEM((2, JOINED, tokens + EXTRA, width), BF),
                pltpu.VMEM((2, 3, width, TILE), F32),
                pltpu.SMEM((experts,), jnp.int32),
                pltpu.SemaphoreType.DMA((2, 2)),
                pltpu.SemaphoreType.DMA((2, 3)),
            ],
        ),
        out_shape=jax.ShapeDtypeStruct((experts, width, 3 * FF), F32),
        compiler_params=pltpu.CompilerParams(vmem_limit_bytes=VMEM),
        cost_estimate=time_of(80),
        name="far_weight_grads",
    )(place, router_t, second, grads, w_experts, w_experts, w_experts)


def per_device(
    tokens,
    query_key_value_weight,
    output_weight,
    routing_weight,
    gain_attn,
    gain_moe,
    w_experts,
    doc_starts,
    routes,
    cotangent,
):
    spans = lax.axis_size("ctx")
    shards = lax.axis_size("fsdp")
    here = lax.axis_index("ctx")
    shard = lax.axis_index("fsdp")
    place = jnp.stack([here, shard]).astype(jnp.int32)
    x, grad = tokens[0], cotangent[0]
    tok_count, width = x.shape
    shard_rows = query_key_value_weight.shape[0]
    copies = spans // HK
    head = here // copies
    length = spans * tok_count
    blocks = spans * shards

    side = jnp.concatenate(
        [
            routing_weight.T,
            gain_attn[None],
            gain_moe[None],
            jnp.zeros((EXTRA - EXPERTS - 2, shard_rows), BF),
        ]
    )
    head_w = jnp.concatenate(
        [
            lax.dynamic_slice_in_dim(query_key_value_weight, head * HEAD, HEAD, 1),
            lax.dynamic_slice_in_dim(query_key_value_weight, Q_COLS + head * HD, HD, 1),
            lax.dynamic_slice_in_dim(query_key_value_weight, Q_COLS + K_COLS + head * HD, HD, 1),
        ],
        axis=1,
    )
    side = jnp.stack(near_blocks(side))
    side = jnp.take(side, jnp.arange(shards, dtype=jnp.int32) ^ shard, axis=0)
    side = side.swapaxes(0, 1).reshape(EXTRA, width)
    head_w = near_blocks(head_w)
    out_w = gathered(output_weight, "fsdp")
    qkv_w = gathered(after(query_key_value_weight, out_w), "fsdp")
    pieces = span_pieces(x, side, head_w)

    payload = jnp.concatenate(
        [grad, jnp.pad(routes[0].T.astype(BF), ((0, EXTRA - 2), (0, width - tok_count)))]
    )
    payload = after(payload, pieces)
    grads_near = near_blocks(payload)
    grads_line = line_blocks(payload)

    normed, mixed, attended_low, attended, log_norm = stream_attention(
        place, doc_starts[0], pieces, head_w, side, copies
    )

    grads_all = all_blocks(after(grads_line, attended_low))
    own = to_all(attended_low, "ctx").reshape(spans, tok_count, HEAD)
    middle, second = home_forward(own, x, side, out_w, copies)
    second_near = near_blocks(second)
    second_line = line_blocks(second)

    branch, back = near_experts(place, second_near, grads_near, side, w_experts)
    second_all = all_blocks(after(second_line, back))
    attended_pieces = span_pieces(after(attended_low, own), back)
    terms = after(near_terms(back), grads_all)
    branch_terms = near_terms(branch)
    output = sum((term.astype(F32) for term in branch_terms), middle).astype(BF)

    d_middle, sent, small = home_turn(
        terms, middle, second, grad, routes[0], side, out_w, spans
    )

    sent = to_all(sent.reshape(length, -1), "ctx")
    d_mixed, grads_out = stream_backward(
        place, doc_starts[0], attended_pieces, sent, mixed, attended, log_norm, normed, small, shards
    )
    late = near_terms([grads_out[r] for r in range(shards)])
    late = sum((term.astype(F32) for term in late[1:]), late[0].astype(F32)).astype(BF)
    late = lax.all_gather(after(late, second_all), "ctx", axis=0)

    d_home = to_all(d_mixed, "ctx").reshape(spans, tok_count, HEAD_COLS)

    second_all = second_all.reshape(blocks, tok_count, width)
    grads_all = grads_all.reshape(blocks, tok_count + EXTRA, width)
    segment = min(blocks, SEGMENT)
    parts = [
        far_weight_grads(
            place, side, second_all[i : i + segment], grads_all[i : i + segment], w_experts
        )
        for i in range(0, blocks, segment)
    ]
    d_w_experts = sum(parts[1:], parts[0])

    d_home = after(d_home, d_w_experts)
    d_tokens = home_backward(d_home, x, side, d_middle, qkv_w, copies)
    d_qkv_w, d_out_w, small, d_gain_attn = collected(
        late, query_key_value_weight, width, copies
    )
    return (
        output[None],
        d_tokens[None],
        d_qkv_w,
        d_out_w,
        small[:EXPERTS].T,
        d_gain_attn[:, 0] / gain_attn.astype(F32),
        small[EXPERTS],
        d_w_experts,
    )


def solution(mesh):
    placed = (
        P("fsdp", "ctx", None),
        P("fsdp", None),
        P("fsdp", None),
        P("fsdp", None),
        P("fsdp"),
        P("fsdp"),
        P("fsdp", None, None),
        P("fsdp", None),
        P("fsdp", "ctx", None),
        P("fsdp", "ctx", None),
    )
    return jax.shard_map(
        per_device,
        mesh=mesh,
        in_specs=placed,
        out_specs=(
            P("fsdp", "ctx", None),
            P("fsdp", "ctx", None),
            P("fsdp", None),
            P("fsdp", None),
            P("fsdp", None),
            P("fsdp"),
            P("fsdp"),
            P("fsdp", None, None),
        ),
        check_vma=False,
    )
```

```python
import functools

import jax
import jax.numpy as jnp
from jax import lax
from jax.experimental import pallas as pl
from jax.experimental.pallas import tpu as pltpu
from jax.sharding import PartitionSpec as P

HQ = 24
HK = 8
HD = 64
GROUP = HQ // HK
FF = 1024
EXPERTS = 8
CAP = 64
Q_COLS = HQ * HD
K_COLS = HK * HD
HEAD = GROUP * HD
HEAD_COLS = HEAD + 2 * HD
SCALE = HD**-0.5
EXTRA = 16
LANES = 128
TILE = 256
CHUNK = 256
SEGMENT = 32
JOINED = 2
AHEAD = 4
QUERIES = 256
DEPTHS = (1, 2, 3, 4, 6, 8)
VMEM = 58 * 1024 * 1024

NORM_EPS = 1e-05
MASK_NEG = -1e30
BF = jnp.bfloat16
F32 = jnp.float32


def dot(a, b):
    return jnp.dot(a, b, preferred_element_type=F32)


def dot_t(a, b):
    return lax.dot_general(a, b, (((1,), (1,)), ((), ())), preferred_element_type=F32)


def t_dot(a, b):
    return lax.dot_general(a, b, (((0,), (0,)), ((), ())), preferred_element_type=F32)


def iota(shape, axis):
    return lax.broadcasted_iota(jnp.int32, shape, axis)


def rms_factor(values):
    return lax.rsqrt(jnp.mean(values * values, axis=-1, keepdims=True) + NORM_EPS)


def rms_input_grad(values, factor, gain_vec, incoming):
    inner = incoming * gain_vec
    cubed = factor * factor * factor
    return factor * inner - values * cubed * jnp.mean(inner * values, axis=-1, keepdims=True)


def to_all(value, axis):
    return lax.all_to_all(value, axis, 0, 0, tiled=True)


def gathered(value, axis):
    return lax.all_gather(value, axis, axis=0, tiled=True)


def exchanged(value, axis, distance):
    count = lax.axis_size(axis)
    return lax.ppermute(value, axis, [(i, i ^ distance) for i in range(count)])


def near_blocks(own):
    blocks = {0: own}
    distance = lax.axis_size("fsdp") // 2
    while distance:
        blocks.update({r ^ distance: exchanged(b, "fsdp", distance) for r, b in blocks.items()})
        distance //= 2
    return [blocks[r] for r in range(len(blocks))]


def near_terms(blocks):
    shards = lax.axis_size("fsdp")
    terms = {r: [block] for r, block in enumerate(blocks)}
    distance = 1

    def total(parts):
        if len(parts) == 1:
            return parts[0]
        return sum((part.astype(F32) for part in parts[1:]), parts[0].astype(F32)).astype(BF)

    while distance < shards:
        terms = {
            r: terms[r] + [exchanged(total(terms[r ^ distance]), "fsdp", distance)]
            for r in range(0, shards, 2 * distance)
        }
        distance *= 2
    return terms[0]


def line_blocks(own):
    return [own] + [exchanged(own, "ctx", d) for d in range(2, lax.axis_size("ctx"), 2)]


def all_blocks(line):
    spans, shards = lax.axis_size("ctx"), lax.axis_size("fsdp")
    sets = [
        [(2 * pair + side) * shards + f for side in range(2) for f in range(shards)]
        for pair in range(spans // 2)
    ]
    return lax.all_gather(line, ("ctx", "fsdp"), axis=0, tiled=True, axis_index_groups=sets)


def after(values, *others):
    return lax.optimization_barrier((values, others))[0]


def time_of(microseconds):
    return pl.CostEstimate(flops=0, bytes_accessed=microseconds * 3_600_000, transcendentals=0)


def whole(array):
    shape = array.shape
    return pl.BlockSpec(shape, lambda *_: (0,) * len(shape))


def anywhere():
    return pl.BlockSpec(memory_space=pl.ANY)


def place_pieces(here, pieces, target, sems):
    copies = []
    for i, piece in enumerate(pieces):
        odd, last = divmod(i, 2)
        rows = piece.shape[1]
        for j in range(piece.shape[0]):
            copies.append(
                pltpu.make_async_copy(
                    piece.at[j],
                    target.at[here ^ (2 * j + odd), pl.ds(last * rows, rows)],
                    sems.at[i, j],
                )
            )
    for copy in copies:
        copy.start()
    return copies


def doc_of(starts, positions):
    found = jnp.zeros(positions.shape, jnp.int32)
    for i in range(starts.shape[0]):
        found = found + (positions >= starts[i]).astype(jnp.int32)
    return found


def visible(starts, here, copies, tokens, first, rows, keys):
    query = first + iota((rows, 1), 0)
    key = iota((1, keys), 1)
    allowed = (key <= query) & (doc_of(starts, key) == doc_of(starts, query))
    if copies > 1:
        allowed = allowed & (lax.rem(query // tokens, copies) == lax.rem(here, copies))
    return allowed


def stream_kernel(
    copies,
    place,
    starts,
    *refs,
):
    shards = len(refs) - 15
    pieces, weights, side = refs[:4], refs[4 : 4 + shards], refs[4 + shards]
    normed, mixed, attended_low, attended, log_norm, rows, weight, piece_sems, weight_sems = refs[
        5 + shards : 14 + shards
    ]
    here, shard = place[0], place[1]
    spans, tokens, width = rows.shape
    length = spans * tokens
    copying = place_pieces(here, pieces, rows, piece_sems)
    loading = [
        pltpu.make_async_copy(ref, weight.at[shard ^ r], weight_sems.at[r])
        for r, ref in enumerate(weights)
    ]
    for copy in loading:
        copy.start()
    for copy in loading + copying:
        copy.wait()
    head_weight = weight[...].reshape(width, HEAD_COLS)
    gain = side[EXPERTS : EXPERTS + 1, :].astype(F32)

    @pl.loop(0, spans)
    def _(span):
        x = rows[span].astype(F32)
        low = (x * rms_factor(x) * gain).astype(BF)
        at = pl.ds(pl.multiple_of(span * tokens, tokens), tokens)
        normed[at, :] = low
        mixed[at, :] = dot(low, head_weight).astype(BF)

    for first in range(0, length, QUERIES):
        keys = first + QUERIES
        at = slice(first, keys)
        allowed = visible(starts, here, copies, tokens, first, QUERIES, keys)
        for g in range(GROUP):
            columns = slice(g * HD, (g + 1) * HD)
            scores = dot_t(mixed[at, columns], mixed[:keys, HEAD : HEAD + HD]) * SCALE
            scores = jnp.where(allowed, scores, MASK_NEG)
            highest = jnp.max(scores, axis=1, keepdims=True)
            parts = jnp.where(allowed, jnp.exp(scores - highest), 0.0)
            total = jnp.sum(parts, axis=1, keepdims=True)
            total = jnp.where(total == 0.0, 1.0, total)
            log_norm[at, g : g + 1] = highest + jnp.log(total)
            result = dot((parts / total).astype(BF), mixed[:keys, HEAD + HD :])
            attended[at, columns] = result
            attended_low[at, columns] = result.astype(BF)


def stream_attention(place, starts, pieces, head_weights, side, copies):
    spans, tokens = 2 * pieces[0].shape[0], 2 * pieces[0].shape[1]
    width = pieces[0].shape[2]
    length = spans * tokens
    shards = len(head_weights)
    return pl.pallas_call(
        functools.partial(stream_kernel, copies),
        grid_spec=pltpu.PrefetchScalarGridSpec(
            num_scalar_prefetch=2,
            grid=(1,),
            in_specs=[anywhere()] * (4 + shards) + [whole(side)],
            out_specs=[
                pl.BlockSpec((length, columns), lambda *_: (0, 0))
                for columns in (width, HEAD_COLS, HEAD, HEAD, LANES)
            ],
            scratch_shapes=[
                pltpu.VMEM((spans, tokens, width), BF),
                pltpu.VMEM((shards, width // shards, HEAD_COLS), BF),
                pltpu.SemaphoreType.DMA((4, spans // 2)),
                pltpu.SemaphoreType.DMA((shards,)),
                pltpu.SMEM((1,), jnp.int32),
            ],
        ),
        out_shape=[
            jax.ShapeDtypeStruct((length, columns), kind)
            for columns, kind in (
                (width, BF),
                (HEAD_COLS, BF),
                (HEAD, BF),
                (HEAD, F32),
                (LANES, F32),
            )
        ],
        compiler_params=pltpu.CompilerParams(vmem_limit_bytes=VMEM),
        cost_estimate=time_of(16),
        name="stream_attention",
    )(place, starts, *pieces, *head_weights, side)


def home_kernel(copies, own, tokens, side, weight, middle, second):
    total = tokens[...].astype(F32)
    for head in range(HK):
        part = own[head * copies]
        for i in range(1, copies):
            part = part + own[head * copies + i]
        total = total + dot(part, weight[head * HEAD : (head + 1) * HEAD, :])
    middle[...] = total
    gain = side[EXPERTS + 1 : EXPERTS + 2, :].astype(F32)
    second[...] = (total * rms_factor(total) * gain).astype(BF)


def home_forward(own, tokens, side, weight, copies):
    args = (own, tokens, side, weight)
    return pl.pallas_call(
        functools.partial(home_kernel, copies),
        grid=(1,),
        in_specs=[whole(a) for a in args],
        out_specs=[whole(tokens)] * 2,
        out_shape=[
            jax.ShapeDtypeStruct(tokens.shape, F32),
            jax.ShapeDtypeStruct(tokens.shape, BF),
        ],
        compiler_params=pltpu.CompilerParams(vmem_limit_bytes=VMEM),
        cost_estimate=time_of(5),
        name="home_forward",
    )(*args)


def turn_kernel(copies, term_count, *refs):
    terms, refs = refs[:term_count], refs[term_count:]
    middle_ref, second_ref, grad, routes, side, weight, d_middle_out, sent, small = refs
    width = middle_ref.shape[1]
    back = terms[0][...].astype(F32)
    for term in terms[1:]:
        back = back + term[...].astype(F32)
    middle, second = middle_ref[...], second_ref[...]
    d_gates = back[:, width : width + EXTRA]
    ids = iota(d_gates.shape, 1)
    d_gates = d_gates + back[:, width + EXPERTS : width + EXPERTS + EXTRA]
    picked = (ids == routes[:, 0:1]) | (ids == routes[:, 1:2])
    logits = jnp.where(picked, dot_t(second, side[...]), MASK_NEG)
    gates = jnp.where(picked, jnp.exp(logits - jnp.max(logits, axis=1, keepdims=True)), 0.0)
    gates = gates / jnp.sum(gates, axis=1, keepdims=True)
    d_gates = jnp.where(picked, d_gates, 0.0)
    d_picked = gates * (d_gates - jnp.sum(gates * d_gates, axis=1, keepdims=True))
    d_logits = d_picked.astype(BF)
    d_second = dot(d_logits, side[...]) + back[:, :width]
    factor = rms_factor(middle)
    small[...] = t_dot(d_logits, second)
    small[EXPERTS : EXPERTS + 1, :] = jnp.sum(d_second * middle * factor, axis=0, keepdims=True)
    gain = side[EXPERTS + 1 : EXPERTS + 2, :].astype(F32)
    d_middle = grad[...].astype(F32) + rms_input_grad(middle, factor, gain, d_second)
    d_middle_out[...] = d_middle
    d_proj = d_middle.astype(BF)
    for head in range(HK):
        d_head = dot_t(d_proj, weight[head * HEAD : (head + 1) * HEAD, :]).astype(BF)
        for i in range(copies):
            sent[head * copies + i, :, :HEAD] = d_head
    chunk = sent.shape[2] - HEAD
    for span in range(sent.shape[0]):
        sent[span, :, HEAD:] = d_proj[:, span * chunk : (span + 1) * chunk]


def home_turn(terms, middle, second, grad, routes, side, weight, spans):
    args = (*terms, middle, second, grad, routes, side, weight)
    tokens, width = middle.shape
    shapes = [
        jax.ShapeDtypeStruct((tokens, width), F32),
        jax.ShapeDtypeStruct((spans, tokens, HEAD + width // spans), BF),
        jax.ShapeDtypeStruct((EXTRA, width), F32),
    ]
    return pl.pallas_call(
        functools.partial(turn_kernel, spans // HK, len(terms)),
        grid=(1,),
        in_specs=[whole(a) for a in args],
        out_specs=[whole(shape) for shape in shapes],
        out_shape=shapes,
        compiler_params=pltpu.CompilerParams(vmem_limit_bytes=VMEM),
        cost_estimate=time_of(7),
        name="home_turn",
    )(*args)


def stream_grad_kernel(
    copies, place, starts, pieces0, pieces1, pieces2, pieces3, sent, mixed, attended, log_norm,
    normed, small, d_mixed, out, everyones, d_kv, sems
):
    here, shard = place[0], place[1]
    length, width = normed.shape
    spans = everyones.shape[0]
    tokens = length // spans
    shards = out.shape[0]
    shard_rows = width // shards
    heads = HK // shards
    copying = place_pieces(here, (pieces0, pieces1, pieces2, pieces3), everyones, sems)
    d_kv[...] = jnp.zeros_like(d_kv)
    for first in range(0, length, QUERIES):
        keys = first + QUERIES
        at = slice(first, keys)
        allowed = visible(starts, here, copies, tokens, first, QUERIES, keys)
        k, v = mixed[:keys, HEAD : HEAD + HD], mixed[:keys, HEAD + HD :]
        for g in range(GROUP):
            columns = slice(g * HD, (g + 1) * HD)
            q, grad = mixed[at, columns], sent[at, columns]
            delta = jnp.sum(grad.astype(F32) * attended[at, columns], axis=1, keepdims=True)
            scores = dot_t(q, k) * SCALE
            probs = jnp.where(allowed, jnp.exp(scores - log_norm[at, g : g + 1]), 0.0)
            d_scores = (probs * (dot_t(grad, v) - delta)).astype(BF)
            d_mixed[at, columns] = (dot(d_scores, k) * SCALE).astype(BF)
            d_kv[0, :keys, :] += t_dot(d_scores, q)
            d_kv[1, :keys, :] += t_dot(probs.astype(BF), grad)
    d_mixed[:, HEAD : HEAD + HD] = (d_kv[0] * SCALE).astype(BF)
    d_mixed[:, HEAD + HD :] = d_kv[1].astype(BF)
    for copy in copying:
        copy.wait()
    d_proj = sent[:, HEAD:]
    low = small[...].astype(BF)
    for f in range(shards):
        spot = shard ^ f
        columns = slice(f * shard_rows, (f + 1) * shard_rows)
        out[spot, :shard_rows, :HEAD_COLS] = t_dot(normed[:, columns], d_mixed[...]).astype(BF)
        for h in range(heads):
            first = (f * heads + h) * copies
            part = everyones[first]
            for i in range(1, copies):
                part = part + everyones[first + i]
            out[spot, h * HEAD : (h + 1) * HEAD, HEAD_COLS:] = t_dot(part, d_proj).astype(BF)
        out[spot, shard_rows:, :] = jnp.zeros((EXTRA, out.shape[2]), BF)
        out[spot, shard_rows:, :shard_rows] = low[:, columns]


def stream_backward(place, starts, pieces, sent, mixed, attended, log_norm, normed, small, shards):
    args = (sent, mixed, attended, log_norm, normed, small)
    length, width = normed.shape
    spans = 2 * pieces[0].shape[0]
    shapes = [
        jax.ShapeDtypeStruct(mixed.shape, BF),
        jax.ShapeDtypeStruct(
            (shards, width // shards + EXTRA, HEAD_COLS + width // spans), BF
        ),
    ]
    return pl.pallas_call(
        functools.partial(stream_grad_kernel, spans // HK),
        grid_spec=pltpu.PrefetchScalarGridSpec(
            num_scalar_prefetch=2,
            grid=(1,),
            in_specs=[anywhere()] * 4 + [whole(a) for a in args],
            out_specs=[whole(shape) for shape in shapes],
            scratch_shapes=[
                pltpu.VMEM((spans, length, HEAD), BF),
                pltpu.VMEM((2, length, HD), F32),
                pltpu.SemaphoreType.DMA((4, spans // 2)),
            ],
        ),
        out_shape=shapes,
        compiler_params=pltpu.CompilerParams(vmem_limit_bytes=VMEM),
        cost_estimate=time_of(17),
        name="stream_backward",
    )(place, starts, *pieces, *args)


def home_grad_kernel(copies, d_home, tokens, side, d_middle, weight, d_tokens, mixed):
    for head in range(HK):
        part = d_home[head * copies]
        if copies > 1:
            part = part.astype(F32)
            for i in range(1, copies):
                part = part + d_home[head * copies + i].astype(F32)
            part = part.astype(BF)
        mixed[:, head * HEAD : (head + 1) * HEAD] = part[:, :HEAD]
        key = Q_COLS + head * HD
        mixed[:, key : key + HD] = part[:, HEAD : HEAD + HD]
        value = key + K_COLS
        mixed[:, value : value + HD] = part[:, HEAD + HD :]
    d_normed = dot_t(mixed[...], weight[...])
    x = tokens[...].astype(F32)
    gain = side[EXPERTS : EXPERTS + 1, :].astype(F32)
    d_x = rms_input_grad(x, rms_factor(x), gain, d_normed)
    d_tokens[...] = (d_middle[...] + d_x).astype(BF)


def home_backward(d_home, tokens, side, d_middle, weight, copies):
    args = (d_home, tokens, side, d_middle, weight)
    return pl.pallas_call(
        functools.partial(home_grad_kernel, copies),
        grid=(1,),
        in_specs=[whole(a) for a in args],
        out_specs=whole(tokens),
        scratch_shapes=[pltpu.VMEM((tokens.shape[0], Q_COLS + 2 * K_COLS), BF)],
        out_shape=jax.ShapeDtypeStruct(tokens.shape, BF),
        compiler_params=pltpu.CompilerParams(vmem_limit_bytes=VMEM),
        cost_estimate=time_of(8),
        name="home_backward",
    )(*args)


def collect_kernel(copies, late, own_weight, d_qkv, d_out, small, d_gain):
    rows = own_weight.shape[0]
    chunk = late.shape[2] - HEAD_COLS
    for head in range(HK):
        part = late[head * copies, :rows, :HEAD_COLS].astype(F32)
        for i in range(1, copies):
            part = part + late[head * copies + i, :rows, :HEAD_COLS].astype(F32)
        d_qkv[:, head * HEAD : (head + 1) * HEAD] = part[:, :HEAD]
        key = Q_COLS + head * HD
        d_qkv[:, key : key + HD] = part[:, HEAD : HEAD + HD]
        value = key + K_COLS
        d_qkv[:, value : value + HD] = part[:, HEAD + HD :]
    total = jnp.zeros((EXTRA, rows), F32)
    for span in range(late.shape[0]):
        d_out[:, span * chunk : (span + 1) * chunk] = late[span, :rows, HEAD_COLS:].astype(F32)
        total = total + late[span, rows:, :rows].astype(F32)
    small[...] = total
    d_gain[...] = jnp.sum(d_qkv[...] * own_weight[...].astype(F32), axis=1, keepdims=True)


def collected(late, own_weight, width, copies):
    rows, columns = own_weight.shape
    shapes = [
        jax.ShapeDtypeStruct((rows, columns), F32),
        jax.ShapeDtypeStruct((rows, width), F32),
        jax.ShapeDtypeStruct((EXTRA, rows), F32),
        jax.ShapeDtypeStruct((rows, 1), F32),
    ]
    return pl.pallas_call(
        functools.partial(collect_kernel, copies),
        grid=(1,),
        in_specs=[whole(late), whole(own_weight)],
        out_specs=[whole(shape) for shape in shapes],
        out_shape=shapes,
        compiler_params=pltpu.CompilerParams(vmem_limit_bytes=VMEM),
        cost_estimate=time_of(7),
        name="collected",
    )(late, own_weight)


def picked_gates(second, router_t, chosen):
    logits = dot_t(router_t, second)
    ids = iota(logits.shape, 0)
    picked = (ids == chosen[0:1, :]) | (ids == chosen[1:2, :])
    logits = jnp.where(picked, logits, MASK_NEG)
    parts = jnp.where(picked, jnp.exp(logits - jnp.max(logits, axis=0, keepdims=True)), 0.0)
    return picked, parts / jnp.sum(parts, axis=0, keepdims=True)


def swiglu_grads(gate, up, d_hidden):
    sigma = 1.0 / (1.0 + jnp.exp(-gate))
    passed = gate * sigma
    d_gate = d_hidden * up * sigma * (1.0 + gate * (1.0 - sigma))
    return (passed * up).astype(BF), d_gate.astype(BF), (d_hidden * passed).astype(BF)


def near_kernel(shards, place, *refs):
    second, grads = refs[:shards], refs[shards : 2 * shards]
    router_t, w_gate, w_up, w_down = refs[2 * shards : 2 * shards + 4]
    branch_out = refs[2 * shards + 4 : 3 * shards + 4]
    back_out = refs[3 * shards + 4 : 4 * shards + 4]
    hot, rows, cots, d_outs, slot_gate, out_acc, row_acc, branch_acc, back_acc = refs[
        4 * shards + 4 :
    ]
    expert, tile = pl.program_id(0), pl.program_id(1)
    tokens = second[0].shape[0]
    width = second[0].shape[1]
    wanted = place[1] * pl.num_programs(0) + expert

    @pl.when(tile == 0)
    def _():
        before = (iota((tokens, tokens), 0) < iota((tokens, tokens), 1)).astype(BF)
        for f in range(shards):
            chosen = grads[f][tokens : tokens + EXTRA, :tokens].astype(F32).astype(jnp.int32)
            picked, gates = picked_gates(second[f][...], router_t[...], chosen)
            ranks = dot(picked.astype(BF), before)
            found = (iota(ranks.shape, 0) == wanted) & picked
            rank = jnp.sum(jnp.where(found, ranks + 1.0, 0.0), axis=0, keepdims=True)
            gate = jnp.sum(jnp.where(found, gates, 0.0), axis=0, keepdims=True)
            match = iota((CAP, tokens), 0).astype(F32) + 1.0 == rank
            one_hot = match.astype(BF)
            place = pl.ds(f * CAP, CAP)
            hot[f] = one_hot
            found_gate = jnp.sum(jnp.where(match, gate, 0.0), axis=1, keepdims=True)
            slot_gate[place, :] = jnp.broadcast_to(found_gate, (CAP, LANES))
            rows[place, :] = dot(one_hot, second[f][...]).astype(BF)
            cot = dot(one_hot, grads[f][:tokens, :])
            cots[place, :] = cot.astype(BF)
            d_outs[place, :] = (found_gate * cot).astype(BF)
        out_acc[...] = jnp.zeros_like(out_acc)
        row_acc[...] = jnp.zeros_like(row_acc)

    hidden, d_gate, d_up = swiglu_grads(
        dot(rows[...], w_gate[0]), dot(rows[...], w_up[0]), dot(d_outs[...], w_down[0])
    )
    out_acc[...] += dot_t(hidden, w_down[0])
    row_acc[...] += dot_t(d_gate, w_gate[0]) + dot_t(d_up, w_up[0])

    @pl.when(tile == pl.num_programs(1) - 1)
    def _():
        last = expert == pl.num_programs(0) - 1
        for f in range(shards):
            place = pl.ds(f * CAP, CAP)
            out = out_acc[place, :].astype(BF).astype(F32)
            d_gates = jnp.sum(cots[place, :].astype(F32) * out, axis=1, keepdims=True)
            gated = (slot_gate[place, 0:1] * out).astype(BF)
            lane = iota((CAP, LANES), 1)
            coarse = d_gates.astype(BF).astype(F32)
            extra = jnp.where(lane == wanted, coarse, 0.0)
            extra = extra + jnp.where(lane == EXPERTS + wanted, d_gates - coarse, 0.0)

            def add(acc, part, columns):
                @pl.when(expert == 0)
                def _():
                    acc[f, :, columns] = part

                @pl.when(expert > 0)
                def _():
                    acc[f, :, columns] += part

            add(branch_acc, t_dot(hot[f], gated), slice(0, width))
            add(back_acc, t_dot(hot[f], row_acc[place, :].astype(BF)), slice(0, width))
            add(back_acc, t_dot(hot[f], extra.astype(BF)), slice(width, width + LANES))

            @pl.when(last)
            def _():
                branch_out[f][...] = branch_acc[f].astype(BF)
                back_out[f][...] = back_acc[f].astype(BF)


def near_experts(place, second, grads, router_t, w_experts):
    shards = len(second)
    tokens, width = second[0].shape
    experts = w_experts.shape[0]
    slots = shards * CAP
    tiles = FF // TILE
    shapes = [jax.ShapeDtypeStruct((tokens, width), BF)] * shards
    shapes += [jax.ShapeDtypeStruct((tokens, width + LANES), BF)] * shards

    def weight(part):
        return pl.BlockSpec((1, width, TILE), lambda e, j, s: (e, 0, part * tiles + j))

    outs = pl.pallas_call(
        functools.partial(near_kernel, shards),
        grid_spec=pltpu.PrefetchScalarGridSpec(
            num_scalar_prefetch=1,
            grid=(experts, tiles),
            in_specs=[whole(a) for a in (*second, *grads, router_t)]
            + [weight(0), weight(1), weight(2)],
            out_specs=[whole(shape) for shape in shapes],
            scratch_shapes=[
                pltpu.VMEM((shards, CAP, tokens), BF),
                pltpu.VMEM((slots, width), BF),
                pltpu.VMEM((slots, width), BF),
                pltpu.VMEM((slots, width), BF),
                pltpu.VMEM((slots, LANES), F32),
                pltpu.VMEM((slots, width), F32),
                pltpu.VMEM((slots, width), F32),
                pltpu.VMEM((shards, tokens, width), F32),
                pltpu.VMEM((shards, tokens, width + LANES), F32),
            ],
        ),
        out_shape=shapes,
        compiler_params=pltpu.CompilerParams(vmem_limit_bytes=VMEM),
        cost_estimate=time_of(26),
        name="near_experts",
    )(place, *second, *grads, router_t, w_experts, w_experts, w_experts)
    return outs[:shards], outs[shards:]


def far_kernel(
    place,
    router_t,
    second_ref,
    grads_ref,
    w_gate,
    w_up,
    w_down,
    out_ref,
    rows,
    d_outs,
    act,
    fetched_rows,
    fetched_grads,
    tile_out,
    counts,
    fetch_sem,
    store_sem,
):
    experts = rows.shape[0]
    expert, tile = pl.program_id(0), pl.program_id(1)
    tiles = pl.num_programs(1)
    step = expert * tiles + tile
    slot = lax.rem(step, 2)
    groups = second_ref.shape[0] // JOINED
    tokens, width = second_ref.shape[1:]
    size = JOINED * tokens
    window = JOINED * CAP + 16

    def stores(which, e, j):
        return [
            pltpu.make_async_copy(
                tile_out.at[which, i],
                out_ref.at[e, :, pl.ds(pl.multiple_of(i * FF + j * TILE, TILE), TILE)],
                store_sem.at[which, i],
            )
            for i in range(3)
        ]

    def fetches(which, g):
        at = pl.ds(g * JOINED, JOINED)
        return [
            pltpu.make_async_copy(ref.at[at], buffer.at[which], fetch_sem.at[which, i])
            for i, (ref, buffer) in enumerate(
                ((second_ref, fetched_rows), (grads_ref, fetched_grads))
            )
        ]

    @pl.when(step == 0)
    def _():
        ahead = min(AHEAD, groups)
        for g in range(ahead):
            for copy in fetches(g, g):
                copy.start()
        before = (iota((size, size), 0) < iota((size, size), 1)).astype(BF)

        def gather(g, starts):
            which = lax.rem(g, AHEAD)
            for copy in fetches(which, g):
                copy.wait()
            second = fetched_rows[which].reshape(size, width)
            grads = fetched_grads[which, :, :tokens].reshape(size, width)
            chosen = jnp.concatenate(
                [fetched_grads[which, b, tokens : tokens + EXTRA, :LANES] for b in range(JOINED)],
                axis=1,
            )
            chosen = chosen.astype(F32).astype(jnp.int32)
            picked, gates = picked_gates(second, router_t[...], chosen)
            ranks = dot(picked.astype(BF), before)
            ids = iota(ranks.shape, 0)
            bases = [start // 16 * 16 for start in starts]
            matches, found_gates, ends = [], [], []
            for e in range(experts):
                found = (ids == place[1] * experts + e) & picked
                gate = jnp.sum(jnp.where(found, gates, 0.0), axis=0, keepdims=True)
                rank = jnp.sum(jnp.where(found, ranks + 1.0, 0.0), axis=0, keepdims=True)
                shift = (starts[e] - bases[e]).astype(F32)
                spot = jnp.where(rank > 0.0, rank + (shift - 1.0), -1.0)
                match = iota((window, size), 0).astype(F32) == spot
                matches.append(match.astype(BF))
                found_gates.append(
                    jnp.sum(jnp.where(match, gate, 0.0), axis=1, keepdims=True)
                )
                ends.append(starts[e] + jnp.sum((rank > 0.0).astype(jnp.int32)))
            one_hot = jnp.concatenate(matches, axis=0)
            new_rows = dot(one_hot, second).astype(BF)
            new_grads = (jnp.concatenate(found_gates, axis=0) * dot(one_hot, grads)).astype(BF)
            for e in range(experts):
                at = pl.ds(pl.multiple_of(bases[e], 16), 16)
                rest = pl.ds(pl.multiple_of(bases[e] + 16, 16), window - 16)
                held = iota((16, width), 0) < starts[e] - bases[e]
                for ref, new in ((rows, new_rows), (d_outs, new_grads)):
                    new = new[e * window : (e + 1) * window]
                    ref[e, at, :] = jnp.where(held, ref[e, at, :], new[:16])
                    ref[e, rest, :] = new[16:]

            @pl.when(g + AHEAD < groups)
            def _():
                for copy in fetches(which, g + AHEAD):
                    copy.start()

            return tuple(ends)

        ends = lax.fori_loop(0, groups, gather, (jnp.int32(0),) * experts)
        for e in range(experts):
            counts[e] = ends[e]
            spare = pl.ds(pl.multiple_of((ends[e] + 15) // 16 * 16, 16), CHUNK)
            rows[e, spare, :] = jnp.zeros((CHUNK, width), BF)
            d_outs[e, spare, :] = jnp.zeros((CHUNK, width), BF)

    chunks = jnp.maximum((counts[expert] + CHUNK - 1) // CHUNK, 1)

    @pl.loop(0, chunks)
    def _(i):
        at = pl.ds(pl.multiple_of(i * CHUNK, CHUNK), CHUNK)
        row, d_out = rows[expert, at, :], d_outs[expert, at, :]
        hidden, d_gate, d_up = swiglu_grads(
            dot(row, w_gate[0]), dot(row, w_up[0]), dot(d_out, w_down[0])
        )
        act[0, at, :] = d_gate
        act[1, at, :] = d_up
        act[2, at, :] = hidden

    @pl.when(step >= 2)
    def _():
        for copy in stores(slot, (step - 2) // tiles, lax.rem(step - 2, tiles)):
            copy.wait()

    most = act.shape[1] // CHUNK
    depths = [k for k in DEPTHS if k < most] + [most]
    for low, k in zip([0] + depths[:-1], depths):

        @pl.when((chunks > low) & (chunks <= k))
        def _():
            for extra in range(low + 1, k):

                @pl.when(chunks == extra)
                def _():
                    spare = slice(extra * CHUNK, k * CHUNK)
                    empty = jnp.zeros(((k - extra) * CHUNK, width), BF)
                    rows[expert, spare, :] = empty
                    d_outs[expert, spare, :] = empty
                    for i in range(3):
                        act[i, spare, :] = empty[:, :TILE]

            upto = k * CHUNK
            for i, left in enumerate((rows, rows, d_outs)):
                tile_out[slot, i] = t_dot(left[expert, :upto, :], act[i, :upto, :])

    for copy in stores(slot, expert, tile):
        copy.start()

    @pl.when(step == pl.num_programs(0) * tiles - 1)
    def _():
        for copy in stores(1 - slot, (step - 1) // tiles, lax.rem(step - 1, tiles)):
            copy.wait()
        for copy in stores(slot, expert, tile):
            copy.wait()


def far_weight_grads(place, router_t, second, grads, w_experts):
    experts, width = w_experts.shape[:2]
    blocks, tokens = second.shape[:2]
    tiles = FF // TILE
    most = blocks * CAP
    held = most + CHUNK + 16

    def weight(part):
        return pl.BlockSpec((1, width, TILE), lambda e, j, s: (e, 0, part * tiles + j))

    return pl.pallas_call(
        far_kernel,
        grid_spec=pltpu.PrefetchScalarGridSpec(
            num_scalar_prefetch=1,
            grid=(experts, tiles),
            in_specs=[
                whole(router_t),
                anywhere(),
                anywhere(),
                weight(0),
                weight(1),
                weight(2),
            ],
            out_specs=anywhere(),
            scratch_shapes=[
                pltpu.VMEM((experts, held, width), BF),
                pltpu.VMEM((experts, held, width), BF),
                pltpu.VMEM((3, most, TILE), BF),
                pltpu.VMEM((AHEAD, JOINED, tokens, width), BF),
                pltpu.VMEM((AHEAD, JOINED, tokens + EXTRA, width), BF),
                pltpu.VMEM((2, 3, width, TILE), F32),
                pltpu.SMEM((experts,), jnp.int32),
                pltpu.SemaphoreType.DMA((AHEAD, 2)),
                pltpu.SemaphoreType.DMA((2, 3)),
            ],
        ),
        out_shape=jax.ShapeDtypeStruct((experts, width, 3 * FF), F32),
        compiler_params=pltpu.CompilerParams(vmem_limit_bytes=VMEM),
        cost_estimate=time_of(80),
        name="far_weight_grads",
    )(place, router_t, second, grads, w_experts, w_experts, w_experts)


def per_device(
    tokens,
    query_key_value_weight,
    output_weight,
    routing_weight,
    gain_attn,
    gain_moe,
    w_experts,
    doc_starts,
    routes,
    cotangent,
):
    spans = lax.axis_size("ctx")
    shards = lax.axis_size("fsdp")
    here = lax.axis_index("ctx")
    shard = lax.axis_index("fsdp")
    place = jnp.stack([here, shard]).astype(jnp.int32)
    x, grad = tokens[0], cotangent[0]
    tok_count, width = x.shape
    shard_rows = query_key_value_weight.shape[0]
    copies = spans // HK
    head = here // copies
    length = spans * tok_count
    blocks = spans * shards

    side = jnp.concatenate(
        [
            routing_weight.T,
            gain_attn[None],
            gain_moe[None],
            jnp.zeros((EXTRA - EXPERTS - 2, shard_rows), BF),
        ]
    )
    head_w = jnp.concatenate(
        [
            lax.dynamic_slice_in_dim(query_key_value_weight, head * HEAD, HEAD, 1),
            lax.dynamic_slice_in_dim(query_key_value_weight, Q_COLS + head * HD, HD, 1),
            lax.dynamic_slice_in_dim(query_key_value_weight, Q_COLS + K_COLS + head * HD, HD, 1),
        ],
        axis=1,
    )
    side = jnp.stack(near_blocks(side))
    side = jnp.take(side, jnp.arange(shards, dtype=jnp.int32) ^ shard, axis=0)
    side = side.swapaxes(0, 1).reshape(EXTRA, width)
    head_w = near_blocks(head_w)
    out_w = gathered(after(output_weight, side, head_w), "fsdp")
    qkv_w = gathered(after(query_key_value_weight, out_w), "fsdp")
    half = tok_count // 2
    first = jnp.stack(after(line_blocks(x[:half]), side, head_w))
    last = jnp.stack(line_blocks(after(x[half:], first)))
    pieces = [first, last, exchanged(first, "ctx", 1), exchanged(last, "ctx", 1)]

    payload = jnp.concatenate(
        [grad, jnp.pad(routes[0].T.astype(BF), ((0, EXTRA - 2), (0, width - tok_count)))]
    )
    payload = after(payload, pieces)
    grads_near = near_blocks(payload)
    grads_line = line_blocks(payload)

    normed, mixed, attended_low, attended, log_norm = stream_attention(
        place, doc_starts[0], pieces, head_w, side, copies
    )

    own = to_all(attended_low, "ctx").reshape(spans, tok_count, HEAD)
    grads_all = all_blocks(jnp.stack(after(grads_line, own)))
    middle, second = home_forward(own, x, side, out_w, copies)
    second_near = near_blocks(second)
    second_line = line_blocks(second)

    branch, back = near_experts(place, second_near, grads_near, side, w_experts)
    second_all = all_blocks(jnp.stack(after(second_line, back)))
    half = length // 2
    attended_low = after(attended_low, own)
    lines = [line_blocks(part) for part in (attended_low[:half], attended_low[half:])]
    attended_pieces = [jnp.stack(line) for line in after(lines, back)]
    attended_pieces += [exchanged(piece, "ctx", 1) for piece in attended_pieces]
    terms = after(near_terms(back), grads_all, attended_pieces[:2])
    branch_terms = near_terms(branch)
    output = sum((term.astype(F32) for term in branch_terms), middle).astype(BF)

    d_middle, sent, small = home_turn(
        terms, middle, second, grad, routes[0], side, out_w, spans
    )

    sent = after(to_all(sent.reshape(length, -1), "ctx"), output)
    d_mixed, grads_out = stream_backward(
        place, doc_starts[0], attended_pieces, sent, mixed, attended, log_norm, normed, small, shards
    )
    late = near_terms([grads_out[r] for r in range(shards)])
    late = sum((term.astype(F32) for term in late[1:]), late[0].astype(F32)).astype(BF)
    late = lax.all_gather(after(late, second_all), "ctx", axis=0)

    d_home = to_all(d_mixed, "ctx").reshape(spans, tok_count, HEAD_COLS)

    second_all = second_all.reshape(blocks, tok_count, width)
    grads_all = grads_all.reshape(blocks, tok_count + EXTRA, width)
    segment = min(blocks, SEGMENT)
    parts = [
        far_weight_grads(
            place, side, second_all[i : i + segment], grads_all[i : i + segment], w_experts
        )
        for i in range(0, blocks, segment)
    ]
    d_w_experts = sum(parts[1:], parts[0])

    d_home = after(d_home, d_w_experts)
    d_tokens = home_backward(d_home, x, side, d_middle, qkv_w, copies)
    d_qkv_w, d_out_w, small, d_gain_attn = collected(
        late, query_key_value_weight, width, copies
    )
    return (
        output[None],
        d_tokens[None],
        d_qkv_w,
        d_out_w,
        small[:EXPERTS].T,
        d_gain_attn[:, 0] / gain_attn.astype(F32),
        small[EXPERTS],
        d_w_experts,
    )


def solution(mesh):
    placed = (
        P("fsdp", "ctx", None),
        P("fsdp", None),
        P("fsdp", None),
        P("fsdp", None),
        P("fsdp"),
        P("fsdp"),
        P("fsdp", None, None),
        P("fsdp", None),
        P("fsdp", "ctx", None),
        P("fsdp", "ctx", None),
    )
    return jax.shard_map(
        per_device,
        mesh=mesh,
        in_specs=placed,
        out_specs=(
            P("fsdp", "ctx", None),
            P("fsdp", "ctx", None),
            P("fsdp", None),
            P("fsdp", None),
            P("fsdp", None),
            P("fsdp"),
            P("fsdp"),
            P("fsdp", None, None),
        ),
        check_vma=False,
    )
```

```python
import functools

import jax
import jax.numpy as jnp
from jax import lax
from jax.experimental import pallas as pl
from jax.experimental.pallas import tpu as pltpu
from jax.sharding import PartitionSpec as P

HQ = 24
HK = 8
HD = 64
GROUP = HQ // HK
FF = 1024
EXPERTS = 8
CAP = 64
Q_COLS = HQ * HD
K_COLS = HK * HD
HEAD = GROUP * HD
HEAD_COLS = HEAD + 2 * HD
HEAD_PACK = 384
SCALE = HD**-0.5
EXTRA = 16
LANES = 128
TILE = 256
CHUNK = 256
SEGMENT = 32
JOINED = 2
AHEAD = 4
QUERIES = 256
DEPTHS = (1, 2, 3, 4, 6, 8)
VMEM = 58 * 1024 * 1024

NORM_EPS = 1e-05
MASK_NEG = -1e30
BF = jnp.bfloat16
F32 = jnp.float32


def dot(a, b):
    return jnp.dot(a, b, preferred_element_type=F32)


def dot_t(a, b):
    return lax.dot_general(a, b, (((1,), (1,)), ((), ())), preferred_element_type=F32)


def t_dot(a, b):
    return lax.dot_general(a, b, (((0,), (0,)), ((), ())), preferred_element_type=F32)


def iota(shape, axis):
    return lax.broadcasted_iota(jnp.int32, shape, axis)


def rms_factor(values):
    return lax.rsqrt(jnp.mean(values * values, axis=-1, keepdims=True) + NORM_EPS)


def rms_input_grad(values, factor, gain_vec, incoming):
    inner = incoming * gain_vec
    cubed = factor * factor * factor
    return factor * inner - values * cubed * jnp.mean(inner * values, axis=-1, keepdims=True)


def to_all(value, axis):
    return lax.all_to_all(value, axis, 0, 0, tiled=True)


def gathered(value, axis):
    return lax.all_gather(value, axis, axis=0, tiled=True)


def exchanged(value, axis, distance):
    count = lax.axis_size(axis)
    return lax.ppermute(value, axis, [(i, i ^ distance) for i in range(count)])


def near_blocks(own):
    blocks = {0: own}
    distance = lax.axis_size("fsdp") // 2
    while distance:
        blocks.update({r ^ distance: exchanged(b, "fsdp", distance) for r, b in blocks.items()})
        distance //= 2
    return [blocks[r] for r in range(len(blocks))]


def near_terms(blocks):
    shards = lax.axis_size("fsdp")
    terms = {r: [block] for r, block in enumerate(blocks)}
    distance = 1

    def total(parts):
        if len(parts) == 1:
            return parts[0]
        return sum((part.astype(F32) for part in parts[1:]), parts[0].astype(F32)).astype(BF)

    while distance < shards:
        terms = {
            r: terms[r] + [exchanged(total(terms[r ^ distance]), "fsdp", distance)]
            for r in range(0, shards, 2 * distance)
        }
        distance *= 2
    return terms[0]


def line_blocks(own):
    return [own] + [exchanged(own, "ctx", d) for d in range(2, lax.axis_size("ctx"), 2)]


def near_direct(own):
    return [own] + [exchanged(own, "fsdp", r) for r in range(1, lax.axis_size("fsdp"))]


def all_blocks(own):
    spans, shards = lax.axis_size("ctx"), lax.axis_size("fsdp")
    pairs, sides, near = range(spans // 2), range(2), range(shards)
    everyone = ("ctx", "fsdp")
    lines = [[(2 * p + side) * shards + f for p in pairs] for side in sides for f in near]
    planes = [[(2 * p + side) * shards + f for side in sides for f in near] for p in pairs]
    line = lax.all_gather(own, everyone, axis=0, axis_index_groups=lines)
    return lax.all_gather(line, everyone, axis=0, tiled=True, axis_index_groups=planes)


def after(values, *others):
    return lax.optimization_barrier((values, others))[0]


def time_of(microseconds):
    return pl.CostEstimate(flops=0, bytes_accessed=microseconds * 3_600_000, transcendentals=0)


def whole(array):
    shape = array.shape
    return pl.BlockSpec(shape, lambda *_: (0,) * len(shape))


def anywhere():
    return pl.BlockSpec(memory_space=pl.ANY)


def packed_out(packed):
    return pl.BlockSpec((packed.shape[0], Q_COLS), lambda *_: (0, 0))


def packed_head(packed):
    return pl.BlockSpec((packed.shape[0], HEAD_PACK), lambda *_: (0, Q_COLS // HEAD_PACK))


def place_pieces(here, pieces, target, sems):
    copies = []
    for i, piece in enumerate(pieces):
        odd, last = divmod(i, 2)
        rows = piece.shape[1]
        for j in range(piece.shape[0]):
            copies.append(
                pltpu.make_async_copy(
                    piece.at[j],
                    target.at[here ^ (2 * j + odd), pl.ds(last * rows, rows)],
                    sems.at[i, j],
                )
            )
    for copy in copies:
        copy.start()
    return copies


def doc_of(starts, positions):
    found = jnp.zeros(positions.shape, jnp.int32)
    for i in range(starts.shape[0]):
        found = found + (positions >= starts[i]).astype(jnp.int32)
    return found


def visible(starts, here, copies, tokens, first, rows, keys):
    query = first + iota((rows, 1), 0)
    key = iota((1, keys), 1)
    allowed = (key <= query) & (doc_of(starts, key) == doc_of(starts, query))
    if copies > 1:
        allowed = allowed & (lax.rem(query // tokens, copies) == lax.rem(here, copies))
    return allowed


def stream_kernel(
    copies,
    place,
    starts,
    *refs,
):
    pieces, (weight, side) = refs[:4], refs[4:6]
    normed, mixed, attended_low, attended, log_norm, rows, piece_sems = refs[6:]
    here = place[0]
    spans, tokens, width = rows.shape
    length = spans * tokens
    copying = place_pieces(here, pieces, rows, piece_sems)
    for copy in copying:
        copy.wait()
    head_weight = weight[:, :HEAD_COLS]
    gain = side[EXPERTS : EXPERTS + 1, :].astype(F32)

    @pl.loop(0, spans)
    def _(span):
        x = rows[span].astype(F32)
        low = (x * rms_factor(x) * gain).astype(BF)
        at = pl.ds(pl.multiple_of(span * tokens, tokens), tokens)
        normed[at, :] = low
        mixed[at, :] = dot(low, head_weight).astype(BF)

    for first in range(0, length, QUERIES):
        keys = first + QUERIES
        at = slice(first, keys)
        allowed = visible(starts, here, copies, tokens, first, QUERIES, keys)
        for g in range(GROUP):
            columns = slice(g * HD, (g + 1) * HD)
            scores = dot_t(mixed[at, columns], mixed[:keys, HEAD : HEAD + HD]) * SCALE
            scores = jnp.where(allowed, scores, MASK_NEG)
            highest = jnp.max(scores, axis=1, keepdims=True)
            parts = jnp.where(allowed, jnp.exp(scores - highest), 0.0)
            total = jnp.sum(parts, axis=1, keepdims=True)
            total = jnp.where(total == 0.0, 1.0, total)
            log_norm[at, g : g + 1] = highest + jnp.log(total)
            result = dot((parts / total).astype(BF), mixed[:keys, HEAD + HD :])
            attended[at, columns] = result
            attended_low[at, columns] = result.astype(BF)


def stream_attention(place, starts, pieces, packed, side, copies):
    spans, tokens = 2 * pieces[0].shape[0], 2 * pieces[0].shape[1]
    width = pieces[0].shape[2]
    length = spans * tokens
    return pl.pallas_call(
        functools.partial(stream_kernel, copies),
        grid_spec=pltpu.PrefetchScalarGridSpec(
            num_scalar_prefetch=2,
            grid=(1,),
            in_specs=[anywhere()] * 4 + [packed_head(packed), whole(side)],
            out_specs=[
                pl.BlockSpec((length, columns), lambda *_: (0, 0))
                for columns in (width, HEAD_COLS, HEAD, HEAD, LANES)
            ],
            scratch_shapes=[
                pltpu.VMEM((spans, tokens, width), BF),
                pltpu.SemaphoreType.DMA((4, spans // 2)),
            ],
        ),
        out_shape=[
            jax.ShapeDtypeStruct((length, columns), kind)
            for columns, kind in (
                (width, BF),
                (HEAD_COLS, BF),
                (HEAD, BF),
                (HEAD, F32),
                (LANES, F32),
            )
        ],
        compiler_params=pltpu.CompilerParams(vmem_limit_bytes=VMEM),
        cost_estimate=time_of(16),
        name="stream_attention",
    )(place, starts, *pieces, packed, side)


def home_kernel(copies, own, tokens, side, weight, middle, second):
    total = tokens[...].astype(F32)
    for head in range(HK):
        part = own[head * copies]
        for i in range(1, copies):
            part = part + own[head * copies + i]
        total = total + dot(part, weight[head * HEAD : (head + 1) * HEAD, :])
    middle[...] = total
    gain = side[EXPERTS + 1 : EXPERTS + 2, :].astype(F32)
    second[...] = (total * rms_factor(total) * gain).astype(BF)


def home_forward(own, tokens, side, weight, copies):
    args = (own, tokens, side, weight)
    return pl.pallas_call(
        functools.partial(home_kernel, copies),
        grid=(1,),
        in_specs=[whole(a) for a in args[:-1]] + [packed_out(weight)],
        out_specs=[whole(tokens)] * 2,
        out_shape=[
            jax.ShapeDtypeStruct(tokens.shape, F32),
            jax.ShapeDtypeStruct(tokens.shape, BF),
        ],
        compiler_params=pltpu.CompilerParams(vmem_limit_bytes=VMEM),
        cost_estimate=time_of(5),
        name="home_forward",
    )(*args)


def turn_kernel(copies, term_count, *refs):
    terms, refs = refs[:term_count], refs[term_count:]
    middle_ref, second_ref, grad, routes, side, weight, d_middle_out, sent, small = refs
    width = middle_ref.shape[1]
    back = terms[0][...].astype(F32)
    for term in terms[1:]:
        back = back + term[...].astype(F32)
    middle, second = middle_ref[...], second_ref[...]
    d_gates = back[:, width : width + EXTRA]
    ids = iota(d_gates.shape, 1)
    d_gates = d_gates + back[:, width + EXPERTS : width + EXPERTS + EXTRA]
    picked = (ids == routes[:, 0:1]) | (ids == routes[:, 1:2])
    logits = jnp.where(picked, dot_t(second, side[...]), MASK_NEG)
    gates = jnp.where(picked, jnp.exp(logits - jnp.max(logits, axis=1, keepdims=True)), 0.0)
    gates = gates / jnp.sum(gates, axis=1, keepdims=True)
    d_gates = jnp.where(picked, d_gates, 0.0)
    d_picked = gates * (d_gates - jnp.sum(gates * d_gates, axis=1, keepdims=True))
    d_logits = d_picked.astype(BF)
    d_second = dot(d_logits, side[...]) + back[:, :width]
    factor = rms_factor(middle)
    small[...] = t_dot(d_logits, second)
    small[EXPERTS : EXPERTS + 1, :] = jnp.sum(d_second * middle * factor, axis=0, keepdims=True)
    gain = side[EXPERTS + 1 : EXPERTS + 2, :].astype(F32)
    d_middle = grad[...].astype(F32) + rms_input_grad(middle, factor, gain, d_second)
    d_middle_out[...] = d_middle
    d_proj = d_middle.astype(BF)
    for head in range(HK):
        d_head = dot_t(d_proj, weight[head * HEAD : (head + 1) * HEAD, :]).astype(BF)
        for i in range(copies):
            sent[head * copies + i, :, :HEAD] = d_head
    chunk = sent.shape[2] - HEAD
    for span in range(sent.shape[0]):
        sent[span, :, HEAD:] = d_proj[:, span * chunk : (span + 1) * chunk]


def home_turn(terms, middle, second, grad, routes, side, weight, spans):
    args = (*terms, middle, second, grad, routes, side, weight)
    tokens, width = middle.shape
    shapes = [
        jax.ShapeDtypeStruct((tokens, width), F32),
        jax.ShapeDtypeStruct((spans, tokens, HEAD + width // spans), BF),
        jax.ShapeDtypeStruct((EXTRA, width), F32),
    ]
    return pl.pallas_call(
        functools.partial(turn_kernel, spans // HK, len(terms)),
        grid=(1,),
        in_specs=[whole(a) for a in args[:-1]] + [packed_out(weight)],
        out_specs=[whole(shape) for shape in shapes],
        out_shape=shapes,
        compiler_params=pltpu.CompilerParams(vmem_limit_bytes=VMEM),
        cost_estimate=time_of(7),
        name="home_turn",
    )(*args)


def stream_grad_kernel(
    copies, place, starts, pieces0, pieces1, pieces2, pieces3, sent, mixed, attended, log_norm,
    normed, small, d_mixed, out, everyones, d_kv, sems
):
    here, shard = place[0], place[1]
    length, width = normed.shape
    spans = everyones.shape[0]
    tokens = length // spans
    shards = out.shape[0]
    shard_rows = width // shards
    heads = HK // shards
    copying = place_pieces(here, (pieces0, pieces1, pieces2, pieces3), everyones, sems)
    d_kv[...] = jnp.zeros_like(d_kv)
    for first in range(0, length, QUERIES):
        keys = first + QUERIES
        at = slice(first, keys)
        allowed = visible(starts, here, copies, tokens, first, QUERIES, keys)
        k, v = mixed[:keys, HEAD : HEAD + HD], mixed[:keys, HEAD + HD :]
        for g in range(GROUP):
            columns = slice(g * HD, (g + 1) * HD)
            q, grad = mixed[at, columns], sent[at, columns]
            delta = jnp.sum(grad.astype(F32) * attended[at, columns], axis=1, keepdims=True)
            scores = dot_t(q, k) * SCALE
            probs = jnp.where(allowed, jnp.exp(scores - log_norm[at, g : g + 1]), 0.0)
            d_scores = (probs * (dot_t(grad, v) - delta)).astype(BF)
            d_mixed[at, columns] = (dot(d_scores, k) * SCALE).astype(BF)
            d_kv[0, :keys, :] += t_dot(d_scores, q)
            d_kv[1, :keys, :] += t_dot(probs.astype(BF), grad)
    d_mixed[:, HEAD : HEAD + HD] = (d_kv[0] * SCALE).astype(BF)
    d_mixed[:, HEAD + HD :] = d_kv[1].astype(BF)
    for copy in copying:
        copy.wait()
    d_proj = sent[:, HEAD:]
    low = small[...].astype(BF)
    for f in range(shards):
        spot = shard ^ f
        columns = slice(f * shard_rows, (f + 1) * shard_rows)
        out[spot, :shard_rows, :HEAD_COLS] = t_dot(normed[:, columns], d_mixed[...]).astype(BF)
        for h in range(heads):
            first = (f * heads + h) * copies
            part = everyones[first]
            for i in range(1, copies):
                part = part + everyones[first + i]
            out[spot, h * HEAD : (h + 1) * HEAD, HEAD_COLS:] = t_dot(part, d_proj).astype(BF)
        out[spot, shard_rows:, :] = jnp.zeros((EXTRA, out.shape[2]), BF)
        out[spot, shard_rows:, :shard_rows] = low[:, columns]


def stream_backward(place, starts, pieces, sent, mixed, attended, log_norm, normed, small, shards):
    args = (sent, mixed, attended, log_norm, normed, small)
    length, width = normed.shape
    spans = 2 * pieces[0].shape[0]
    shapes = [
        jax.ShapeDtypeStruct(mixed.shape, BF),
        jax.ShapeDtypeStruct(
            (shards, width // shards + EXTRA, HEAD_COLS + width // spans), BF
        ),
    ]
    return pl.pallas_call(
        functools.partial(stream_grad_kernel, spans // HK),
        grid_spec=pltpu.PrefetchScalarGridSpec(
            num_scalar_prefetch=2,
            grid=(1,),
            in_specs=[anywhere()] * 4 + [whole(a) for a in args],
            out_specs=[whole(shape) for shape in shapes],
            scratch_shapes=[
                pltpu.VMEM((spans, length, HEAD), BF),
                pltpu.VMEM((2, length, HD), F32),
                pltpu.SemaphoreType.DMA((4, spans // 2)),
            ],
        ),
        out_shape=shapes,
        compiler_params=pltpu.CompilerParams(vmem_limit_bytes=VMEM),
        cost_estimate=time_of(17),
        name="stream_backward",
    )(place, starts, *pieces, *args)


def home_grad_kernel(copies, place, d_home, tokens, side, d_middle, *refs):
    weight_refs, (d_tokens, weight, mixed, d_normed, sems) = refs[:-5], refs[-5:]
    shards = len(weight_refs)
    loading = [
        pltpu.make_async_copy(ref, weight.at[place[1] ^ r], sems.at[r])
        for r, ref in enumerate(weight_refs)
    ]
    for copy in loading:
        copy.start()
    for head in range(HK):
        part = d_home[head * copies]
        if copies > 1:
            part = part.astype(F32)
            for i in range(1, copies):
                part = part + d_home[head * copies + i].astype(F32)
            part = part.astype(BF)
        mixed[:, head * HEAD : (head + 1) * HEAD] = part[:, :HEAD]
        key = Q_COLS + head * HD
        mixed[:, key : key + HD] = part[:, HEAD : HEAD + HD]
        value = key + K_COLS
        mixed[:, value : value + HD] = part[:, HEAD + HD :]
    for copy in loading:
        copy.wait()
    rows = weight.shape[1]
    for f in range(shards):
        d_normed[:, f * rows : (f + 1) * rows] = dot_t(mixed[...], weight[f])
    x = tokens[...].astype(F32)
    gain = side[EXPERTS : EXPERTS + 1, :].astype(F32)
    d_x = rms_input_grad(x, rms_factor(x), gain, d_normed[...])
    d_tokens[...] = (d_middle[...] + d_x).astype(BF)


def home_backward(place, d_home, tokens, side, d_middle, weights, copies):
    args = (d_home, tokens, side, d_middle)
    count, width = tokens.shape
    shards = len(weights)
    columns = Q_COLS + 2 * K_COLS
    return pl.pallas_call(
        functools.partial(home_grad_kernel, copies),
        grid_spec=pltpu.PrefetchScalarGridSpec(
            num_scalar_prefetch=1,
            grid=(1,),
            in_specs=[whole(a) for a in args] + [anywhere()] * shards,
            out_specs=whole(tokens),
            scratch_shapes=[
                pltpu.VMEM((shards, width // shards, columns), BF),
                pltpu.VMEM((count, columns), BF),
                pltpu.VMEM((count, width), F32),
                pltpu.SemaphoreType.DMA((shards,)),
            ],
        ),
        out_shape=jax.ShapeDtypeStruct(tokens.shape, BF),
        compiler_params=pltpu.CompilerParams(vmem_limit_bytes=VMEM),
        cost_estimate=time_of(8),
        name="home_backward",
    )(place, *args, *weights)


def collect_kernel(copies, late, own_weight, d_qkv, d_out, small, d_gain):
    rows = own_weight.shape[0]
    chunk = late.shape[2] - HEAD_COLS
    for head in range(HK):
        part = late[head * copies, :rows, :HEAD_COLS].astype(F32)
        for i in range(1, copies):
            part = part + late[head * copies + i, :rows, :HEAD_COLS].astype(F32)
        d_qkv[:, head * HEAD : (head + 1) * HEAD] = part[:, :HEAD]
        key = Q_COLS + head * HD
        d_qkv[:, key : key + HD] = part[:, HEAD : HEAD + HD]
        value = key + K_COLS
        d_qkv[:, value : value + HD] = part[:, HEAD + HD :]
    total = jnp.zeros((EXTRA, rows), F32)
    for span in range(late.shape[0]):
        d_out[:, span * chunk : (span + 1) * chunk] = late[span, :rows, HEAD_COLS:].astype(F32)
        total = total + late[span, rows:, :rows].astype(F32)
    small[...] = total
    d_gain[...] = jnp.sum(d_qkv[...] * own_weight[...].astype(F32), axis=1, keepdims=True)


def collected(late, own_weight, width, copies):
    rows, columns = own_weight.shape
    shapes = [
        jax.ShapeDtypeStruct((rows, columns), F32),
        jax.ShapeDtypeStruct((rows, width), F32),
        jax.ShapeDtypeStruct((EXTRA, rows), F32),
        jax.ShapeDtypeStruct((rows, 1), F32),
    ]
    return pl.pallas_call(
        functools.partial(collect_kernel, copies),
        grid=(1,),
        in_specs=[whole(late), whole(own_weight)],
        out_specs=[whole(shape) for shape in shapes],
        out_shape=shapes,
        compiler_params=pltpu.CompilerParams(vmem_limit_bytes=VMEM),
        cost_estimate=time_of(7),
        name="collected",
    )(late, own_weight)


def picked_gates(second, router_t, chosen):
    logits = dot_t(router_t, second)
    ids = iota(logits.shape, 0)
    picked = (ids == chosen[0:1, :]) | (ids == chosen[1:2, :])
    logits = jnp.where(picked, logits, MASK_NEG)
    parts = jnp.where(picked, jnp.exp(logits - jnp.max(logits, axis=0, keepdims=True)), 0.0)
    return picked, parts / jnp.sum(parts, axis=0, keepdims=True)


def swiglu_grads(gate, up, d_hidden):
    sigma = 1.0 / (1.0 + jnp.exp(-gate))
    passed = gate * sigma
    d_gate = d_hidden * up * sigma * (1.0 + gate * (1.0 - sigma))
    return (passed * up).astype(BF), d_gate.astype(BF), (d_hidden * passed).astype(BF)


def near_kernel(shards, place, *refs):
    second, grads = refs[:shards], refs[shards : 2 * shards]
    router_t, w_gate, w_up, w_down = refs[2 * shards : 2 * shards + 4]
    branch_out = refs[2 * shards + 4 : 3 * shards + 4]
    back_out = refs[3 * shards + 4 : 4 * shards + 4]
    hot, rows, cots, d_outs, slot_gate, out_acc, row_acc, branch_acc, back_acc = refs[
        4 * shards + 4 :
    ]
    expert, tile = pl.program_id(0), pl.program_id(1)
    tokens = second[0].shape[0]
    width = second[0].shape[1]
    wanted = place[1] * pl.num_programs(0) + expert

    @pl.when(tile == 0)
    def _():
        before = (iota((tokens, tokens), 0) < iota((tokens, tokens), 1)).astype(BF)
        for f in range(shards):
            chosen = grads[f][tokens : tokens + EXTRA, :tokens].astype(F32).astype(jnp.int32)
            picked, gates = picked_gates(second[f][...], router_t[...], chosen)
            ranks = dot(picked.astype(BF), before)
            found = (iota(ranks.shape, 0) == wanted) & picked
            rank = jnp.sum(jnp.where(found, ranks + 1.0, 0.0), axis=0, keepdims=True)
            gate = jnp.sum(jnp.where(found, gates, 0.0), axis=0, keepdims=True)
            match = iota((CAP, tokens), 0).astype(F32) + 1.0 == rank
            one_hot = match.astype(BF)
            place = pl.ds(f * CAP, CAP)
            hot[f] = one_hot
            found_gate = jnp.sum(jnp.where(match, gate, 0.0), axis=1, keepdims=True)
            slot_gate[place, :] = jnp.broadcast_to(found_gate, (CAP, LANES))
            rows[place, :] = dot(one_hot, second[f][...]).astype(BF)
            cot = dot(one_hot, grads[f][:tokens, :])
            cots[place, :] = cot.astype(BF)
            d_outs[place, :] = (found_gate * cot).astype(BF)
        out_acc[...] = jnp.zeros_like(out_acc)
        row_acc[...] = jnp.zeros_like(row_acc)

    hidden, d_gate, d_up = swiglu_grads(
        dot(rows[...], w_gate[0]), dot(rows[...], w_up[0]), dot(d_outs[...], w_down[0])
    )
    out_acc[...] += dot_t(hidden, w_down[0])
    row_acc[...] += dot_t(d_gate, w_gate[0]) + dot_t(d_up, w_up[0])

    @pl.when(tile == pl.num_programs(1) - 1)
    def _():
        last = expert == pl.num_programs(0) - 1
        for f in range(shards):
            place = pl.ds(f * CAP, CAP)
            out = out_acc[place, :].astype(BF).astype(F32)
            d_gates = jnp.sum(cots[place, :].astype(F32) * out, axis=1, keepdims=True)
            gated = (slot_gate[place, 0:1] * out).astype(BF)
            lane = iota((CAP, LANES), 1)
            coarse = d_gates.astype(BF).astype(F32)
            extra = jnp.where(lane == wanted, coarse, 0.0)
            extra = extra + jnp.where(lane == EXPERTS + wanted, d_gates - coarse, 0.0)

            def add(acc, part, columns):
                @pl.when(expert == 0)
                def _():
                    acc[f, :, columns] = part

                @pl.when(expert > 0)
                def _():
                    acc[f, :, columns] += part

            add(branch_acc, t_dot(hot[f], gated), slice(0, width))
            add(back_acc, t_dot(hot[f], row_acc[place, :].astype(BF)), slice(0, width))
            add(back_acc, t_dot(hot[f], extra.astype(BF)), slice(width, width + LANES))

            @pl.when(last)
            def _():
                branch_out[f][...] = branch_acc[f].astype(BF)
                back_out[f][...] = back_acc[f].astype(BF)


def near_experts(place, second, grads, router_t, w_experts):
    shards = len(second)
    tokens, width = second[0].shape
    experts = w_experts.shape[0]
    slots = shards * CAP
    tiles = FF // TILE
    shapes = [jax.ShapeDtypeStruct((tokens, width), BF)] * shards
    shapes += [jax.ShapeDtypeStruct((tokens, width + LANES), BF)] * shards

    def weight(part):
        return pl.BlockSpec((1, width, TILE), lambda e, j, s: (e, 0, part * tiles + j))

    outs = pl.pallas_call(
        functools.partial(near_kernel, shards),
        grid_spec=pltpu.PrefetchScalarGridSpec(
            num_scalar_prefetch=1,
            grid=(experts, tiles),
            in_specs=[whole(a) for a in (*second, *grads, router_t)]
            + [weight(0), weight(1), weight(2)],
            out_specs=[whole(shape) for shape in shapes],
            scratch_shapes=[
                pltpu.VMEM((shards, CAP, tokens), BF),
                pltpu.VMEM((slots, width), BF),
                pltpu.VMEM((slots, width), BF),
                pltpu.VMEM((slots, width), BF),
                pltpu.VMEM((slots, LANES), F32),
                pltpu.VMEM((slots, width), F32),
                pltpu.VMEM((slots, width), F32),
                pltpu.VMEM((shards, tokens, width), F32),
                pltpu.VMEM((shards, tokens, width + LANES), F32),
            ],
        ),
        out_shape=shapes,
        compiler_params=pltpu.CompilerParams(vmem_limit_bytes=VMEM),
        cost_estimate=time_of(26),
        name="near_experts",
    )(place, *second, *grads, router_t, w_experts, w_experts, w_experts)
    return outs[:shards], outs[shards:]


def far_kernel(
    first_block,
    segment,
    per_line,
    place,
    router_t,
    second_ref,
    grads_ref,
    w_gate,
    w_up,
    w_down,
    out_ref,
    rows,
    d_outs,
    act,
    fetched_rows,
    fetched_grads,
    tile_out,
    counts,
    fetch_sem,
    store_sem,
):
    experts = rows.shape[0]
    expert, tile = pl.program_id(0), pl.program_id(1)
    tiles = pl.num_programs(1)
    step = expert * tiles + tile
    slot = lax.rem(step, 2)
    groups = segment // JOINED
    per_plane = second_ref.shape[0] // per_line
    tokens, width = second_ref.shape[1:]
    size = JOINED * tokens
    window = JOINED * CAP + 16

    def stores(which, e, j):
        return [
            pltpu.make_async_copy(
                tile_out.at[which, i],
                out_ref.at[e, :, pl.ds(pl.multiple_of(i * FF + j * TILE, TILE), TILE)],
                store_sem.at[which, i],
            )
            for i in range(3)
        ]

    def fetches(which, g):
        copies = []
        for i in range(JOINED):
            block = first_block + g * JOINED + i
            across = lax.rem(block, per_plane) * per_line + block // per_plane
            copies += [
                pltpu.make_async_copy(
                    second_ref.at[block], fetched_rows.at[which, i], fetch_sem.at[which, 0, i]
                ),
                pltpu.make_async_copy(
                    grads_ref.at[across], fetched_grads.at[which, i], fetch_sem.at[which, 1, i]
                ),
            ]
        return copies

    @pl.when(step == 0)
    def _():
        ahead = min(AHEAD, groups)
        for g in range(ahead):
            for copy in fetches(g, g):
                copy.start()
        before = (iota((size, size), 0) < iota((size, size), 1)).astype(BF)

        def gather(g, starts):
            which = lax.rem(g, AHEAD)
            for copy in fetches(which, g):
                copy.wait()
            second = fetched_rows[which].reshape(size, width)
            grads = fetched_grads[which, :, :tokens].reshape(size, width)
            chosen = jnp.concatenate(
                [fetched_grads[which, b, tokens : tokens + EXTRA, :LANES] for b in range(JOINED)],
                axis=1,
            )
            chosen = chosen.astype(F32).astype(jnp.int32)
            picked, gates = picked_gates(second, router_t[...], chosen)
            ranks = dot(picked.astype(BF), before)
            ids = iota(ranks.shape, 0)
            bases = [start // 16 * 16 for start in starts]
            matches, found_gates, ends = [], [], []
            for e in range(experts):
                found = (ids == place[1] * experts + e) & picked
                gate = jnp.sum(jnp.where(found, gates, 0.0), axis=0, keepdims=True)
                rank = jnp.sum(jnp.where(found, ranks + 1.0, 0.0), axis=0, keepdims=True)
                shift = (starts[e] - bases[e]).astype(F32)
                spot = jnp.where(rank > 0.0, rank + (shift - 1.0), -1.0)
                match = iota((window, size), 0).astype(F32) == spot
                matches.append(match.astype(BF))
                found_gates.append(
                    jnp.sum(jnp.where(match, gate, 0.0), axis=1, keepdims=True)
                )
                ends.append(starts[e] + jnp.sum((rank > 0.0).astype(jnp.int32)))
            one_hot = jnp.concatenate(matches, axis=0)
            new_rows = dot(one_hot, second).astype(BF)
            new_grads = (jnp.concatenate(found_gates, axis=0) * dot(one_hot, grads)).astype(BF)
            for e in range(experts):
                at = pl.ds(pl.multiple_of(bases[e], 16), 16)
                rest = pl.ds(pl.multiple_of(bases[e] + 16, 16), window - 16)
                held = iota((16, width), 0) < starts[e] - bases[e]
                for ref, new in ((rows, new_rows), (d_outs, new_grads)):
                    new = new[e * window : (e + 1) * window]
                    ref[e, at, :] = jnp.where(held, ref[e, at, :], new[:16])
                    ref[e, rest, :] = new[16:]

            @pl.when(g + AHEAD < groups)
            def _():
                for copy in fetches(which, g + AHEAD):
                    copy.start()

            return tuple(ends)

        ends = lax.fori_loop(0, groups, gather, (jnp.int32(0),) * experts)
        for e in range(experts):
            counts[e] = ends[e]
            spare = pl.ds(pl.multiple_of((ends[e] + 15) // 16 * 16, 16), CHUNK)
            rows[e, spare, :] = jnp.zeros((CHUNK, width), BF)
            d_outs[e, spare, :] = jnp.zeros((CHUNK, width), BF)

    chunks = jnp.maximum((counts[expert] + CHUNK - 1) // CHUNK, 1)

    @pl.loop(0, chunks)
    def _(i):
        at = pl.ds(pl.multiple_of(i * CHUNK, CHUNK), CHUNK)
        row, d_out = rows[expert, at, :], d_outs[expert, at, :]
        hidden, d_gate, d_up = swiglu_grads(
            dot(row, w_gate[0]), dot(row, w_up[0]), dot(d_out, w_down[0])
        )
        act[0, at, :] = d_gate
        act[1, at, :] = d_up
        act[2, at, :] = hidden

    @pl.when(step >= 2)
    def _():
        for copy in stores(slot, (step - 2) // tiles, lax.rem(step - 2, tiles)):
            copy.wait()

    most = act.shape[1] // CHUNK
    depths = [k for k in DEPTHS if k < most] + [most]
    for low, k in zip([0] + depths[:-1], depths):

        @pl.when((chunks > low) & (chunks <= k))
        def _():
            for extra in range(low + 1, k):

                @pl.when(chunks == extra)
                def _():
                    spare = slice(extra * CHUNK, k * CHUNK)
                    empty = jnp.zeros(((k - extra) * CHUNK, width), BF)
                    rows[expert, spare, :] = empty
                    d_outs[expert, spare, :] = empty
                    for i in range(3):
                        act[i, spare, :] = empty[:, :TILE]

            upto = k * CHUNK
            for i, left in enumerate((rows, rows, d_outs)):
                tile_out[slot, i] = t_dot(left[expert, :upto, :], act[i, :upto, :])

    for copy in stores(slot, expert, tile):
        copy.start()

    @pl.when(step == pl.num_programs(0) * tiles - 1)
    def _():
        for copy in stores(1 - slot, (step - 1) // tiles, lax.rem(step - 1, tiles)):
            copy.wait()
        for copy in stores(slot, expert, tile):
            copy.wait()


def far_weight_grads(first, segment, per_line, place, router_t, second, grads, w_experts):
    experts, width = w_experts.shape[:2]
    tokens = second.shape[1]
    tiles = FF // TILE
    most = segment * CAP
    held = most + CHUNK + 16

    def weight(part):
        return pl.BlockSpec((1, width, TILE), lambda e, j, s: (e, 0, part * tiles + j))

    return pl.pallas_call(
        functools.partial(far_kernel, first, segment, per_line),
        grid_spec=pltpu.PrefetchScalarGridSpec(
            num_scalar_prefetch=1,
            grid=(experts, tiles),
            in_specs=[
                whole(router_t),
                anywhere(),
                anywhere(),
                weight(0),
                weight(1),
                weight(2),
            ],
            out_specs=anywhere(),
            scratch_shapes=[
                pltpu.VMEM((experts, held, width), BF),
                pltpu.VMEM((experts, held, width), BF),
                pltpu.VMEM((3, most, TILE), BF),
                pltpu.VMEM((AHEAD, JOINED, tokens, width), BF),
                pltpu.VMEM((AHEAD, JOINED, tokens + EXTRA, width), BF),
                pltpu.VMEM((2, 3, width, TILE), F32),
                pltpu.SMEM((experts,), jnp.int32),
                pltpu.SemaphoreType.DMA((AHEAD, 2, JOINED)),
                pltpu.SemaphoreType.DMA((2, 3)),
            ],
        ),
        out_shape=jax.ShapeDtypeStruct((experts, width, 3 * FF), F32),
        compiler_params=pltpu.CompilerParams(vmem_limit_bytes=VMEM),
        cost_estimate=time_of(80),
        name="far_weight_grads",
    )(place, router_t, second, grads, w_experts, w_experts, w_experts)


def per_device(
    tokens,
    query_key_value_weight,
    output_weight,
    routing_weight,
    gain_attn,
    gain_moe,
    w_experts,
    doc_starts,
    routes,
    cotangent,
):
    spans = lax.axis_size("ctx")
    shards = lax.axis_size("fsdp")
    here = lax.axis_index("ctx")
    shard = lax.axis_index("fsdp")
    place = jnp.stack([here, shard]).astype(jnp.int32)
    x, grad = tokens[0], cotangent[0]
    tok_count, width = x.shape
    shard_rows = query_key_value_weight.shape[0]
    copies = spans // HK
    head = here // copies
    length = spans * tok_count
    blocks = spans * shards

    packed = jnp.concatenate(
        [
            output_weight,
            lax.dynamic_slice_in_dim(query_key_value_weight, head * HEAD, HEAD, 1),
            lax.dynamic_slice_in_dim(query_key_value_weight, Q_COLS + head * HD, HD, 1),
            lax.dynamic_slice_in_dim(query_key_value_weight, Q_COLS + K_COLS + head * HD, HD, 1),
            routing_weight,
            gain_attn[:, None],
            gain_moe[:, None],
            jnp.zeros((shard_rows, HEAD_PACK - HEAD_COLS - EXPERTS - 2), BF),
        ],
        axis=1,
    )
    packed = gathered(packed, "fsdp")
    side = packed[:, Q_COLS + HEAD_COLS : Q_COLS + HEAD_COLS + EXTRA].T

    half = tok_count // 2
    first = jnp.stack(line_blocks(x[:half]))
    last = jnp.stack(line_blocks(after(x[half:], first)))
    pieces = [first, last, exchanged(first, "ctx", 1), exchanged(last, "ctx", 1)]
    payload = jnp.concatenate(
        [grad, jnp.pad(routes[0].T.astype(BF), ((0, EXTRA - 2), (0, width - tok_count)))]
    )
    grads_near = near_blocks(payload)
    grads_all = all_blocks(after(payload, packed))
    pieces = after(pieces, grads_near)

    normed, mixed, attended_low, attended, log_norm = stream_attention(
        place, doc_starts[0], pieces, packed, side, copies
    )

    own = to_all(attended_low, "ctx").reshape(spans, tok_count, HEAD)
    middle, second = home_forward(own, x, side, packed, copies)
    second_near = near_blocks(second)
    second_all = lax.all_gather(second, ("ctx", "fsdp"), axis=0)

    branch, back = near_experts(place, second_near, grads_near, side, w_experts)
    half = length // 2
    attended_low = after(attended_low, own)
    lines = [line_blocks(part) for part in (attended_low[:half], attended_low[half:])]
    back, lines = after((back, lines), grads_all)
    attended_pieces = [jnp.stack(line) for line in lines]
    attended_pieces += [exchanged(piece, "ctx", 1) for piece in attended_pieces]
    terms = near_terms(back)
    branch_terms = near_terms(branch)
    output = sum((term.astype(F32) for term in branch_terms), middle).astype(BF)

    d_middle, sent, small = home_turn(
        terms, middle, second, grad, routes[0], side, packed, spans
    )

    sent = after(to_all(sent.reshape(length, -1), "ctx"), output)
    d_mixed, grads_out = stream_backward(
        place, doc_starts[0], attended_pieces, sent, mixed, attended, log_norm, normed, small, shards
    )
    late = near_terms([grads_out[r] for r in range(shards)])
    late = sum((term.astype(F32) for term in late[1:]), late[0].astype(F32)).astype(BF)
    late = lax.all_gather(after(late, second_all), "ctx", axis=0)

    d_home = to_all(d_mixed, "ctx").reshape(spans, tok_count, HEAD_COLS)

    segment = min(blocks, SEGMENT)
    parts = [
        far_weight_grads(
            i, segment, spans // 2, place, side, second_all, grads_all, w_experts
        )
        for i in range(0, blocks, segment)
    ]
    d_w_experts = sum(parts[1:], parts[0])

    d_home = after(d_home, d_w_experts)
    d_tokens = home_backward(
        place, d_home, x, side, d_middle, near_direct(query_key_value_weight), copies
    )
    d_qkv_w, d_out_w, small, d_gain_attn = collected(
        late, query_key_value_weight, width, copies
    )
    return (
        output[None],
        d_tokens[None],
        d_qkv_w,
        d_out_w,
        small[:EXPERTS].T,
        d_gain_attn[:, 0] / gain_attn.astype(F32),
        small[EXPERTS],
        d_w_experts,
    )


def solution(mesh):
    placed = (
        P("fsdp", "ctx", None),
        P("fsdp", None),
        P("fsdp", None),
        P("fsdp", None),
        P("fsdp"),
        P("fsdp"),
        P("fsdp", None, None),
        P("fsdp", None),
        P("fsdp", "ctx", None),
        P("fsdp", "ctx", None),
    )
    return jax.shard_map(
        per_device,
        mesh=mesh,
        in_specs=placed,
        out_specs=(
            P("fsdp", "ctx", None),
            P("fsdp", "ctx", None),
            P("fsdp", None),
            P("fsdp", None),
            P("fsdp", None),
            P("fsdp"),
            P("fsdp"),
            P("fsdp", None, None),
        ),
        check_vma=False,
    )
```

```python
import functools

import jax
import jax.numpy as jnp
from jax import lax
from jax.experimental import pallas as pl
from jax.experimental.pallas import tpu as pltpu
from jax.sharding import PartitionSpec as P

HQ = 24
HK = 8
HD = 64
GROUP = HQ // HK
FF = 1024
EXPERTS = 8
CAP = 64
Q_COLS = HQ * HD
K_COLS = HK * HD
HEAD = GROUP * HD
HEAD_COLS = HEAD + 2 * HD
HEAD_PACK = 384
SCALE = HD**-0.5
EXTRA = 16
LANES = 128
TILE = 256
CHUNK = 256
SEGMENT = 32
JOINED = 2
AHEAD = 4
QUERIES = 256
DEPTHS = (1, 2, 3, 4, 6, 8)
VMEM = 58 * 1024 * 1024

NORM_EPS = 1e-05
MASK_NEG = -1e30
BF = jnp.bfloat16
F32 = jnp.float32


def dot(a, b):
    return jnp.dot(a, b, preferred_element_type=F32)


def dot_t(a, b):
    return lax.dot_general(a, b, (((1,), (1,)), ((), ())), preferred_element_type=F32)


def t_dot(a, b):
    return lax.dot_general(a, b, (((0,), (0,)), ((), ())), preferred_element_type=F32)


def iota(shape, axis):
    return lax.broadcasted_iota(jnp.int32, shape, axis)


def rms_factor(values):
    return lax.rsqrt(jnp.mean(values * values, axis=-1, keepdims=True) + NORM_EPS)


def rms_input_grad(values, factor, gain_vec, incoming):
    inner = incoming * gain_vec
    cubed = factor * factor * factor
    return factor * inner - values * cubed * jnp.mean(inner * values, axis=-1, keepdims=True)


def to_all(value, axis):
    return lax.all_to_all(value, axis, 0, 0, tiled=True)


def gathered(value, axis):
    return lax.all_gather(value, axis, axis=0, tiled=True)


def exchanged(value, axis, distance):
    count = lax.axis_size(axis)
    return lax.ppermute(value, axis, [(i, i ^ distance) for i in range(count)])


def near_blocks(own):
    blocks = {0: own}
    distance = lax.axis_size("fsdp") // 2
    while distance:
        blocks.update({r ^ distance: exchanged(b, "fsdp", distance) for r, b in blocks.items()})
        distance //= 2
    return [blocks[r] for r in range(len(blocks))]


def near_terms(blocks):
    shards = lax.axis_size("fsdp")
    terms = {r: [block] for r, block in enumerate(blocks)}
    distance = 1

    def total(parts):
        if len(parts) == 1:
            return parts[0]
        return sum((part.astype(F32) for part in parts[1:]), parts[0].astype(F32)).astype(BF)

    while distance < shards:
        terms = {
            r: terms[r] + [exchanged(total(terms[r ^ distance]), "fsdp", distance)]
            for r in range(0, shards, 2 * distance)
        }
        distance *= 2
    return terms[0]


def line_blocks(own):
    return [own] + [exchanged(own, "ctx", d) for d in range(2, lax.axis_size("ctx"), 2)]


def near_direct(own):
    return [own] + [exchanged(own, "fsdp", r) for r in range(1, lax.axis_size("fsdp"))]


def planes_of(line):
    spans, shards = lax.axis_size("ctx"), lax.axis_size("fsdp")
    planes = [
        [(2 * pair + side) * shards + f for side in range(2) for f in range(shards)]
        for pair in range(spans // 2)
    ]
    return lax.all_gather(line, ("ctx", "fsdp"), axis=0, tiled=True, axis_index_groups=planes)


def all_blocks(own):
    spans, shards = lax.axis_size("ctx"), lax.axis_size("fsdp")
    lines = [
        [(2 * pair + side) * shards + f for pair in range(spans // 2)]
        for side in range(2)
        for f in range(shards)
    ]
    line = lax.all_gather(own, ("ctx", "fsdp"), axis=0, axis_index_groups=lines)
    return planes_of(line)


def after(values, *others):
    return lax.optimization_barrier((values, others))[0]


def time_of(microseconds):
    return pl.CostEstimate(flops=0, bytes_accessed=microseconds * 3_600_000, transcendentals=0)


def whole(array):
    shape = array.shape
    return pl.BlockSpec(shape, lambda *_: (0,) * len(shape))


def anywhere():
    return pl.BlockSpec(memory_space=pl.ANY)


def place_pieces(here, pieces, target, sems):
    copies = []
    for i, piece in enumerate(pieces):
        odd, last = divmod(i, 2)
        rows = piece.shape[1]
        for j in range(piece.shape[0]):
            copies.append(
                pltpu.make_async_copy(
                    piece.at[j],
                    target.at[here ^ (2 * j + odd), pl.ds(last * rows, rows)],
                    sems.at[i, j],
                )
            )
    for copy in copies:
        copy.start()
    return copies


def doc_of(starts, positions):
    found = jnp.zeros(positions.shape, jnp.int32)
    for i in range(starts.shape[0]):
        found = found + (positions >= starts[i]).astype(jnp.int32)
    return found


def visible(starts, here, copies, tokens, first, rows, keys):
    query = first + iota((rows, 1), 0)
    key = iota((1, keys), 1)
    allowed = (key <= query) & (doc_of(starts, key) == doc_of(starts, query))
    if copies > 1:
        allowed = allowed & (lax.rem(query // tokens, copies) == lax.rem(here, copies))
    return allowed


def stream_kernel(
    copies,
    place,
    starts,
    *refs,
):
    pieces, (weight, side) = refs[:4], refs[4:6]
    normed, mixed, attended_low, attended, log_norm, rows, piece_sems = refs[6:]
    here = place[0]
    spans, tokens, width = rows.shape
    length = spans * tokens
    copying = place_pieces(here, pieces, rows, piece_sems)
    for copy in copying:
        copy.wait()
    head_weight = weight[:, :HEAD_COLS]
    gain = side[EXPERTS : EXPERTS + 1, :].astype(F32)

    @pl.loop(0, spans)
    def _(span):
        x = rows[span].astype(F32)
        low = (x * rms_factor(x) * gain).astype(BF)
        at = pl.ds(pl.multiple_of(span * tokens, tokens), tokens)
        normed[at, :] = low
        mixed[at, :] = dot(low, head_weight).astype(BF)

    for first in range(0, length, QUERIES):
        keys = first + QUERIES
        at = slice(first, keys)
        allowed = visible(starts, here, copies, tokens, first, QUERIES, keys)
        for g in range(GROUP):
            columns = slice(g * HD, (g + 1) * HD)
            scores = dot_t(mixed[at, columns], mixed[:keys, HEAD : HEAD + HD]) * SCALE
            scores = jnp.where(allowed, scores, MASK_NEG)
            highest = jnp.max(scores, axis=1, keepdims=True)
            parts = jnp.where(allowed, jnp.exp(scores - highest), 0.0)
            total = jnp.sum(parts, axis=1, keepdims=True)
            total = jnp.where(total == 0.0, 1.0, total)
            log_norm[at, g : g + 1] = highest + jnp.log(total)
            result = dot((parts / total).astype(BF), mixed[:keys, HEAD + HD :])
            attended[at, columns] = result
            attended_low[at, columns] = result.astype(BF)


def stream_attention(place, starts, pieces, packed, side, copies):
    spans, tokens = 2 * pieces[0].shape[0], 2 * pieces[0].shape[1]
    width = pieces[0].shape[2]
    length = spans * tokens
    return pl.pallas_call(
        functools.partial(stream_kernel, copies),
        grid_spec=pltpu.PrefetchScalarGridSpec(
            num_scalar_prefetch=2,
            grid=(1,),
            in_specs=[anywhere()] * 4 + [whole(packed), whole(side)],
            out_specs=[
                pl.BlockSpec((length, columns), lambda *_: (0, 0))
                for columns in (width, HEAD_COLS, HEAD, HEAD, LANES)
            ],
            scratch_shapes=[
                pltpu.VMEM((spans, tokens, width), BF),
                pltpu.SemaphoreType.DMA((4, spans // 2)),
            ],
        ),
        out_shape=[
            jax.ShapeDtypeStruct((length, columns), kind)
            for columns, kind in (
                (width, BF),
                (HEAD_COLS, BF),
                (HEAD, BF),
                (HEAD, F32),
                (LANES, F32),
            )
        ],
        compiler_params=pltpu.CompilerParams(vmem_limit_bytes=VMEM),
        cost_estimate=time_of(16),
        name="stream_attention",
    )(place, starts, *pieces, packed, side)


def home_kernel(copies, place, own, tokens, side, *refs):
    weights, (middle, second, columns) = refs[:-3], refs[-3:]
    heads = HK // len(weights)
    total = tokens[...].astype(F32)
    for r, weight in enumerate(weights):
        first = (place[1] ^ r) * heads
        for h in range(heads):
            part = own[(first + h) * copies]
            for i in range(1, copies):
                part = part + own[(first + h) * copies + i]
            columns[r, :, h * HEAD : (h + 1) * HEAD] = part
            total = total + dot(part, weight[h * HEAD : (h + 1) * HEAD, :])
    middle[...] = total
    gain = side[EXPERTS + 1 : EXPERTS + 2, :].astype(F32)
    second[...] = (total * rms_factor(total) * gain).astype(BF)


def home_forward(place, own, tokens, side, weights, copies):
    args = (own, tokens, side, *weights)
    count, width = tokens.shape
    shapes = [
        jax.ShapeDtypeStruct(tokens.shape, F32),
        jax.ShapeDtypeStruct(tokens.shape, BF),
        jax.ShapeDtypeStruct((len(weights), count, width // len(weights)), BF),
    ]
    return pl.pallas_call(
        functools.partial(home_kernel, copies),
        grid_spec=pltpu.PrefetchScalarGridSpec(
            num_scalar_prefetch=1,
            grid=(1,),
            in_specs=[whole(a) for a in args],
            out_specs=[whole(shape) for shape in shapes],
        ),
        out_shape=shapes,
        compiler_params=pltpu.CompilerParams(vmem_limit_bytes=VMEM),
        cost_estimate=time_of(5),
        name="home_forward",
    )(place, *args)


def turn_kernel(copies, term_count, place, *refs):
    terms, refs = refs[:term_count], refs[term_count:]
    middle_ref, second_ref, grad, routes, side, *weights = refs[:-4]
    d_middle_out, d_proj_out, sent, small = refs[-4:]
    heads = HK // len(weights)
    width = middle_ref.shape[1]
    back = terms[0][...].astype(F32)
    for term in terms[1:]:
        back = back + term[...].astype(F32)
    middle, second = middle_ref[...], second_ref[...]
    d_gates = back[:, width : width + EXTRA]
    ids = iota(d_gates.shape, 1)
    d_gates = d_gates + back[:, width + EXPERTS : width + EXPERTS + EXTRA]
    picked = (ids == routes[:, 0:1]) | (ids == routes[:, 1:2])
    logits = jnp.where(picked, dot_t(second, side[...]), MASK_NEG)
    gates = jnp.where(picked, jnp.exp(logits - jnp.max(logits, axis=1, keepdims=True)), 0.0)
    gates = gates / jnp.sum(gates, axis=1, keepdims=True)
    d_gates = jnp.where(picked, d_gates, 0.0)
    d_picked = gates * (d_gates - jnp.sum(gates * d_gates, axis=1, keepdims=True))
    d_logits = d_picked.astype(BF)
    d_second = dot(d_logits, side[...]) + back[:, :width]
    factor = rms_factor(middle)
    small[...] = t_dot(d_logits, second)
    small[EXPERTS : EXPERTS + 1, :] = jnp.sum(d_second * middle * factor, axis=0, keepdims=True)
    gain = side[EXPERTS + 1 : EXPERTS + 2, :].astype(F32)
    d_middle = grad[...].astype(F32) + rms_input_grad(middle, factor, gain, d_second)
    d_middle_out[...] = d_middle
    d_proj = d_middle.astype(BF)
    d_proj_out[...] = d_proj
    for r, weight in enumerate(weights):
        d_heads = dot_t(d_proj, weight[...]).astype(BF)
        for h in range(heads):
            for i in range(copies):
                spot = ((place[1] ^ r) * heads + h) * copies + i
                sent[spot] = d_heads[:, h * HEAD : (h + 1) * HEAD]


def home_turn(place, terms, middle, second, grad, routes, side, weights, spans):
    args = (*terms, middle, second, grad, routes, side, *weights)
    tokens, width = middle.shape
    shapes = [
        jax.ShapeDtypeStruct((tokens, width), F32),
        jax.ShapeDtypeStruct((tokens, width), BF),
        jax.ShapeDtypeStruct((spans, tokens, HEAD), BF),
        jax.ShapeDtypeStruct((EXTRA, width), F32),
    ]
    return pl.pallas_call(
        functools.partial(turn_kernel, spans // HK, len(terms)),
        grid_spec=pltpu.PrefetchScalarGridSpec(
            num_scalar_prefetch=1,
            grid=(1,),
            in_specs=[whole(a) for a in args],
            out_specs=[whole(shape) for shape in shapes],
        ),
        out_shape=shapes,
        compiler_params=pltpu.CompilerParams(vmem_limit_bytes=VMEM),
        cost_estimate=time_of(7),
        name="home_turn",
    )(place, *args)


def out_grad_kernel(*refs):
    count = (len(refs) - 1) // 2
    total = t_dot(refs[0][...], refs[count][...])
    for r in range(1, count):
        total = total + t_dot(refs[r][...], refs[count + r][...])
    refs[-1][...] = total.astype(BF)


def out_grad(columns, d_projs):
    args = (*columns, *d_projs)
    shape = jax.ShapeDtypeStruct((columns[0].shape[1], d_projs[0].shape[1]), BF)
    return pl.pallas_call(
        out_grad_kernel,
        grid=(1,),
        in_specs=[whole(a) for a in args],
        out_specs=whole(shape),
        out_shape=shape,
        compiler_params=pltpu.CompilerParams(vmem_limit_bytes=VMEM),
        cost_estimate=time_of(4),
        name="out_grad",
    )(*args)


def stream_grad_kernel(
    copies, tokens, place, starts, sent, mixed, attended, log_norm, normed, small, d_mixed, out, d_kv
):
    here, shard = place[0], place[1]
    length, width = normed.shape
    shards = out.shape[0]
    shard_rows = width // shards
    d_kv[...] = jnp.zeros_like(d_kv)
    for first in range(0, length, QUERIES):
        keys = first + QUERIES
        at = slice(first, keys)
        allowed = visible(starts, here, copies, tokens, first, QUERIES, keys)
        k, v = mixed[:keys, HEAD : HEAD + HD], mixed[:keys, HEAD + HD :]
        for g in range(GROUP):
            columns = slice(g * HD, (g + 1) * HD)
            q, grad = mixed[at, columns], sent[at, columns]
            delta = jnp.sum(grad.astype(F32) * attended[at, columns], axis=1, keepdims=True)
            scores = dot_t(q, k) * SCALE
            probs = jnp.where(allowed, jnp.exp(scores - log_norm[at, g : g + 1]), 0.0)
            d_scores = (probs * (dot_t(grad, v) - delta)).astype(BF)
            d_mixed[at, columns] = (dot(d_scores, k) * SCALE).astype(BF)
            d_kv[0, :keys, :] += t_dot(d_scores, q)
            d_kv[1, :keys, :] += t_dot(probs.astype(BF), grad)
    d_mixed[:, HEAD : HEAD + HD] = (d_kv[0] * SCALE).astype(BF)
    d_mixed[:, HEAD + HD :] = d_kv[1].astype(BF)
    low = small[...].astype(BF)
    for f in range(shards):
        spot = shard ^ f
        columns = slice(f * shard_rows, (f + 1) * shard_rows)
        out[spot] = jnp.zeros(out.shape[1:], BF)
        out[spot, :shard_rows, :HEAD_COLS] = t_dot(normed[:, columns], d_mixed[...]).astype(BF)
        for i in range(0, shard_rows, LANES):
            size = min(LANES, shard_rows - i)
            row = shard_rows + i // LANES * EXTRA
            out[spot, row : row + EXTRA, :size] = low[:, f * shard_rows + i :][:, :size]


def stream_backward(place, starts, sent, mixed, attended, log_norm, normed, small, spans, shards):
    args = (sent, mixed, attended, log_norm, normed, small)
    length, width = normed.shape
    rows = width // shards
    shapes = [
        jax.ShapeDtypeStruct(mixed.shape, BF),
        jax.ShapeDtypeStruct((shards, rows + -(-rows // LANES) * EXTRA, HEAD_PACK), BF),
    ]
    return pl.pallas_call(
        functools.partial(stream_grad_kernel, spans // HK, length // spans),
        grid_spec=pltpu.PrefetchScalarGridSpec(
            num_scalar_prefetch=2,
            grid=(1,),
            in_specs=[whole(a) for a in args],
            out_specs=[whole(shape) for shape in shapes],
            scratch_shapes=[pltpu.VMEM((2, length, HD), F32)],
        ),
        out_shape=shapes,
        compiler_params=pltpu.CompilerParams(vmem_limit_bytes=VMEM),
        cost_estimate=time_of(17),
        name="stream_backward",
    )(place, starts, *args)


def home_grad_kernel(copies, place, d_home, tokens, side, d_middle, *refs):
    weight_refs, (d_tokens, weight, mixed, d_normed, sems) = refs[:-5], refs[-5:]
    shards = len(weight_refs)
    loading = [
        pltpu.make_async_copy(ref, weight.at[place[1] ^ r], sems.at[r])
        for r, ref in enumerate(weight_refs)
    ]
    for copy in loading:
        copy.start()
    for head in range(HK):
        part = d_home[head * copies]
        if copies > 1:
            part = part.astype(F32)
            for i in range(1, copies):
                part = part + d_home[head * copies + i].astype(F32)
            part = part.astype(BF)
        mixed[:, head * HEAD : (head + 1) * HEAD] = part[:, :HEAD]
        key = Q_COLS + head * HD
        mixed[:, key : key + HD] = part[:, HEAD : HEAD + HD]
        value = key + K_COLS
        mixed[:, value : value + HD] = part[:, HEAD + HD :]
    for copy in loading:
        copy.wait()
    rows = weight.shape[1]
    for f in range(shards):
        d_normed[:, f * rows : (f + 1) * rows] = dot_t(mixed[...], weight[f])
    x = tokens[...].astype(F32)
    gain = side[EXPERTS : EXPERTS + 1, :].astype(F32)
    d_x = rms_input_grad(x, rms_factor(x), gain, d_normed[...])
    d_tokens[...] = (d_middle[...] + d_x).astype(BF)


def home_backward(place, d_home, tokens, side, d_middle, weights, copies):
    args = (d_home, tokens, side, d_middle)
    count, width = tokens.shape
    shards = len(weights)
    columns = Q_COLS + 2 * K_COLS
    return pl.pallas_call(
        functools.partial(home_grad_kernel, copies),
        grid_spec=pltpu.PrefetchScalarGridSpec(
            num_scalar_prefetch=1,
            grid=(1,),
            in_specs=[whole(a) for a in args] + [anywhere()] * shards,
            out_specs=whole(tokens),
            scratch_shapes=[
                pltpu.VMEM((shards, width // shards, columns), BF),
                pltpu.VMEM((count, columns), BF),
                pltpu.VMEM((count, width), F32),
                pltpu.SemaphoreType.DMA((shards,)),
            ],
        ),
        out_shape=jax.ShapeDtypeStruct(tokens.shape, BF),
        compiler_params=pltpu.CompilerParams(vmem_limit_bytes=VMEM),
        cost_estimate=time_of(8),
        name="home_backward",
    )(place, *args, *weights)


def collect_kernel(copies, late, own_weight, d_qkv, d_out, small, d_gain):
    rows = own_weight.shape[0]
    for head in range(HK):
        part = late[head * copies, :rows, :HEAD_COLS].astype(F32)
        for i in range(1, copies):
            part = part + late[head * copies + i, :rows, :HEAD_COLS].astype(F32)
        d_qkv[:, head * HEAD : (head + 1) * HEAD] = part[:, :HEAD]
        key = Q_COLS + head * HD
        d_qkv[:, key : key + HD] = part[:, HEAD : HEAD + HD]
        value = key + K_COLS
        d_qkv[:, value : value + HD] = part[:, HEAD + HD :]
    for i in range(0, rows, LANES):
        row = rows + i // LANES * EXTRA
        size = min(LANES, rows - i)
        total = jnp.zeros((EXTRA, size), F32)
        for span in range(late.shape[0]):
            total = total + late[span, row : row + EXTRA, :size].astype(F32)
        small[:, i : i + size] = total
    spans, width = late.shape[0], d_out.shape[1]
    each = rows // spans
    first = late.shape[1] - width // HEAD_PACK * each
    for span in range(spans):
        for i in range(width // HEAD_PACK):
            columns = slice(i * HEAD_PACK, (i + 1) * HEAD_PACK)
            part = late[span, first + i * each : first + (i + 1) * each, :]
            d_out[span * each : (span + 1) * each, columns] = part.astype(F32)
    d_gain[...] = jnp.sum(d_qkv[...] * own_weight[...].astype(F32), axis=1, keepdims=True)


def collected(late, own_weight, width, copies):
    rows, columns = own_weight.shape
    shapes = [
        jax.ShapeDtypeStruct((rows, columns), F32),
        jax.ShapeDtypeStruct((rows, width), F32),
        jax.ShapeDtypeStruct((EXTRA, rows), F32),
        jax.ShapeDtypeStruct((rows, 1), F32),
    ]
    return pl.pallas_call(
        functools.partial(collect_kernel, copies),
        grid=(1,),
        in_specs=[whole(late), whole(own_weight)],
        out_specs=[whole(shape) for shape in shapes],
        out_shape=shapes,
        compiler_params=pltpu.CompilerParams(vmem_limit_bytes=VMEM),
        cost_estimate=time_of(7),
        name="collected",
    )(late, own_weight)


def picked_gates(second, router_t, chosen):
    logits = dot_t(router_t, second)
    ids = iota(logits.shape, 0)
    picked = (ids == chosen[0:1, :]) | (ids == chosen[1:2, :])
    logits = jnp.where(picked, logits, MASK_NEG)
    parts = jnp.where(picked, jnp.exp(logits - jnp.max(logits, axis=0, keepdims=True)), 0.0)
    return picked, parts / jnp.sum(parts, axis=0, keepdims=True)


def swiglu_grads(gate, up, d_hidden):
    sigma = 1.0 / (1.0 + jnp.exp(-gate))
    passed = gate * sigma
    d_gate = d_hidden * up * sigma * (1.0 + gate * (1.0 - sigma))
    return (passed * up).astype(BF), d_gate.astype(BF), (d_hidden * passed).astype(BF)


def near_kernel(shards, place, *refs):
    second, grads = refs[:shards], refs[shards : 2 * shards]
    router_t, w_gate, w_up, w_down = refs[2 * shards : 2 * shards + 4]
    branch_out = refs[2 * shards + 4 : 3 * shards + 4]
    back_out = refs[3 * shards + 4 : 4 * shards + 4]
    hot, rows, cots, d_outs, slot_gate, out_acc, row_acc, branch_acc, back_acc = refs[
        4 * shards + 4 :
    ]
    expert, tile = pl.program_id(0), pl.program_id(1)
    tokens = second[0].shape[0]
    width = second[0].shape[1]
    wanted = place[1] * pl.num_programs(0) + expert

    @pl.when(tile == 0)
    def _():
        before = (iota((tokens, tokens), 0) < iota((tokens, tokens), 1)).astype(BF)
        for f in range(shards):
            chosen = grads[f][tokens : tokens + EXTRA, :tokens].astype(F32).astype(jnp.int32)
            picked, gates = picked_gates(second[f][...], router_t[...], chosen)
            ranks = dot(picked.astype(BF), before)
            found = (iota(ranks.shape, 0) == wanted) & picked
            rank = jnp.sum(jnp.where(found, ranks + 1.0, 0.0), axis=0, keepdims=True)
            gate = jnp.sum(jnp.where(found, gates, 0.0), axis=0, keepdims=True)
            match = iota((CAP, tokens), 0).astype(F32) + 1.0 == rank
            one_hot = match.astype(BF)
            place = pl.ds(f * CAP, CAP)
            hot[f] = one_hot
            found_gate = jnp.sum(jnp.where(match, gate, 0.0), axis=1, keepdims=True)
            slot_gate[place, :] = jnp.broadcast_to(found_gate, (CAP, LANES))
            rows[place, :] = dot(one_hot, second[f][...]).astype(BF)
            cot = dot(one_hot, grads[f][:tokens, :])
            cots[place, :] = cot.astype(BF)
            d_outs[place, :] = (found_gate * cot).astype(BF)
        out_acc[...] = jnp.zeros_like(out_acc)
        row_acc[...] = jnp.zeros_like(row_acc)

    hidden, d_gate, d_up = swiglu_grads(
        dot(rows[...], w_gate[0]), dot(rows[...], w_up[0]), dot(d_outs[...], w_down[0])
    )
    out_acc[...] += dot_t(hidden, w_down[0])
    row_acc[...] += dot_t(d_gate, w_gate[0]) + dot_t(d_up, w_up[0])

    @pl.when(tile == pl.num_programs(1) - 1)
    def _():
        last = expert == pl.num_programs(0) - 1
        for f in range(shards):
            place = pl.ds(f * CAP, CAP)
            out = out_acc[place, :].astype(BF).astype(F32)
            d_gates = jnp.sum(cots[place, :].astype(F32) * out, axis=1, keepdims=True)
            gated = (slot_gate[place, 0:1] * out).astype(BF)
            lane = iota((CAP, LANES), 1)
            coarse = d_gates.astype(BF).astype(F32)
            extra = jnp.where(lane == wanted, coarse, 0.0)
            extra = extra + jnp.where(lane == EXPERTS + wanted, d_gates - coarse, 0.0)

            def add(acc, part, columns):
                @pl.when(expert == 0)
                def _():
                    acc[f, :, columns] = part

                @pl.when(expert > 0)
                def _():
                    acc[f, :, columns] += part

            add(branch_acc, t_dot(hot[f], gated), slice(0, width))
            add(back_acc, t_dot(hot[f], row_acc[place, :].astype(BF)), slice(0, width))
            add(back_acc, t_dot(hot[f], extra.astype(BF)), slice(width, width + LANES))

            @pl.when(last)
            def _():
                branch_out[f][...] = branch_acc[f].astype(BF)
                back_out[f][...] = back_acc[f].astype(BF)


def near_experts(place, second, grads, router_t, w_experts):
    shards = len(second)
    tokens, width = second[0].shape
    experts = w_experts.shape[0]
    slots = shards * CAP
    tiles = FF // TILE
    shapes = [jax.ShapeDtypeStruct((tokens, width), BF)] * shards
    shapes += [jax.ShapeDtypeStruct((tokens, width + LANES), BF)] * shards

    def weight(part):
        return pl.BlockSpec((1, width, TILE), lambda e, j, s: (e, 0, part * tiles + j))

    outs = pl.pallas_call(
        functools.partial(near_kernel, shards),
        grid_spec=pltpu.PrefetchScalarGridSpec(
            num_scalar_prefetch=1,
            grid=(experts, tiles),
            in_specs=[whole(a) for a in (*second, *grads, router_t)]
            + [weight(0), weight(1), weight(2)],
            out_specs=[whole(shape) for shape in shapes],
            scratch_shapes=[
                pltpu.VMEM((shards, CAP, tokens), BF),
                pltpu.VMEM((slots, width), BF),
                pltpu.VMEM((slots, width), BF),
                pltpu.VMEM((slots, width), BF),
                pltpu.VMEM((slots, LANES), F32),
                pltpu.VMEM((slots, width), F32),
                pltpu.VMEM((slots, width), F32),
                pltpu.VMEM((shards, tokens, width), F32),
                pltpu.VMEM((shards, tokens, width + LANES), F32),
            ],
        ),
        out_shape=shapes,
        compiler_params=pltpu.CompilerParams(vmem_limit_bytes=VMEM),
        cost_estimate=time_of(26),
        name="near_experts",
    )(place, *second, *grads, router_t, w_experts, w_experts, w_experts)
    return outs[:shards], outs[shards:]


def far_kernel(
    first_block,
    segment,
    per_line,
    place,
    router_t,
    second_ref,
    grads_ref,
    w_gate,
    w_up,
    w_down,
    out_ref,
    rows,
    d_outs,
    act,
    fetched_rows,
    fetched_grads,
    tile_out,
    counts,
    fetch_sem,
    store_sem,
):
    experts = rows.shape[0]
    expert, tile = pl.program_id(0), pl.program_id(1)
    tiles = pl.num_programs(1)
    step = expert * tiles + tile
    slot = lax.rem(step, 2)
    groups = segment // JOINED
    tokens, width = second_ref.shape[1:]
    size = JOINED * tokens
    window = JOINED * CAP + 16

    def stores(which, e, j):
        return [
            pltpu.make_async_copy(
                tile_out.at[which, i],
                out_ref.at[e, :, pl.ds(pl.multiple_of(i * FF + j * TILE, TILE), TILE)],
                store_sem.at[which, i],
            )
            for i in range(3)
        ]

    def fetches(which, g):
        copies = []
        for i in range(JOINED):
            block = first_block + g * JOINED + i
            turned = lax.rem(block, per_line) ^ (place[0] // 2)
            across = block // per_line * per_line + turned
            copies += [
                pltpu.make_async_copy(
                    second_ref.at[block], fetched_rows.at[which, i], fetch_sem.at[which, 0, i]
                ),
                pltpu.make_async_copy(
                    grads_ref.at[across], fetched_grads.at[which, i], fetch_sem.at[which, 1, i]
                ),
            ]
        return copies

    @pl.when(step == 0)
    def _():
        ahead = min(AHEAD, groups)
        for g in range(ahead):
            for copy in fetches(g, g):
                copy.start()
        before = (iota((size, size), 0) < iota((size, size), 1)).astype(BF)

        def gather(g, starts):
            which = lax.rem(g, AHEAD)
            for copy in fetches(which, g):
                copy.wait()
            second = fetched_rows[which].reshape(size, width)
            grads = fetched_grads[which, :, :tokens].reshape(size, width)
            chosen = jnp.concatenate(
                [fetched_grads[which, b, tokens : tokens + EXTRA, :LANES] for b in range(JOINED)],
                axis=1,
            )
            chosen = chosen.astype(F32).astype(jnp.int32)
            picked, gates = picked_gates(second, router_t[...], chosen)
            ranks = dot(picked.astype(BF), before)
            ids = iota(ranks.shape, 0)
            bases = [start // 16 * 16 for start in starts]
            matches, found_gates, ends = [], [], []
            for e in range(experts):
                found = (ids == place[1] * experts + e) & picked
                gate = jnp.sum(jnp.where(found, gates, 0.0), axis=0, keepdims=True)
                rank = jnp.sum(jnp.where(found, ranks + 1.0, 0.0), axis=0, keepdims=True)
                shift = (starts[e] - bases[e]).astype(F32)
                spot = jnp.where(rank > 0.0, rank + (shift - 1.0), -1.0)
                match = iota((window, size), 0).astype(F32) == spot
                matches.append(match.astype(BF))
                found_gates.append(
                    jnp.sum(jnp.where(match, gate, 0.0), axis=1, keepdims=True)
                )
                ends.append(starts[e] + jnp.sum((rank > 0.0).astype(jnp.int32)))
            one_hot = jnp.concatenate(matches, axis=0)
            new_rows = dot(one_hot, second).astype(BF)
            new_grads = (jnp.concatenate(found_gates, axis=0) * dot(one_hot, grads)).astype(BF)
            for e in range(experts):
                at = pl.ds(pl.multiple_of(bases[e], 16), 16)
                rest = pl.ds(pl.multiple_of(bases[e] + 16, 16), window - 16)
                held = iota((16, width), 0) < starts[e] - bases[e]
                for ref, new in ((rows, new_rows), (d_outs, new_grads)):
                    new = new[e * window : (e + 1) * window]
                    ref[e, at, :] = jnp.where(held, ref[e, at, :], new[:16])
                    ref[e, rest, :] = new[16:]

            @pl.when(g + AHEAD < groups)
            def _():
                for copy in fetches(which, g + AHEAD):
                    copy.start()

            return tuple(ends)

        ends = lax.fori_loop(0, groups, gather, (jnp.int32(0),) * experts)
        for e in range(experts):
            counts[e] = ends[e]
            spare = pl.ds(pl.multiple_of((ends[e] + 15) // 16 * 16, 16), CHUNK)
            rows[e, spare, :] = jnp.zeros((CHUNK, width), BF)
            d_outs[e, spare, :] = jnp.zeros((CHUNK, width), BF)

    chunks = jnp.maximum((counts[expert] + CHUNK - 1) // CHUNK, 1)

    @pl.loop(0, chunks)
    def _(i):
        at = pl.ds(pl.multiple_of(i * CHUNK, CHUNK), CHUNK)
        row, d_out = rows[expert, at, :], d_outs[expert, at, :]
        hidden, d_gate, d_up = swiglu_grads(
            dot(row, w_gate[0]), dot(row, w_up[0]), dot(d_out, w_down[0])
        )
        act[0, at, :] = d_gate
        act[1, at, :] = d_up
        act[2, at, :] = hidden

    @pl.when(step >= 2)
    def _():
        for copy in stores(slot, (step - 2) // tiles, lax.rem(step - 2, tiles)):
            copy.wait()

    most = act.shape[1] // CHUNK
    depths = [k for k in DEPTHS if k < most] + [most]
    for low, k in zip([0] + depths[:-1], depths):

        @pl.when((chunks > low) & (chunks <= k))
        def _():
            for extra in range(low + 1, k):

                @pl.when(chunks == extra)
                def _():
                    spare = slice(extra * CHUNK, k * CHUNK)
                    empty = jnp.zeros(((k - extra) * CHUNK, width), BF)
                    rows[expert, spare, :] = empty
                    d_outs[expert, spare, :] = empty
                    for i in range(3):
                        act[i, spare, :] = empty[:, :TILE]

            upto = k * CHUNK
            for i, left in enumerate((rows, rows, d_outs)):
                tile_out[slot, i] = t_dot(left[expert, :upto, :], act[i, :upto, :])

    for copy in stores(slot, expert, tile):
        copy.start()

    @pl.when(step == pl.num_programs(0) * tiles - 1)
    def _():
        for copy in stores(1 - slot, (step - 1) // tiles, lax.rem(step - 1, tiles)):
            copy.wait()
        for copy in stores(slot, expert, tile):
            copy.wait()


def far_weight_grads(first, segment, per_line, place, router_t, second, grads, w_experts):
    experts, width = w_experts.shape[:2]
    tokens = second.shape[1]
    tiles = FF // TILE
    most = segment * CAP
    held = most + CHUNK + 16

    def weight(part):
        return pl.BlockSpec((1, width, TILE), lambda e, j, s: (e, 0, part * tiles + j))

    return pl.pallas_call(
        functools.partial(far_kernel, first, segment, per_line),
        grid_spec=pltpu.PrefetchScalarGridSpec(
            num_scalar_prefetch=1,
            grid=(experts, tiles),
            in_specs=[
                whole(router_t),
                anywhere(),
                anywhere(),
                weight(0),
                weight(1),
                weight(2),
            ],
            out_specs=anywhere(),
            scratch_shapes=[
                pltpu.VMEM((experts, held, width), BF),
                pltpu.VMEM((experts, held, width), BF),
                pltpu.VMEM((3, most, TILE), BF),
                pltpu.VMEM((AHEAD, JOINED, tokens, width), BF),
                pltpu.VMEM((AHEAD, JOINED, tokens + EXTRA, width), BF),
                pltpu.VMEM((2, 3, width, TILE), F32),
                pltpu.SMEM((experts,), jnp.int32),
                pltpu.SemaphoreType.DMA((AHEAD, 2, JOINED)),
                pltpu.SemaphoreType.DMA((2, 3)),
            ],
        ),
        out_shape=jax.ShapeDtypeStruct((experts, width, 3 * FF), F32),
        compiler_params=pltpu.CompilerParams(vmem_limit_bytes=VMEM),
        cost_estimate=time_of(80),
        name="far_weight_grads",
    )(place, router_t, second, grads, w_experts, w_experts, w_experts)


def per_device(
    tokens,
    query_key_value_weight,
    output_weight,
    routing_weight,
    gain_attn,
    gain_moe,
    w_experts,
    doc_starts,
    routes,
    cotangent,
):
    spans = lax.axis_size("ctx")
    shards = lax.axis_size("fsdp")
    here = lax.axis_index("ctx")
    shard = lax.axis_index("fsdp")
    place = jnp.stack([here, shard]).astype(jnp.int32)
    x, grad = tokens[0], cotangent[0]
    tok_count, width = x.shape
    shard_rows = query_key_value_weight.shape[0]
    copies = spans // HK
    head = here // copies
    length = spans * tok_count
    blocks = spans * shards

    half = tok_count // 2
    first = jnp.stack(line_blocks(x[:half]))
    packed = jnp.concatenate(
        [
            lax.dynamic_slice_in_dim(query_key_value_weight, head * HEAD, HEAD, 1),
            lax.dynamic_slice_in_dim(query_key_value_weight, Q_COLS + head * HD, HD, 1),
            lax.dynamic_slice_in_dim(query_key_value_weight, Q_COLS + K_COLS + head * HD, HD, 1),
            routing_weight,
            gain_attn[:, None],
            gain_moe[:, None],
            jnp.zeros((shard_rows, HEAD_PACK - HEAD_COLS - EXPERTS - 2), BF),
        ],
        axis=1,
    )
    packed = gathered(after(packed, first), "fsdp")
    side = packed[:, HEAD_COLS : HEAD_COLS + EXTRA].T
    last = jnp.stack(line_blocks(after(x[half:], first)))
    swapped = exchanged(first, "ctx", 1)
    out_w = near_blocks(after(output_weight, first))

    payload = jnp.concatenate(
        [grad, jnp.pad(routes[0].T.astype(BF), ((0, EXTRA - 2), (0, width - tok_count)))]
    )
    grads_near = near_blocks(payload)
    pieces = [first, last, swapped, exchanged(last, "ctx", 1)]
    grads_all = all_blocks(after(payload, packed, pieces, out_w, grads_near))

    normed, mixed, attended_low, attended, log_norm = stream_attention(
        place, doc_starts[0], pieces, packed, side, copies
    )

    own = to_all(attended_low, "ctx").reshape(spans, tok_count, HEAD)
    middle, second, columns = home_forward(place, own, x, side, out_w, copies)
    second_near = near_blocks(second)
    second_line = line_blocks(second)

    branch, back = near_experts(place, second_near, grads_near, side, w_experts)
    back, second_line = after((back, second_line), grads_all)
    second_all = planes_of(jnp.stack(second_line))
    terms = near_terms(back)
    branch_terms = near_terms(branch)
    output = sum((term.astype(F32) for term in branch_terms), middle).astype(BF)

    d_middle, d_proj, sent, small = home_turn(
        place, terms, middle, second, grad, routes[0], side, out_w, spans
    )

    sent = to_all(sent.reshape(length, -1), "ctx")
    columns = [columns[0]] + [exchanged(columns[r], "fsdp", r) for r in range(1, shards)]
    d_out_w = out_grad(columns, near_blocks(d_proj))
    out_rows = to_all(d_out_w, "ctx").reshape(spans, -1, width)
    sent = after(sent, d_out_w, output)
    d_mixed, grads_out = stream_backward(
        place, doc_starts[0], sent, mixed, attended, log_norm, normed, small, spans, shards
    )
    late = near_terms([grads_out[r] for r in range(shards)])
    late = sum((term.astype(F32) for term in late[1:]), late[0].astype(F32)).astype(BF)
    out_rows = jnp.sum(out_rows.astype(F32), axis=0).astype(BF)
    out_rows = [out_rows[:, i : i + HEAD_PACK] for i in range(0, width, HEAD_PACK)]
    late = after(jnp.concatenate([late, *out_rows]), second_all)
    late = lax.all_gather(late, "ctx", axis=0)

    d_home = to_all(d_mixed, "ctx").reshape(spans, tok_count, HEAD_COLS)

    segment = min(blocks, SEGMENT)
    parts = [
        far_weight_grads(
            i, segment, spans // 2, place, side, second_all, grads_all, w_experts
        )
        for i in range(0, blocks, segment)
    ]
    d_w_experts = sum(parts[1:], parts[0])

    d_home = after(d_home, d_w_experts)
    d_tokens = home_backward(
        place, d_home, x, side, d_middle, near_direct(query_key_value_weight), copies
    )
    d_qkv_w, d_out_w, small, d_gain_attn = collected(
        late, query_key_value_weight, width, copies
    )
    return (
        output[None],
        d_tokens[None],
        d_qkv_w,
        d_out_w,
        small[:EXPERTS].T,
        d_gain_attn[:, 0] / gain_attn.astype(F32),
        small[EXPERTS],
        d_w_experts,
    )


def solution(mesh):
    placed = (
        P("fsdp", "ctx", None),
        P("fsdp", None),
        P("fsdp", None),
        P("fsdp", None),
        P("fsdp"),
        P("fsdp"),
        P("fsdp", None, None),
        P("fsdp", None),
        P("fsdp", "ctx", None),
        P("fsdp", "ctx", None),
    )
    return jax.shard_map(
        per_device,
        mesh=mesh,
        in_specs=placed,
        out_specs=(
            P("fsdp", "ctx", None),
            P("fsdp", "ctx", None),
            P("fsdp", None),
            P("fsdp", None),
            P("fsdp", None),
            P("fsdp"),
            P("fsdp"),
            P("fsdp", None, None),
        ),
        check_vma=False,
    )
```

```python
import functools

import jax
import jax.numpy as jnp
from jax import lax
from jax.experimental import pallas as pl
from jax.experimental.pallas import tpu as pltpu
from jax.sharding import PartitionSpec as P

HQ = 24
HK = 8
HD = 64
GROUP = HQ // HK
FF = 1024
EXPERTS = 8
CAP = 64
Q_COLS = HQ * HD
K_COLS = HK * HD
HEAD = GROUP * HD
HEAD_COLS = HEAD + 2 * HD
HEAD_PACK = 384
SCALE = HD**-0.5
EXTRA = 16
LANES = 128
TILE = 256
CHUNK = 256
SEGMENT = 32
JOINED = 2
AHEAD = 4
WIDE = 2
QUERIES = 256
DEPTHS = (1, 2, 3, 4, 5, 6, 7)
VMEM = 58 * 1024 * 1024

NORM_EPS = 1e-05
MASK_NEG = -1e30
BF = jnp.bfloat16
F32 = jnp.float32


def dot(a, b):
    return jnp.dot(a, b, preferred_element_type=F32)


def dot_t(a, b):
    return lax.dot_general(a, b, (((1,), (1,)), ((), ())), preferred_element_type=F32)


def t_dot(a, b):
    return lax.dot_general(a, b, (((0,), (0,)), ((), ())), preferred_element_type=F32)


def iota(shape, axis):
    return lax.broadcasted_iota(jnp.int32, shape, axis)


def rms_factor(values):
    return lax.rsqrt(jnp.mean(values * values, axis=-1, keepdims=True) + NORM_EPS)


def rms_input_grad(values, factor, gain_vec, incoming):
    inner = incoming * gain_vec
    cubed = factor * factor * factor
    return factor * inner - values * cubed * jnp.mean(inner * values, axis=-1, keepdims=True)


def to_all(value, axis):
    return lax.all_to_all(value, axis, 0, 0, tiled=True)


def gathered(value, axis):
    return lax.all_gather(value, axis, axis=0, tiled=True)


def exchanged(value, axis, distance):
    count = lax.axis_size(axis)
    return lax.ppermute(value, axis, [(i, i ^ distance) for i in range(count)])


def near_blocks(own):
    blocks = {0: own}
    distance = lax.axis_size("fsdp") // 2
    while distance:
        blocks.update({r ^ distance: exchanged(b, "fsdp", distance) for r, b in blocks.items()})
        distance //= 2
    return [blocks[r] for r in range(len(blocks))]


def near_terms(blocks):
    shards = lax.axis_size("fsdp")
    terms = {r: [block] for r, block in enumerate(blocks)}
    distance = 1

    def total(parts):
        if len(parts) == 1:
            return parts[0]
        return sum((part.astype(F32) for part in parts[1:]), parts[0].astype(F32)).astype(BF)

    while distance < shards:
        terms = {
            r: terms[r] + [exchanged(total(terms[r ^ distance]), "fsdp", distance)]
            for r in range(0, shards, 2 * distance)
        }
        distance *= 2
    return terms[0]


def line_blocks(own):
    return [own] + [exchanged(own, "ctx", d) for d in range(2, lax.axis_size("ctx"), 2)]


def near_direct(own):
    return [own] + [exchanged(own, "fsdp", r) for r in range(1, lax.axis_size("fsdp"))]


def planes_of(line):
    spans, shards = lax.axis_size("ctx"), lax.axis_size("fsdp")
    planes = [
        [(2 * pair + side) * shards + f for side in range(2) for f in range(shards)]
        for pair in range(spans // 2)
    ]
    return lax.all_gather(line, ("ctx", "fsdp"), axis=0, tiled=True, axis_index_groups=planes)


def whole_line(own):
    spans, shards = lax.axis_size("ctx"), lax.axis_size("fsdp")
    lines = [
        [(2 * pair + side) * shards + f for pair in range(spans // 2)]
        for side in range(2)
        for f in range(shards)
    ]
    return lax.all_gather(own, ("ctx", "fsdp"), axis=0, axis_index_groups=lines)


def after(values, *others):
    return lax.optimization_barrier((values, others))[0]


def time_of(microseconds):
    return pl.CostEstimate(flops=0, bytes_accessed=microseconds * 3_600_000, transcendentals=0)


def whole(array):
    shape = array.shape
    return pl.BlockSpec(shape, lambda *_: (0,) * len(shape))


def anywhere():
    return pl.BlockSpec(memory_space=pl.ANY)


def place_pieces(here, pieces, target, sems):
    copies = []
    for i, piece in enumerate(pieces):
        odd, last = divmod(i, 2)
        rows = piece.shape[1]
        for j in range(piece.shape[0]):
            copies.append(
                pltpu.make_async_copy(
                    piece.at[j],
                    target.at[here ^ (2 * j + odd), pl.ds(last * rows, rows)],
                    sems.at[i, j],
                )
            )
    for copy in copies:
        copy.start()
    return copies


def doc_of(starts, positions):
    found = jnp.zeros(positions.shape, jnp.int32)
    for i in range(starts.shape[0]):
        found = found + (positions >= starts[i]).astype(jnp.int32)
    return found


def visible(starts, here, copies, tokens, first, rows, keys):
    query = first + iota((rows, 1), 0)
    key = iota((1, keys), 1)
    allowed = (key <= query) & (doc_of(starts, key) == doc_of(starts, query))
    if copies > 1:
        allowed = allowed & (lax.rem(query // tokens, copies) == lax.rem(here, copies))
    return allowed


def stream_kernel(
    copies,
    place,
    starts,
    *refs,
):
    pieces, (weight, side) = refs[:4], refs[4:6]
    normed, mixed, attended_low, attended, log_norm, rows, piece_sems = refs[6:]
    here = place[0]
    spans, tokens, width = rows.shape
    length = spans * tokens
    copying = place_pieces(here, pieces, rows, piece_sems)
    for copy in copying:
        copy.wait()
    head_weight = weight[:, :HEAD_COLS]
    gain = side[EXPERTS : EXPERTS + 1, :].astype(F32)

    @pl.loop(0, spans)
    def _(span):
        x = rows[span].astype(F32)
        low = (x * rms_factor(x) * gain).astype(BF)
        at = pl.ds(pl.multiple_of(span * tokens, tokens), tokens)
        normed[at, :] = low
        mixed[at, :] = dot(low, head_weight).astype(BF)

    for first in range(0, length, QUERIES):
        keys = first + QUERIES
        at = slice(first, keys)
        allowed = visible(starts, here, copies, tokens, first, QUERIES, keys)
        for g in range(GROUP):
            columns = slice(g * HD, (g + 1) * HD)
            scores = dot_t(mixed[at, columns], mixed[:keys, HEAD : HEAD + HD]) * SCALE
            scores = jnp.where(allowed, scores, MASK_NEG)
            highest = jnp.max(scores, axis=1, keepdims=True)
            parts = jnp.where(allowed, jnp.exp(scores - highest), 0.0)
            total = jnp.sum(parts, axis=1, keepdims=True)
            total = jnp.where(total == 0.0, 1.0, total)
            log_norm[at, g : g + 1] = highest + jnp.log(total)
            result = dot((parts / total).astype(BF), mixed[:keys, HEAD + HD :])
            attended[at, columns] = result
            attended_low[at, columns] = result.astype(BF)


def stream_attention(place, starts, pieces, packed, side, copies):
    spans, tokens = 2 * pieces[0].shape[0], 2 * pieces[0].shape[1]
    width = pieces[0].shape[2]
    length = spans * tokens
    return pl.pallas_call(
        functools.partial(stream_kernel, copies),
        grid_spec=pltpu.PrefetchScalarGridSpec(
            num_scalar_prefetch=2,
            grid=(1,),
            in_specs=[anywhere()] * 4 + [whole(packed), whole(side)],
            out_specs=[
                pl.BlockSpec((length, columns), lambda *_: (0, 0))
                for columns in (width, HEAD_COLS, HEAD, HEAD, LANES)
            ],
            scratch_shapes=[
                pltpu.VMEM((spans, tokens, width), BF),
                pltpu.SemaphoreType.DMA((4, spans // 2)),
            ],
        ),
        out_shape=[
            jax.ShapeDtypeStruct((length, columns), kind)
            for columns, kind in (
                (width, BF),
                (HEAD_COLS, BF),
                (HEAD, BF),
                (HEAD, F32),
                (LANES, F32),
            )
        ],
        compiler_params=pltpu.CompilerParams(vmem_limit_bytes=VMEM),
        cost_estimate=time_of(16),
        name="stream_attention",
    )(place, starts, *pieces, packed, side)


def home_kernel(copies, place, own, tokens, side, *refs):
    weights, (middle, second, columns) = refs[:-3], refs[-3:]
    heads = HK // len(weights)
    total = tokens[...].astype(F32)
    for r, weight in enumerate(weights):
        first = (place[1] ^ r) * heads
        for h in range(heads):
            part = own[(first + h) * copies]
            for i in range(1, copies):
                part = part + own[(first + h) * copies + i]
            columns[r, :, h * HEAD : (h + 1) * HEAD] = part
            total = total + dot(part, weight[h * HEAD : (h + 1) * HEAD, :])
    middle[...] = total
    gain = side[EXPERTS + 1 : EXPERTS + 2, :].astype(F32)
    second[...] = (total * rms_factor(total) * gain).astype(BF)


def home_forward(place, own, tokens, side, weights, copies):
    args = (own, tokens, side, *weights)
    count, width = tokens.shape
    shapes = [
        jax.ShapeDtypeStruct(tokens.shape, F32),
        jax.ShapeDtypeStruct(tokens.shape, BF),
        jax.ShapeDtypeStruct((len(weights), count, width // len(weights)), BF),
    ]
    return pl.pallas_call(
        functools.partial(home_kernel, copies),
        grid_spec=pltpu.PrefetchScalarGridSpec(
            num_scalar_prefetch=1,
            grid=(1,),
            in_specs=[whole(a) for a in args],
            out_specs=[whole(shape) for shape in shapes],
        ),
        out_shape=shapes,
        compiler_params=pltpu.CompilerParams(vmem_limit_bytes=VMEM),
        cost_estimate=time_of(5),
        name="home_forward",
    )(place, *args)


def turn_kernel(copies, term_count, place, *refs):
    terms, refs = refs[:term_count], refs[term_count:]
    middle_ref, second_ref, grad, routes, side, *weights = refs[:-4]
    d_middle_out, d_proj_out, sent, small = refs[-4:]
    heads = HK // len(weights)
    width = middle_ref.shape[1]
    back = terms[0][...].astype(F32)
    for term in terms[1:]:
        back = back + term[...].astype(F32)
    middle, second = middle_ref[...], second_ref[...]
    d_gates = back[:, width : width + EXTRA]
    ids = iota(d_gates.shape, 1)
    d_gates = d_gates + back[:, width + EXPERTS : width + EXPERTS + EXTRA]
    picked = (ids == routes[:, 0:1]) | (ids == routes[:, 1:2])
    logits = jnp.where(picked, dot_t(second, side[...]), MASK_NEG)
    gates = jnp.where(picked, jnp.exp(logits - jnp.max(logits, axis=1, keepdims=True)), 0.0)
    gates = gates / jnp.sum(gates, axis=1, keepdims=True)
    d_gates = jnp.where(picked, d_gates, 0.0)
    d_picked = gates * (d_gates - jnp.sum(gates * d_gates, axis=1, keepdims=True))
    d_logits = d_picked.astype(BF)
    d_second = dot(d_logits, side[...]) + back[:, :width]
    factor = rms_factor(middle)
    small[...] = t_dot(d_logits, second)
    small[EXPERTS : EXPERTS + 1, :] = jnp.sum(d_second * middle * factor, axis=0, keepdims=True)
    gain = side[EXPERTS + 1 : EXPERTS + 2, :].astype(F32)
    d_middle = grad[...].astype(F32) + rms_input_grad(middle, factor, gain, d_second)
    d_middle_out[...] = d_middle
    d_proj = d_middle.astype(BF)
    d_proj_out[...] = d_proj
    for r, weight in enumerate(weights):
        d_heads = dot_t(d_proj, weight[...]).astype(BF)
        for h in range(heads):
            for i in range(copies):
                spot = ((place[1] ^ r) * heads + h) * copies + i
                sent[spot] = d_heads[:, h * HEAD : (h + 1) * HEAD]


def home_turn(place, terms, middle, second, grad, routes, side, weights, spans):
    args = (*terms, middle, second, grad, routes, side, *weights)
    tokens, width = middle.shape
    shapes = [
        jax.ShapeDtypeStruct((tokens, width), F32),
        jax.ShapeDtypeStruct((tokens, width), BF),
        jax.ShapeDtypeStruct((spans, tokens, HEAD), BF),
        jax.ShapeDtypeStruct((EXTRA, width), F32),
    ]
    return pl.pallas_call(
        functools.partial(turn_kernel, spans // HK, len(terms)),
        grid_spec=pltpu.PrefetchScalarGridSpec(
            num_scalar_prefetch=1,
            grid=(1,),
            in_specs=[whole(a) for a in args],
            out_specs=[whole(shape) for shape in shapes],
        ),
        out_shape=shapes,
        compiler_params=pltpu.CompilerParams(vmem_limit_bytes=VMEM),
        cost_estimate=time_of(7),
        name="home_turn",
    )(place, *args)


def out_grad_kernel(*refs):
    count = (len(refs) - 1) // 2
    total = t_dot(refs[0][...], refs[count][...])
    for r in range(1, count):
        total = total + t_dot(refs[r][...], refs[count + r][...])
    refs[-1][...] = total.astype(BF)


def out_grad(columns, d_projs):
    args = (*columns, *d_projs)
    shape = jax.ShapeDtypeStruct((columns[0].shape[1], d_projs[0].shape[1]), BF)
    return pl.pallas_call(
        out_grad_kernel,
        grid=(1,),
        in_specs=[whole(a) for a in args],
        out_specs=whole(shape),
        out_shape=shape,
        compiler_params=pltpu.CompilerParams(vmem_limit_bytes=VMEM),
        cost_estimate=time_of(4),
        name="out_grad",
    )(*args)


def stream_grad_kernel(
    copies, tokens, place, starts, sent, mixed, attended, log_norm, normed, small, d_mixed, out, d_kv
):
    here, shard = place[0], place[1]
    length, width = normed.shape
    shards = out.shape[0]
    shard_rows = width // shards
    d_kv[...] = jnp.zeros_like(d_kv)
    for first in range(0, length, QUERIES):
        keys = first + QUERIES
        at = slice(first, keys)
        allowed = visible(starts, here, copies, tokens, first, QUERIES, keys)
        k, v = mixed[:keys, HEAD : HEAD + HD], mixed[:keys, HEAD + HD :]
        for g in range(GROUP):
            columns = slice(g * HD, (g + 1) * HD)
            q, grad = mixed[at, columns], sent[at, columns]
            delta = jnp.sum(grad.astype(F32) * attended[at, columns], axis=1, keepdims=True)
            scores = dot_t(q, k) * SCALE
            probs = jnp.where(allowed, jnp.exp(scores - log_norm[at, g : g + 1]), 0.0)
            d_scores = (probs * (dot_t(grad, v) - delta)).astype(BF)
            d_mixed[at, columns] = (dot(d_scores, k) * SCALE).astype(BF)
            d_kv[0, :keys, :] += t_dot(d_scores, q)
            d_kv[1, :keys, :] += t_dot(probs.astype(BF), grad)
    d_mixed[:, HEAD : HEAD + HD] = (d_kv[0] * SCALE).astype(BF)
    d_mixed[:, HEAD + HD :] = d_kv[1].astype(BF)
    low = small[...].astype(BF)
    for f in range(shards):
        spot = shard ^ f
        columns = slice(f * shard_rows, (f + 1) * shard_rows)
        out[spot] = jnp.zeros(out.shape[1:], BF)
        out[spot, :shard_rows, :HEAD_COLS] = t_dot(normed[:, columns], d_mixed[...]).astype(BF)
        for i in range(0, shard_rows, LANES):
            size = min(LANES, shard_rows - i)
            row = shard_rows + i // LANES * EXTRA
            out[spot, row : row + EXTRA, :size] = low[:, f * shard_rows + i :][:, :size]


def stream_backward(place, starts, sent, mixed, attended, log_norm, normed, small, spans, shards):
    args = (sent, mixed, attended, log_norm, normed, small)
    length, width = normed.shape
    rows = width // shards
    shapes = [
        jax.ShapeDtypeStruct(mixed.shape, BF),
        jax.ShapeDtypeStruct((shards, rows + -(-rows // LANES) * EXTRA, HEAD_PACK), BF),
    ]
    return pl.pallas_call(
        functools.partial(stream_grad_kernel, spans // HK, length // spans),
        grid_spec=pltpu.PrefetchScalarGridSpec(
            num_scalar_prefetch=2,
            grid=(1,),
            in_specs=[whole(a) for a in args],
            out_specs=[whole(shape) for shape in shapes],
            scratch_shapes=[pltpu.VMEM((2, length, HD), F32)],
        ),
        out_shape=shapes,
        compiler_params=pltpu.CompilerParams(vmem_limit_bytes=VMEM),
        cost_estimate=time_of(17),
        name="stream_backward",
    )(place, starts, *args)


def home_grad_kernel(copies, place, d_home, tokens, side, d_middle, *refs):
    weight_refs, (d_tokens, weight, mixed, d_normed, sems) = refs[:-5], refs[-5:]
    shards = len(weight_refs)
    loading = [
        pltpu.make_async_copy(ref, weight.at[place[1] ^ r], sems.at[r])
        for r, ref in enumerate(weight_refs)
    ]
    for copy in loading:
        copy.start()
    for head in range(HK):
        part = d_home[head * copies]
        if copies > 1:
            part = part.astype(F32)
            for i in range(1, copies):
                part = part + d_home[head * copies + i].astype(F32)
            part = part.astype(BF)
        mixed[:, head * HEAD : (head + 1) * HEAD] = part[:, :HEAD]
        key = Q_COLS + head * HD
        mixed[:, key : key + HD] = part[:, HEAD : HEAD + HD]
        value = key + K_COLS
        mixed[:, value : value + HD] = part[:, HEAD + HD :]
    for copy in loading:
        copy.wait()
    rows = weight.shape[1]
    for f in range(shards):
        d_normed[:, f * rows : (f + 1) * rows] = dot_t(mixed[...], weight[f])
    x = tokens[...].astype(F32)
    gain = side[EXPERTS : EXPERTS + 1, :].astype(F32)
    d_x = rms_input_grad(x, rms_factor(x), gain, d_normed[...])
    d_tokens[...] = (d_middle[...] + d_x).astype(BF)


def home_backward(place, d_home, tokens, side, d_middle, weights, copies):
    args = (d_home, tokens, side, d_middle)
    count, width = tokens.shape
    shards = len(weights)
    columns = Q_COLS + 2 * K_COLS
    return pl.pallas_call(
        functools.partial(home_grad_kernel, copies),
        grid_spec=pltpu.PrefetchScalarGridSpec(
            num_scalar_prefetch=1,
            grid=(1,),
            in_specs=[whole(a) for a in args] + [anywhere()] * shards,
            out_specs=whole(tokens),
            scratch_shapes=[
                pltpu.VMEM((shards, width // shards, columns), BF),
                pltpu.VMEM((count, columns), BF),
                pltpu.VMEM((count, width), F32),
                pltpu.SemaphoreType.DMA((shards,)),
            ],
        ),
        out_shape=jax.ShapeDtypeStruct(tokens.shape, BF),
        compiler_params=pltpu.CompilerParams(vmem_limit_bytes=VMEM),
        cost_estimate=time_of(8),
        name="home_backward",
    )(place, *args, *weights)


def collect_kernel(copies, late, own_weight, d_qkv, d_out, small, d_gain):
    rows = own_weight.shape[0]
    for head in range(HK):
        part = late[head * copies, :rows, :HEAD_COLS].astype(F32)
        for i in range(1, copies):
            part = part + late[head * copies + i, :rows, :HEAD_COLS].astype(F32)
        d_qkv[:, head * HEAD : (head + 1) * HEAD] = part[:, :HEAD]
        key = Q_COLS + head * HD
        d_qkv[:, key : key + HD] = part[:, HEAD : HEAD + HD]
        value = key + K_COLS
        d_qkv[:, value : value + HD] = part[:, HEAD + HD :]
    for i in range(0, rows, LANES):
        row = rows + i // LANES * EXTRA
        size = min(LANES, rows - i)
        total = jnp.zeros((EXTRA, size), F32)
        for span in range(late.shape[0]):
            total = total + late[span, row : row + EXTRA, :size].astype(F32)
        small[:, i : i + size] = total
    spans, width = late.shape[0], d_out.shape[1]
    each = rows // spans
    first = late.shape[1] - width // HEAD_PACK * each
    for span in range(spans):
        for i in range(width // HEAD_PACK):
            columns = slice(i * HEAD_PACK, (i + 1) * HEAD_PACK)
            part = late[span, first + i * each : first + (i + 1) * each, :]
            d_out[span * each : (span + 1) * each, columns] = part.astype(F32)
    d_gain[...] = jnp.sum(d_qkv[...] * own_weight[...].astype(F32), axis=1, keepdims=True)


def collected(late, own_weight, width, copies):
    rows, columns = own_weight.shape
    shapes = [
        jax.ShapeDtypeStruct((rows, columns), F32),
        jax.ShapeDtypeStruct((rows, width), F32),
        jax.ShapeDtypeStruct((EXTRA, rows), F32),
        jax.ShapeDtypeStruct((rows, 1), F32),
    ]
    return pl.pallas_call(
        functools.partial(collect_kernel, copies),
        grid=(1,),
        in_specs=[whole(late), whole(own_weight)],
        out_specs=[whole(shape) for shape in shapes],
        out_shape=shapes,
        compiler_params=pltpu.CompilerParams(vmem_limit_bytes=VMEM),
        cost_estimate=time_of(7),
        name="collected",
    )(late, own_weight)


def picked_gates(second, router_t, chosen):
    logits = dot_t(router_t, second)
    ids = iota(logits.shape, 0)
    picked = (ids == chosen[0:1, :]) | (ids == chosen[1:2, :])
    logits = jnp.where(picked, logits, MASK_NEG)
    parts = jnp.where(picked, jnp.exp(logits - jnp.max(logits, axis=0, keepdims=True)), 0.0)
    return picked, parts / jnp.sum(parts, axis=0, keepdims=True)


def swiglu_grads(gate, up, d_hidden):
    sigma = 1.0 / (1.0 + jnp.exp(-gate))
    passed = gate * sigma
    d_gate = d_hidden * up * sigma * (1.0 + gate * (1.0 - sigma))
    return (passed * up).astype(BF), d_gate.astype(BF), (d_hidden * passed).astype(BF)


def near_kernel(shards, place, *refs):
    second, grads = refs[:shards], refs[shards : 2 * shards]
    router_t, w_gate, w_up, w_down = refs[2 * shards : 2 * shards + 4]
    branch_out = refs[2 * shards + 4 : 3 * shards + 4]
    back_out = refs[3 * shards + 4 : 4 * shards + 4]
    hot, rows, cots, d_outs, slot_gate, out_acc, row_acc, gated, backs = refs[4 * shards + 4 :]
    expert, tile = pl.program_id(0), pl.program_id(1)
    experts = rows.shape[0]
    tokens, width = second[0].shape

    @pl.when((expert == 0) & (tile == 0))
    def _():
        before = (iota((tokens, tokens), 0) < iota((tokens, tokens), 1)).astype(BF)
        for f in range(shards):
            chosen = grads[f][tokens : tokens + EXTRA, :tokens].astype(F32).astype(jnp.int32)
            picked, gates = picked_gates(second[f][...], router_t[...], chosen)
            ranks = dot(picked.astype(BF), before)
            matches, found_gates = [], []
            for e in range(experts):
                found = (iota(ranks.shape, 0) == place[1] * experts + e) & picked
                rank = jnp.sum(jnp.where(found, ranks + 1.0, 0.0), axis=0, keepdims=True)
                gate = jnp.sum(jnp.where(found, gates, 0.0), axis=0, keepdims=True)
                match = iota((CAP, tokens), 0).astype(F32) + 1.0 == rank
                matches.append(match.astype(BF))
                found_gates.append(jnp.sum(jnp.where(match, gate, 0.0), axis=1, keepdims=True))
            one_hot = jnp.concatenate(matches, axis=0)
            hot[f] = one_hot
            found_rows = dot(one_hot, second[f][...]).astype(BF)
            found_cots = dot(one_hot, grads[f][:tokens, :])
            found_outs = (jnp.concatenate(found_gates, axis=0) * found_cots).astype(BF)
            found_cots = found_cots.astype(BF)
            spot = pl.ds(f * CAP, CAP)
            for e in range(experts):
                part = slice(e * CAP, (e + 1) * CAP)
                rows[e, spot, :] = found_rows[part]
                cots[e, spot, :] = found_cots[part]
                d_outs[e, spot, :] = found_outs[part]
                slot_gate[e, spot, :] = jnp.broadcast_to(found_gates[e], (CAP, LANES))

    row = rows[expert]
    hidden, d_gate, d_up = swiglu_grads(
        dot(row, w_gate[0]), dot(row, w_up[0]), dot(d_outs[expert], w_down[0])
    )
    out_part = dot_t(hidden, w_down[0])
    row_part = dot_t(d_gate, w_gate[0]) + dot_t(d_up, w_up[0])

    @pl.when(tile == 0)
    def _():
        out_acc[...] = out_part
        row_acc[...] = row_part

    @pl.when(tile > 0)
    def _():
        out_acc[...] += out_part
        row_acc[...] += row_part

    @pl.when(tile == pl.num_programs(1) - 1)
    def _():
        out = out_acc[...].astype(BF).astype(F32)
        d_gates = jnp.sum(cots[expert].astype(F32) * out, axis=1, keepdims=True)
        weighted = (slot_gate[expert, :, 0:1] * out).astype(BF)
        lane = iota((shards * CAP, LANES), 1)
        wanted = place[1] * experts + expert
        coarse = d_gates.astype(BF).astype(F32)
        extra = jnp.where(lane == wanted, coarse, 0.0)
        extra = extra + jnp.where(lane == EXPERTS + wanted, d_gates - coarse, 0.0)
        extra = extra.astype(BF)
        d_rows = row_acc[...].astype(BF)
        at = pl.ds(pl.multiple_of(expert * CAP, CAP), CAP)
        for f in range(shards):
            part = slice(f * CAP, (f + 1) * CAP)
            gated[f, at, :] = weighted[part]
            backs[f, at, :width] = d_rows[part]
            backs[f, at, width:] = extra[part]

        @pl.when(expert == experts - 1)
        def _():
            for f in range(shards):
                branch_out[f][...] = t_dot(hot[f], gated[f]).astype(BF)
                back_out[f][...] = t_dot(hot[f], backs[f]).astype(BF)


def near_experts(place, second, grads, router_t, w_experts):
    shards = len(second)
    tokens, width = second[0].shape
    experts = w_experts.shape[0]
    slots = shards * CAP
    tiles = FF // TILE
    shapes = [jax.ShapeDtypeStruct((tokens, width), BF)] * shards
    shapes += [jax.ShapeDtypeStruct((tokens, width + LANES), BF)] * shards

    def weight(part):
        return pl.BlockSpec((1, width, TILE), lambda e, j, s: (e, 0, part * tiles + j))

    outs = pl.pallas_call(
        functools.partial(near_kernel, shards),
        grid_spec=pltpu.PrefetchScalarGridSpec(
            num_scalar_prefetch=1,
            grid=(experts, tiles),
            in_specs=[whole(a) for a in (*second, *grads, router_t)]
            + [weight(0), weight(1), weight(2)],
            out_specs=[whole(shape) for shape in shapes],
            scratch_shapes=[
                pltpu.VMEM((shards, experts * CAP, tokens), BF),
                pltpu.VMEM((experts, slots, width), BF),
                pltpu.VMEM((experts, slots, width), BF),
                pltpu.VMEM((experts, slots, width), BF),
                pltpu.VMEM((experts, slots, LANES), F32),
                pltpu.VMEM((slots, width), F32),
                pltpu.VMEM((slots, width), F32),
                pltpu.VMEM((shards, experts * CAP, width), BF),
                pltpu.VMEM((shards, experts * CAP, width + LANES), BF),
            ],
        ),
        out_shape=shapes,
        compiler_params=pltpu.CompilerParams(vmem_limit_bytes=VMEM),
        cost_estimate=time_of(26),
        name="near_experts",
    )(place, *second, *grads, router_t, w_experts, w_experts, w_experts)
    return outs[:shards], outs[shards:]


def grads_block(block, per_line, here):
    return block // per_line * per_line + (lax.rem(block, per_line) ^ (here // 2))


def prepare_kernel(
    first_block,
    per_line,
    place,
    grads_ref,
    w_down,
    raw,
    cots_ref,
    spots,
    chosen_out,
    starts_out,
    cots,
    fetched,
    fetch_sem,
    store_sem,
):
    experts = cots.shape[0]
    expert, tile = pl.program_id(0), pl.program_id(1)
    step = expert * pl.num_programs(1) + tile
    groups, _, size = chosen_out.shape
    tokens = size // JOINED
    width = cots.shape[2]
    window = JOINED * CAP + 16
    stores = [
        pltpu.make_async_copy(cots.at[e], cots_ref.at[e], store_sem.at[e]) for e in range(experts)
    ]

    def fetches(which, g):
        return [
            pltpu.make_async_copy(
                grads_ref.at[grads_block(first_block + g * JOINED + i, per_line, place[0])],
                fetched.at[which, i],
                fetch_sem.at[which, i],
            )
            for i in range(JOINED)
        ]

    @pl.when(step == 0)
    def _():
        for g in range(min(AHEAD, groups)):
            for copy in fetches(g, g):
                copy.start()
        before = (iota((size, size), 0) < iota((size, size), 1)).astype(BF)

        def gather(g, starts):
            which = lax.rem(g, AHEAD)
            for copy in fetches(which, g):
                copy.wait()
            grads = fetched[which, :, :tokens].reshape(size, width)
            chosen = jnp.concatenate(
                [fetched[which, i, tokens : tokens + EXTRA, :tokens] for i in range(JOINED)], axis=1
            )
            chosen = chosen.astype(F32).astype(jnp.int32)
            chosen_out[g] = chosen
            ids = iota(chosen.shape, 0)
            picked = (ids == chosen[0:1, :]) | (ids == chosen[1:2, :])
            ranks = dot(picked.astype(BF), before)
            bases = [start // 16 * 16 for start in starts]
            matches, ends = [], []
            for e in range(experts):
                found = (ids == place[1] * experts + e) & picked
                rank = jnp.sum(jnp.where(found, ranks + 1.0, 0.0), axis=0, keepdims=True)
                shift = (starts[e] - bases[e]).astype(F32)
                spot = jnp.where(rank > 0.0, rank + (shift - 1.0), -1.0)
                spots[e, pl.ds(g, 1), :] = spot
                starts_out[e, g] = starts[e]
                matches.append((iota((window, size), 0).astype(F32) == spot).astype(BF))
                ends.append(starts[e] + jnp.sum((rank > 0.0).astype(jnp.int32)))
            new = dot(jnp.concatenate(matches, axis=0), grads).astype(BF)
            for e in range(experts):
                at = pl.ds(pl.multiple_of(bases[e], 16), 16)
                rest = pl.ds(pl.multiple_of(bases[e] + 16, 16), window - 16)
                held = iota((16, width), 0) < starts[e] - bases[e]
                part = new[e * window : (e + 1) * window]
                cots[e, at, :] = jnp.where(held, cots[e, at, :], part[:16])
                cots[e, rest, :] = part[16:]

            @pl.when(g + AHEAD < groups)
            def _():
                for copy in fetches(which, g + AHEAD):
                    copy.start()

            return tuple(ends)

        ends = lax.fori_loop(0, groups, gather, (jnp.int32(0),) * experts)
        for e in range(experts):
            starts_out[e, groups] = ends[e]
            spare = pl.ds(pl.multiple_of((ends[e] + 15) // 16 * 16, 16), CHUNK)
            cots[e, spare, :] = jnp.zeros((CHUNK, width), BF)
            stores[e].start()

    @pl.loop(0, (starts_out[expert, groups] + CHUNK - 1) // CHUNK)
    def _(i):
        at = pl.ds(pl.multiple_of(i * CHUNK, CHUNK), CHUNK)
        raw[0, at, :] = dot(cots[expert, at, :], w_down[0]).astype(BF)

    @pl.when(step == experts * pl.num_programs(1) - 1)
    def _():
        for copy in stores:
            copy.wait()


def far_prepare(first, segment, per_line, place, grads, w_experts):
    experts, width = w_experts.shape[:2]
    tokens = grads.shape[1] - EXTRA
    tiles = FF // TILE
    groups = segment // JOINED
    most = segment * CAP
    held = most + CHUNK + 16
    shapes = [
        jax.ShapeDtypeStruct((experts, most, FF), BF),
        jax.ShapeDtypeStruct((experts, held, width), BF),
        jax.ShapeDtypeStruct((experts, groups, JOINED * tokens), F32),
        jax.ShapeDtypeStruct((groups, EXTRA, JOINED * tokens), jnp.int32),
        jax.ShapeDtypeStruct((experts, groups + 1), jnp.int32),
    ]
    return pl.pallas_call(
        functools.partial(prepare_kernel, first, per_line),
        grid_spec=pltpu.PrefetchScalarGridSpec(
            num_scalar_prefetch=1,
            grid=(experts, tiles),
            in_specs=[
                anywhere(),
                pl.BlockSpec((1, width, TILE), lambda e, j, s: (e, 0, 2 * tiles + j)),
            ],
            out_specs=[
                pl.BlockSpec((1, most, TILE), lambda e, j, s: (e, 0, j)),
                anywhere(),
                whole(shapes[2]),
                whole(shapes[3]),
                pl.BlockSpec(memory_space=pltpu.SMEM),
            ],
            scratch_shapes=[
                pltpu.VMEM((experts, held, width), BF),
                pltpu.VMEM((AHEAD, JOINED, tokens + EXTRA, width), BF),
                pltpu.SemaphoreType.DMA((AHEAD, JOINED)),
                pltpu.SemaphoreType.DMA((experts,)),
            ],
        ),
        out_shape=shapes,
        compiler_params=pltpu.CompilerParams(vmem_limit_bytes=VMEM),
        cost_estimate=time_of(28),
        name="far_weight_prepare",
    )(place, grads, w_experts)


def far_kernel(
    first_block,
    place,
    starts,
    chosen,
    spots,
    router_t,
    second_ref,
    cots_ref,
    raw,
    w_gate,
    w_up,
    out_ref,
    rows,
    cots,
    slot_gate,
    act,
    fetched,
    tile_out,
    fetch_sem,
    load_sem,
    store_sem,
):
    experts = rows.shape[0]
    expert, tile = pl.program_id(0), pl.program_id(1)
    tiles = pl.num_programs(1)
    step = expert * tiles + tile
    slot = lax.rem(step, 2)
    groups, _, size = chosen.shape
    width = rows.shape[2]
    window = JOINED * CAP + 16

    def stores(which, e, j):
        return [
            pltpu.make_async_copy(
                tile_out.at[which, i],
                out_ref.at[e, :, pl.ds(pl.multiple_of(i * FF + j * TILE, TILE), TILE)],
                store_sem.at[which, i],
            )
            for i in range(3)
        ]

    def fetch(which, g):
        return pltpu.make_async_copy(
            second_ref.at[pl.ds(first_block + g * JOINED, JOINED)],
            fetched.at[which],
            fetch_sem.at[which],
        )

    @pl.when(step == 0)
    def _():
        for g in range(min(AHEAD, groups)):
            fetch(g, g).start()
        loads = [
            pltpu.make_async_copy(cots_ref.at[e], cots.at[e], load_sem.at[e])
            for e in range(experts)
        ]
        for copy in loads:
            copy.start()

        @pl.loop(0, groups)
        def _(g):
            which = lax.rem(g, AHEAD)
            fetch(which, g).wait()
            second = fetched[which].reshape(size, width)
            picked, gates = picked_gates(second, router_t[...], chosen[g])
            matches, found_gates = [], []
            for e in range(experts):
                found = (iota(gates.shape, 0) == place[1] * experts + e) & picked
                gate = jnp.sum(jnp.where(found, gates, 0.0), axis=0, keepdims=True)
                match = iota((window, size), 0).astype(F32) == spots[e, pl.ds(g, 1), :]
                matches.append(match.astype(BF))
                found_gates.append(jnp.sum(jnp.where(match, gate, 0.0), axis=1, keepdims=True))
            new = dot(jnp.concatenate(matches, axis=0), second).astype(BF)
            for e in range(experts):
                base = starts[e, g] // 16 * 16
                at = pl.ds(pl.multiple_of(base, 16), 16)
                rest = pl.ds(pl.multiple_of(base + 16, 16), window - 16)
                part = new[e * window : (e + 1) * window]
                found_gate = jnp.broadcast_to(found_gates[e], (window, LANES))
                kept = starts[e, g] - base
                rows[e, at, :] = jnp.where(iota((16, width), 0) < kept, rows[e, at, :], part[:16])
                rows[e, rest, :] = part[16:]
                slot_gate[e, at, :] = jnp.where(
                    iota((16, LANES), 0) < kept, slot_gate[e, at, :], found_gate[:16]
                )
                slot_gate[e, rest, :] = found_gate[16:]

            @pl.when(g + AHEAD < groups)
            def _():
                fetch(which, g + AHEAD).start()

        for e in range(experts):
            spare = pl.ds(pl.multiple_of((starts[e, groups] + 15) // 16 * 16, 16), CHUNK)
            rows[e, spare, :] = jnp.zeros((CHUNK, width), BF)
            slot_gate[e, spare, :] = jnp.zeros((CHUNK, LANES), F32)
        for copy in loads:
            copy.wait()

    used = (starts[expert, groups] + CHUNK - 1) // CHUNK
    chunks = jnp.maximum(used, 1)

    def recompute(first, size):
        at = pl.ds(pl.multiple_of(first, CHUNK), size)
        row, weight = rows[expert, at, :], slot_gate[expert, at, 0:1]
        gate, up = dot(row, w_gate[0]), dot(row, w_up[0])
        d_hidden = weight * raw[0, at, :].astype(F32)
        sigma = 1.0 / (1.0 + jnp.exp(-gate))
        passed = gate * sigma
        act[0, at, :] = (d_hidden * up * sigma * (1.0 + gate * (1.0 - sigma))).astype(BF)
        act[1, at, :] = (d_hidden * passed).astype(BF)
        act[2, at, :] = (weight * (passed * up)).astype(BF)

    @pl.loop(0, used // WIDE)
    def _(i):
        recompute(i * (WIDE * CHUNK), WIDE * CHUNK)

    @pl.loop(used // WIDE * WIDE, used)
    def _(i):
        recompute(i * CHUNK, CHUNK)

    @pl.when(used == 0)
    def _():
        for i in range(3):
            act[i, :CHUNK, :] = jnp.zeros((CHUNK, TILE), BF)

    @pl.when(step >= 2)
    def _():
        for copy in stores(slot, (step - 2) // tiles, lax.rem(step - 2, tiles)):
            copy.wait()

    most = act.shape[1] // CHUNK
    depths = [k for k in DEPTHS if k < most] + [most]
    for low, k in zip([0] + depths[:-1], depths):

        @pl.when((chunks > low) & (chunks <= k))
        def _():
            for extra in range(low + 1, k):

                @pl.when(chunks == extra)
                def _():
                    spare = slice(extra * CHUNK, k * CHUNK)
                    empty = jnp.zeros(((k - extra) * CHUNK, width), BF)
                    rows[expert, spare, :] = empty
                    cots[expert, spare, :] = empty
                    for i in range(3):
                        act[i, spare, :] = empty[:, :TILE]

            upto = k * CHUNK
            for i, left in enumerate((rows, rows, cots)):
                tile_out[slot, i] = t_dot(left[expert, :upto, :], act[i, :upto, :])

    for copy in stores(slot, expert, tile):
        copy.start()

    @pl.when(step == pl.num_programs(0) * tiles - 1)
    def _():
        for copy in stores(1 - slot, (step - 1) // tiles, lax.rem(step - 1, tiles)):
            copy.wait()
        for copy in stores(slot, expert, tile):
            copy.wait()


def far_weight_grads(first, segment, place, router_t, second, prepared, w_experts):
    raw, cots, spots, chosen, starts = prepared
    experts, width = w_experts.shape[:2]
    tokens = second.shape[1]
    tiles = FF // TILE
    most = segment * CAP
    held = most + CHUNK + 16

    def weight(part):
        return pl.BlockSpec((1, width, TILE), lambda e, j, s: (e, 0, part * tiles + j))

    return pl.pallas_call(
        functools.partial(far_kernel, first),
        grid_spec=pltpu.PrefetchScalarGridSpec(
            num_scalar_prefetch=1,
            grid=(experts, tiles),
            in_specs=[
                pl.BlockSpec(memory_space=pltpu.SMEM),
                whole(chosen),
                whole(spots),
                whole(router_t),
                anywhere(),
                anywhere(),
                pl.BlockSpec((1, most, TILE), lambda e, j, s: (e, 0, j)),
                weight(0),
                weight(1),
            ],
            out_specs=anywhere(),
            scratch_shapes=[
                pltpu.VMEM((experts, held, width), BF),
                pltpu.VMEM((experts, held, width), BF),
                pltpu.VMEM((experts, held, LANES), F32),
                pltpu.VMEM((3, most, TILE), BF),
                pltpu.VMEM((AHEAD, JOINED, tokens, width), BF),
                pltpu.VMEM((2, 3, width, TILE), F32),
                pltpu.SemaphoreType.DMA((AHEAD,)),
                pltpu.SemaphoreType.DMA((experts,)),
                pltpu.SemaphoreType.DMA((2, 3)),
            ],
        ),
        out_shape=jax.ShapeDtypeStruct((experts, width, 3 * FF), F32),
        compiler_params=pltpu.CompilerParams(vmem_limit_bytes=VMEM),
        cost_estimate=time_of(75),
        name="far_weight_grads",
    )(place, starts, chosen, spots, router_t, second, cots, raw, w_experts, w_experts)


def per_device(
    tokens,
    query_key_value_weight,
    output_weight,
    routing_weight,
    gain_attn,
    gain_moe,
    w_experts,
    doc_starts,
    routes,
    cotangent,
):
    spans = lax.axis_size("ctx")
    shards = lax.axis_size("fsdp")
    here = lax.axis_index("ctx")
    shard = lax.axis_index("fsdp")
    place = jnp.stack([here, shard]).astype(jnp.int32)
    x, grad = tokens[0], cotangent[0]
    tok_count, width = x.shape
    shard_rows = query_key_value_weight.shape[0]
    copies = spans // HK
    head = here // copies
    length = spans * tok_count
    blocks = spans * shards

    half = tok_count // 2
    packed = jnp.concatenate(
        [
            lax.dynamic_slice_in_dim(query_key_value_weight, head * HEAD, HEAD, 1),
            lax.dynamic_slice_in_dim(query_key_value_weight, Q_COLS + head * HD, HD, 1),
            lax.dynamic_slice_in_dim(query_key_value_weight, Q_COLS + K_COLS + head * HD, HD, 1),
            routing_weight,
            gain_attn[:, None],
            gain_moe[:, None],
            jnp.zeros((shard_rows, HEAD_PACK - HEAD_COLS - EXPERTS - 2), BF),
        ],
        axis=1,
    )
    payload = jnp.concatenate(
        [grad, jnp.pad(routes[0].T.astype(BF), ((0, EXTRA - 2), (0, width - tok_count)))]
    )
    grads_near = near_blocks(payload)
    first = jnp.stack(after(line_blocks(x[:half]), packed, grads_near[shards // 2]))
    packed = gathered(after(packed, first), "fsdp")
    side = packed[:, HEAD_COLS : HEAD_COLS + EXTRA].T
    swapped = exchanged(first, "ctx", 1)

    out_w = near_blocks(output_weight)
    last = line_blocks(after(x[half:], first))
    last = jnp.stack(after(last, swapped, out_w[shards // 2]))
    pieces = [first, last, swapped, exchanged(last, "ctx", 1)]
    grads_line = whole_line(after(payload, packed, last))

    normed, mixed, attended_low, attended, log_norm = stream_attention(
        place, doc_starts[0], pieces, packed, side, copies
    )

    grads_all = planes_of(after(grads_line, attended_low))
    own = to_all(attended_low, "ctx").reshape(spans, tok_count, HEAD)
    middle, second, columns = home_forward(place, own, x, side, out_w, copies)
    second_near = near_blocks(second)
    second_line = line_blocks(second)

    branch, back = near_experts(place, second_near, grads_near, side, w_experts)
    terms = near_terms(back)
    branch_terms = near_terms(branch)
    second_all = planes_of(jnp.stack(after(second_line, grads_all, terms)))

    d_middle, d_proj, sent, small = home_turn(
        place, terms, middle, second, grad, routes[0], side, out_w, spans
    )

    sent = to_all(sent.reshape(length, -1), "ctx")
    columns = [columns[0]] + [exchanged(columns[r], "fsdp", r) for r in range(1, shards)]
    d_mixed, grads_out = stream_backward(
        place, doc_starts[0], sent, mixed, attended, log_norm, normed, small, spans, shards
    )
    d_out_w = out_grad(after(columns, d_mixed), near_blocks(d_proj))
    out_rows = to_all(d_out_w, "ctx").reshape(spans, -1, width)
    late = near_terms([grads_out[r] for r in range(shards)])
    segment = min(blocks, SEGMENT)
    ready = after(grads_all, d_out_w, late[1])
    prepared = [
        far_prepare(i, segment, spans // 2, place, ready, w_experts)
        for i in range(0, blocks, segment)
    ]
    d_home = to_all(d_mixed, "ctx").reshape(spans, tok_count, HEAD_COLS)
    late, out_rows, branch_terms, d_home = after(
        (late, out_rows, branch_terms, d_home), prepared
    )
    output = sum((term.astype(F32) for term in branch_terms), middle).astype(BF)
    late = sum((term.astype(F32) for term in late[1:]), late[0].astype(F32)).astype(BF)
    out_rows = jnp.sum(out_rows.astype(F32), axis=0).astype(BF)
    out_rows = [out_rows[:, i : i + HEAD_PACK] for i in range(0, width, HEAD_PACK)]
    late = after(jnp.concatenate([late, *out_rows]), second_all, output)
    later_qkv = after(query_key_value_weight, late)
    late = lax.all_gather(late, "ctx", axis=0)

    parts = [
        far_weight_grads(
            i * segment, segment, place, side, second_all, prepared[i], w_experts
        )
        for i in range(blocks // segment)
    ]
    d_w_experts = sum(parts[1:], parts[0])


    d_home = after(d_home, d_w_experts)
    d_tokens = home_backward(
        place, d_home, x, side, d_middle, near_direct(later_qkv), copies
    )
    d_qkv_w, d_out_w, small, d_gain_attn = collected(
        late, query_key_value_weight, width, copies
    )
    return (
        output[None],
        d_tokens[None],
        d_qkv_w,
        d_out_w,
        small[:EXPERTS].T,
        d_gain_attn[:, 0] / gain_attn.astype(F32),
        small[EXPERTS],
        d_w_experts,
    )


def solution(mesh):
    placed = (
        P("fsdp", "ctx", None),
        P("fsdp", None),
        P("fsdp", None),
        P("fsdp", None),
        P("fsdp"),
        P("fsdp"),
        P("fsdp", None, None),
        P("fsdp", None),
        P("fsdp", "ctx", None),
        P("fsdp", "ctx", None),
    )
    return jax.shard_map(
        per_device,
        mesh=mesh,
        in_specs=placed,
        out_specs=(
            P("fsdp", "ctx", None),
            P("fsdp", "ctx", None),
            P("fsdp", None),
            P("fsdp", None),
            P("fsdp", None),
            P("fsdp"),
            P("fsdp"),
            P("fsdp", None, None),
        ),
        check_vma=False,
    )
```
